32 devices in a mesh: tile: 8 (over y, x, core), date: 4 (over z).
Axes of the slice: x: 2, y: 2, z: 4, core: 2. Of those that a mesh axis runs over, the one named last changes fastest.
Arguments:
- secondary: bfloat16 [4, 2, 3072, 1024], P('date', None, 'tile'), may hold values from -6 to 6
- primary: bfloat16 [2, 3072, 1024], P(None, 'tile', 'date'), may hold values from -6 to 6
- margin_mask: int32 [3072], P('tile'), may hold values from 0 to 1, as said below
- az_off: int32 [4, 8], P('date', 'tile'), may hold values from -16 to 16
- rg_off: int32 [4, 8], P('date', 'tile'), may hold values from -16 to 16
- az_frac: float32 [4, 8], P('date', 'tile'), may hold values from 0 to 1
- rg_frac: float32 [4, 8], P('date', 'tile'), may hold values from 0 to 1
Outputs:
- looks: float32 [4, 2, 1536, 128], P('date', None, 'tile')
The draws below stay inside these ranges and needn't reach their ends.
Inputs may be any that keep to these rules, and one draw needn't show every extreme that they name: `margin_mask`: ones lie only in the last 64 rows of each tile of 384 rows, and the last row of every tile is 1.
All inputs are finite; a program needn't handle non-finite values.
Results may differ from the reference program's by a relative error of at most 0.017.
Values may be sent and summed in bfloat16 or wider, within the bound.
No kernel may reach another device: no remote copies, remote signals or barrier semaphores. Data moves between devices by JAX's collectives and lax.ppermute only.
A program may use at most 128 MiB of HBM per device.

```python
import jax
import jax.numpy as jnp
from jax import lax

ROWS = 3072
COLS = 1024
KA = 16
KR = 16
LAG = 64
LA = 2
LR = 8
DATES = 4
TILES = 8
ROW_DEV = 384


def draw_margin_mask(key, part):
    random_bits = jax.random.randint(jax.random.fold_in(key, 11), (ROWS,), 0, 2)
    position = jnp.arange(ROWS, dtype=jnp.int32) % ROW_DEV
    near_end = position >= ROW_DEV - LAG
    last_row = position == ROW_DEV - 1
    chosen = near_end & ((random_bits == 1) | last_row)
    return jnp.where(chosen, 1, 0).astype(jnp.int32)


def plant(values, stream_key, smallest, top_value):
    spot = [jax.random.randint(jax.random.fold_in(stream_key, axis), (), 0, length) for axis, length in enumerate(values.shape)]
    widest = values.shape.index(max(values.shape))
    beside = spot[:widest] + [(spot[widest] + 1) % values.shape[widest]] + spot[widest + 1:]
    return values.at[tuple(spot)].set(smallest).at[tuple(beside)].set(top_value)


def levels(stream_key, extent, cuts, low, largest):
    gain, own = 1.0, jax.random.fold_in(stream_key, 6)
    for axis_at, shards_of in cuts:
        steps = jnp.exp(jax.random.uniform(jax.random.fold_in(own, axis_at), (shards_of,), jnp.float32, low / len(cuts), largest / len(cuts)))
        gain = gain * jnp.repeat(steps, extent[axis_at] // shards_of).reshape([-1 if axis == axis_at else 1 for axis in range(len(extent))])
    return gain


def centred(own_key, extent, deviation, most, shards=(), held_as=jnp.bfloat16):
    level = levels(own_key, extent, shards, -0.22, 0.18) if shards else 1.0
    result = jax.random.normal(own_key, extent, jnp.float32) * deviation * level
    return jnp.minimum(jnp.maximum(result, -most), most).astype(held_as)


def setup_inputs(seed: int = 0) -> dict:
    arg_keys = jax.random.split(jax.random.key(seed), 8)
    return {
        "secondary": centred(arg_keys[0], (DATES, 2, ROWS, COLS), 1.0, 6.0, ((0, 4), (2, 8))),
        "primary": centred(arg_keys[1], (2, ROWS, COLS), 1.0, 6.0, ((1, 8), (2, 4))),
        "margin_mask": draw_margin_mask(jax.random.fold_in(arg_keys[7], 71), 0),
        "az_off": plant(jax.random.randint(arg_keys[3], (DATES, TILES), -KA, KA + 1), jax.random.fold_in(arg_keys[3], 1), -KA, KA).astype(jnp.int32),
        "rg_off": plant(jax.random.randint(arg_keys[4], (DATES, TILES), -KR, KR + 1), jax.random.fold_in(arg_keys[4], 1), -KR, KR).astype(jnp.int32),
        "az_frac": jnp.clip(1.0 * jax.random.uniform(arg_keys[5], (DATES, TILES), jnp.float32) ** levels(arg_keys[5], (DATES, TILES), ((0, 4), (1, 8)), -0.2, 0.2), 0.0, 1.0),
        "rg_frac": jnp.clip(1.0 * jax.random.uniform(arg_keys[6], (DATES, TILES), jnp.float32) ** levels(arg_keys[6], (DATES, TILES), ((0, 4), (1, 8)), -0.2, 0.2), 0.0, 1.0),
    }


def window(dist):
    return jnp.sinc(dist) * (0.5 + 0.5 * jnp.cos(jnp.pi * dist / 4.0))

def reference(secondary, primary, margin_mask, az_off, rg_off, az_frac, rg_frac):
    rim_rows = KA + 4
    rim_cols = KR + 4
    prim = primary.astype(jnp.float32)
    weight = margin_mask.astype(jnp.float32)[:, None]
    count = jnp.sum(margin_mask.astype(jnp.float32)) * COLS

    def one_date(items):
        image, a_row, r_row, fa_row, fr_row = items
        padded = jnp.pad(image, ((0, 0), (rim_rows, rim_rows), (0, 0)))

        def tile_az(tile_id, shift, frac):
            block = lax.dynamic_slice_in_dim(padded, (tile_id * ROW_DEV).astype(jnp.int32), ROW_DEV + 2 * rim_rows, axis=1)
            total = jnp.zeros((2, ROW_DEV, COLS), jnp.float32)
            for step in range(8):
                offset = step - 3
                coeff = window(jnp.float32(offset) - frac).astype(jnp.bfloat16).astype(jnp.float32)
                piece = lax.dynamic_slice_in_dim(block, (shift + rim_rows + offset).astype(jnp.int32), ROW_DEV, axis=1)
                total = total + coeff * piece.astype(jnp.float32)
            return total.astype(jnp.bfloat16)
        azim = jax.vmap(tile_az)(jnp.arange(TILES, dtype=jnp.int32), a_row, fa_row)
        cpad = jnp.pad(azim, ((0, 0), (0, 0), (0, 0), (rim_cols, rim_cols)))

        def tile_rg(block, shift, frac):
            total = jnp.zeros((2, ROW_DEV, COLS), jnp.float32)
            for step in range(8):
                offset = step - 3
                coeff = window(jnp.float32(offset) - frac).astype(jnp.bfloat16).astype(jnp.float32)
                piece = lax.dynamic_slice_in_dim(block, (shift + rim_cols + offset).astype(jnp.int32), COLS, axis=2)
                total = total + coeff * piece.astype(jnp.float32)
            return total.astype(jnp.bfloat16)
        resampled = jax.vmap(tile_rg)(cpad, r_row, fr_row)
        resampled = resampled.transpose(1, 0, 2, 3).reshape(2, ROWS, COLS).astype(jnp.float32)
        ifg_re = prim[0] * resampled[0] + prim[1] * resampled[1]
        ifg_im = prim[1] * resampled[0] - prim[0] * resampled[1]
        tail = jnp.zeros((LAG, COLS), jnp.float32)
        l_re = jnp.concatenate([ifg_re[LAG:], tail], axis=0)
        l_im = jnp.concatenate([ifg_im[LAG:], tail], axis=0)
        e_re = jnp.sum(weight * (ifg_re * l_re + ifg_im * l_im))
        e_im = jnp.sum(weight * (ifg_im * l_re - ifg_re * l_im))
        power = jnp.sum(weight * 0.5 * (ifg_re * ifg_re + ifg_im * ifg_im + l_re * l_re + l_im * l_im))
        magnitude = jnp.sqrt(e_re * e_re + e_im * e_im)
        floor_val = (power + 1e-06) / jnp.sqrt(jnp.maximum(count, 1.0))
        denom = jnp.maximum(magnitude, floor_val)
        u_re = e_re / denom
        u_im = e_im / denom
        c_re = ifg_re * u_re + ifg_im * u_im
        c_im = ifg_im * u_re - ifg_re * u_im
        both = jnp.stack([c_re, c_im], axis=0)
        return both.reshape(2, ROWS // LA, LA, COLS // LR, LR).mean(axis=(2, 4))
    return lax.map(one_date, (secondary, az_off, rg_off, az_frac, rg_frac))
```

```python
import functools

import jax
import jax.numpy as jnp
from jax import lax
from jax.experimental import pallas as pl
from jax.experimental.pallas import tpu as pltpu
from jax.sharding import PartitionSpec as P

KA = 16
LAG = 64
LA = 2
LR = 8
LANE = 128
BAND = 128
HALO = 32
VMEM_LIMIT = 40 * 1024 * 1024


def passed_along(value, axis, steps):
    count = lax.axis_size(axis)
    initial, last = (max(0, -steps), min(count, count - steps))
    return lax.ppermute(value, axis, [(source, source + steps) for source in range(initial, last)])


def window(dist):
    return jnp.sinc(dist) * (0.5 + 0.5 * jnp.cos(jnp.pi * dist / 4.0))


def tap_rows(frac):
    dist = lax.broadcasted_iota(jnp.int32, (8, LANE), 0).astype(jnp.float32) - 3.0 - frac
    angle = jnp.pi * dist
    sinc = jnp.where(dist == 0.0, 1.0, jnp.sin(angle) / jnp.where(dist == 0.0, 1.0, angle))
    taps = sinc * (0.5 + 0.5 * jnp.cos(jnp.pi * dist / 4.0))
    return taps.astype(jnp.bfloat16).astype(jnp.float32)


def band(shape, distance, taps):
    total = jnp.zeros(shape, jnp.float32)
    for j in range(8):
        total = jnp.where(distance == j - 3, taps[j : j + 1, :1], total)
    return total.astype(jnp.bfloat16)


def resample_kernel(sec_ref, low_ref, high_ref, ao_ref, ro_ref, af_ref, rf_ref, out_ref, azim_ref):
    rows_n, cols_n = sec_ref.shape[2:]
    span = BAND + 2 * HALO
    shape = (BAND, span)
    offset = lax.broadcasted_iota(jnp.int32, shape, 1) - lax.broadcasted_iota(jnp.int32, shape, 0)
    az_band = band(shape, offset - HALO - ao_ref[...], tap_rows(af_ref[...]))
    for part in range(2):
        for start in range(0, rows_n, BAND):
            pieces = []
            if start == 0:
                pieces.append(low_ref[part])
            pieces.append(sec_ref[0, part, max(0, start - HALO) : min(rows_n, start + BAND + HALO)])
            if start + BAND == rows_n:
                pieces.append(high_ref[part])
            rows = jnp.concatenate(pieces, axis=0) if len(pieces) > 1 else pieces[0]
            azim_ref[part, start : start + BAND] = jnp.dot(
                az_band, rows, preferred_element_type=jnp.float32
            ).astype(jnp.bfloat16)

    square = (LANE, LANE)
    offset = lax.broadcasted_iota(jnp.int32, square, 0) - lax.broadcasted_iota(jnp.int32, square, 1)
    taps = tap_rows(rf_ref[...])
    before, same, after = [
        band(square, offset + shift - ro_ref[...], taps) for shift in (-LANE, 0, LANE)
    ]
    none = jnp.zeros(square, jnp.bfloat16)
    blocks_n, _, _, width = out_ref.shape
    lanes_n = width // LANE
    columns = []
    for lane in range(lanes_n):
        column = [none] * (lanes_n + 2)
        column[lane], column[lane + 1], column[lane + 2] = before, same, after
        columns.append(jnp.concatenate(column, axis=0))
    rg_band = jnp.concatenate(columns, axis=1)
    for block in range(blocks_n):
        first = block * width - LANE
        last = (block + 1) * width + LANE
        taken = slice(max(first, 0), min(last, cols_n))
        used = rg_band[taken.start - first : taken.stop - first]
        for part in range(2):
            out_ref[block, part] = jnp.dot(
                azim_ref[part, :, taken], used, preferred_element_type=jnp.float32
            ).astype(jnp.bfloat16)


def interfere(prim_re, prim_im, sec_re, sec_im):
    p_re, p_im = prim_re.astype(jnp.float32), prim_im.astype(jnp.float32)
    s_re, s_im = sec_re.astype(jnp.float32), sec_im.astype(jnp.float32)
    return p_re * s_re + p_im * s_im, p_im * s_re - p_re * s_im


def look_columns(width, block, looks_n):
    shape = (width, looks_n)
    col = lax.broadcasted_iota(jnp.int32, shape, 0) + block * width
    look = lax.broadcasted_iota(jnp.int32, shape, 1) * LR
    return jnp.where((col >= look) & (col < look + LR), 1.0, 0.0).astype(jnp.bfloat16)


def look_rows(sums_ref, part, start, rows_n):
    count = rows_n // LA
    total = sums_ref[part, pl.ds(start, count, LA)]
    for row in range(1, LA):
        total = total + sums_ref[part, pl.ds(start + row, count, LA)]
    return total


def margin_kernel(prim_ref, res_ref, first_ref, last_ref, looks_ref, sums_ref):
    blocks_n, _, rows_n, width = res_ref.shape
    looks_n = looks_ref.shape[2]
    totals = [None, None]
    for block in range(blocks_n):
        select = look_columns(width, block, looks_n)
        columns = slice(block * width, (block + 1) * width)
        halves = []
        for held, start, target in ((0, 0, first_ref), (LAG, rows_n - LAG, last_ref)):
            pair = interfere(
                prim_ref[block, 0, held : held + LAG],
                prim_ref[block, 1, held : held + LAG],
                res_ref[block, 0, start : start + LAG],
                res_ref[block, 1, start : start + LAG],
            )
            pair = [value.astype(jnp.bfloat16) for value in pair]
            for part in range(2):
                target[part, :, columns] = pair[part]
            halves.append(pair)
        for part in range(2):
            both = jnp.concatenate([halves[0][part], halves[1][part]], axis=0)
            summed = jnp.dot(both, select, preferred_element_type=jnp.float32)
            totals[part] = summed if block == 0 else totals[part] + summed
    for part in range(2):
        sums_ref[part] = totals[part]
        looks_ref[part] = look_rows(sums_ref, part, 0, 2 * LAG)


def stats_kernel(last_ref, later_ref, weight_ref, stats_ref):
    cols_n = last_ref.shape[2]
    i_re, i_im = last_ref[0].astype(jnp.float32), last_ref[1].astype(jnp.float32)
    l_re, l_im = later_ref[0].astype(jnp.float32), later_ref[1].astype(jnp.float32)
    weight = weight_ref[...]
    values = (
        i_re * l_re + i_im * l_im,
        i_im * l_re - i_re * l_im,
        0.5 * (i_re * i_re + i_im * i_im + l_re * l_re + l_im * l_im),
    )
    rows = []
    for value in values:
        folded = value[:, :LANE]
        for start in range(LANE, cols_n, LANE):
            folded = folded + value[:, start : start + LANE]
        rows.append(jnp.sum(folded * weight, axis=0, keepdims=True))
    rows.append(jnp.sum(weight, axis=0, keepdims=True) * (cols_n // LANE))
    rows.append(jnp.zeros((4, LANE), jnp.float32))
    stats_ref[...] = jnp.concatenate(rows, axis=0)


def finish_kernel(prim_ref, res_ref, looks_ref, stats_ref, out_ref, sums_ref):
    blocks_n, _, rows_n, width = res_ref.shape
    looks_n = out_ref.shape[3]
    middle_n = rows_n - 2 * LAG
    totals = [None, None]
    for block in range(blocks_n):
        select = look_columns(width, block, looks_n)
        pair = interfere(
            prim_ref[block, 0],
            prim_ref[block, 1],
            res_ref[block, 0, LAG : rows_n - LAG],
            res_ref[block, 1, LAG : rows_n - LAG],
        )
        for part in range(2):
            summed = jnp.dot(
                pair[part].astype(jnp.bfloat16), select, preferred_element_type=jnp.float32
            )
            totals[part] = summed if block == 0 else totals[part] + summed
    stats = jnp.sum(stats_ref[...], axis=1, keepdims=True)
    e_re, e_im, power, count = [stats[row : row + 1] for row in range(4)]
    magnitude = jnp.sqrt(e_re * e_re + e_im * e_im)
    floor_val = (power + 1e-06) / jnp.sqrt(jnp.maximum(count, 1.0))
    denom = jnp.maximum(magnitude, floor_val)
    u_re = e_re / denom * (1.0 / (LA * LR))
    u_im = e_im / denom * (1.0 / (LA * LR))
    edge = LAG // LA
    for part in range(2):
        sums_ref[part] = totals[part]
    for out_at, held, rows in (
        (0, looks_ref[:, :edge], edge),
        (edge, [look_rows(sums_ref, part, 0, middle_n) for part in range(2)], middle_n // LA),
        (edge + middle_n // LA, looks_ref[:, edge:], edge),
    ):
        out_ref[0, 0, out_at : out_at + rows] = held[0] * u_re + held[1] * u_im
        out_ref[0, 1, out_at : out_at + rows] = held[1] * u_re - held[0] * u_im


def call(kernel, outs, scratch, cost, *args):
    whole = pl.BlockSpec(memory_space=pltpu.VMEM)
    return pl.pallas_call(
        kernel,
        out_shape=outs,
        in_specs=[whole] * len(args),
        out_specs=jax.tree.map(lambda _: whole, outs),
        scratch_shapes=scratch,
        compiler_params=pltpu.CompilerParams(vmem_limit_bytes=VMEM_LIMIT),
        cost_estimate=pl.CostEstimate(flops=cost[0], bytes_accessed=cost[1], transcendentals=0),
    )(*args)


def fused(secondary, primary, margin_mask, az_off, rg_off, az_frac, rg_frac):
    _, _, rows_n, cols_n = secondary.shape
    width = primary.shape[2]
    dates_n = lax.axis_size("date")
    bf16, f32 = jnp.bfloat16, jnp.float32
    shape = jax.ShapeDtypeStruct
    looks_n = cols_n // LR

    edges = jnp.concatenate([primary[:, :LAG], primary[:, rows_n - LAG :]], axis=1)
    edges = lax.all_gather(edges, "date", axis=0)
    middle = lax.all_gather(primary[:, LAG : rows_n - LAG], "date", axis=0)

    image = secondary[0]
    low = passed_along(image[:, rows_n - HALO :], "tile", 1)
    high = passed_along(image[:, :HALO], "tile", -1)
    weight = jnp.broadcast_to(margin_mask[rows_n - LAG :].astype(f32)[:, None], (LAG, LANE))

    res = call(
        resample_kernel,
        shape((dates_n, 2, rows_n, width), bf16),
        [pltpu.VMEM((2, rows_n, cols_n), bf16)],
        (2 * 2 * rows_n * cols_n * (2 * HALO + BAND + 2 * width), 8 * rows_n * cols_n),
        secondary, low, high, az_off, rg_off, az_frac, rg_frac,
    )
    margin = shape((2, LAG, cols_n), bf16)
    first, last, looks = call(
        margin_kernel,
        (margin, margin, shape((2, 2 * LAG // LA, looks_n), f32)),
        [pltpu.VMEM((2, 2 * LAG, looks_n), f32)],
        (2 * 2 * 2 * LAG * cols_n * looks_n, 24 * LAG * cols_n),
        edges, res,
    )
    later = passed_along(first, "tile", -1)
    stats = call(
        stats_kernel,
        shape((8, LANE), f32),
        [],
        (20 * LAG * cols_n, 8 * LAG * cols_n),
        last, later, weight,
    )
    stats = lax.psum(stats, "tile")
    return call(
        finish_kernel,
        shape((1, 2, rows_n // LA, looks_n), f32),
        [pltpu.VMEM((2, rows_n - 2 * LAG, looks_n), f32)],
        (2 * 2 * rows_n * cols_n * looks_n, 8 * rows_n * cols_n),
        middle, res, looks, stats,
    )


def padded(block, sides, width):
    for axis, dim in sides:
        low = passed_along(
            lax.slice_in_dim(block, block.shape[dim] - width, None, axis=dim), axis, 1
        )
        high = passed_along(lax.slice_in_dim(block, 0, width, axis=dim), axis, -1)
        block = jnp.concatenate([low, block, high], axis=dim)
    return block


def band_taps(offset, frac):
    inside = (offset >= -3) & (offset <= 4)
    return jnp.where(inside, window(offset.astype(jnp.float32) - frac), 0.0).astype(jnp.bfloat16)


def multilook(values):
    depth, rows_n, cols_n = values.shape
    return values.reshape(depth, rows_n // LA, LA, cols_n // LR, LR).mean(axis=(2, 4))


def plain(secondary, primary, margin_mask, az_off, rg_off, az_frac, rg_frac):
    rim_rows = KA + 4
    block_cols = 256
    image = secondary[0]
    rows_n = image.shape[1]
    cols_n = image.shape[2]
    extended = padded(image, (("tile", 1),), rim_rows)
    row_out = lax.broadcasted_iota(jnp.int32, (rows_n, rows_n + 2 * rim_rows), 0)
    row_in = lax.broadcasted_iota(jnp.int32, (rows_n, rows_n + 2 * rim_rows), 1)
    azim_taps = band_taps(row_in - row_out - az_off[0, 0] - rim_rows, az_frac[0, 0])
    azim = jnp.einsum(
        "im,kmc->kic", azim_taps, extended, preferred_element_type=jnp.float32
    ).astype(jnp.bfloat16)
    blocks_n = cols_n // block_cols
    col_pad = jnp.pad(azim, ((0, 0), (0, 0), (block_cols // 2, block_cols // 2)))
    pieces = col_pad.reshape(2, rows_n, blocks_n + 1, block_cols)
    inputs = jnp.concatenate([pieces[:, :, :-1], pieces[:, :, 1:]], axis=3)
    col_in = lax.broadcasted_iota(jnp.int32, (2 * block_cols, block_cols), 0)
    col_out = lax.broadcasted_iota(jnp.int32, (2 * block_cols, block_cols), 1)
    range_taps = band_taps(col_in - block_cols // 2 - col_out - rg_off[0, 0], rg_frac[0, 0])
    resampled = jnp.einsum("kibm,mn->kibn", inputs, range_taps, preferred_element_type=jnp.float32)
    resampled = resampled.reshape(2, rows_n, cols_n).astype(jnp.bfloat16)
    prim = lax.all_gather(primary, "date", axis=2, tiled=True)[None]
    sec_f = resampled[None].astype(jnp.float32)
    prim_f = prim.astype(jnp.float32)
    ifg_re = prim_f[:, 0] * sec_f[:, 0] + prim_f[:, 1] * sec_f[:, 1]
    ifg_im = prim_f[:, 1] * sec_f[:, 0] - prim_f[:, 0] * sec_f[:, 1]
    interf = jnp.stack((ifg_re, ifg_im), axis=1)
    upcoming = passed_along(interf[:, :, :LAG, :], "tile", -1)
    later = jnp.concatenate([interf[:, :, LAG:, :], upcoming], axis=2)
    l_re = later[:, 0]
    l_im = later[:, 1]
    weight = margin_mask.astype(jnp.float32)[None, :, None]
    e_re = jnp.sum(weight * (ifg_re * l_re + ifg_im * l_im), axis=(1, 2))
    e_im = jnp.sum(weight * (ifg_im * l_re - ifg_re * l_im), axis=(1, 2))
    power = jnp.sum(
        weight * 0.5 * (ifg_re * ifg_re + ifg_im * ifg_im + l_re * l_re + l_im * l_im), axis=(1, 2)
    )
    count = jnp.zeros_like(e_re) + jnp.sum(margin_mask.astype(jnp.float32)) * interf.shape[3]
    stats = jnp.stack((e_re, e_im, power, count), axis=1)
    totals = lax.psum(stats, "tile")
    magnitude = jnp.sqrt(totals[:, 0] * totals[:, 0] + totals[:, 1] * totals[:, 1])
    floor_val = (totals[:, 2] + 1e-06) / jnp.sqrt(jnp.maximum(totals[:, 3], 1.0))
    denom = jnp.maximum(magnitude, floor_val)
    u_re = (totals[:, 0] / denom)[:, None, None]
    u_im = (totals[:, 1] / denom)[:, None, None]
    c_re = multilook(ifg_re * u_re + ifg_im * u_im)
    c_im = multilook(ifg_im * u_re - ifg_re * u_im)
    return jnp.stack((c_re, c_im), axis=1)


def shards(secondary, primary, *rest):
    rows_n, width = primary.shape[1:]
    fits = rows_n % BAND == 0 and rows_n > 2 * LAG + BAND and width % LANE == 0
    return (fused if fits else plain)(secondary, primary, *rest)


def solution(mesh):
    return jax.shard_map(
        shards,
        mesh=mesh,
        in_specs=(
            P("date", None, "tile", None),
            P(None, "tile", "date"),
            P("tile"),
            P("date", "tile"),
            P("date", "tile"),
            P("date", "tile"),
            P("date", "tile"),
        ),
        out_specs=P("date", None, "tile", None),
        check_vma=False,
    )
```

```python
import functools

import jax
import jax.numpy as jnp
from jax import lax
from jax.experimental import pallas as pl
from jax.experimental.pallas import tpu as pltpu
from jax.sharding import PartitionSpec as P

KA = 16
LAG = 64
LA = 2
LR = 8
LANE = 128
BAND = 128
HALO = 32
VMEM_LIMIT = 40 * 1024 * 1024


def passed_along(value, axis, steps):
    count = lax.axis_size(axis)
    initial, last = (max(0, -steps), min(count, count - steps))
    return lax.ppermute(value, axis, [(source, source + steps) for source in range(initial, last)])


def window(dist):
    return jnp.sinc(dist) * (0.5 + 0.5 * jnp.cos(jnp.pi * dist / 4.0))


def tap_rows(frac):
    dist = lax.broadcasted_iota(jnp.int32, (8, LANE), 0).astype(jnp.float32) - 3.0 - frac
    angle = jnp.pi * dist
    sinc = jnp.where(dist == 0.0, 1.0, jnp.sin(angle) / jnp.where(dist == 0.0, 1.0, angle))
    taps = sinc * (0.5 + 0.5 * jnp.cos(jnp.pi * dist / 4.0))
    return taps.astype(jnp.bfloat16).astype(jnp.float32)


def band(shape, distance, taps):
    total = jnp.zeros(shape, jnp.float32)
    for j in range(8):
        total = jnp.where(distance == j - 3, taps[j : j + 1, :1], total)
    return total.astype(jnp.bfloat16)


def prepare_kernel(sec_ref, prim_ref, edges_ref, middle_ref, down_ref, up_ref, sems):
    rows_n = sec_ref.shape[2]
    pieces = (
        (prim_ref.at[:, :LAG], edges_ref.at[:, :LAG]),
        (prim_ref.at[:, rows_n - LAG :], edges_ref.at[:, LAG:]),
        (sec_ref.at[0, :, rows_n - HALO :], down_ref),
        (sec_ref.at[0, :, :HALO], up_ref),
        (prim_ref.at[:, LAG : rows_n - LAG], middle_ref),
    )
    copies = [pltpu.make_async_copy(*piece, sems.at[at]) for at, piece in enumerate(pieces)]
    for copy in copies:
        copy.start()
    for copy in copies:
        copy.wait()


def resample_kernel(
    sec_ref, low_ref, high_ref, ao_hbm, ro_hbm, af_hbm, rf_hbm, out_ref,
    azim_ref, ao_ref, ro_ref, af_ref, rf_ref, sems,
):
    numbers = ((ao_hbm, ao_ref), (ro_hbm, ro_ref), (af_hbm, af_ref), (rf_hbm, rf_ref))
    copies = [pltpu.make_async_copy(*pair, sems.at[at]) for at, pair in enumerate(numbers)]
    for copy in copies:
        copy.start()
    for copy in copies:
        copy.wait()
    rows_n, cols_n = sec_ref.shape[2:]
    span = BAND + 2 * HALO
    shape = (BAND, span)
    offset = lax.broadcasted_iota(jnp.int32, shape, 1) - lax.broadcasted_iota(jnp.int32, shape, 0)
    az_band = band(shape, offset - HALO - ao_ref[0, 0], tap_rows(af_ref[0, 0]))
    for part in range(2):
        for start in range(0, rows_n, BAND):
            pieces = []
            if start == 0:
                pieces.append(low_ref[part])
            pieces.append(sec_ref[0, part, max(0, start - HALO) : min(rows_n, start + BAND + HALO)])
            if start + BAND == rows_n:
                pieces.append(high_ref[part])
            rows = jnp.concatenate(pieces, axis=0) if len(pieces) > 1 else pieces[0]
            azim_ref[part, start : start + BAND] = jnp.dot(
                az_band, rows, preferred_element_type=jnp.float32
            ).astype(jnp.bfloat16)

    square = (LANE, LANE)
    offset = lax.broadcasted_iota(jnp.int32, square, 0) - lax.broadcasted_iota(jnp.int32, square, 1)
    taps = tap_rows(rf_ref[0, 0])
    before, same, after = [
        band(square, offset + shift - ro_ref[0, 0], taps) for shift in (-LANE, 0, LANE)
    ]
    none = jnp.zeros(square, jnp.bfloat16)
    blocks_n, _, _, width = out_ref.shape
    lanes_n = width // LANE
    columns = []
    for lane in range(lanes_n):
        column = [none] * (lanes_n + 2)
        column[lane], column[lane + 1], column[lane + 2] = before, same, after
        columns.append(jnp.concatenate(column, axis=0))
    rg_band = jnp.concatenate(columns, axis=1)
    for block in range(blocks_n):
        first = block * width - LANE
        last = (block + 1) * width + LANE
        taken = slice(max(first, 0), min(last, cols_n))
        used = rg_band[taken.start - first : taken.stop - first]
        for part in range(2):
            out_ref[block, part] = jnp.dot(
                azim_ref[part, :, taken], used, preferred_element_type=jnp.float32
            ).astype(jnp.bfloat16)


def interfere(prim_re, prim_im, sec_re, sec_im):
    p_re, p_im = prim_re.astype(jnp.float32), prim_im.astype(jnp.float32)
    s_re, s_im = sec_re.astype(jnp.float32), sec_im.astype(jnp.float32)
    return p_re * s_re + p_im * s_im, p_im * s_re - p_re * s_im


def look_columns(width, block, looks_n):
    shape = (width, looks_n)
    col = lax.broadcasted_iota(jnp.int32, shape, 0) + block * width
    look = lax.broadcasted_iota(jnp.int32, shape, 1) * LR
    return jnp.where((col >= look) & (col < look + LR), 1.0, 0.0).astype(jnp.bfloat16)


def look_rows(sums_ref, part, start, rows_n):
    count = rows_n // LA
    total = sums_ref[part, pl.ds(start, count, LA)]
    for row in range(1, LA):
        total = total + sums_ref[part, pl.ds(start + row, count, LA)]
    return total


def margin_kernel(*refs):
    blocks_n, _, rows_n, width = refs[4].shape
    prims, (res_ref, first_ref, last_ref, looks_ref, sums_ref) = refs[:4], refs[4:]
    looks_n = looks_ref.shape[2]
    here = lax.axis_index("date")
    totals = [None, None]
    for step in range(blocks_n):
        block = lax.rem(here + (blocks_n - step), blocks_n)
        prim_ref = prims[step]
        select = look_columns(width, block, looks_n)
        columns = pl.ds(pl.multiple_of(block * width, width), width)
        halves = []
        for held, start, target in ((0, 0, first_ref), (LAG, rows_n - LAG, last_ref)):
            pair = interfere(
                prim_ref[0, held : held + LAG],
                prim_ref[1, held : held + LAG],
                res_ref[block, 0, start : start + LAG],
                res_ref[block, 1, start : start + LAG],
            )
            pair = [value.astype(jnp.bfloat16) for value in pair]
            for part in range(2):
                target[part, :, columns] = pair[part]
            halves.append(pair)
        for part in range(2):
            both = jnp.concatenate([halves[0][part], halves[1][part]], axis=0)
            summed = jnp.dot(both, select, preferred_element_type=jnp.float32)
            totals[part] = summed if step == 0 else totals[part] + summed
    for part in range(2):
        sums_ref[part] = totals[part]
        looks_ref[part] = look_rows(sums_ref, part, 0, 2 * LAG)


def stats_kernel(last_ref, later_ref, weight_ref, stats_ref):
    cols_n = last_ref.shape[2]
    i_re, i_im = last_ref[0].astype(jnp.float32), last_ref[1].astype(jnp.float32)
    l_re, l_im = later_ref[0].astype(jnp.float32), later_ref[1].astype(jnp.float32)
    weight = weight_ref[...]
    values = (
        i_re * l_re + i_im * l_im,
        i_im * l_re - i_re * l_im,
        0.5 * (i_re * i_re + i_im * i_im + l_re * l_re + l_im * l_im),
    )
    rows = []
    for value in values:
        folded = value[:, :LANE]
        for start in range(LANE, cols_n, LANE):
            folded = folded + value[:, start : start + LANE]
        rows.append(jnp.sum(folded * weight, axis=0, keepdims=True))
    rows.append(jnp.sum(weight, axis=0, keepdims=True) * (cols_n // LANE))
    rows.append(jnp.zeros((4, LANE), jnp.float32))
    stats_ref[...] = jnp.concatenate(rows, axis=0)


def finish_kernel(
    own_ref, beside_ref, near_ref, near_end_ref, far_ref, far_end_ref,
    res_ref, looks_ref, mine_ref, other_ref, out_ref, sums_ref,
):
    _, _, rows_n, width = res_ref.shape
    looks_n = out_ref.shape[3]
    middle_n = rows_n - 2 * LAG
    here = lax.axis_index("date")
    inner = (here == 1) | (here == 2)
    low = here < 2
    totals = [None, None]
    for step, (block, prim_ref, end_ref) in enumerate((
        (here, own_ref, None),
        (jnp.where(lax.rem(here, 2) == 0, here + 1, here - 1), beside_ref, None),
        (jnp.where(low, 2, 1), near_ref, near_end_ref),
        (jnp.where(low, 3, 0), far_ref, far_end_ref),
    )):
        select = look_columns(width, block, looks_n)
        if end_ref is None:
            prim = prim_ref[...]
        else:
            prim = jnp.where(inner, prim_ref[...], end_ref[...])
        pair = interfere(
            prim[0],
            prim[1],
            res_ref[block, 0, LAG : rows_n - LAG],
            res_ref[block, 1, LAG : rows_n - LAG],
        )
        for part in range(2):
            summed = jnp.dot(
                pair[part].astype(jnp.bfloat16), select, preferred_element_type=jnp.float32
            )
            totals[part] = summed if step == 0 else totals[part] + summed
    stats = jnp.sum(mine_ref[...] + other_ref[...], axis=1, keepdims=True)
    e_re, e_im, power, count = [stats[row : row + 1] for row in range(4)]
    magnitude = jnp.sqrt(e_re * e_re + e_im * e_im)
    floor_val = (power + 1e-06) / jnp.sqrt(jnp.maximum(count, 1.0))
    denom = jnp.maximum(magnitude, floor_val)
    u_re = e_re / denom * (1.0 / (LA * LR))
    u_im = e_im / denom * (1.0 / (LA * LR))
    edge = LAG // LA
    for part in range(2):
        sums_ref[part] = totals[part]
    for out_at, held, rows in (
        (0, looks_ref[:, :edge], edge),
        (edge, [look_rows(sums_ref, part, 0, middle_n) for part in range(2)], middle_n // LA),
        (edge + middle_n // LA, looks_ref[:, edge:], edge),
    ):
        out_ref[0, 0, out_at : out_at + rows] = held[0] * u_re + held[1] * u_im
        out_ref[0, 1, out_at : out_at + rows] = held[1] * u_re - held[0] * u_im


def call(kernel, outs, scratch, cost, *args, places=None):
    vmem = pl.BlockSpec(memory_space=pltpu.VMEM)
    return pl.pallas_call(
        kernel,
        out_shape=outs,
        in_specs=places or [vmem] * len(args),
        out_specs=jax.tree.map(lambda _: vmem, outs),
        scratch_shapes=scratch,
        compiler_params=pltpu.CompilerParams(vmem_limit_bytes=VMEM_LIMIT),
        cost_estimate=pl.CostEstimate(flops=cost[0], bytes_accessed=cost[1], transcendentals=0),
    )(*args)


def fused(secondary, primary, margin_mask, az_off, rg_off, az_frac, rg_frac):
    _, _, rows_n, cols_n = secondary.shape
    width = primary.shape[2]
    dates_n = lax.axis_size("date")
    tiles_n = lax.axis_size("tile")
    bf16, f32 = jnp.bfloat16, jnp.float32
    shape = jax.ShapeDtypeStruct
    looks_n = cols_n // LR
    middle_n = rows_n - 2 * LAG
    vmem = pl.BlockSpec(memory_space=pltpu.VMEM)
    hbm = pl.BlockSpec(memory_space=pl.ANY)

    halo = shape((2, HALO, cols_n), bf16)
    edges, middle, down, up = call(
        prepare_kernel,
        (shape((2, 2 * LAG, width), bf16), shape((2, middle_n, width), bf16), halo, halo),
        [pltpu.SemaphoreType.DMA((5,))],
        (0, 4 * 2 * rows_n * width),
        secondary, primary, places=[hbm] * 2,
    )
    low = passed_along(down, "tile", 1)
    high = passed_along(up, "tile", -1)
    around = [edges] + [
        lax.ppermute(edges, "date", [(at, (at + step) % dates_n) for at in range(dates_n)])
        for step in range(1, dates_n)
    ]
    beside = lax.ppermute(middle, "date", [(0, 1), (1, 0), (2, 3), (3, 2)])
    near = lax.ppermute(middle, "date", [(1, 2), (2, 1)])
    far = lax.ppermute(beside, "date", [(1, 2), (2, 1)])
    near_end = lax.ppermute(near, "date", [(1, 0), (2, 3)])
    far_end = lax.ppermute(far, "date", [(1, 0), (2, 3)])
    weight = jnp.broadcast_to(margin_mask[rows_n - LAG :].astype(f32)[:, None], (LAG, LANE))

    res = call(
        resample_kernel,
        shape((dates_n, 2, rows_n, width), bf16),
        [
            pltpu.VMEM((2, rows_n, cols_n), bf16),
            pltpu.SMEM((1, 1), jnp.int32),
            pltpu.SMEM((1, 1), jnp.int32),
            pltpu.SMEM((1, 1), f32),
            pltpu.SMEM((1, 1), f32),
            pltpu.SemaphoreType.DMA((4,)),
        ],
        (2 * 2 * rows_n * cols_n * (2 * HALO + BAND + 2 * width), 8 * rows_n * cols_n),
        secondary, low, high, az_off, rg_off, az_frac, rg_frac,
        places=[vmem] * 3 + [hbm] * 4,
    )
    margin = shape((2, LAG, cols_n), bf16)
    first, last, looks = call(
        margin_kernel,
        (margin, margin, shape((2, 2 * LAG // LA, looks_n), f32)),
        [pltpu.VMEM((2, 2 * LAG, looks_n), f32)],
        (2 * 2 * 2 * LAG * cols_n * looks_n, 24 * LAG * cols_n),
        *around, res,
    )
    later = passed_along(first, "tile", -1)
    stats = call(
        stats_kernel,
        shape((8, LANE), f32),
        [],
        (20 * LAG * cols_n, 8 * LAG * cols_n),
        last, later, weight,
    )
    stride = 1
    other = jnp.zeros_like(stats)
    while stride < tiles_n:
        stats = stats + other if stride > 1 else stats
        other = lax.ppermute(stats, "tile", [(at, at ^ stride) for at in range(tiles_n)])
        stride *= 2
    return call(
        finish_kernel,
        shape((1, 2, rows_n // LA, looks_n), f32),
        [pltpu.VMEM((2, middle_n, looks_n), f32)],
        (2 * 2 * rows_n * cols_n * looks_n, 8 * rows_n * cols_n),
        middle, beside, near, near_end, far, far_end, res, looks, stats, other,
    )


def padded(block, sides, width):
    for axis, dim in sides:
        low = passed_along(
            lax.slice_in_dim(block, block.shape[dim] - width, None, axis=dim), axis, 1
        )
        high = passed_along(lax.slice_in_dim(block, 0, width, axis=dim), axis, -1)
        block = jnp.concatenate([low, block, high], axis=dim)
    return block


def band_taps(offset, frac):
    inside = (offset >= -3) & (offset <= 4)
    return jnp.where(inside, window(offset.astype(jnp.float32) - frac), 0.0).astype(jnp.bfloat16)


def multilook(values):
    depth, rows_n, cols_n = values.shape
    return values.reshape(depth, rows_n // LA, LA, cols_n // LR, LR).mean(axis=(2, 4))


def plain(secondary, primary, margin_mask, az_off, rg_off, az_frac, rg_frac):
    rim_rows = KA + 4
    block_cols = 256
    image = secondary[0]
    rows_n = image.shape[1]
    cols_n = image.shape[2]
    extended = padded(image, (("tile", 1),), rim_rows)
    row_out = lax.broadcasted_iota(jnp.int32, (rows_n, rows_n + 2 * rim_rows), 0)
    row_in = lax.broadcasted_iota(jnp.int32, (rows_n, rows_n + 2 * rim_rows), 1)
    azim_taps = band_taps(row_in - row_out - az_off[0, 0] - rim_rows, az_frac[0, 0])
    azim = jnp.einsum(
        "im,kmc->kic", azim_taps, extended, preferred_element_type=jnp.float32
    ).astype(jnp.bfloat16)
    blocks_n = cols_n // block_cols
    col_pad = jnp.pad(azim, ((0, 0), (0, 0), (block_cols // 2, block_cols // 2)))
    pieces = col_pad.reshape(2, rows_n, blocks_n + 1, block_cols)
    inputs = jnp.concatenate([pieces[:, :, :-1], pieces[:, :, 1:]], axis=3)
    col_in = lax.broadcasted_iota(jnp.int32, (2 * block_cols, block_cols), 0)
    col_out = lax.broadcasted_iota(jnp.int32, (2 * block_cols, block_cols), 1)
    range_taps = band_taps(col_in - block_cols // 2 - col_out - rg_off[0, 0], rg_frac[0, 0])
    resampled = jnp.einsum("kibm,mn->kibn", inputs, range_taps, preferred_element_type=jnp.float32)
    resampled = resampled.reshape(2, rows_n, cols_n).astype(jnp.bfloat16)
    prim = lax.all_gather(primary, "date", axis=2, tiled=True)[None]
    sec_f = resampled[None].astype(jnp.float32)
    prim_f = prim.astype(jnp.float32)
    ifg_re = prim_f[:, 0] * sec_f[:, 0] + prim_f[:, 1] * sec_f[:, 1]
    ifg_im = prim_f[:, 1] * sec_f[:, 0] - prim_f[:, 0] * sec_f[:, 1]
    interf = jnp.stack((ifg_re, ifg_im), axis=1)
    upcoming = passed_along(interf[:, :, :LAG, :], "tile", -1)
    later = jnp.concatenate([interf[:, :, LAG:, :], upcoming], axis=2)
    l_re = later[:, 0]
    l_im = later[:, 1]
    weight = margin_mask.astype(jnp.float32)[None, :, None]
    e_re = jnp.sum(weight * (ifg_re * l_re + ifg_im * l_im), axis=(1, 2))
    e_im = jnp.sum(weight * (ifg_im * l_re - ifg_re * l_im), axis=(1, 2))
    power = jnp.sum(
        weight * 0.5 * (ifg_re * ifg_re + ifg_im * ifg_im + l_re * l_re + l_im * l_im), axis=(1, 2)
    )
    count = jnp.zeros_like(e_re) + jnp.sum(margin_mask.astype(jnp.float32)) * interf.shape[3]
    stats = jnp.stack((e_re, e_im, power, count), axis=1)
    totals = lax.psum(stats, "tile")
    magnitude = jnp.sqrt(totals[:, 0] * totals[:, 0] + totals[:, 1] * totals[:, 1])
    floor_val = (totals[:, 2] + 1e-06) / jnp.sqrt(jnp.maximum(totals[:, 3], 1.0))
    denom = jnp.maximum(magnitude, floor_val)
    u_re = (totals[:, 0] / denom)[:, None, None]
    u_im = (totals[:, 1] / denom)[:, None, None]
    c_re = multilook(ifg_re * u_re + ifg_im * u_im)
    c_im = multilook(ifg_im * u_re - ifg_re * u_im)
    return jnp.stack((c_re, c_im), axis=1)


def shards(secondary, primary, *rest):
    rows_n, width = primary.shape[1:]
    tiles_n = lax.axis_size("tile")
    fits = rows_n % BAND == 0 and rows_n > 2 * LAG + BAND and width % LANE == 0
    fits = fits and lax.axis_size("date") == 4 and tiles_n & (tiles_n - 1) == 0
    return (fused if fits else plain)(secondary, primary, *rest)


def solution(mesh):
    return jax.shard_map(
        shards,
        mesh=mesh,
        in_specs=(
            P("date", None, "tile", None),
            P(None, "tile", "date"),
            P("tile"),
            P("date", "tile"),
            P("date", "tile"),
            P("date", "tile"),
            P("date", "tile"),
        ),
        out_specs=P("date", None, "tile", None),
        check_vma=False,
    )
```

```python
import functools

import jax
import jax.numpy as jnp
from jax import lax
from jax.experimental import pallas as pl
from jax.experimental.pallas import tpu as pltpu
from jax.sharding import PartitionSpec as P

KA = 16
LAG = 64
LA = 2
LR = 8
LANE = 128
BAND = 128
HALO = 32
VMEM_LIMIT = 40 * 1024 * 1024


def passed_along(value, axis, steps):
    count = lax.axis_size(axis)
    initial, last = (max(0, -steps), min(count, count - steps))
    return lax.ppermute(value, axis, [(source, source + steps) for source in range(initial, last)])


def window(dist):
    return jnp.sinc(dist) * (0.5 + 0.5 * jnp.cos(jnp.pi * dist / 4.0))


def tap_rows(frac):
    dist = lax.broadcasted_iota(jnp.int32, (8, LANE), 0).astype(jnp.float32) - 3.0 - frac
    angle = jnp.pi * dist
    sinc = jnp.where(dist == 0.0, 1.0, jnp.sin(angle) / jnp.where(dist == 0.0, 1.0, angle))
    taps = sinc * (0.5 + 0.5 * jnp.cos(jnp.pi * dist / 4.0))
    return taps.astype(jnp.bfloat16).astype(jnp.float32)


def band(shape, distance, taps):
    total = jnp.zeros(shape, jnp.float32)
    for j in range(8):
        total = jnp.where(distance == j - 3, taps[j : j + 1, :1], total)
    return total.astype(jnp.bfloat16)


def start_all(pairs, sems):
    copies = [pltpu.make_async_copy(*pair, sems.at[at]) for at, pair in enumerate(pairs)]
    for copy in copies:
        copy.start()
    return copies


def prepare_kernel(sec_ref, prim_ref, edges_ref, down_ref, up_ref, sems):
    rows_n = sec_ref.shape[2]
    pieces = [(sec_ref.at[0, :, rows_n - HALO :], down_ref), (sec_ref.at[0, :, :HALO], up_ref)]
    for to in range(edges_ref.shape[0]):
        pieces.append((prim_ref.at[:, :LAG], edges_ref.at[to, :, :LAG]))
        pieces.append((prim_ref.at[:, rows_n - LAG :], edges_ref.at[to, :, LAG:]))
    for copy in start_all(pieces, sems):
        copy.wait()


def resample_kernel(
    sec_ref, low_ref, high_ref, prim_hbm, ao_hbm, ro_hbm, af_hbm, rf_hbm, out_ref, middle_ref,
    azim_ref, ao_ref, ro_ref, af_ref, rf_ref, sems,
):
    last = prim_hbm.shape[1] - LAG
    numbers = [(ao_hbm, ao_ref), (ro_hbm, ro_ref), (af_hbm, af_ref), (rf_hbm, rf_ref)]
    *copies, middle = start_all(numbers + [(prim_hbm.at[:, LAG:last], middle_ref)], sems)
    for copy in copies:
        copy.wait()
    rows_n, cols_n = sec_ref.shape[2:]
    span = BAND + 2 * HALO
    shape = (BAND, span)
    offset = lax.broadcasted_iota(jnp.int32, shape, 1) - lax.broadcasted_iota(jnp.int32, shape, 0)
    az_band = band(shape, offset - HALO - ao_ref[0, 0], tap_rows(af_ref[0, 0]))
    for part in range(2):
        for start in range(0, rows_n, BAND):
            pieces = []
            if start == 0:
                pieces.append(low_ref[part])
            pieces.append(sec_ref[0, part, max(0, start - HALO) : min(rows_n, start + BAND + HALO)])
            if start + BAND == rows_n:
                pieces.append(high_ref[part])
            rows = jnp.concatenate(pieces, axis=0) if len(pieces) > 1 else pieces[0]
            azim_ref[part, start : start + BAND] = jnp.dot(
                az_band, rows, preferred_element_type=jnp.float32
            ).astype(jnp.bfloat16)

    square = (LANE, LANE)
    offset = lax.broadcasted_iota(jnp.int32, square, 0) - lax.broadcasted_iota(jnp.int32, square, 1)
    taps = tap_rows(rf_ref[0, 0])
    before, same, after = [
        band(square, offset + shift - ro_ref[0, 0], taps) for shift in (-LANE, 0, LANE)
    ]
    none = jnp.zeros(square, jnp.bfloat16)
    blocks_n, _, _, width = out_ref.shape
    lanes_n = width // LANE
    columns = []
    for lane in range(lanes_n):
        column = [none] * (lanes_n + 2)
        column[lane], column[lane + 1], column[lane + 2] = before, same, after
        columns.append(jnp.concatenate(column, axis=0))
    rg_band = jnp.concatenate(columns, axis=1)
    for block in range(blocks_n):
        first = block * width - LANE
        last = (block + 1) * width + LANE
        taken = slice(max(first, 0), min(last, cols_n))
        used = rg_band[taken.start - first : taken.stop - first]
        for part in range(2):
            out_ref[block, part] = jnp.dot(
                azim_ref[part, :, taken], used, preferred_element_type=jnp.float32
            ).astype(jnp.bfloat16)
    middle.wait()


def interfere(prim_re, prim_im, sec_re, sec_im):
    p_re, p_im = prim_re.astype(jnp.float32), prim_im.astype(jnp.float32)
    s_re, s_im = sec_re.astype(jnp.float32), sec_im.astype(jnp.float32)
    return p_re * s_re + p_im * s_im, p_im * s_re - p_re * s_im


def look_columns(width, block, looks_n):
    shape = (width, looks_n)
    col = lax.broadcasted_iota(jnp.int32, shape, 0) + block * width
    look = lax.broadcasted_iota(jnp.int32, shape, 1) * LR
    return jnp.where((col >= look) & (col < look + LR), 1.0, 0.0).astype(jnp.bfloat16)


def look_rows(sums_ref, part, start, rows_n):
    count = rows_n // LA
    total = sums_ref[part, pl.ds(start, count, LA)]
    for row in range(1, LA):
        total = total + sums_ref[part, pl.ds(start + row, count, LA)]
    return total


def margin_kernel(prim_ref, res_ref, first_ref, last_ref, looks_ref, sums_ref):
    blocks_n, _, rows_n, width = res_ref.shape
    looks_n = looks_ref.shape[2]
    totals = [None, None]
    for block in range(blocks_n):
        select = look_columns(width, block, looks_n)
        columns = slice(block * width, (block + 1) * width)
        halves = []
        for held, start, target in ((0, 0, first_ref), (LAG, rows_n - LAG, last_ref)):
            pair = interfere(
                prim_ref[block, 0, held : held + LAG],
                prim_ref[block, 1, held : held + LAG],
                res_ref[block, 0, start : start + LAG],
                res_ref[block, 1, start : start + LAG],
            )
            pair = [value.astype(jnp.bfloat16) for value in pair]
            for part in range(2):
                target[part, :, columns] = pair[part]
            halves.append(pair)
        for part in range(2):
            both = jnp.concatenate([halves[0][part], halves[1][part]], axis=0)
            summed = jnp.dot(both, select, preferred_element_type=jnp.float32)
            totals[part] = summed if block == 0 else totals[part] + summed
    for part in range(2):
        sums_ref[part] = totals[part]
        looks_ref[part] = look_rows(sums_ref, part, 0, 2 * LAG)


def stats_kernel(last_ref, later_ref, mask_ref, stats_ref):
    _, lag, cols_n = last_ref.shape
    rows_n = mask_ref.shape[0]
    mask = mask_ref[...].reshape(1, rows_n).astype(jnp.float32)
    shape = (lag, rows_n)
    row = lax.broadcasted_iota(jnp.int32, shape, 0) + (rows_n - lag)
    picked = jnp.where(row == lax.broadcasted_iota(jnp.int32, shape, 1), mask, 0.0)
    weight = jnp.dot(
        picked.astype(jnp.bfloat16),
        jnp.ones((rows_n, LANE), jnp.bfloat16),
        preferred_element_type=jnp.float32,
    )
    i_re, i_im = last_ref[0].astype(jnp.float32), last_ref[1].astype(jnp.float32)
    l_re, l_im = later_ref[0].astype(jnp.float32), later_ref[1].astype(jnp.float32)
    values = (
        i_re * l_re + i_im * l_im,
        i_im * l_re - i_re * l_im,
        0.5 * (i_re * i_re + i_im * i_im + l_re * l_re + l_im * l_im),
    )
    rows = []
    for value in values:
        folded = value[:, :LANE]
        for start in range(LANE, cols_n, LANE):
            folded = folded + value[:, start : start + LANE]
        rows.append(jnp.sum(folded * weight, axis=0, keepdims=True))
    rows.append(jnp.sum(weight, axis=0, keepdims=True) * (cols_n // LANE))
    rows.append(jnp.zeros((4, LANE), jnp.float32))
    stats = jnp.concatenate(rows, axis=0)
    for to in range(stats_ref.shape[0]):
        stats_ref[to] = stats


def finish_kernel(
    own_ref, beside_ref, near_ref, skip_ref, far_ref, res_ref, looks_ref, stats_ref,
    out_ref, sums_ref,
):
    _, _, rows_n, width = res_ref.shape
    looks_n = out_ref.shape[3]
    middle_n = rows_n - 2 * LAG
    here = lax.axis_index("date")
    inner = (here == 1) | (here == 2)
    low = here < 2
    totals = [None, None]
    for step, (block, prim_ref, end_ref) in enumerate((
        (here, own_ref, None),
        (jnp.where(lax.rem(here, 2) == 0, here + 1, here - 1), beside_ref, None),
        (jnp.where(low, 2, 1), near_ref, skip_ref),
        (jnp.where(low, 3, 0), skip_ref, far_ref),
    )):
        select = look_columns(width, block, looks_n)
        if end_ref is None:
            prim = prim_ref[...]
        else:
            prim = jnp.where(inner, prim_ref[...], end_ref[...])
        pair = interfere(
            prim[0],
            prim[1],
            res_ref[block, 0, LAG : rows_n - LAG],
            res_ref[block, 1, LAG : rows_n - LAG],
        )
        for part in range(2):
            summed = jnp.dot(
                pair[part].astype(jnp.bfloat16), select, preferred_element_type=jnp.float32
            )
            totals[part] = summed if step == 0 else totals[part] + summed
    stats = jnp.sum(jnp.sum(stats_ref[...], axis=0), axis=1, keepdims=True)
    e_re, e_im, power, count = [stats[row : row + 1] for row in range(4)]
    magnitude = jnp.sqrt(e_re * e_re + e_im * e_im)
    floor_val = (power + 1e-06) / jnp.sqrt(jnp.maximum(count, 1.0))
    denom = jnp.maximum(magnitude, floor_val)
    u_re = e_re / denom * (1.0 / (LA * LR))
    u_im = e_im / denom * (1.0 / (LA * LR))
    edge = LAG // LA
    for part in range(2):
        sums_ref[part] = totals[part]
    for out_at, held, rows in (
        (0, looks_ref[:, :edge], edge),
        (edge, [look_rows(sums_ref, part, 0, middle_n) for part in range(2)], middle_n // LA),
        (edge + middle_n // LA, looks_ref[:, edge:], edge),
    ):
        out_ref[0, 0, out_at : out_at + rows] = held[0] * u_re + held[1] * u_im
        out_ref[0, 1, out_at : out_at + rows] = held[1] * u_re - held[0] * u_im


def call(kernel, outs, scratch, cost, *args, places=None):
    vmem = pl.BlockSpec(memory_space=pltpu.VMEM)
    return pl.pallas_call(
        kernel,
        out_shape=outs,
        in_specs=places or [vmem] * len(args),
        out_specs=jax.tree.map(lambda _: vmem, outs),
        scratch_shapes=scratch,
        compiler_params=pltpu.CompilerParams(vmem_limit_bytes=VMEM_LIMIT),
        cost_estimate=pl.CostEstimate(flops=cost[0], bytes_accessed=cost[1], transcendentals=0),
    )(*args)


def fused(secondary, primary, margin_mask, az_off, rg_off, az_frac, rg_frac):
    _, _, rows_n, cols_n = secondary.shape
    width = primary.shape[2]
    dates_n = lax.axis_size("date")
    tiles_n = lax.axis_size("tile")
    bf16, f32 = jnp.bfloat16, jnp.float32
    shape = jax.ShapeDtypeStruct
    looks_n = cols_n // LR
    middle_n = rows_n - 2 * LAG
    vmem = pl.BlockSpec(memory_space=pltpu.VMEM)
    hbm = pl.BlockSpec(memory_space=pltpu.HBM)

    halo = shape((2, HALO, cols_n), bf16)
    edges, down, up = call(
        prepare_kernel,
        (shape((dates_n, 2, 2 * LAG, width), bf16), halo, halo),
        [pltpu.SemaphoreType.DMA((2 + 2 * dates_n,))],
        (0, 4 * 2 * rows_n * width),
        secondary, primary, places=[hbm] * 2,
    )
    edges = lax.all_to_all(edges, "date", 0, 0, tiled=True)
    low = passed_along(down, "tile", 1)
    high = passed_along(up, "tile", -1)
    res, middle = call(
        resample_kernel,
        (shape((dates_n, 2, rows_n, width), bf16), shape((2, middle_n, width), bf16)),
        [
            pltpu.VMEM((2, rows_n, cols_n), bf16),
            pltpu.SMEM((1, 1), jnp.int32),
            pltpu.SMEM((1, 1), jnp.int32),
            pltpu.SMEM((1, 1), f32),
            pltpu.SMEM((1, 1), f32),
            pltpu.SemaphoreType.DMA((5,)),
        ],
        (2 * 2 * rows_n * cols_n * (2 * HALO + BAND + 2 * width), 8 * rows_n * cols_n),
        secondary, low, high, primary, az_off, rg_off, az_frac, rg_frac,
        places=[vmem] * 3 + [hbm] * 5,
    )
    skip = lax.ppermute(middle, "date", [(0, 2), (2, 0), (1, 3), (3, 1)])
    beside = lax.ppermute(middle, "date", [(0, 1), (1, 0), (2, 3), (3, 2)])
    near = lax.ppermute(middle, "date", [(1, 2), (2, 1)])
    far = lax.ppermute(skip, "date", [(1, 0), (2, 3)])
    margin = shape((2, LAG, cols_n), bf16)
    first, last, looks = call(
        margin_kernel,
        (margin, margin, shape((2, 2 * LAG // LA, looks_n), f32)),
        [pltpu.VMEM((2, 2 * LAG, looks_n), f32)],
        (2 * 2 * 2 * LAG * cols_n * looks_n, 24 * LAG * cols_n),
        edges, res,
    )
    later = passed_along(first, "tile", -1)
    stats = call(
        stats_kernel,
        shape((tiles_n, 8, LANE), f32),
        [],
        (20 * LAG * cols_n, 8 * LAG * cols_n),
        last, later, margin_mask,
    )
    stats = lax.all_to_all(stats, "tile", 0, 0, tiled=True)
    return call(
        finish_kernel,
        shape((1, 2, rows_n // LA, looks_n), f32),
        [pltpu.VMEM((2, middle_n, looks_n), f32)],
        (2 * 2 * rows_n * cols_n * looks_n, 8 * rows_n * cols_n),
        middle, beside, near, skip, far, res, looks, stats,
    )


def padded(block, sides, width):
    for axis, dim in sides:
        low = passed_along(
            lax.slice_in_dim(block, block.shape[dim] - width, None, axis=dim), axis, 1
        )
        high = passed_along(lax.slice_in_dim(block, 0, width, axis=dim), axis, -1)
        block = jnp.concatenate([low, block, high], axis=dim)
    return block


def band_taps(offset, frac):
    inside = (offset >= -3) & (offset <= 4)
    return jnp.where(inside, window(offset.astype(jnp.float32) - frac), 0.0).astype(jnp.bfloat16)


def multilook(values):
    depth, rows_n, cols_n = values.shape
    return values.reshape(depth, rows_n // LA, LA, cols_n // LR, LR).mean(axis=(2, 4))


def plain(secondary, primary, margin_mask, az_off, rg_off, az_frac, rg_frac):
    rim_rows = KA + 4
    block_cols = 256
    image = secondary[0]
    rows_n = image.shape[1]
    cols_n = image.shape[2]
    extended = padded(image, (("tile", 1),), rim_rows)
    row_out = lax.broadcasted_iota(jnp.int32, (rows_n, rows_n + 2 * rim_rows), 0)
    row_in = lax.broadcasted_iota(jnp.int32, (rows_n, rows_n + 2 * rim_rows), 1)
    azim_taps = band_taps(row_in - row_out - az_off[0, 0] - rim_rows, az_frac[0, 0])
    azim = jnp.einsum(
        "im,kmc->kic", azim_taps, extended, preferred_element_type=jnp.float32
    ).astype(jnp.bfloat16)
    blocks_n = cols_n // block_cols
    col_pad = jnp.pad(azim, ((0, 0), (0, 0), (block_cols // 2, block_cols // 2)))
    pieces = col_pad.reshape(2, rows_n, blocks_n + 1, block_cols)
    inputs = jnp.concatenate([pieces[:, :, :-1], pieces[:, :, 1:]], axis=3)
    col_in = lax.broadcasted_iota(jnp.int32, (2 * block_cols, block_cols), 0)
    col_out = lax.broadcasted_iota(jnp.int32, (2 * block_cols, block_cols), 1)
    range_taps = band_taps(col_in - block_cols // 2 - col_out - rg_off[0, 0], rg_frac[0, 0])
    resampled = jnp.einsum("kibm,mn->kibn", inputs, range_taps, preferred_element_type=jnp.float32)
    resampled = resampled.reshape(2, rows_n, cols_n).astype(jnp.bfloat16)
    prim = lax.all_gather(primary, "date", axis=2, tiled=True)[None]
    sec_f = resampled[None].astype(jnp.float32)
    prim_f = prim.astype(jnp.float32)
    ifg_re = prim_f[:, 0] * sec_f[:, 0] + prim_f[:, 1] * sec_f[:, 1]
    ifg_im = prim_f[:, 1] * sec_f[:, 0] - prim_f[:, 0] * sec_f[:, 1]
    interf = jnp.stack((ifg_re, ifg_im), axis=1)
    upcoming = passed_along(interf[:, :, :LAG, :], "tile", -1)
    later = jnp.concatenate([interf[:, :, LAG:, :], upcoming], axis=2)
    l_re = later[:, 0]
    l_im = later[:, 1]
    weight = margin_mask.astype(jnp.float32)[None, :, None]
    e_re = jnp.sum(weight * (ifg_re * l_re + ifg_im * l_im), axis=(1, 2))
    e_im = jnp.sum(weight * (ifg_im * l_re - ifg_re * l_im), axis=(1, 2))
    power = jnp.sum(
        weight * 0.5 * (ifg_re * ifg_re + ifg_im * ifg_im + l_re * l_re + l_im * l_im), axis=(1, 2)
    )
    count = jnp.zeros_like(e_re) + jnp.sum(margin_mask.astype(jnp.float32)) * interf.shape[3]
    stats = jnp.stack((e_re, e_im, power, count), axis=1)
    totals = lax.psum(stats, "tile")
    magnitude = jnp.sqrt(totals[:, 0] * totals[:, 0] + totals[:, 1] * totals[:, 1])
    floor_val = (totals[:, 2] + 1e-06) / jnp.sqrt(jnp.maximum(totals[:, 3], 1.0))
    denom = jnp.maximum(magnitude, floor_val)
    u_re = (totals[:, 0] / denom)[:, None, None]
    u_im = (totals[:, 1] / denom)[:, None, None]
    c_re = multilook(ifg_re * u_re + ifg_im * u_im)
    c_im = multilook(ifg_im * u_re - ifg_re * u_im)
    return jnp.stack((c_re, c_im), axis=1)


def shards(secondary, primary, *rest):
    rows_n, width = primary.shape[1:]
    fits = rows_n % BAND == 0 and rows_n > 2 * LAG + BAND and width % LANE == 0
    fits = fits and lax.axis_size("date") == 4
    return (fused if fits else plain)(secondary, primary, *rest)


def solution(mesh):
    return jax.shard_map(
        shards,
        mesh=mesh,
        in_specs=(
            P("date", None, "tile", None),
            P(None, "tile", "date"),
            P("tile"),
            P("date", "tile"),
            P("date", "tile"),
            P("date", "tile"),
            P("date", "tile"),
        ),
        out_specs=P("date", None, "tile", None),
        check_vma=False,
    )
```

```python
import functools

import jax
import jax.numpy as jnp
from jax import lax
from jax.experimental import pallas as pl
from jax.experimental.pallas import tpu as pltpu
from jax.sharding import PartitionSpec as P

KA = 16
LAG = 64
LA = 2
LR = 8
LANE = 128
BAND = 128
HALO = 32
VMEM_LIMIT = 40 * 1024 * 1024
VMEM_ALL = 63 * 1024 * 1024


def passed_along(value, axis, steps):
    count = lax.axis_size(axis)
    initial, last = (max(0, -steps), min(count, count - steps))
    return lax.ppermute(value, axis, [(source, source + steps) for source in range(initial, last)])


def window(dist):
    return jnp.sinc(dist) * (0.5 + 0.5 * jnp.cos(jnp.pi * dist / 4.0))


def tap_rows(frac):
    dist = lax.broadcasted_iota(jnp.int32, (8, LANE), 0).astype(jnp.float32) - 3.0 - frac
    angle = jnp.pi * dist
    sinc = jnp.where(dist == 0.0, 1.0, jnp.sin(angle) / jnp.where(dist == 0.0, 1.0, angle))
    taps = sinc * (0.5 + 0.5 * jnp.cos(jnp.pi * dist / 4.0))
    return taps.astype(jnp.bfloat16).astype(jnp.float32)


def band(shape, distance, taps):
    total = jnp.zeros(shape, jnp.float32)
    for j in range(8):
        total = jnp.where(distance == j - 3, taps[j : j + 1, :1], total)
    return total.astype(jnp.bfloat16)


def start_all(pairs, sems):
    copies = [pltpu.make_async_copy(*pair, sems.at[at]) for at, pair in enumerate(pairs)]
    for copy in copies:
        copy.start()
    return copies


def prepare_kernel(sec_ref, prim_ref, edges_ref, middle_ref, down_ref, up_ref, sems):
    rows_n = sec_ref.shape[2]
    pieces = (
        (prim_ref.at[:, :LAG], edges_ref.at[:, :LAG]),
        (prim_ref.at[:, rows_n - LAG :], edges_ref.at[:, LAG:]),
        (sec_ref.at[0, :, rows_n - HALO :], down_ref),
        (sec_ref.at[0, :, :HALO], up_ref),
        (prim_ref.at[:, LAG : rows_n - LAG], middle_ref),
    )
    for copy in start_all(pieces, sems):
        copy.wait()


def resample_kernel(sec_ref, low_ref, high_ref, ao_ref, ro_ref, af_ref, rf_ref, out_ref, azim_ref):
    rows_n, cols_n = sec_ref.shape[2:]
    span = BAND + 2 * HALO
    shape = (BAND, span)
    offset = lax.broadcasted_iota(jnp.int32, shape, 1) - lax.broadcasted_iota(jnp.int32, shape, 0)
    az_band = band(shape, offset - HALO - ao_ref[...], tap_rows(af_ref[...]))
    for part in range(2):
        for start in range(0, rows_n, BAND):
            pieces = []
            if start == 0:
                pieces.append(low_ref[part])
            pieces.append(sec_ref[0, part, max(0, start - HALO) : min(rows_n, start + BAND + HALO)])
            if start + BAND == rows_n:
                pieces.append(high_ref[part])
            rows = jnp.concatenate(pieces, axis=0) if len(pieces) > 1 else pieces[0]
            azim_ref[part, start : start + BAND] = jnp.dot(
                az_band, rows, preferred_element_type=jnp.float32
            ).astype(jnp.bfloat16)

    square = (LANE, LANE)
    offset = lax.broadcasted_iota(jnp.int32, square, 0) - lax.broadcasted_iota(jnp.int32, square, 1)
    taps = tap_rows(rf_ref[...])
    before, same, after = [
        band(square, offset + shift - ro_ref[...], taps) for shift in (-LANE, 0, LANE)
    ]
    none = jnp.zeros(square, jnp.bfloat16)
    blocks_n, _, _, width = out_ref.shape
    lanes_n = width // LANE
    columns = []
    for lane in range(lanes_n):
        column = [none] * (lanes_n + 2)
        column[lane], column[lane + 1], column[lane + 2] = before, same, after
        columns.append(jnp.concatenate(column, axis=0))
    rg_band = jnp.concatenate(columns, axis=1)
    for block in range(blocks_n):
        first = block * width - LANE
        last = (block + 1) * width + LANE
        taken = slice(max(first, 0), min(last, cols_n))
        used = rg_band[taken.start - first : taken.stop - first]
        for part in range(2):
            out_ref[block, part] = jnp.dot(
                azim_ref[part, :, taken], used, preferred_element_type=jnp.float32
            ).astype(jnp.bfloat16)


def interfere(prim_re, prim_im, sec_re, sec_im):
    p_re, p_im = prim_re.astype(jnp.float32), prim_im.astype(jnp.float32)
    s_re, s_im = sec_re.astype(jnp.float32), sec_im.astype(jnp.float32)
    return p_re * s_re + p_im * s_im, p_im * s_re - p_re * s_im


def look_columns(width, block, looks_n):
    shape = (width, looks_n)
    col = lax.broadcasted_iota(jnp.int32, shape, 0) + block * width
    look = lax.broadcasted_iota(jnp.int32, shape, 1) * LR
    return jnp.where((col >= look) & (col < look + LR), 1.0, 0.0).astype(jnp.bfloat16)


def look_rows(sums_ref, part, start, rows_n):
    count = rows_n // LA
    total = sums_ref[part, pl.ds(start, count, LA)]
    for row in range(1, LA):
        total = total + sums_ref[part, pl.ds(start + row, count, LA)]
    return total


def slots(own_ref, beside_ref, near_ref, skip_ref, far_ref):
    here = lax.axis_index("date")
    inner = (here == 1) | (here == 2)
    low = here < 2
    return (
        (here, lambda part: own_ref[part]),
        (jnp.where(lax.rem(here, 2) == 0, here + 1, here - 1), lambda part: beside_ref[part]),
        (jnp.where(low, 2, 1), lambda part: jnp.where(inner, near_ref[part], skip_ref[part])),
        (jnp.where(low, 3, 0), lambda part: jnp.where(inner, skip_ref[part], far_ref[part])),
    )


def margin_kernel(
    own_ref, beside_ref, near_ref, skip_ref, far_ref, res_ref, first_ref, last_ref, looks_ref, sums_ref
):
    _, _, rows_n, width = res_ref.shape
    looks_n = looks_ref.shape[2]
    totals = [None, None]
    for step, (block, read) in enumerate(slots(own_ref, beside_ref, near_ref, skip_ref, far_ref)):
        prim_re, prim_im = read(0), read(1)
        select = look_columns(width, block, looks_n)
        columns = pl.ds(pl.multiple_of(block * width, width), width)
        halves = []
        for held, start, target in ((0, 0, first_ref), (LAG, rows_n - LAG, last_ref)):
            pair = interfere(
                prim_re[held : held + LAG],
                prim_im[held : held + LAG],
                res_ref[block, 0, start : start + LAG],
                res_ref[block, 1, start : start + LAG],
            )
            pair = [value.astype(jnp.bfloat16) for value in pair]
            for part in range(2):
                target[part, :, columns] = pair[part]
            halves.append(pair)
        for part in range(2):
            both = jnp.concatenate([halves[0][part], halves[1][part]], axis=0)
            summed = jnp.dot(both, select, preferred_element_type=jnp.float32)
            totals[part] = summed if step == 0 else totals[part] + summed
    for part in range(2):
        sums_ref[part] = totals[part]
        looks_ref[part] = look_rows(sums_ref, part, 0, 2 * LAG)


def stats_kernel(last_ref, later_ref, weight_ref, stats_ref):
    cols_n = last_ref.shape[2]
    weight = weight_ref[...]
    i_re, i_im = last_ref[0].astype(jnp.float32), last_ref[1].astype(jnp.float32)
    l_re, l_im = later_ref[0].astype(jnp.float32), later_ref[1].astype(jnp.float32)
    values = (
        i_re * l_re + i_im * l_im,
        i_im * l_re - i_re * l_im,
        0.5 * (i_re * i_re + i_im * i_im + l_re * l_re + l_im * l_im),
    )
    rows = []
    for value in values:
        folded = value[:, :LANE]
        for start in range(LANE, cols_n, LANE):
            folded = folded + value[:, start : start + LANE]
        rows.append(jnp.sum(folded * weight, axis=0, keepdims=True))
    rows.append(jnp.sum(weight, axis=0, keepdims=True) * (cols_n // LANE))
    rows.append(jnp.zeros((4, LANE), jnp.float32))
    stats_ref[...] = jnp.concatenate(rows, axis=0)


def look_sums(pieces, res_ref, looks_n):
    _, _, rows_n, width = res_ref.shape
    totals = [None, None]
    for step, (block, read) in enumerate(pieces):
        select = look_columns(width, block, looks_n)
        pair = interfere(
            read(0),
            read(1),
            res_ref[block, 0, LAG : rows_n - LAG],
            res_ref[block, 1, LAG : rows_n - LAG],
        )
        for part in range(2):
            summed = jnp.dot(
                pair[part].astype(jnp.bfloat16), select, preferred_element_type=jnp.float32
            )
            totals[part] = summed if step == 0 else totals[part] + summed
    return totals


def middle_kernel(own_ref, beside_ref, near_ref, skip_ref, res_ref, out_ref):
    pieces = slots(own_ref, beside_ref, near_ref, skip_ref, None)[:3]
    for part, total in enumerate(look_sums(pieces, res_ref, out_ref.shape[2])):
        out_ref[part] = total


def finish_kernel(
    skip_ref, far_ref, res_ref, before_ref, looks_ref, mine_ref, other_ref, out_ref, sums_ref
):
    looks_n = out_ref.shape[3]
    middle_n = before_ref.shape[1]
    totals = look_sums(slots(None, None, None, skip_ref, far_ref)[3:], res_ref, looks_n)
    totals = [total + before_ref[part] for part, total in enumerate(totals)]
    stats = jnp.sum(mine_ref[...] + other_ref[...], axis=1, keepdims=True)
    e_re, e_im, power, count = [stats[row : row + 1] for row in range(4)]
    magnitude = jnp.sqrt(e_re * e_re + e_im * e_im)
    floor_val = (power + 1e-06) / jnp.sqrt(jnp.maximum(count, 1.0))
    denom = jnp.maximum(magnitude, floor_val)
    u_re = e_re / denom * (1.0 / (LA * LR))
    u_im = e_im / denom * (1.0 / (LA * LR))
    edge = LAG // LA
    for part in range(2):
        sums_ref[part] = totals[part]
    for out_at, held, rows in (
        (0, looks_ref[:, :edge], edge),
        (edge, [look_rows(sums_ref, part, 0, middle_n) for part in range(2)], middle_n // LA),
        (edge + middle_n // LA, looks_ref[:, edge:], edge),
    ):
        out_ref[0, 0, out_at : out_at + rows] = held[0] * u_re + held[1] * u_im
        out_ref[0, 1, out_at : out_at + rows] = held[1] * u_re - held[0] * u_im


def call(kernel, outs, scratch, cost, *args, places=None, limit=VMEM_LIMIT):
    vmem = pl.BlockSpec(memory_space=pltpu.VMEM)
    return pl.pallas_call(
        kernel,
        out_shape=outs,
        in_specs=[places or vmem] * len(args),
        out_specs=jax.tree.map(lambda _: places or vmem, outs),
        scratch_shapes=scratch,
        compiler_params=pltpu.CompilerParams(vmem_limit_bytes=limit),
        cost_estimate=pl.CostEstimate(flops=cost[0], bytes_accessed=cost[1], transcendentals=0),
    )(*args)


def spread(block):
    skip = lax.ppermute(block, "date", [(0, 2), (2, 0), (1, 3), (3, 1)])
    beside = lax.ppermute(block, "date", [(0, 1), (1, 0), (2, 3), (3, 2)])
    near = lax.ppermute(block, "date", [(1, 2), (2, 1)])
    far = lax.ppermute(skip, "date", [(1, 0), (2, 3)])
    return beside, near, skip, far


def fused(secondary, primary, margin_mask, az_off, rg_off, az_frac, rg_frac):
    _, _, rows_n, cols_n = secondary.shape
    width = primary.shape[2]
    dates_n = lax.axis_size("date")
    tiles_n = lax.axis_size("tile")
    bf16, f32 = jnp.bfloat16, jnp.float32
    shape = jax.ShapeDtypeStruct
    looks_n = cols_n // LR
    middle_n = rows_n - 2 * LAG
    hbm = pl.BlockSpec(memory_space=pltpu.HBM)

    halo = shape((2, HALO, cols_n), bf16)
    edges, middle, down, up = call(
        prepare_kernel,
        (shape((2, 2 * LAG, width), bf16), shape((2, middle_n, width), bf16), halo, halo),
        [pltpu.SemaphoreType.DMA((5,))],
        (0, 4 * 2 * rows_n * width),
        secondary, primary, places=hbm, limit=VMEM_ALL,
    )
    around = spread(edges)
    low = passed_along(down, "tile", 1)
    high = passed_along(up, "tile", -1)
    weight = jnp.broadcast_to(margin_mask[rows_n - LAG :].astype(f32)[:, None], (LAG, LANE))
    res = call(
        resample_kernel,
        shape((dates_n, 2, rows_n, width), bf16),
        [pltpu.VMEM((2, rows_n, cols_n), bf16)],
        (2 * 2 * rows_n * cols_n * (2 * HALO + BAND + 2 * width), 8 * rows_n * cols_n),
        secondary, low, high, az_off, rg_off, az_frac, rg_frac,
    )
    others = spread(middle)
    margin = shape((2, LAG, cols_n), bf16)
    first, last, looks = call(
        margin_kernel,
        (margin, margin, shape((2, 2 * LAG // LA, looks_n), f32)),
        [pltpu.VMEM((2, 2 * LAG, looks_n), f32)],
        (2 * 2 * 2 * LAG * cols_n * looks_n, 24 * LAG * cols_n),
        edges, *around, res,
    )
    later = passed_along(first, "tile", -1)
    stats = call(
        stats_kernel,
        shape((8, LANE), f32),
        [],
        (20 * LAG * cols_n, 8 * LAG * cols_n),
        last, later, weight,
    )
    beside, near, skip, far = others
    before = call(
        middle_kernel,
        shape((2, middle_n, looks_n), f32),
        [],
        (2 * 2 * middle_n * cols_n * looks_n, 8 * rows_n * cols_n),
        middle, beside, near, skip, res,
    )
    stride = 1
    other = jnp.zeros_like(stats)
    while stride < tiles_n:
        stats = stats + other if stride > 1 else stats
        other = lax.ppermute(stats, "tile", [(at, at ^ stride) for at in range(tiles_n)])
        stride *= 2
    return call(
        finish_kernel,
        shape((1, 2, rows_n // LA, looks_n), f32),
        [pltpu.VMEM((2, middle_n, looks_n), f32)],
        (2 * middle_n * cols_n * looks_n, 4 * rows_n * cols_n),
        skip, far, res, before, looks, stats, other,
    )


def padded(block, sides, width):
    for axis, dim in sides:
        low = passed_along(
            lax.slice_in_dim(block, block.shape[dim] - width, None, axis=dim), axis, 1
        )
        high = passed_along(lax.slice_in_dim(block, 0, width, axis=dim), axis, -1)
        block = jnp.concatenate([low, block, high], axis=dim)
    return block


def band_taps(offset, frac):
    inside = (offset >= -3) & (offset <= 4)
    return jnp.where(inside, window(offset.astype(jnp.float32) - frac), 0.0).astype(jnp.bfloat16)


def multilook(values):
    depth, rows_n, cols_n = values.shape
    return values.reshape(depth, rows_n // LA, LA, cols_n // LR, LR).mean(axis=(2, 4))


def plain(secondary, primary, margin_mask, az_off, rg_off, az_frac, rg_frac):
    rim_rows = KA + 4
    block_cols = 256
    image = secondary[0]
    rows_n = image.shape[1]
    cols_n = image.shape[2]
    extended = padded(image, (("tile", 1),), rim_rows)
    row_out = lax.broadcasted_iota(jnp.int32, (rows_n, rows_n + 2 * rim_rows), 0)
    row_in = lax.broadcasted_iota(jnp.int32, (rows_n, rows_n + 2 * rim_rows), 1)
    azim_taps = band_taps(row_in - row_out - az_off[0, 0] - rim_rows, az_frac[0, 0])
    azim = jnp.einsum(
        "im,kmc->kic", azim_taps, extended, preferred_element_type=jnp.float32
    ).astype(jnp.bfloat16)
    blocks_n = cols_n // block_cols
    col_pad = jnp.pad(azim, ((0, 0), (0, 0), (block_cols // 2, block_cols // 2)))
    pieces = col_pad.reshape(2, rows_n, blocks_n + 1, block_cols)
    inputs = jnp.concatenate([pieces[:, :, :-1], pieces[:, :, 1:]], axis=3)
    col_in = lax.broadcasted_iota(jnp.int32, (2 * block_cols, block_cols), 0)
    col_out = lax.broadcasted_iota(jnp.int32, (2 * block_cols, block_cols), 1)
    range_taps = band_taps(col_in - block_cols // 2 - col_out - rg_off[0, 0], rg_frac[0, 0])
    resampled = jnp.einsum("kibm,mn->kibn", inputs, range_taps, preferred_element_type=jnp.float32)
    resampled = resampled.reshape(2, rows_n, cols_n).astype(jnp.bfloat16)
    prim = lax.all_gather(primary, "date", axis=2, tiled=True)[None]
    sec_f = resampled[None].astype(jnp.float32)
    prim_f = prim.astype(jnp.float32)
    ifg_re = prim_f[:, 0] * sec_f[:, 0] + prim_f[:, 1] * sec_f[:, 1]
    ifg_im = prim_f[:, 1] * sec_f[:, 0] - prim_f[:, 0] * sec_f[:, 1]
    interf = jnp.stack((ifg_re, ifg_im), axis=1)
    upcoming = passed_along(interf[:, :, :LAG, :], "tile", -1)
    later = jnp.concatenate([interf[:, :, LAG:, :], upcoming], axis=2)
    l_re = later[:, 0]
    l_im = later[:, 1]
    weight = margin_mask.astype(jnp.float32)[None, :, None]
    e_re = jnp.sum(weight * (ifg_re * l_re + ifg_im * l_im), axis=(1, 2))
    e_im = jnp.sum(weight * (ifg_im * l_re - ifg_re * l_im), axis=(1, 2))
    power = jnp.sum(
        weight * 0.5 * (ifg_re * ifg_re + ifg_im * ifg_im + l_re * l_re + l_im * l_im), axis=(1, 2)
    )
    count = jnp.zeros_like(e_re) + jnp.sum(margin_mask.astype(jnp.float32)) * interf.shape[3]
    stats = jnp.stack((e_re, e_im, power, count), axis=1)
    totals = lax.psum(stats, "tile")
    magnitude = jnp.sqrt(totals[:, 0] * totals[:, 0] + totals[:, 1] * totals[:, 1])
    floor_val = (totals[:, 2] + 1e-06) / jnp.sqrt(jnp.maximum(totals[:, 3], 1.0))
    denom = jnp.maximum(magnitude, floor_val)
    u_re = (totals[:, 0] / denom)[:, None, None]
    u_im = (totals[:, 1] / denom)[:, None, None]
    c_re = multilook(ifg_re * u_re + ifg_im * u_im)
    c_im = multilook(ifg_im * u_re - ifg_re * u_im)
    return jnp.stack((c_re, c_im), axis=1)


def shards(secondary, primary, *rest):
    rows_n, width = primary.shape[1:]
    fits = rows_n % BAND == 0 and rows_n > 2 * LAG + BAND and width % LANE == 0
    tiles_n = lax.axis_size("tile")
    fits = fits and lax.axis_size("date") == 4 and tiles_n & (tiles_n - 1) == 0
    return (fused if fits else plain)(secondary, primary, *rest)


def solution(mesh):
    return jax.shard_map(
        shards,
        mesh=mesh,
        in_specs=(
            P("date", None, "tile", None),
            P(None, "tile", "date"),
            P("tile"),
            P("date", "tile"),
            P("date", "tile"),
            P("date", "tile"),
            P("date", "tile"),
        ),
        out_specs=P("date", None, "tile", None),
        check_vma=False,
    )
```

```python
import functools

import jax
import jax.numpy as jnp
from jax import lax
from jax.experimental import pallas as pl
from jax.experimental.pallas import tpu as pltpu
from jax.sharding import PartitionSpec as P

KA = 16
LAG = 64
LA = 2
LR = 8
LANE = 128
BAND = 128
HALO = 32
VMEM_LIMIT = 40 * 1024 * 1024


def passed_along(value, axis, steps):
    count = lax.axis_size(axis)
    initial, last = (max(0, -steps), min(count, count - steps))
    return lax.ppermute(value, axis, [(source, source + steps) for source in range(initial, last)])


def window(dist):
    return jnp.sinc(dist) * (0.5 + 0.5 * jnp.cos(jnp.pi * dist / 4.0))


def tap_rows(frac):
    dist = lax.broadcasted_iota(jnp.int32, (8, LANE), 0).astype(jnp.float32) - 3.0 - frac
    angle = jnp.pi * dist
    sinc = jnp.where(dist == 0.0, 1.0, jnp.sin(angle) / jnp.where(dist == 0.0, 1.0, angle))
    taps = sinc * (0.5 + 0.5 * jnp.cos(jnp.pi * dist / 4.0))
    return taps.astype(jnp.bfloat16).astype(jnp.float32)


def band(shape, distance, taps):
    total = jnp.zeros(shape, jnp.float32)
    for j in range(8):
        total = jnp.where(distance == j - 3, taps[j : j + 1, :1], total)
    return total.astype(jnp.bfloat16)


def cut_edges_kernel(prim_ref, edges_ref):
    rows_n = prim_ref.shape[1]
    edges_ref[:, :LAG] = prim_ref[:, :LAG]
    edges_ref[:, LAG:] = prim_ref[:, rows_n - LAG :]


def cut_halo_kernel(sec_ref, down_ref, up_ref):
    rows_n = sec_ref.shape[2]
    down_ref[...] = sec_ref[0, :, rows_n - HALO :]
    up_ref[...] = sec_ref[0, :, :HALO]


def cut_middle_kernel(prim_ref, *refs):
    refs[-1][...] = prim_ref[:, LAG : prim_ref.shape[1] - LAG]


def resample_kernel(sec_ref, low_ref, high_ref, ao_ref, ro_ref, af_ref, rf_ref, out_ref, azim_ref):
    rows_n, cols_n = sec_ref.shape[2:]
    span = BAND + 2 * HALO
    shape = (BAND, span)
    offset = lax.broadcasted_iota(jnp.int32, shape, 1) - lax.broadcasted_iota(jnp.int32, shape, 0)
    az_band = band(shape, offset - HALO - ao_ref[...], tap_rows(af_ref[...]))
    for part in range(2):
        for start in range(0, rows_n, BAND):
            pieces = []
            if start == 0:
                pieces.append(low_ref[part])
            pieces.append(sec_ref[0, part, max(0, start - HALO) : min(rows_n, start + BAND + HALO)])
            if start + BAND == rows_n:
                pieces.append(high_ref[part])
            rows = jnp.concatenate(pieces, axis=0) if len(pieces) > 1 else pieces[0]
            azim_ref[part, start : start + BAND] = jnp.dot(
                az_band, rows, preferred_element_type=jnp.float32
            ).astype(jnp.bfloat16)

    square = (LANE, LANE)
    offset = lax.broadcasted_iota(jnp.int32, square, 0) - lax.broadcasted_iota(jnp.int32, square, 1)
    taps = tap_rows(rf_ref[...])
    before, same, after = [
        band(square, offset + shift - ro_ref[...], taps) for shift in (-LANE, 0, LANE)
    ]
    none = jnp.zeros(square, jnp.bfloat16)
    blocks_n, _, _, width = out_ref.shape
    lanes_n = width // LANE
    columns = []
    for lane in range(lanes_n):
        column = [none] * (lanes_n + 2)
        column[lane], column[lane + 1], column[lane + 2] = before, same, after
        columns.append(jnp.concatenate(column, axis=0))
    rg_band = jnp.concatenate(columns, axis=1)
    for block in range(blocks_n):
        first = block * width - LANE
        last = (block + 1) * width + LANE
        taken = slice(max(first, 0), min(last, cols_n))
        used = rg_band[taken.start - first : taken.stop - first]
        for part in range(2):
            out_ref[block, part] = jnp.dot(
                azim_ref[part, :, taken], used, preferred_element_type=jnp.float32
            ).astype(jnp.bfloat16)


def interfere(prim_re, prim_im, sec_re, sec_im):
    p_re, p_im = prim_re.astype(jnp.float32), prim_im.astype(jnp.float32)
    s_re, s_im = sec_re.astype(jnp.float32), sec_im.astype(jnp.float32)
    return p_re * s_re + p_im * s_im, p_im * s_re - p_re * s_im


def look_columns(width, block, looks_n):
    shape = (width, looks_n)
    col = lax.broadcasted_iota(jnp.int32, shape, 0) + block * width
    look = lax.broadcasted_iota(jnp.int32, shape, 1) * LR
    return jnp.where((col >= look) & (col < look + LR), 1.0, 0.0).astype(jnp.bfloat16)


def look_rows(sums_ref, part, start, rows_n):
    count = rows_n // LA
    total = sums_ref[part, pl.ds(start, count, LA)]
    for row in range(1, LA):
        total = total + sums_ref[part, pl.ds(start + row, count, LA)]
    return total


def slots(own_ref, beside_ref, near_ref, skip_ref, far_ref):
    here = lax.axis_index("date")
    inner = (here == 1) | (here == 2)
    low = here < 2
    return (
        (here, lambda part: own_ref[part]),
        (jnp.where(lax.rem(here, 2) == 0, here + 1, here - 1), lambda part: beside_ref[part]),
        (jnp.where(low, 2, 1), lambda part: jnp.where(inner, near_ref[part], skip_ref[part])),
        (jnp.where(low, 3, 0), lambda part: jnp.where(inner, skip_ref[part], far_ref[part])),
    )


def margin_kernel(
    own_ref, beside_ref, near_ref, skip_ref, far_ref, res_ref, first_ref, last_ref, looks_ref, sums_ref
):
    _, _, rows_n, width = res_ref.shape
    looks_n = looks_ref.shape[2]
    totals = [None, None]
    for step, (block, read) in enumerate(slots(own_ref, beside_ref, near_ref, skip_ref, far_ref)):
        prim_re, prim_im = read(0), read(1)
        select = look_columns(width, block, looks_n)
        columns = pl.ds(pl.multiple_of(block * width, width), width)
        halves = []
        for held, start, target in ((0, 0, first_ref), (LAG, rows_n - LAG, last_ref)):
            pair = interfere(
                prim_re[held : held + LAG],
                prim_im[held : held + LAG],
                res_ref[block, 0, start : start + LAG],
                res_ref[block, 1, start : start + LAG],
            )
            pair = [value.astype(jnp.bfloat16) for value in pair]
            for part in range(2):
                target[part, :, columns] = pair[part]
            halves.append(pair)
        for part in range(2):
            both = jnp.concatenate([halves[0][part], halves[1][part]], axis=0)
            summed = jnp.dot(both, select, preferred_element_type=jnp.float32)
            totals[part] = summed if step == 0 else totals[part] + summed
    for part in range(2):
        sums_ref[part] = totals[part]
        looks_ref[part] = look_rows(sums_ref, part, 0, 2 * LAG)


def stats_kernel(last_ref, later_ref, weight_ref, stats_ref):
    cols_n = last_ref.shape[2]
    weight = weight_ref[...]
    i_re, i_im = last_ref[0].astype(jnp.float32), last_ref[1].astype(jnp.float32)
    l_re, l_im = later_ref[0].astype(jnp.float32), later_ref[1].astype(jnp.float32)
    values = (
        i_re * l_re + i_im * l_im,
        i_im * l_re - i_re * l_im,
        0.5 * (i_re * i_re + i_im * i_im + l_re * l_re + l_im * l_im),
    )
    rows = []
    for value in values:
        folded = value[:, :LANE]
        for start in range(LANE, cols_n, LANE):
            folded = folded + value[:, start : start + LANE]
        rows.append(jnp.sum(folded * weight, axis=0, keepdims=True))
    rows.append(jnp.sum(weight, axis=0, keepdims=True) * (cols_n // LANE))
    rows.append(jnp.zeros((4, LANE), jnp.float32))
    stats_ref[...] = jnp.concatenate(rows, axis=0)


def look_sums(pieces, res_ref, looks_n):
    _, _, rows_n, width = res_ref.shape
    totals = [None, None]
    for step, (block, read) in enumerate(pieces):
        select = look_columns(width, block, looks_n)
        pair = interfere(
            read(0),
            read(1),
            res_ref[block, 0, LAG : rows_n - LAG],
            res_ref[block, 1, LAG : rows_n - LAG],
        )
        for part in range(2):
            summed = jnp.dot(
                pair[part].astype(jnp.bfloat16), select, preferred_element_type=jnp.float32
            )
            totals[part] = summed if step == 0 else totals[part] + summed
    return totals


def middle_kernel(own_ref, beside_ref, near_ref, skip_ref, res_ref, out_ref):
    pieces = slots(own_ref, beside_ref, near_ref, skip_ref, None)[:3]
    for part, total in enumerate(look_sums(pieces, res_ref, out_ref.shape[2])):
        out_ref[part] = total


def finish_kernel(
    skip_ref, far_ref, res_ref, before_ref, looks_ref, mine_ref, other_ref, out_ref, sums_ref
):
    looks_n = out_ref.shape[3]
    middle_n = before_ref.shape[1]
    totals = look_sums(slots(None, None, None, skip_ref, far_ref)[3:], res_ref, looks_n)
    totals = [total + before_ref[part] for part, total in enumerate(totals)]
    stats = jnp.sum(mine_ref[...] + other_ref[...], axis=1, keepdims=True)
    e_re, e_im, power, count = [stats[row : row + 1] for row in range(4)]
    magnitude = jnp.sqrt(e_re * e_re + e_im * e_im)
    floor_val = (power + 1e-06) / jnp.sqrt(jnp.maximum(count, 1.0))
    denom = jnp.maximum(magnitude, floor_val)
    u_re = e_re / denom * (1.0 / (LA * LR))
    u_im = e_im / denom * (1.0 / (LA * LR))
    edge = LAG // LA
    for part in range(2):
        sums_ref[part] = totals[part]
    for out_at, held, rows in (
        (0, looks_ref[:, :edge], edge),
        (edge, [look_rows(sums_ref, part, 0, middle_n) for part in range(2)], middle_n // LA),
        (edge + middle_n // LA, looks_ref[:, edge:], edge),
    ):
        out_ref[0, 0, out_at : out_at + rows] = held[0] * u_re + held[1] * u_im
        out_ref[0, 1, out_at : out_at + rows] = held[1] * u_re - held[0] * u_im


def call(kernel, outs, scratch, cost, *args):
    vmem = pl.BlockSpec(memory_space=pltpu.VMEM)
    return pl.pallas_call(
        kernel,
        out_shape=outs,
        in_specs=[vmem] * len(args),
        out_specs=jax.tree.map(lambda _: vmem, outs),
        scratch_shapes=scratch,
        compiler_params=pltpu.CompilerParams(vmem_limit_bytes=VMEM_LIMIT),
        cost_estimate=pl.CostEstimate(flops=cost[0], bytes_accessed=cost[1], transcendentals=0),
    )(*args)


def spread(block):
    skip = lax.ppermute(block, "date", [(0, 2), (2, 0), (1, 3), (3, 1)])
    beside = lax.ppermute(block, "date", [(0, 1), (1, 0), (2, 3), (3, 2)])
    near = lax.ppermute(block, "date", [(1, 2), (2, 1)])
    far = lax.ppermute(skip, "date", [(1, 0), (2, 3)])
    return beside, near, skip, far


def fused(secondary, primary, margin_mask, az_off, rg_off, az_frac, rg_frac):
    _, _, rows_n, cols_n = secondary.shape
    width = primary.shape[2]
    dates_n = lax.axis_size("date")
    tiles_n = lax.axis_size("tile")
    bf16, f32 = jnp.bfloat16, jnp.float32
    shape = jax.ShapeDtypeStruct
    looks_n = cols_n // LR
    middle_n = rows_n - 2 * LAG
    edges = call(
        cut_edges_kernel, shape((2, 2 * LAG, width), bf16), [], (0, 16 * LAG * width), primary
    )
    around = spread(edges)
    halo = shape((2, HALO, cols_n), bf16)
    down, up = call(cut_halo_kernel, (halo, halo), [], (0, 16 * HALO * cols_n), secondary)
    low = passed_along(down, "tile", 1)
    high = passed_along(up, "tile", -1)
    middle = call(
        cut_middle_kernel,
        shape((2, middle_n, width), bf16),
        [],
        (0, 8 * middle_n * width),
        primary, *around[:2],
    )
    weight = jnp.broadcast_to(margin_mask[rows_n - LAG :].astype(f32)[:, None], (LAG, LANE))
    res = call(
        resample_kernel,
        shape((dates_n, 2, rows_n, width), bf16),
        [pltpu.VMEM((2, rows_n, cols_n), bf16)],
        (2 * 2 * rows_n * cols_n * (2 * HALO + BAND + 2 * width), 8 * rows_n * cols_n),
        secondary, low, high, az_off, rg_off, az_frac, rg_frac,
    )
    others = spread(middle)
    margin = shape((2, LAG, cols_n), bf16)
    first, last, looks = call(
        margin_kernel,
        (margin, margin, shape((2, 2 * LAG // LA, looks_n), f32)),
        [pltpu.VMEM((2, 2 * LAG, looks_n), f32)],
        (2 * 2 * 2 * LAG * cols_n * looks_n, 24 * LAG * cols_n),
        edges, *around, res,
    )
    later = passed_along(first, "tile", -1)
    stats = call(
        stats_kernel,
        shape((8, LANE), f32),
        [],
        (20 * LAG * cols_n, 8 * LAG * cols_n),
        last, later, weight,
    )
    beside, near, skip, far = others
    before = call(
        middle_kernel,
        shape((2, middle_n, looks_n), f32),
        [],
        (2 * 2 * middle_n * cols_n * looks_n, 8 * rows_n * cols_n),
        middle, beside, near, skip, res,
    )
    stride = 1
    other = jnp.zeros_like(stats)
    while stride < tiles_n:
        stats = stats + other if stride > 1 else stats
        other = lax.ppermute(stats, "tile", [(at, at ^ stride) for at in range(tiles_n)])
        stride *= 2
    return call(
        finish_kernel,
        shape((1, 2, rows_n // LA, looks_n), f32),
        [pltpu.VMEM((2, middle_n, looks_n), f32)],
        (2 * middle_n * cols_n * looks_n, 4 * rows_n * cols_n),
        skip, far, res, before, looks, stats, other,
    )


def padded(block, sides, width):
    for axis, dim in sides:
        low = passed_along(
            lax.slice_in_dim(block, block.shape[dim] - width, None, axis=dim), axis, 1
        )
        high = passed_along(lax.slice_in_dim(block, 0, width, axis=dim), axis, -1)
        block = jnp.concatenate([low, block, high], axis=dim)
    return block


def band_taps(offset, frac):
    inside = (offset >= -3) & (offset <= 4)
    return jnp.where(inside, window(offset.astype(jnp.float32) - frac), 0.0).astype(jnp.bfloat16)


def multilook(values):
    depth, rows_n, cols_n = values.shape
    return values.reshape(depth, rows_n // LA, LA, cols_n // LR, LR).mean(axis=(2, 4))


def plain(secondary, primary, margin_mask, az_off, rg_off, az_frac, rg_frac):
    rim_rows = KA + 4
    block_cols = 256
    image = secondary[0]
    rows_n = image.shape[1]
    cols_n = image.shape[2]
    extended = padded(image, (("tile", 1),), rim_rows)
    row_out = lax.broadcasted_iota(jnp.int32, (rows_n, rows_n + 2 * rim_rows), 0)
    row_in = lax.broadcasted_iota(jnp.int32, (rows_n, rows_n + 2 * rim_rows), 1)
    azim_taps = band_taps(row_in - row_out - az_off[0, 0] - rim_rows, az_frac[0, 0])
    azim = jnp.einsum(
        "im,kmc->kic", azim_taps, extended, preferred_element_type=jnp.float32
    ).astype(jnp.bfloat16)
    blocks_n = cols_n // block_cols
    col_pad = jnp.pad(azim, ((0, 0), (0, 0), (block_cols // 2, block_cols // 2)))
    pieces = col_pad.reshape(2, rows_n, blocks_n + 1, block_cols)
    inputs = jnp.concatenate([pieces[:, :, :-1], pieces[:, :, 1:]], axis=3)
    col_in = lax.broadcasted_iota(jnp.int32, (2 * block_cols, block_cols), 0)
    col_out = lax.broadcasted_iota(jnp.int32, (2 * block_cols, block_cols), 1)
    range_taps = band_taps(col_in - block_cols // 2 - col_out - rg_off[0, 0], rg_frac[0, 0])
    resampled = jnp.einsum("kibm,mn->kibn", inputs, range_taps, preferred_element_type=jnp.float32)
    resampled = resampled.reshape(2, rows_n, cols_n).astype(jnp.bfloat16)
    prim = lax.all_gather(primary, "date", axis=2, tiled=True)[None]
    sec_f = resampled[None].astype(jnp.float32)
    prim_f = prim.astype(jnp.float32)
    ifg_re = prim_f[:, 0] * sec_f[:, 0] + prim_f[:, 1] * sec_f[:, 1]
    ifg_im = prim_f[:, 1] * sec_f[:, 0] - prim_f[:, 0] * sec_f[:, 1]
    interf = jnp.stack((ifg_re, ifg_im), axis=1)
    upcoming = passed_along(interf[:, :, :LAG, :], "tile", -1)
    later = jnp.concatenate([interf[:, :, LAG:, :], upcoming], axis=2)
    l_re = later[:, 0]
    l_im = later[:, 1]
    weight = margin_mask.astype(jnp.float32)[None, :, None]
    e_re = jnp.sum(weight * (ifg_re * l_re + ifg_im * l_im), axis=(1, 2))
    e_im = jnp.sum(weight * (ifg_im * l_re - ifg_re * l_im), axis=(1, 2))
    power = jnp.sum(
        weight * 0.5 * (ifg_re * ifg_re + ifg_im * ifg_im + l_re * l_re + l_im * l_im), axis=(1, 2)
    )
    count = jnp.zeros_like(e_re) + jnp.sum(margin_mask.astype(jnp.float32)) * interf.shape[3]
    stats = jnp.stack((e_re, e_im, power, count), axis=1)
    totals = lax.psum(stats, "tile")
    magnitude = jnp.sqrt(totals[:, 0] * totals[:, 0] + totals[:, 1] * totals[:, 1])
    floor_val = (totals[:, 2] + 1e-06) / jnp.sqrt(jnp.maximum(totals[:, 3], 1.0))
    denom = jnp.maximum(magnitude, floor_val)
    u_re = (totals[:, 0] / denom)[:, None, None]
    u_im = (totals[:, 1] / denom)[:, None, None]
    c_re = multilook(ifg_re * u_re + ifg_im * u_im)
    c_im = multilook(ifg_im * u_re - ifg_re * u_im)
    return jnp.stack((c_re, c_im), axis=1)


def shards(secondary, primary, *rest):
    rows_n, width = primary.shape[1:]
    fits = rows_n % BAND == 0 and rows_n > 2 * LAG + BAND and width % LANE == 0
    tiles_n = lax.axis_size("tile")
    fits = fits and lax.axis_size("date") == 4 and tiles_n & (tiles_n - 1) == 0
    return (fused if fits else plain)(secondary, primary, *rest)


def solution(mesh):
    return jax.shard_map(
        shards,
        mesh=mesh,
        in_specs=(
            P("date", None, "tile", None),
            P(None, "tile", "date"),
            P("tile"),
            P("date", "tile"),
            P("date", "tile"),
            P("date", "tile"),
            P("date", "tile"),
        ),
        out_specs=P("date", None, "tile", None),
        check_vma=False,
    )
```

```python
import functools

import jax
import jax.numpy as jnp
from jax import lax
from jax.experimental import pallas as pl
from jax.experimental.pallas import tpu as pltpu
from jax.sharding import PartitionSpec as P

KA = 16
LAG = 64
LA = 2
LR = 8
LANE = 128
BAND = 128
HALO = 32
VMEM_LIMIT = 40 * 1024 * 1024


def passed_along(value, axis, steps):
    count = lax.axis_size(axis)
    initial, last = (max(0, -steps), min(count, count - steps))
    return lax.ppermute(value, axis, [(source, source + steps) for source in range(initial, last)])


def window(dist):
    return jnp.sinc(dist) * (0.5 + 0.5 * jnp.cos(jnp.pi * dist / 4.0))


def tap_rows(frac):
    dist = lax.broadcasted_iota(jnp.int32, (8, LANE), 0).astype(jnp.float32) - 3.0 - frac
    angle = jnp.pi * dist
    sinc = jnp.where(dist == 0.0, 1.0, jnp.sin(angle) / jnp.where(dist == 0.0, 1.0, angle))
    taps = sinc * (0.5 + 0.5 * jnp.cos(jnp.pi * dist / 4.0))
    return taps.astype(jnp.bfloat16).astype(jnp.float32)


def band(shape, distance, taps):
    total = jnp.zeros(shape, jnp.float32)
    for j in range(8):
        total = jnp.where(distance == j - 3, taps[j : j + 1, :1], total)
    return total.astype(jnp.bfloat16)


def cut_edges_kernel(prim_ref, edges_ref):
    rows_n = prim_ref.shape[1]
    edges_ref[:, :LAG] = prim_ref[:, :LAG]
    edges_ref[:, LAG:] = prim_ref[:, rows_n - LAG :]


def cut_halo_kernel(sec_ref, down_ref, up_ref):
    rows_n = sec_ref.shape[2]
    down_ref[...] = sec_ref[0, :, rows_n - HALO :]
    up_ref[...] = sec_ref[0, :, :HALO]


def cut_middle_kernel(prim_ref, *refs):
    cut_ref = refs[-1]
    cut_ref[...] = prim_ref[:, LAG : LAG + cut_ref.shape[1]]


def relay_kernel(block_ref, stats_ref, out_ref):
    del stats_ref
    out_ref[...] = block_ref[:, : out_ref.shape[1]]


def resample_kernel(sec_ref, low_ref, high_ref, ao_ref, ro_ref, af_ref, rf_ref, out_ref, azim_ref):
    rows_n, cols_n = sec_ref.shape[2:]
    span = BAND + 2 * HALO
    shape = (BAND, span)
    offset = lax.broadcasted_iota(jnp.int32, shape, 1) - lax.broadcasted_iota(jnp.int32, shape, 0)
    az_band = band(shape, offset - HALO - ao_ref[...], tap_rows(af_ref[...]))
    for part in range(2):
        for start in range(0, rows_n, BAND):
            pieces = []
            if start == 0:
                pieces.append(low_ref[part])
            pieces.append(sec_ref[0, part, max(0, start - HALO) : min(rows_n, start + BAND + HALO)])
            if start + BAND == rows_n:
                pieces.append(high_ref[part])
            rows = jnp.concatenate(pieces, axis=0) if len(pieces) > 1 else pieces[0]
            azim_ref[part, start : start + BAND] = jnp.dot(
                az_band, rows, preferred_element_type=jnp.float32
            ).astype(jnp.bfloat16)

    square = (LANE, LANE)
    offset = lax.broadcasted_iota(jnp.int32, square, 0) - lax.broadcasted_iota(jnp.int32, square, 1)
    taps = tap_rows(rf_ref[...])
    before, same, after = [
        band(square, offset + shift - ro_ref[...], taps) for shift in (-LANE, 0, LANE)
    ]
    none = jnp.zeros(square, jnp.bfloat16)
    blocks_n, _, _, width = out_ref.shape
    lanes_n = width // LANE
    columns = []
    for lane in range(lanes_n):
        column = [none] * (lanes_n + 2)
        column[lane], column[lane + 1], column[lane + 2] = before, same, after
        columns.append(jnp.concatenate(column, axis=0))
    rg_band = jnp.concatenate(columns, axis=1)
    for block in range(blocks_n):
        first = block * width - LANE
        last = (block + 1) * width + LANE
        taken = slice(max(first, 0), min(last, cols_n))
        used = rg_band[taken.start - first : taken.stop - first]
        for part in range(2):
            out_ref[block, part] = jnp.dot(
                azim_ref[part, :, taken], used, preferred_element_type=jnp.float32
            ).astype(jnp.bfloat16)


def interfere(prim_re, prim_im, sec_re, sec_im):
    p_re, p_im = prim_re.astype(jnp.float32), prim_im.astype(jnp.float32)
    s_re, s_im = sec_re.astype(jnp.float32), sec_im.astype(jnp.float32)
    return p_re * s_re + p_im * s_im, p_im * s_re - p_re * s_im


def look_columns(width, block, looks_n):
    shape = (width, looks_n)
    col = lax.broadcasted_iota(jnp.int32, shape, 0) + block * width
    look = lax.broadcasted_iota(jnp.int32, shape, 1) * LR
    return jnp.where((col >= look) & (col < look + LR), 1.0, 0.0).astype(jnp.bfloat16)


def look_rows(sums_ref, part, start, rows_n):
    count = rows_n // LA
    total = sums_ref[part, pl.ds(start, count, LA)]
    for row in range(1, LA):
        total = total + sums_ref[part, pl.ds(start + row, count, LA)]
    return total


def margin_kernel(
    own_ref, one_ref, two_ref, three_ref, res_ref, first_ref, last_ref, looks_ref, sums_ref
):
    here = lax.axis_index("date")
    _, _, rows_n, width = res_ref.shape
    whole, edges = (0, rows_n - LAG), (0, LAG)
    looks_n = looks_ref.shape[2]
    totals = [None, None]
    for step, (prim_ref, starts) in enumerate(
        ((own_ref, whole), (one_ref, whole), (two_ref, edges), (three_ref, edges))
    ):
        block = jnp.bitwise_xor(here, step)
        select = look_columns(width, block, looks_n)
        columns = pl.ds(pl.multiple_of(block * width, width), width)
        halves = []
        for held, start, target in zip(starts, whole, (first_ref, last_ref)):
            pair = interfere(
                prim_ref[0, held : held + LAG],
                prim_ref[1, held : held + LAG],
                res_ref[block, 0, start : start + LAG],
                res_ref[block, 1, start : start + LAG],
            )
            pair = [value.astype(jnp.bfloat16) for value in pair]
            for part in range(2):
                target[part, :, columns] = pair[part]
            halves.append(pair)
        for part in range(2):
            both = jnp.concatenate([halves[0][part], halves[1][part]], axis=0)
            summed = jnp.dot(both, select, preferred_element_type=jnp.float32)
            totals[part] = summed if step == 0 else totals[part] + summed
    for part in range(2):
        sums_ref[part] = totals[part]
        looks_ref[part] = look_rows(sums_ref, part, 0, 2 * LAG)


def stats_kernel(last_ref, later_ref, weight_ref, stats_ref):
    cols_n = last_ref.shape[2]
    weight = weight_ref[...]
    i_re, i_im = last_ref[0].astype(jnp.float32), last_ref[1].astype(jnp.float32)
    l_re, l_im = later_ref[0].astype(jnp.float32), later_ref[1].astype(jnp.float32)
    values = (
        i_re * l_re + i_im * l_im,
        i_im * l_re - i_re * l_im,
        0.5 * (i_re * i_re + i_im * i_im + l_re * l_re + l_im * l_im),
    )
    rows = []
    for value in values:
        folded = value[:, :LANE]
        for start in range(LANE, cols_n, LANE):
            folded = folded + value[:, start : start + LANE]
        rows.append(jnp.sum(folded * weight, axis=0, keepdims=True))
    rows.append(jnp.sum(weight, axis=0, keepdims=True) * (cols_n // LANE))
    rows.append(jnp.zeros((4, LANE), jnp.float32))
    stats_ref[...] = jnp.concatenate(rows, axis=0)


def look_sums(pieces, res_ref, looks_n):
    here = lax.axis_index("date")
    _, _, rows_n, width = res_ref.shape
    middle_n = rows_n - 2 * LAG
    totals = [None, None]
    for at, (step, prim_ref) in enumerate(pieces):
        block = jnp.bitwise_xor(here, step)
        first = LAG if prim_ref.shape[1] == rows_n else 0
        select = look_columns(width, block, looks_n)
        pair = interfere(
            prim_ref[0, first : first + middle_n],
            prim_ref[1, first : first + middle_n],
            res_ref[block, 0, LAG : rows_n - LAG],
            res_ref[block, 1, LAG : rows_n - LAG],
        )
        for part in range(2):
            summed = jnp.dot(
                pair[part].astype(jnp.bfloat16), select, preferred_element_type=jnp.float32
            )
            totals[part] = summed if at == 0 else totals[part] + summed
    return totals


def middle_kernel(own_ref, one_ref, two_ref, res_ref, out_ref):
    pieces = ((0, own_ref), (1, one_ref), (2, two_ref))
    for part, total in enumerate(look_sums(pieces, res_ref, out_ref.shape[2])):
        out_ref[part] = total


def finish_kernel(
    three_ref, res_ref, before_ref, looks_ref, mine_ref, other_ref, out_ref, sums_ref
):
    looks_n = out_ref.shape[3]
    middle_n = before_ref.shape[1]
    totals = look_sums(((3, three_ref),), res_ref, looks_n)
    totals = [total + before_ref[part] for part, total in enumerate(totals)]
    stats = jnp.sum(mine_ref[...] + other_ref[...], axis=1, keepdims=True)
    e_re, e_im, power, count = [stats[row : row + 1] for row in range(4)]
    magnitude = jnp.sqrt(e_re * e_re + e_im * e_im)
    floor_val = (power + 1e-06) / jnp.sqrt(jnp.maximum(count, 1.0))
    denom = jnp.maximum(magnitude, floor_val)
    u_re = e_re / denom * (1.0 / (LA * LR))
    u_im = e_im / denom * (1.0 / (LA * LR))
    edge = LAG // LA
    for part in range(2):
        sums_ref[part] = totals[part]
    for out_at, held, rows in (
        (0, looks_ref[:, :edge], edge),
        (edge, [look_rows(sums_ref, part, 0, middle_n) for part in range(2)], middle_n // LA),
        (edge + middle_n // LA, looks_ref[:, edge:], edge),
    ):
        out_ref[0, 0, out_at : out_at + rows] = held[0] * u_re + held[1] * u_im
        out_ref[0, 1, out_at : out_at + rows] = held[1] * u_re - held[0] * u_im


def call(kernel, outs, scratch, cost, *args):
    vmem = pl.BlockSpec(memory_space=pltpu.VMEM)
    return pl.pallas_call(
        kernel,
        out_shape=outs,
        in_specs=[vmem] * len(args),
        out_specs=jax.tree.map(lambda _: vmem, outs),
        scratch_shapes=scratch,
        compiler_params=pltpu.CompilerParams(vmem_limit_bytes=VMEM_LIMIT),
        cost_estimate=pl.CostEstimate(flops=cost[0], bytes_accessed=cost[1], transcendentals=0),
    )(*args)


def swap(value, axis, step):
    return lax.ppermute(value, axis, [(at, at ^ step) for at in range(lax.axis_size(axis))])


def fused(secondary, primary, margin_mask, az_off, rg_off, az_frac, rg_frac):
    _, _, rows_n, cols_n = secondary.shape
    width = primary.shape[2]
    dates_n = lax.axis_size("date")
    tiles_n = lax.axis_size("tile")
    bf16, f32 = jnp.bfloat16, jnp.float32
    shape = jax.ShapeDtypeStruct
    looks_n = cols_n // LR
    middle_n = rows_n - 2 * LAG
    edges = call(
        cut_edges_kernel, shape((2, 2 * LAG, width), bf16), [], (0, 16 * LAG * width), primary
    )
    one = swap(primary, "date", 1)
    edges_two, edges_three = [swap(edges, "date", step) for step in (2, 3)]
    halo = shape((2, HALO, cols_n), bf16)
    down, up = call(cut_halo_kernel, (halo, halo), [], (0, 16 * HALO * cols_n), secondary)
    low = passed_along(down, "tile", 1)
    high = passed_along(up, "tile", -1)
    middle = call(
        cut_middle_kernel,
        shape((2, middle_n + 16, width), bf16),
        [],
        (0, 0),
        primary, edges_two,
    )
    weight = jnp.broadcast_to(margin_mask[rows_n - LAG :].astype(f32)[:, None], (LAG, LANE))
    res = call(
        resample_kernel,
        shape((dates_n, 2, rows_n, width), bf16),
        [pltpu.VMEM((2, rows_n, cols_n), bf16)],
        (0, 0),
        secondary, low, high, az_off, rg_off, az_frac, rg_frac,
    )
    two = swap(middle, "date", 2)
    margin = shape((2, LAG, cols_n), bf16)
    first, last, looks = call(
        margin_kernel,
        (margin, margin, shape((2, 2 * LAG // LA, looks_n), f32)),
        [pltpu.VMEM((2, 2 * LAG, looks_n), f32)],
        (0, 0),
        primary, one, edges_two, edges_three, res,
    )
    later = passed_along(first, "tile", -1)
    stats = call(
        stats_kernel,
        shape((8, LANE), f32),
        [],
        (0, 0),
        last, later, weight,
    )
    before = call(
        middle_kernel,
        shape((2, middle_n, looks_n), f32),
        [],
        (2 * 2 * middle_n * cols_n * looks_n, 8 * rows_n * cols_n),
        primary, one, two, res,
    )
    other = swap(stats, "tile", 1)
    block = shape((2, middle_n, width), bf16)
    relayed = call(relay_kernel, block, [], (0, 0), two, other)
    three = swap(relayed, "date", 1)
    stride = 2
    while stride < tiles_n:
        stats = stats + other
        other = swap(stats, "tile", stride)
        stride *= 2
    return call(
        finish_kernel,
        shape((1, 2, rows_n // LA, looks_n), f32),
        [pltpu.VMEM((2, middle_n, looks_n), f32)],
        (2 * middle_n * cols_n * looks_n, 4 * rows_n * cols_n),
        three, res, before, looks, stats, other,
    )


def padded(block, sides, width):
    for axis, dim in sides:
        low = passed_along(
            lax.slice_in_dim(block, block.shape[dim] - width, None, axis=dim), axis, 1
        )
        high = passed_along(lax.slice_in_dim(block, 0, width, axis=dim), axis, -1)
        block = jnp.concatenate([low, block, high], axis=dim)
    return block


def band_taps(offset, frac):
    inside = (offset >= -3) & (offset <= 4)
    return jnp.where(inside, window(offset.astype(jnp.float32) - frac), 0.0).astype(jnp.bfloat16)


def multilook(values):
    depth, rows_n, cols_n = values.shape
    return values.reshape(depth, rows_n // LA, LA, cols_n // LR, LR).mean(axis=(2, 4))


def plain(secondary, primary, margin_mask, az_off, rg_off, az_frac, rg_frac):
    rim_rows = KA + 4
    block_cols = 256
    image = secondary[0]
    rows_n = image.shape[1]
    cols_n = image.shape[2]
    extended = padded(image, (("tile", 1),), rim_rows)
    row_out = lax.broadcasted_iota(jnp.int32, (rows_n, rows_n + 2 * rim_rows), 0)
    row_in = lax.broadcasted_iota(jnp.int32, (rows_n, rows_n + 2 * rim_rows), 1)
    azim_taps = band_taps(row_in - row_out - az_off[0, 0] - rim_rows, az_frac[0, 0])
    azim = jnp.einsum(
        "im,kmc->kic", azim_taps, extended, preferred_element_type=jnp.float32
    ).astype(jnp.bfloat16)
    blocks_n = cols_n // block_cols
    col_pad = jnp.pad(azim, ((0, 0), (0, 0), (block_cols // 2, block_cols // 2)))
    pieces = col_pad.reshape(2, rows_n, blocks_n + 1, block_cols)
    inputs = jnp.concatenate([pieces[:, :, :-1], pieces[:, :, 1:]], axis=3)
    col_in = lax.broadcasted_iota(jnp.int32, (2 * block_cols, block_cols), 0)
    col_out = lax.broadcasted_iota(jnp.int32, (2 * block_cols, block_cols), 1)
    range_taps = band_taps(col_in - block_cols // 2 - col_out - rg_off[0, 0], rg_frac[0, 0])
    resampled = jnp.einsum("kibm,mn->kibn", inputs, range_taps, preferred_element_type=jnp.float32)
    resampled = resampled.reshape(2, rows_n, cols_n).astype(jnp.bfloat16)
    prim = lax.all_gather(primary, "date", axis=2, tiled=True)[None]
    sec_f = resampled[None].astype(jnp.float32)
    prim_f = prim.astype(jnp.float32)
    ifg_re = prim_f[:, 0] * sec_f[:, 0] + prim_f[:, 1] * sec_f[:, 1]
    ifg_im = prim_f[:, 1] * sec_f[:, 0] - prim_f[:, 0] * sec_f[:, 1]
    interf = jnp.stack((ifg_re, ifg_im), axis=1)
    upcoming = passed_along(interf[:, :, :LAG, :], "tile", -1)
    later = jnp.concatenate([interf[:, :, LAG:, :], upcoming], axis=2)
    l_re = later[:, 0]
    l_im = later[:, 1]
    weight = margin_mask.astype(jnp.float32)[None, :, None]
    e_re = jnp.sum(weight * (ifg_re * l_re + ifg_im * l_im), axis=(1, 2))
    e_im = jnp.sum(weight * (ifg_im * l_re - ifg_re * l_im), axis=(1, 2))
    power = jnp.sum(
        weight * 0.5 * (ifg_re * ifg_re + ifg_im * ifg_im + l_re * l_re + l_im * l_im), axis=(1, 2)
    )
    count = jnp.zeros_like(e_re) + jnp.sum(margin_mask.astype(jnp.float32)) * interf.shape[3]
    stats = jnp.stack((e_re, e_im, power, count), axis=1)
    totals = lax.psum(stats, "tile")
    magnitude = jnp.sqrt(totals[:, 0] * totals[:, 0] + totals[:, 1] * totals[:, 1])
    floor_val = (totals[:, 2] + 1e-06) / jnp.sqrt(jnp.maximum(totals[:, 3], 1.0))
    denom = jnp.maximum(magnitude, floor_val)
    u_re = (totals[:, 0] / denom)[:, None, None]
    u_im = (totals[:, 1] / denom)[:, None, None]
    c_re = multilook(ifg_re * u_re + ifg_im * u_im)
    c_im = multilook(ifg_im * u_re - ifg_re * u_im)
    return jnp.stack((c_re, c_im), axis=1)


def shards(secondary, primary, *rest):
    rows_n, width = primary.shape[1:]
    fits = rows_n % BAND == 0 and rows_n > 2 * LAG + BAND and width % LANE == 0
    tiles_n = lax.axis_size("tile")
    fits = fits and lax.axis_size("date") == 4 and tiles_n & (tiles_n - 1) == 0
    return (fused if fits else plain)(secondary, primary, *rest)


def solution(mesh):
    return jax.shard_map(
        shards,
        mesh=mesh,
        in_specs=(
            P("date", None, "tile", None),
            P(None, "tile", "date"),
            P("tile"),
            P("date", "tile"),
            P("date", "tile"),
            P("date", "tile"),
            P("date", "tile"),
        ),
        out_specs=P("date", None, "tile", None),
        check_vma=False,
    )
```

```python
import functools

import jax
import jax.numpy as jnp
from jax import lax
from jax.experimental import pallas as pl
from jax.experimental.pallas import tpu as pltpu
from jax.sharding import PartitionSpec as P

KA = 16
LAG = 64
LA = 2
LR = 8
LANE = 128
BAND = 128
HALO = 32
VMEM_LIMIT = 40 * 1024 * 1024


def passed_along(value, axis, steps):
    count = lax.axis_size(axis)
    initial, last = (max(0, -steps), min(count, count - steps))
    return lax.ppermute(value, axis, [(source, source + steps) for source in range(initial, last)])


def window(dist):
    return jnp.sinc(dist) * (0.5 + 0.5 * jnp.cos(jnp.pi * dist / 4.0))


def tap_rows(frac):
    dist = lax.broadcasted_iota(jnp.int32, (8, LANE), 0).astype(jnp.float32) - 3.0 - frac
    angle = jnp.pi * dist
    sinc = jnp.where(dist == 0.0, 1.0, jnp.sin(angle) / jnp.where(dist == 0.0, 1.0, angle))
    taps = sinc * (0.5 + 0.5 * jnp.cos(jnp.pi * dist / 4.0))
    return taps.astype(jnp.bfloat16).astype(jnp.float32)


def band(shape, distance, taps):
    total = jnp.zeros(shape, jnp.float32)
    for j in range(8):
        total = jnp.where(distance == j - 3, taps[j : j + 1, :1], total)
    return total.astype(jnp.bfloat16)


def cut_kernel(prim_ref, sec_ref, edges_ref, inner_ref, outer_ref):
    rows_n = prim_ref.shape[1]
    edges_ref[:, :LAG] = prim_ref[:, :LAG]
    edges_ref[:, LAG:] = prim_ref[:, rows_n - LAG :]
    first = lax.rem(lax.axis_index("tile"), 2) == 0
    down, up = sec_ref[0, :, rows_n - HALO :], sec_ref[0, :, :HALO]
    inner_ref[...] = jnp.where(first, down, up)
    outer_ref[...] = jnp.where(first, up, down)


def cut_middle_kernel(prim_ref, *refs):
    cut_ref = refs[-1]
    cut_ref[...] = prim_ref[:, LAG : LAG + cut_ref.shape[1]]


def relay_kernel(block_ref, stats_ref, out_ref):
    del stats_ref
    out_ref[...] = block_ref[:, : out_ref.shape[1]]


def resample_kernel(sec_ref, inner_ref, outer_ref, ao_ref, ro_ref, af_ref, rf_ref, out_ref, azim_ref):
    rows_n, cols_n = sec_ref.shape[2:]
    span = BAND + 2 * HALO
    shape = (BAND, span)
    offset = lax.broadcasted_iota(jnp.int32, shape, 1) - lax.broadcasted_iota(jnp.int32, shape, 0)
    az_band = band(shape, offset - HALO - ao_ref[...], tap_rows(af_ref[...]))
    first = lax.rem(lax.axis_index("tile"), 2) == 0
    for part in range(2):
        for start in range(0, rows_n, BAND):
            pieces = []
            if start == 0:
                pieces.append(jnp.where(first, outer_ref[part], inner_ref[part]))
            pieces.append(sec_ref[0, part, max(0, start - HALO) : min(rows_n, start + BAND + HALO)])
            if start + BAND == rows_n:
                pieces.append(jnp.where(first, inner_ref[part], outer_ref[part]))
            rows = jnp.concatenate(pieces, axis=0) if len(pieces) > 1 else pieces[0]
            azim_ref[part, start : start + BAND] = jnp.dot(
                az_band, rows, preferred_element_type=jnp.float32
            ).astype(jnp.bfloat16)

    square = (LANE, LANE)
    offset = lax.broadcasted_iota(jnp.int32, square, 0) - lax.broadcasted_iota(jnp.int32, square, 1)
    taps = tap_rows(rf_ref[...])
    before, same, after = [
        band(square, offset + shift - ro_ref[...], taps) for shift in (-LANE, 0, LANE)
    ]
    none = jnp.zeros(square, jnp.bfloat16)
    blocks_n, _, _, width = out_ref.shape
    lanes_n = width // LANE
    columns = []
    for lane in range(lanes_n):
        column = [none] * (lanes_n + 2)
        column[lane], column[lane + 1], column[lane + 2] = before, same, after
        columns.append(jnp.concatenate(column, axis=0))
    rg_band = jnp.concatenate(columns, axis=1)
    for block in range(blocks_n):
        first = block * width - LANE
        last = (block + 1) * width + LANE
        taken = slice(max(first, 0), min(last, cols_n))
        used = rg_band[taken.start - first : taken.stop - first]
        for part in range(2):
            out_ref[block, part] = jnp.dot(
                azim_ref[part, :, taken], used, preferred_element_type=jnp.float32
            ).astype(jnp.bfloat16)


def interfere(prim_re, prim_im, sec_re, sec_im):
    p_re, p_im = prim_re.astype(jnp.float32), prim_im.astype(jnp.float32)
    s_re, s_im = sec_re.astype(jnp.float32), sec_im.astype(jnp.float32)
    return p_re * s_re + p_im * s_im, p_im * s_re - p_re * s_im


def look_columns(width, block, looks_n):
    shape = (width, looks_n)
    col = lax.broadcasted_iota(jnp.int32, shape, 0) + block * width
    look = lax.broadcasted_iota(jnp.int32, shape, 1) * LR
    return jnp.where((col >= look) & (col < look + LR), 1.0, 0.0).astype(jnp.bfloat16)


def look_rows(sums_ref, part, start, rows_n):
    count = rows_n // LA
    total = sums_ref[part, pl.ds(start, count, LA)]
    for row in range(1, LA):
        total = total + sums_ref[part, pl.ds(start + row, count, LA)]
    return total


def margin_kernel(
    own_ref, one_ref, two_ref, three_ref, res_ref, first_ref, last_ref, looks_ref, sums_ref
):
    here = lax.axis_index("date")
    _, _, rows_n, width = res_ref.shape
    whole, edges = (0, rows_n - LAG), (0, LAG)
    looks_n = looks_ref.shape[2]
    totals = [None, None]
    for step, (prim_ref, starts) in enumerate(
        ((own_ref, whole), (one_ref, whole), (two_ref, edges), (three_ref, edges))
    ):
        block = jnp.bitwise_xor(here, step)
        select = look_columns(width, block, looks_n)
        columns = pl.ds(pl.multiple_of(block * width, width), width)
        halves = []
        for held, start, target in zip(starts, whole, (first_ref, last_ref)):
            pair = interfere(
                prim_ref[0, held : held + LAG],
                prim_ref[1, held : held + LAG],
                res_ref[block, 0, start : start + LAG],
                res_ref[block, 1, start : start + LAG],
            )
            pair = [value.astype(jnp.bfloat16) for value in pair]
            for part in range(2):
                target[part, :, columns] = pair[part]
            halves.append(pair)
        for part in range(2):
            both = jnp.concatenate([halves[0][part], halves[1][part]], axis=0)
            summed = jnp.dot(both, select, preferred_element_type=jnp.float32)
            totals[part] = summed if step == 0 else totals[part] + summed
    for part in range(2):
        sums_ref[part] = totals[part]
        looks_ref[part] = look_rows(sums_ref, part, 0, 2 * LAG)


def stats_kernel(last_ref, later_ref, weight_ref, stats_ref):
    cols_n = last_ref.shape[2]
    weight = weight_ref[...]
    i_re, i_im = last_ref[0].astype(jnp.float32), last_ref[1].astype(jnp.float32)
    l_re, l_im = later_ref[0].astype(jnp.float32), later_ref[1].astype(jnp.float32)
    values = (
        i_re * l_re + i_im * l_im,
        i_im * l_re - i_re * l_im,
        0.5 * (i_re * i_re + i_im * i_im + l_re * l_re + l_im * l_im),
    )
    rows = []
    for value in values:
        folded = value[:, :LANE]
        for start in range(LANE, cols_n, LANE):
            folded = folded + value[:, start : start + LANE]
        rows.append(jnp.sum(folded * weight, axis=0, keepdims=True))
    rows.append(jnp.sum(weight, axis=0, keepdims=True) * (cols_n // LANE))
    rows.append(jnp.zeros((4, LANE), jnp.float32))
    stats_ref[...] = jnp.concatenate(rows, axis=0)


def look_sums(pieces, res_ref, looks_n):
    here = lax.axis_index("date")
    _, _, rows_n, width = res_ref.shape
    middle_n = rows_n - 2 * LAG
    totals = [None, None]
    for at, (step, prim_ref) in enumerate(pieces):
        block = jnp.bitwise_xor(here, step)
        first = LAG if prim_ref.shape[1] == rows_n else 0
        select = look_columns(width, block, looks_n)
        pair = interfere(
            prim_ref[0, first : first + middle_n],
            prim_ref[1, first : first + middle_n],
            res_ref[block, 0, LAG : rows_n - LAG],
            res_ref[block, 1, LAG : rows_n - LAG],
        )
        for part in range(2):
            summed = jnp.dot(
                pair[part].astype(jnp.bfloat16), select, preferred_element_type=jnp.float32
            )
            totals[part] = summed if at == 0 else totals[part] + summed
    return totals


def middle_kernel(own_ref, one_ref, two_ref, res_ref, out_ref):
    pieces = ((0, own_ref), (1, one_ref), (2, two_ref))
    for part, total in enumerate(look_sums(pieces, res_ref, out_ref.shape[2])):
        out_ref[part] = total


def finish_kernel(
    three_ref, res_ref, before_ref, looks_ref, mine_ref, other_ref, out_ref, sums_ref
):
    looks_n = out_ref.shape[3]
    middle_n = before_ref.shape[1]
    totals = look_sums(((3, three_ref),), res_ref, looks_n)
    totals = [total + before_ref[part] for part, total in enumerate(totals)]
    stats = jnp.sum(mine_ref[...] + other_ref[...], axis=1, keepdims=True)
    e_re, e_im, power, count = [stats[row : row + 1] for row in range(4)]
    magnitude = jnp.sqrt(e_re * e_re + e_im * e_im)
    floor_val = (power + 1e-06) / jnp.sqrt(jnp.maximum(count, 1.0))
    denom = jnp.maximum(magnitude, floor_val)
    u_re = e_re / denom * (1.0 / (LA * LR))
    u_im = e_im / denom * (1.0 / (LA * LR))
    edge = LAG // LA
    for part in range(2):
        sums_ref[part] = totals[part]
    for out_at, held, rows in (
        (0, looks_ref[:, :edge], edge),
        (edge, [look_rows(sums_ref, part, 0, middle_n) for part in range(2)], middle_n // LA),
        (edge + middle_n // LA, looks_ref[:, edge:], edge),
    ):
        out_ref[0, 0, out_at : out_at + rows] = held[0] * u_re + held[1] * u_im
        out_ref[0, 1, out_at : out_at + rows] = held[1] * u_re - held[0] * u_im


def call(kernel, outs, scratch, cost, *args):
    vmem = pl.BlockSpec(memory_space=pltpu.VMEM)
    return pl.pallas_call(
        kernel,
        out_shape=outs,
        in_specs=[vmem] * len(args),
        out_specs=jax.tree.map(lambda _: vmem, outs),
        scratch_shapes=scratch,
        compiler_params=pltpu.CompilerParams(vmem_limit_bytes=VMEM_LIMIT),
        cost_estimate=pl.CostEstimate(flops=cost[0], bytes_accessed=cost[1], transcendentals=0),
    )(*args)


def swap(value, axis, step):
    return lax.ppermute(value, axis, [(at, at ^ step) for at in range(lax.axis_size(axis))])


def fused(secondary, primary, margin_mask, az_off, rg_off, az_frac, rg_frac):
    _, _, rows_n, cols_n = secondary.shape
    width = primary.shape[2]
    dates_n = lax.axis_size("date")
    tiles_n = lax.axis_size("tile")
    bf16, f32 = jnp.bfloat16, jnp.float32
    shape = jax.ShapeDtypeStruct
    looks_n = cols_n // LR
    middle_n = rows_n - 2 * LAG
    halo = shape((2, HALO, cols_n), bf16)
    edges, inner, outer = call(
        cut_kernel,
        (shape((2, 2 * LAG, width), bf16), halo, halo),
        [],
        (0, 0),
        primary, secondary,
    )
    edges_two = swap(edges, "date", 2)
    one = swap(primary, "date", 1)
    inner = swap(inner, "tile", 1)
    outer = lax.ppermute(
        outer, "tile", [(at, at + 1 if at % 2 else at - 1) for at in range(1, tiles_n - 1)]
    )
    edges_three = swap(edges_two, "date", 1)
    middle = call(
        cut_middle_kernel,
        shape((2, middle_n + 16, width), bf16),
        [],
        (0, 0),
        primary, one,
    )
    weight = jnp.broadcast_to(margin_mask[rows_n - LAG :].astype(f32)[:, None], (LAG, LANE))
    res = call(
        resample_kernel,
        shape((dates_n, 2, rows_n, width), bf16),
        [pltpu.VMEM((2, rows_n, cols_n), bf16)],
        (0, 0),
        secondary, inner, outer, az_off, rg_off, az_frac, rg_frac,
    )
    two = swap(middle, "date", 2)
    margin = shape((2, LAG, cols_n), bf16)
    first, last, looks = call(
        margin_kernel,
        (margin, margin, shape((2, 2 * LAG // LA, looks_n), f32)),
        [pltpu.VMEM((2, 2 * LAG, looks_n), f32)],
        (0, 0),
        primary, one, edges_two, edges_three, res,
    )
    later = passed_along(first, "tile", -1)
    stats = call(
        stats_kernel,
        shape((8, LANE), f32),
        [],
        (0, 0),
        last, later, weight,
    )
    before = call(
        middle_kernel,
        shape((2, middle_n, looks_n), f32),
        [],
        (2 * 2 * middle_n * cols_n * looks_n, 8 * rows_n * cols_n),
        primary, one, two, res,
    )
    other = swap(stats, "tile", 1)
    block = shape((2, middle_n, width), bf16)
    relayed = call(relay_kernel, block, [], (0, 0), two, other)
    three = swap(relayed, "date", 1)
    stride = 2
    while stride < tiles_n:
        stats = stats + other
        other = swap(stats, "tile", stride)
        stride *= 2
    return call(
        finish_kernel,
        shape((1, 2, rows_n // LA, looks_n), f32),
        [pltpu.VMEM((2, middle_n, looks_n), f32)],
        (2 * middle_n * cols_n * looks_n, 4 * rows_n * cols_n),
        three, res, before, looks, stats, other,
    )


def padded(block, sides, width):
    for axis, dim in sides:
        low = passed_along(
            lax.slice_in_dim(block, block.shape[dim] - width, None, axis=dim), axis, 1
        )
        high = passed_along(lax.slice_in_dim(block, 0, width, axis=dim), axis, -1)
        block = jnp.concatenate([low, block, high], axis=dim)
    return block


def band_taps(offset, frac):
    inside = (offset >= -3) & (offset <= 4)
    return jnp.where(inside, window(offset.astype(jnp.float32) - frac), 0.0).astype(jnp.bfloat16)


def multilook(values):
    depth, rows_n, cols_n = values.shape
    return values.reshape(depth, rows_n // LA, LA, cols_n // LR, LR).mean(axis=(2, 4))


def plain(secondary, primary, margin_mask, az_off, rg_off, az_frac, rg_frac):
    rim_rows = KA + 4
    block_cols = 256
    image = secondary[0]
    rows_n = image.shape[1]
    cols_n = image.shape[2]
    extended = padded(image, (("tile", 1),), rim_rows)
    row_out = lax.broadcasted_iota(jnp.int32, (rows_n, rows_n + 2 * rim_rows), 0)
    row_in = lax.broadcasted_iota(jnp.int32, (rows_n, rows_n + 2 * rim_rows), 1)
    azim_taps = band_taps(row_in - row_out - az_off[0, 0] - rim_rows, az_frac[0, 0])
    azim = jnp.einsum(
        "im,kmc->kic", azim_taps, extended, preferred_element_type=jnp.float32
    ).astype(jnp.bfloat16)
    blocks_n = cols_n // block_cols
    col_pad = jnp.pad(azim, ((0, 0), (0, 0), (block_cols // 2, block_cols // 2)))
    pieces = col_pad.reshape(2, rows_n, blocks_n + 1, block_cols)
    inputs = jnp.concatenate([pieces[:, :, :-1], pieces[:, :, 1:]], axis=3)
    col_in = lax.broadcasted_iota(jnp.int32, (2 * block_cols, block_cols), 0)
    col_out = lax.broadcasted_iota(jnp.int32, (2 * block_cols, block_cols), 1)
    range_taps = band_taps(col_in - block_cols // 2 - col_out - rg_off[0, 0], rg_frac[0, 0])
    resampled = jnp.einsum("kibm,mn->kibn", inputs, range_taps, preferred_element_type=jnp.float32)
    resampled = resampled.reshape(2, rows_n, cols_n).astype(jnp.bfloat16)
    prim = lax.all_gather(primary, "date", axis=2, tiled=True)[None]
    sec_f = resampled[None].astype(jnp.float32)
    prim_f = prim.astype(jnp.float32)
    ifg_re = prim_f[:, 0] * sec_f[:, 0] + prim_f[:, 1] * sec_f[:, 1]
    ifg_im = prim_f[:, 1] * sec_f[:, 0] - prim_f[:, 0] * sec_f[:, 1]
    interf = jnp.stack((ifg_re, ifg_im), axis=1)
    upcoming = passed_along(interf[:, :, :LAG, :], "tile", -1)
    later = jnp.concatenate([interf[:, :, LAG:, :], upcoming], axis=2)
    l_re = later[:, 0]
    l_im = later[:, 1]
    weight = margin_mask.astype(jnp.float32)[None, :, None]
    e_re = jnp.sum(weight * (ifg_re * l_re + ifg_im * l_im), axis=(1, 2))
    e_im = jnp.sum(weight * (ifg_im * l_re - ifg_re * l_im), axis=(1, 2))
    power = jnp.sum(
        weight * 0.5 * (ifg_re * ifg_re + ifg_im * ifg_im + l_re * l_re + l_im * l_im), axis=(1, 2)
    )
    count = jnp.zeros_like(e_re) + jnp.sum(margin_mask.astype(jnp.float32)) * interf.shape[3]
    stats = jnp.stack((e_re, e_im, power, count), axis=1)
    totals = lax.psum(stats, "tile")
    magnitude = jnp.sqrt(totals[:, 0] * totals[:, 0] + totals[:, 1] * totals[:, 1])
    floor_val = (totals[:, 2] + 1e-06) / jnp.sqrt(jnp.maximum(totals[:, 3], 1.0))
    denom = jnp.maximum(magnitude, floor_val)
    u_re = (totals[:, 0] / denom)[:, None, None]
    u_im = (totals[:, 1] / denom)[:, None, None]
    c_re = multilook(ifg_re * u_re + ifg_im * u_im)
    c_im = multilook(ifg_im * u_re - ifg_re * u_im)
    return jnp.stack((c_re, c_im), axis=1)


def shards(secondary, primary, *rest):
    rows_n, width = primary.shape[1:]
    fits = rows_n % BAND == 0 and rows_n > 2 * LAG + BAND and width % LANE == 0
    tiles_n = lax.axis_size("tile")
    fits = fits and lax.axis_size("date") == 4 and tiles_n & (tiles_n - 1) == 0
    return (fused if fits else plain)(secondary, primary, *rest)


def solution(mesh):
    return jax.shard_map(
        shards,
        mesh=mesh,
        in_specs=(
            P("date", None, "tile", None),
            P(None, "tile", "date"),
            P("tile"),
            P("date", "tile"),
            P("date", "tile"),
            P("date", "tile"),
            P("date", "tile"),
        ),
        out_specs=P("date", None, "tile", None),
        check_vma=False,
    )
```

```python
import functools

import jax
import jax.numpy as jnp
from jax import lax
from jax.experimental import pallas as pl
from jax.experimental.pallas import tpu as pltpu
from jax.sharding import PartitionSpec as P

KA = 16
LAG = 64
LA = 2
LR = 8
LANE = 128
BAND = 128
HALO = 32
VMEM_LIMIT = 40 * 1024 * 1024


def passed_along(value, axis, steps):
    count = lax.axis_size(axis)
    initial, last = (max(0, -steps), min(count, count - steps))
    return lax.ppermute(value, axis, [(source, source + steps) for source in range(initial, last)])


def window(dist):
    return jnp.sinc(dist) * (0.5 + 0.5 * jnp.cos(jnp.pi * dist / 4.0))


def tap_rows(frac):
    dist = lax.broadcasted_iota(jnp.int32, (8, LANE), 0).astype(jnp.float32) - 3.0 - frac
    angle = jnp.pi * dist
    sinc = jnp.where(dist == 0.0, 1.0, jnp.sin(angle) / jnp.where(dist == 0.0, 1.0, angle))
    taps = sinc * (0.5 + 0.5 * jnp.cos(jnp.pi * dist / 4.0))
    return taps.astype(jnp.bfloat16).astype(jnp.float32)


def band(shape, distance, taps):
    total = jnp.zeros(shape, jnp.float32)
    for j in range(8):
        total = jnp.where(distance == j - 3, taps[j : j + 1, :1], total)
    return total.astype(jnp.bfloat16)


def cut_halo_kernel(sec_ref, inner_ref, outer_ref):
    rows_n = sec_ref.shape[2]
    first = lax.rem(lax.axis_index("tile"), 2) == 0
    down, up = sec_ref[0, :, rows_n - HALO :], sec_ref[0, :, :HALO]
    inner_ref[...] = jnp.where(first, down, up)
    outer_ref[...] = jnp.where(first, up, down)


def cut_middle_kernel(prim_ref, *refs):
    cut_ref = refs[-1]
    cut_ref[...] = prim_ref[:, LAG : LAG + cut_ref.shape[1]]


def relay_kernel(block_ref, awaited_ref, out_ref):
    del awaited_ref
    out_ref[...] = block_ref[:, : out_ref.shape[1]]


def bands_kernel(ao_ref, ro_ref, af_ref, rf_ref, az_ref, rg_ref):
    shape = az_ref.shape
    offset = lax.broadcasted_iota(jnp.int32, shape, 1) - lax.broadcasted_iota(jnp.int32, shape, 0)
    az_ref[...] = band(shape, offset - HALO - ao_ref[...], tap_rows(af_ref[...]))
    square = rg_ref.shape[1:]
    offset = lax.broadcasted_iota(jnp.int32, square, 0) - lax.broadcasted_iota(jnp.int32, square, 1)
    taps = tap_rows(rf_ref[...])
    for at, shift in enumerate((-LANE, 0, LANE)):
        rg_ref[at] = band(square, offset + shift - ro_ref[...], taps)


def resample_kernel(sec_ref, inner_ref, outer_ref, az_ref, rg_ref, out_ref, azim_ref):
    rows_n, cols_n = sec_ref.shape[2:]
    az_band = az_ref[...]
    first = lax.rem(lax.axis_index("tile"), 2) == 0
    for part in range(2):
        for start in range(0, rows_n, BAND):
            pieces = []
            if start == 0:
                pieces.append(jnp.where(first, outer_ref[part], inner_ref[part]))
            pieces.append(sec_ref[0, part, max(0, start - HALO) : min(rows_n, start + BAND + HALO)])
            if start + BAND == rows_n:
                pieces.append(jnp.where(first, inner_ref[part], outer_ref[part]))
            rows = jnp.concatenate(pieces, axis=0) if len(pieces) > 1 else pieces[0]
            azim_ref[part, start : start + BAND] = jnp.dot(
                az_band, rows, preferred_element_type=jnp.float32
            ).astype(jnp.bfloat16)

    before, same, after = [rg_ref[at] for at in range(3)]
    none = jnp.zeros((LANE, LANE), jnp.bfloat16)
    blocks_n, _, _, width = out_ref.shape
    lanes_n = width // LANE
    columns = []
    for lane in range(lanes_n):
        column = [none] * (lanes_n + 2)
        column[lane], column[lane + 1], column[lane + 2] = before, same, after
        columns.append(jnp.concatenate(column, axis=0))
    rg_band = jnp.concatenate(columns, axis=1)
    for block in range(blocks_n):
        first = block * width - LANE
        last = (block + 1) * width + LANE
        taken = slice(max(first, 0), min(last, cols_n))
        used = rg_band[taken.start - first : taken.stop - first]
        for part in range(2):
            out_ref[block, part] = jnp.dot(
                azim_ref[part, :, taken], used, preferred_element_type=jnp.float32
            ).astype(jnp.bfloat16)


def interfere(prim_re, prim_im, sec_re, sec_im):
    p_re, p_im = prim_re.astype(jnp.float32), prim_im.astype(jnp.float32)
    s_re, s_im = sec_re.astype(jnp.float32), sec_im.astype(jnp.float32)
    return p_re * s_re + p_im * s_im, p_im * s_re - p_re * s_im


def look_columns(width, block, looks_n):
    shape = (width, looks_n)
    col = lax.broadcasted_iota(jnp.int32, shape, 0) + block * width
    look = lax.broadcasted_iota(jnp.int32, shape, 1) * LR
    return jnp.where((col >= look) & (col < look + LR), 1.0, 0.0).astype(jnp.bfloat16)


def look_rows(sums_ref, part, start, rows_n):
    count = rows_n // LA
    total = sums_ref[part, pl.ds(start, count, LA)]
    for row in range(1, LA):
        total = total + sums_ref[part, pl.ds(start + row, count, LA)]
    return total


def margin_kernel(
    own_ref, one_ref, two_ref, three_ref, res_ref, first_ref, last_ref, looks_ref, sums_ref
):
    here = lax.axis_index("date")
    _, _, rows_n, width = res_ref.shape
    whole, edges = (0, rows_n - LAG), (0, LAG)
    looks_n = looks_ref.shape[2]
    totals = [None, None]
    for step, (prim_ref, starts) in enumerate(
        ((own_ref, whole), (one_ref, whole), (two_ref, edges), (three_ref, edges))
    ):
        block = jnp.bitwise_xor(here, step)
        select = look_columns(width, block, looks_n)
        columns = pl.ds(pl.multiple_of(block * width, width), width)
        halves = []
        for held, start, target in zip(starts, whole, (first_ref, last_ref)):
            pair = interfere(
                prim_ref[0, held : held + LAG],
                prim_ref[1, held : held + LAG],
                res_ref[block, 0, start : start + LAG],
                res_ref[block, 1, start : start + LAG],
            )
            pair = [value.astype(jnp.bfloat16) for value in pair]
            for part in range(2):
                target[part, :, columns] = pair[part]
            halves.append(pair)
        for part in range(2):
            both = jnp.concatenate([halves[0][part], halves[1][part]], axis=0)
            summed = jnp.dot(both, select, preferred_element_type=jnp.float32)
            totals[part] = summed if step == 0 else totals[part] + summed
    for part in range(2):
        sums_ref[part] = totals[part]
        looks_ref[part] = look_rows(sums_ref, part, 0, 2 * LAG)


def stats_kernel(last_ref, later_ref, weight_ref, stats_ref):
    cols_n = last_ref.shape[2]
    weight = weight_ref[...]
    i_re, i_im = last_ref[0].astype(jnp.float32), last_ref[1].astype(jnp.float32)
    l_re, l_im = later_ref[0].astype(jnp.float32), later_ref[1].astype(jnp.float32)
    values = (
        i_re * l_re + i_im * l_im,
        i_im * l_re - i_re * l_im,
        0.5 * (i_re * i_re + i_im * i_im + l_re * l_re + l_im * l_im),
    )
    rows = []
    for value in values:
        folded = value[:, :LANE]
        for start in range(LANE, cols_n, LANE):
            folded = folded + value[:, start : start + LANE]
        rows.append(jnp.sum(folded * weight, axis=0, keepdims=True))
    rows.append(jnp.sum(weight, axis=0, keepdims=True) * (cols_n // LANE))
    rows.append(jnp.zeros((4, LANE), jnp.float32))
    stats_ref[...] = jnp.concatenate(rows, axis=0)


def look_sums(pieces, res_ref, looks_n):
    here = lax.axis_index("date")
    _, _, rows_n, width = res_ref.shape
    middle_n = rows_n - 2 * LAG
    totals = [None, None]
    for at, (step, prim_ref) in enumerate(pieces):
        block = jnp.bitwise_xor(here, step)
        first = LAG if prim_ref.shape[1] == rows_n else 0
        select = look_columns(width, block, looks_n)
        pair = interfere(
            prim_ref[0, first : first + middle_n],
            prim_ref[1, first : first + middle_n],
            res_ref[block, 0, LAG : rows_n - LAG],
            res_ref[block, 1, LAG : rows_n - LAG],
        )
        for part in range(2):
            summed = jnp.dot(
                pair[part].astype(jnp.bfloat16), select, preferred_element_type=jnp.float32
            )
            totals[part] = summed if at == 0 else totals[part] + summed
    return totals


def middle_kernel(own_ref, one_ref, two_ref, res_ref, out_ref):
    pieces = ((0, own_ref), (1, one_ref), (2, two_ref))
    for part, total in enumerate(look_sums(pieces, res_ref, out_ref.shape[2])):
        out_ref[part] = total


def last_kernel(three_ref, res_ref, before_ref, looks_ref, out_ref, sums_ref):
    middle_n = before_ref.shape[1]
    edge = LAG // LA
    totals = look_sums(((3, three_ref),), res_ref, out_ref.shape[2])
    for part, total in enumerate(totals):
        sums_ref[part] = total + before_ref[part]
        out_ref[part, :edge] = looks_ref[part, :edge]
        out_ref[part, edge : edge + middle_n // LA] = look_rows(sums_ref, part, 0, middle_n)
        out_ref[part, edge + middle_n // LA :] = looks_ref[part, edge:]


def scale_kernel(looks_ref, mine_ref, other_ref, out_ref):
    stats = jnp.sum(mine_ref[...] + other_ref[...], axis=1, keepdims=True)
    e_re, e_im, power, count = [stats[row : row + 1] for row in range(4)]
    magnitude = jnp.sqrt(e_re * e_re + e_im * e_im)
    floor_val = (power + 1e-06) / jnp.sqrt(jnp.maximum(count, 1.0))
    denom = jnp.maximum(magnitude, floor_val)
    u_re = e_re / denom * (1.0 / (LA * LR))
    u_im = e_im / denom * (1.0 / (LA * LR))
    out_ref[0, 0] = looks_ref[0] * u_re + looks_ref[1] * u_im
    out_ref[0, 1] = looks_ref[1] * u_re - looks_ref[0] * u_im


def call(kernel, outs, scratch, cost, *args):
    vmem = pl.BlockSpec(memory_space=pltpu.VMEM)
    return pl.pallas_call(
        kernel,
        out_shape=outs,
        in_specs=[vmem] * len(args),
        out_specs=jax.tree.map(lambda _: vmem, outs),
        scratch_shapes=scratch,
        compiler_params=pltpu.CompilerParams(vmem_limit_bytes=VMEM_LIMIT),
        cost_estimate=pl.CostEstimate(flops=cost[0], bytes_accessed=cost[1], transcendentals=0),
    )(*args)


def swap(value, axis, step):
    return lax.ppermute(value, axis, [(at, at ^ step) for at in range(lax.axis_size(axis))])


def fused(secondary, primary, margin_mask, az_off, rg_off, az_frac, rg_frac):
    _, _, rows_n, cols_n = secondary.shape
    width = primary.shape[2]
    dates_n = lax.axis_size("date")
    tiles_n = lax.axis_size("tile")
    bf16, f32 = jnp.bfloat16, jnp.float32
    shape = jax.ShapeDtypeStruct
    looks_n = cols_n // LR
    middle_n = rows_n - 2 * LAG
    edges = jnp.concatenate([primary[:, :LAG], primary[:, rows_n - LAG :]], axis=1)
    edges_two = swap(edges, "date", 2)
    one = swap(primary, "date", 1)
    halo = shape((2, HALO, cols_n), bf16)
    inner, outer = call(cut_halo_kernel, (halo, halo), [], (0, 0), secondary)
    inner = swap(inner, "tile", 1)
    beyond = [(at, at + 1 if at % 2 else at - 1) for at in range(1, tiles_n - 1)]
    outer = lax.ppermute(outer, "tile", beyond)
    az_band, rg_band = call(
        bands_kernel,
        (shape((BAND, BAND + 2 * HALO), bf16), shape((3, LANE, LANE), bf16)),
        [],
        (0, 0),
        az_off, rg_off, az_frac, rg_frac,
    )
    relayed = call(relay_kernel, edges, [], (0, 0), edges_two, az_band)
    edges_three = swap(relayed, "date", 1)
    middle = call(
        cut_middle_kernel,
        shape((2, middle_n + 16, width), bf16),
        [],
        (0, 0),
        primary, inner,outer,
    )
    weight = jnp.broadcast_to(margin_mask[rows_n - LAG :].astype(f32)[:, None], (LAG, LANE))
    res = call(
        resample_kernel,
        shape((dates_n, 2, rows_n, width), bf16),
        [pltpu.VMEM((2, rows_n, cols_n), bf16)],
        (0, 0),
        secondary, inner, outer, az_band, rg_band,
    )
    two = swap(middle, "date", 2)
    margin = shape((2, LAG, cols_n), bf16)
    first, last, looks = call(
        margin_kernel,
        (margin, margin, shape((2, 2 * LAG // LA, looks_n), f32)),
        [pltpu.VMEM((2, 2 * LAG, looks_n), f32)],
        (0, 0),
        primary, one, edges_two, edges_three, res,
    )
    later = passed_along(first, "tile", -1)
    stats = call(
        stats_kernel,
        shape((8, LANE), f32),
        [],
        (0, 0),
        last, later, weight,
    )
    before = call(
        middle_kernel,
        shape((2, middle_n, looks_n), f32),
        [],
        (2 * 2 * middle_n * cols_n * looks_n, 8 * rows_n * cols_n),
        primary, one, two, res,
    )
    other = swap(stats, "tile", 1)
    block = shape((2, middle_n, width), bf16)
    relayed = call(relay_kernel, block, [], (0, 0), two, other)
    three = swap(relayed, "date", 1)
    stride = 2
    while stride < tiles_n:
        stats = stats + other
        other = swap(stats, "tile", stride)
        stride *= 2
    looks = call(
        last_kernel,
        shape((2, rows_n // LA, looks_n), f32),
        [pltpu.VMEM((2, middle_n, looks_n), f32)],
        (2 * middle_n * cols_n * looks_n, 4 * rows_n * cols_n),
        three, res, before, looks,
    )
    return call(
        scale_kernel,
        shape((1, 2, rows_n // LA, looks_n), f32),
        [],
        (8 * rows_n * looks_n, 8 * rows_n * looks_n),
        looks, stats, other,
    )


def padded(block, sides, width):
    for axis, dim in sides:
        low = passed_along(
            lax.slice_in_dim(block, block.shape[dim] - width, None, axis=dim), axis, 1
        )
        high = passed_along(lax.slice_in_dim(block, 0, width, axis=dim), axis, -1)
        block = jnp.concatenate([low, block, high], axis=dim)
    return block


def band_taps(offset, frac):
    inside = (offset >= -3) & (offset <= 4)
    return jnp.where(inside, window(offset.astype(jnp.float32) - frac), 0.0).astype(jnp.bfloat16)


def multilook(values):
    depth, rows_n, cols_n = values.shape
    return values.reshape(depth, rows_n // LA, LA, cols_n // LR, LR).mean(axis=(2, 4))


def plain(secondary, primary, margin_mask, az_off, rg_off, az_frac, rg_frac):
    rim_rows = KA + 4
    block_cols = 256
    image = secondary[0]
    rows_n = image.shape[1]
    cols_n = image.shape[2]
    extended = padded(image, (("tile", 1),), rim_rows)
    row_out = lax.broadcasted_iota(jnp.int32, (rows_n, rows_n + 2 * rim_rows), 0)
    row_in = lax.broadcasted_iota(jnp.int32, (rows_n, rows_n + 2 * rim_rows), 1)
    azim_taps = band_taps(row_in - row_out - az_off[0, 0] - rim_rows, az_frac[0, 0])
    azim = jnp.einsum(
        "im,kmc->kic", azim_taps, extended, preferred_element_type=jnp.float32
    ).astype(jnp.bfloat16)
    blocks_n = cols_n // block_cols
    col_pad = jnp.pad(azim, ((0, 0), (0, 0), (block_cols // 2, block_cols // 2)))
    pieces = col_pad.reshape(2, rows_n, blocks_n + 1, block_cols)
    inputs = jnp.concatenate([pieces[:, :, :-1], pieces[:, :, 1:]], axis=3)
    col_in = lax.broadcasted_iota(jnp.int32, (2 * block_cols, block_cols), 0)
    col_out = lax.broadcasted_iota(jnp.int32, (2 * block_cols, block_cols), 1)
    range_taps = band_taps(col_in - block_cols // 2 - col_out - rg_off[0, 0], rg_frac[0, 0])
    resampled = jnp.einsum("kibm,mn->kibn", inputs, range_taps, preferred_element_type=jnp.float32)
    resampled = resampled.reshape(2, rows_n, cols_n).astype(jnp.bfloat16)
    prim = lax.all_gather(primary, "date", axis=2, tiled=True)[None]
    sec_f = resampled[None].astype(jnp.float32)
    prim_f = prim.astype(jnp.float32)
    ifg_re = prim_f[:, 0] * sec_f[:, 0] + prim_f[:, 1] * sec_f[:, 1]
    ifg_im = prim_f[:, 1] * sec_f[:, 0] - prim_f[:, 0] * sec_f[:, 1]
    interf = jnp.stack((ifg_re, ifg_im), axis=1)
    upcoming = passed_along(interf[:, :, :LAG, :], "tile", -1)
    later = jnp.concatenate([interf[:, :, LAG:, :], upcoming], axis=2)
    l_re = later[:, 0]
    l_im = later[:, 1]
    weight = margin_mask.astype(jnp.float32)[None, :, None]
    e_re = jnp.sum(weight * (ifg_re * l_re + ifg_im * l_im), axis=(1, 2))
    e_im = jnp.sum(weight * (ifg_im * l_re - ifg_re * l_im), axis=(1, 2))
    power = jnp.sum(
        weight * 0.5 * (ifg_re * ifg_re + ifg_im * ifg_im + l_re * l_re + l_im * l_im), axis=(1, 2)
    )
    count = jnp.zeros_like(e_re) + jnp.sum(margin_mask.astype(jnp.float32)) * interf.shape[3]
    stats = jnp.stack((e_re, e_im, power, count), axis=1)
    totals = lax.psum(stats, "tile")
    magnitude = jnp.sqrt(totals[:, 0] * totals[:, 0] + totals[:, 1] * totals[:, 1])
    floor_val = (totals[:, 2] + 1e-06) / jnp.sqrt(jnp.maximum(totals[:, 3], 1.0))
    denom = jnp.maximum(magnitude, floor_val)
    u_re = (totals[:, 0] / denom)[:, None, None]
    u_im = (totals[:, 1] / denom)[:, None, None]
    c_re = multilook(ifg_re * u_re + ifg_im * u_im)
    c_im = multilook(ifg_im * u_re - ifg_re * u_im)
    return jnp.stack((c_re, c_im), axis=1)


def shards(secondary, primary, *rest):
    rows_n, width = primary.shape[1:]
    fits = rows_n % BAND == 0 and rows_n > 2 * LAG + BAND and width % LANE == 0
    tiles_n = lax.axis_size("tile")
    fits = fits and lax.axis_size("date") == 4 and tiles_n & (tiles_n - 1) == 0
    return (fused if fits else plain)(secondary, primary, *rest)


def solution(mesh):
    return jax.shard_map(
        shards,
        mesh=mesh,
        in_specs=(
            P("date", None, "tile", None),
            P(None, "tile", "date"),
            P("tile"),
            P("date", "tile"),
            P("date", "tile"),
            P("date", "tile"),
            P("date", "tile"),
        ),
        out_specs=P("date", None, "tile", None),
        check_vma=False,
    )
```

```python
import functools

import jax
import jax.numpy as jnp
from jax import lax
from jax.experimental import pallas as pl
from jax.experimental.pallas import tpu as pltpu
from jax.sharding import PartitionSpec as P

KA = 16
LAG = 64
LA = 2
LR = 8
LANE = 128
BAND = 128
HALO = 32
VMEM_LIMIT = 40 * 1024 * 1024


def passed_along(value, axis, steps):
    count = lax.axis_size(axis)
    initial, last = (max(0, -steps), min(count, count - steps))
    return lax.ppermute(value, axis, [(source, source + steps) for source in range(initial, last)])


def window(dist):
    return jnp.sinc(dist) * (0.5 + 0.5 * jnp.cos(jnp.pi * dist / 4.0))


def tap_rows(frac):
    dist = lax.broadcasted_iota(jnp.int32, (8, LANE), 0).astype(jnp.float32) - 3.0 - frac
    angle = jnp.pi * dist
    sinc = jnp.where(dist == 0.0, 1.0, jnp.sin(angle) / jnp.where(dist == 0.0, 1.0, angle))
    taps = sinc * (0.5 + 0.5 * jnp.cos(jnp.pi * dist / 4.0))
    return taps.astype(jnp.bfloat16).astype(jnp.float32)


def band(shape, distance, taps):
    total = jnp.zeros(shape, jnp.float32)
    for j in range(8):
        total = jnp.where(distance == j - 3, taps[j : j + 1, :1], total)
    return total.astype(jnp.bfloat16)


def cut_halo_kernel(sec_ref, inner_ref, outer_ref):
    rows_n = sec_ref.shape[2]
    first = lax.rem(lax.axis_index("tile"), 2) == 0
    down, up = sec_ref[0, :, rows_n - HALO :], sec_ref[0, :, :HALO]
    inner_ref[...] = jnp.where(first, down, up)
    outer_ref[...] = jnp.where(first, up, down)


def cut_middle_kernel(prim_ref, *refs):
    cut_ref = refs[-1]
    cut_ref[...] = prim_ref[:, LAG : LAG + cut_ref.shape[1]]


def relay_kernel(block_ref, awaited_ref, out_ref):
    del awaited_ref
    out_ref[...] = block_ref[:, : out_ref.shape[1]]


def bands_kernel(ao_ref, ro_ref, af_ref, rf_ref, az_ref, rg_ref):
    shape = az_ref.shape
    offset = lax.broadcasted_iota(jnp.int32, shape, 1) - lax.broadcasted_iota(jnp.int32, shape, 0)
    az_ref[...] = band(shape, offset - HALO - ao_ref[...], tap_rows(af_ref[...]))
    square = rg_ref.shape[1:]
    offset = lax.broadcasted_iota(jnp.int32, square, 0) - lax.broadcasted_iota(jnp.int32, square, 1)
    taps = tap_rows(rf_ref[...])
    for at, shift in enumerate((-LANE, 0, LANE)):
        rg_ref[at] = band(square, offset + shift - ro_ref[...], taps)


def resample_kernel(sec_ref, inner_ref, outer_ref, az_ref, rg_ref, out_ref, azim_ref):
    rows_n, cols_n = sec_ref.shape[2:]
    az_band = az_ref[...]
    first = lax.rem(lax.axis_index("tile"), 2) == 0
    for part in range(2):
        for start in range(0, rows_n, BAND):
            pieces = []
            if start == 0:
                pieces.append(jnp.where(first, outer_ref[part], inner_ref[part]))
            pieces.append(sec_ref[0, part, max(0, start - HALO) : min(rows_n, start + BAND + HALO)])
            if start + BAND == rows_n:
                pieces.append(jnp.where(first, inner_ref[part], outer_ref[part]))
            rows = jnp.concatenate(pieces, axis=0) if len(pieces) > 1 else pieces[0]
            azim_ref[part, start : start + BAND] = jnp.dot(
                az_band, rows, preferred_element_type=jnp.float32
            ).astype(jnp.bfloat16)

    before, same, after = [rg_ref[at] for at in range(3)]
    none = jnp.zeros((LANE, LANE), jnp.bfloat16)
    blocks_n, _, _, width = out_ref.shape
    lanes_n = width // LANE
    columns = []
    for lane in range(lanes_n):
        column = [none] * (lanes_n + 2)
        column[lane], column[lane + 1], column[lane + 2] = before, same, after
        columns.append(jnp.concatenate(column, axis=0))
    rg_band = jnp.concatenate(columns, axis=1)
    for block in range(blocks_n):
        first = block * width - LANE
        last = (block + 1) * width + LANE
        taken = slice(max(first, 0), min(last, cols_n))
        used = rg_band[taken.start - first : taken.stop - first]
        for part in range(2):
            out_ref[block, part] = jnp.dot(
                azim_ref[part, :, taken], used, preferred_element_type=jnp.float32
            ).astype(jnp.bfloat16)


def interfere(prim_re, prim_im, sec_re, sec_im):
    p_re, p_im = prim_re.astype(jnp.float32), prim_im.astype(jnp.float32)
    s_re, s_im = sec_re.astype(jnp.float32), sec_im.astype(jnp.float32)
    return p_re * s_re + p_im * s_im, p_im * s_re - p_re * s_im


def look_columns(width, block, looks_n):
    shape = (width, looks_n)
    col = lax.broadcasted_iota(jnp.int32, shape, 0) + block * width
    look = lax.broadcasted_iota(jnp.int32, shape, 1) * LR
    return jnp.where((col >= look) & (col < look + LR), 1.0, 0.0).astype(jnp.bfloat16)


def look_rows(sums_ref, part, start, rows_n):
    count = rows_n // LA
    total = sums_ref[part, pl.ds(start, count, LA)]
    for row in range(1, LA):
        total = total + sums_ref[part, pl.ds(start + row, count, LA)]
    return total


def margin_kernel(
    own_ref, one_ref, two_ref, three_ref, res_ref, first_ref, last_ref, looks_ref, sums_ref
):
    here = lax.axis_index("date")
    _, _, rows_n, width = res_ref.shape
    whole, edges = (0, rows_n - LAG), (0, LAG)
    looks_n = looks_ref.shape[2]
    totals = [None, None]
    for step, (prim_ref, starts) in enumerate(
        ((own_ref, whole), (one_ref, edges), (two_ref, edges), (three_ref, edges))
    ):
        block = jnp.bitwise_xor(here, step)
        select = look_columns(width, block, looks_n)
        columns = pl.ds(pl.multiple_of(block * width, width), width)
        halves = []
        for held, start, target in zip(starts, whole, (first_ref, last_ref)):
            pair = interfere(
                prim_ref[0, held : held + LAG],
                prim_ref[1, held : held + LAG],
                res_ref[block, 0, start : start + LAG],
                res_ref[block, 1, start : start + LAG],
            )
            pair = [value.astype(jnp.bfloat16) for value in pair]
            for part in range(2):
                target[part, :, columns] = pair[part]
            halves.append(pair)
        for part in range(2):
            both = jnp.concatenate([halves[0][part], halves[1][part]], axis=0)
            summed = jnp.dot(both, select, preferred_element_type=jnp.float32)
            totals[part] = summed if step == 0 else totals[part] + summed
    for part in range(2):
        sums_ref[part] = totals[part]
        looks_ref[part] = look_rows(sums_ref, part, 0, 2 * LAG)


def stats_kernel(last_ref, later_ref, weight_ref, stats_ref):
    cols_n = last_ref.shape[2]
    weight = weight_ref[...]
    i_re, i_im = last_ref[0].astype(jnp.float32), last_ref[1].astype(jnp.float32)
    l_re, l_im = later_ref[0].astype(jnp.float32), later_ref[1].astype(jnp.float32)
    values = (
        i_re * l_re + i_im * l_im,
        i_im * l_re - i_re * l_im,
        0.5 * (i_re * i_re + i_im * i_im + l_re * l_re + l_im * l_im),
    )
    rows = []
    for value in values:
        folded = value[:, :LANE]
        for start in range(LANE, cols_n, LANE):
            folded = folded + value[:, start : start + LANE]
        rows.append(jnp.sum(folded * weight, axis=0, keepdims=True))
    rows.append(jnp.sum(weight, axis=0, keepdims=True) * (cols_n // LANE))
    rows.append(jnp.zeros((4, LANE), jnp.float32))
    stats_ref[...] = jnp.concatenate(rows, axis=0)


def look_sums(pieces, res_ref, looks_n):
    here = lax.axis_index("date")
    _, _, rows_n, width = res_ref.shape
    middle_n = rows_n - 2 * LAG
    totals = [None, None]
    for at, (step, prim_ref) in enumerate(pieces):
        block = jnp.bitwise_xor(here, step)
        first = LAG if prim_ref.shape[1] == rows_n else 0
        select = look_columns(width, block, looks_n)
        pair = interfere(
            prim_ref[0, first : first + middle_n],
            prim_ref[1, first : first + middle_n],
            res_ref[block, 0, LAG : rows_n - LAG],
            res_ref[block, 1, LAG : rows_n - LAG],
        )
        for part in range(2):
            summed = jnp.dot(
                pair[part].astype(jnp.bfloat16), select, preferred_element_type=jnp.float32
            )
            totals[part] = summed if at == 0 else totals[part] + summed
    return totals


def middle_kernel(own_ref, one_ref, two_ref, res_ref, out_ref):
    pieces = ((0, own_ref), (1, one_ref), (2, two_ref))
    for part, total in enumerate(look_sums(pieces, res_ref, out_ref.shape[2])):
        out_ref[part] = total


def last_kernel(three_ref, res_ref, before_ref, looks_ref, out_ref, sums_ref):
    middle_n = before_ref.shape[1]
    edge = LAG // LA
    totals = look_sums(((3, three_ref),), res_ref, out_ref.shape[2])
    for part, total in enumerate(totals):
        sums_ref[part] = total + before_ref[part]
        out_ref[part, :edge] = looks_ref[part, :edge]
        out_ref[part, edge : edge + middle_n // LA] = look_rows(sums_ref, part, 0, middle_n)
        out_ref[part, edge + middle_n // LA :] = looks_ref[part, edge:]


def scale_kernel(looks_ref, mine_ref, other_ref, out_ref):
    stats = jnp.sum(mine_ref[...] + other_ref[...], axis=1, keepdims=True)
    e_re, e_im, power, count = [stats[row : row + 1] for row in range(4)]
    magnitude = jnp.sqrt(e_re * e_re + e_im * e_im)
    floor_val = (power + 1e-06) / jnp.sqrt(jnp.maximum(count, 1.0))
    denom = jnp.maximum(magnitude, floor_val)
    u_re = e_re / denom * (1.0 / (LA * LR))
    u_im = e_im / denom * (1.0 / (LA * LR))
    out_ref[0, 0] = looks_ref[0] * u_re + looks_ref[1] * u_im
    out_ref[0, 1] = looks_ref[1] * u_re - looks_ref[0] * u_im


def call(kernel, outs, scratch, cost, *args):
    vmem = pl.BlockSpec(memory_space=pltpu.VMEM)
    return pl.pallas_call(
        kernel,
        out_shape=outs,
        in_specs=[vmem] * len(args),
        out_specs=jax.tree.map(lambda _: vmem, outs),
        scratch_shapes=scratch,
        compiler_params=pltpu.CompilerParams(vmem_limit_bytes=VMEM_LIMIT),
        cost_estimate=pl.CostEstimate(flops=cost[0], bytes_accessed=cost[1], transcendentals=0),
    )(*args)


def swap(value, axis, step):
    return lax.ppermute(value, axis, [(at, at ^ step) for at in range(lax.axis_size(axis))])


def fused(secondary, primary, margin_mask, az_off, rg_off, az_frac, rg_frac):
    _, _, rows_n, cols_n = secondary.shape
    width = primary.shape[2]
    dates_n = lax.axis_size("date")
    tiles_n = lax.axis_size("tile")
    bf16, f32 = jnp.bfloat16, jnp.float32
    shape = jax.ShapeDtypeStruct
    looks_n = cols_n // LR
    middle_n = rows_n - 2 * LAG
    edges = jnp.concatenate([primary[:, :LAG], primary[:, rows_n - LAG :]], axis=1)
    edges_two, edges_three, edges_one = [swap(edges, "date", step) for step in (2, 3, 1)]
    halo = shape((2, HALO, cols_n), bf16)
    inner, outer = call(cut_halo_kernel, (halo, halo), [], (0, 0), secondary)
    inner = swap(inner, "tile", 1)
    beyond = [(at, at + 1 if at % 2 else at - 1) for at in range(1, tiles_n - 1)]
    outer = lax.ppermute(outer, "tile", beyond)
    az_band, rg_band = call(
        bands_kernel,
        (shape((BAND, BAND + 2 * HALO), bf16), shape((3, LANE, LANE), bf16)),
        [],
        (0, 0),
        az_off, rg_off, az_frac, rg_frac,
    )
    weight = jnp.broadcast_to(margin_mask[rows_n - LAG :].astype(f32)[:, None], (LAG, LANE))
    res = call(
        resample_kernel,
        shape((dates_n, 2, rows_n, width), bf16),
        [pltpu.VMEM((2, rows_n, cols_n), bf16)],
        (0, 0),
        secondary, inner, outer, az_band, rg_band,
    )
    middle = call(
        cut_middle_kernel,
        shape((2, middle_n + 16, width), bf16),
        [],
        (0, 0),
        primary, edges_two,edges_three,az_band,
    )
    two, one = [swap(middle, "date", step) for step in (2, 1)]
    margin = shape((2, LAG, cols_n), bf16)
    first, last, looks = call(
        margin_kernel,
        (margin, margin, shape((2, 2 * LAG // LA, looks_n), f32)),
        [pltpu.VMEM((2, 2 * LAG, looks_n), f32)],
        (0, 0),
        primary, edges_one, edges_two, edges_three, res,
    )
    later = passed_along(first, "tile", -1)
    stats = call(
        stats_kernel,
        shape((8, LANE), f32),
        [],
        (0, 0),
        last, later, weight,
    )
    before = call(
        middle_kernel,
        shape((2, middle_n, looks_n), f32),
        [],
        (2 * 2 * middle_n * cols_n * looks_n, 8 * rows_n * cols_n),
        primary, one, two, res,
    )
    other = swap(stats, "tile", 1)
    block = shape((2, middle_n, width), bf16)
    relayed = call(relay_kernel, block, [], (0, 0), two, other)
    three = swap(relayed, "date", 1)
    stride = 2
    while stride < tiles_n:
        stats = stats + other
        other = swap(stats, "tile", stride)
        stride *= 2
    looks = call(
        last_kernel,
        shape((2, rows_n // LA, looks_n), f32),
        [pltpu.VMEM((2, middle_n, looks_n), f32)],
        (2 * middle_n * cols_n * looks_n, 4 * rows_n * cols_n),
        three, res, before, looks,
    )
    return call(
        scale_kernel,
        shape((1, 2, rows_n // LA, looks_n), f32),
        [],
        (8 * rows_n * looks_n, 8 * rows_n * looks_n),
        looks, stats, other,
    )


def padded(block, sides, width):
    for axis, dim in sides:
        low = passed_along(
            lax.slice_in_dim(block, block.shape[dim] - width, None, axis=dim), axis, 1
        )
        high = passed_along(lax.slice_in_dim(block, 0, width, axis=dim), axis, -1)
        block = jnp.concatenate([low, block, high], axis=dim)
    return block


def band_taps(offset, frac):
    inside = (offset >= -3) & (offset <= 4)
    return jnp.where(inside, window(offset.astype(jnp.float32) - frac), 0.0).astype(jnp.bfloat16)


def multilook(values):
    depth, rows_n, cols_n = values.shape
    return values.reshape(depth, rows_n // LA, LA, cols_n // LR, LR).mean(axis=(2, 4))


def plain(secondary, primary, margin_mask, az_off, rg_off, az_frac, rg_frac):
    rim_rows = KA + 4
    block_cols = 256
    image = secondary[0]
    rows_n = image.shape[1]
    cols_n = image.shape[2]
    extended = padded(image, (("tile", 1),), rim_rows)
    row_out = lax.broadcasted_iota(jnp.int32, (rows_n, rows_n + 2 * rim_rows), 0)
    row_in = lax.broadcasted_iota(jnp.int32, (rows_n, rows_n + 2 * rim_rows), 1)
    azim_taps = band_taps(row_in - row_out - az_off[0, 0] - rim_rows, az_frac[0, 0])
    azim = jnp.einsum(
        "im,kmc->kic", azim_taps, extended, preferred_element_type=jnp.float32
    ).astype(jnp.bfloat16)
    blocks_n = cols_n // block_cols
    col_pad = jnp.pad(azim, ((0, 0), (0, 0), (block_cols // 2, block_cols // 2)))
    pieces = col_pad.reshape(2, rows_n, blocks_n + 1, block_cols)
    inputs = jnp.concatenate([pieces[:, :, :-1], pieces[:, :, 1:]], axis=3)
    col_in = lax.broadcasted_iota(jnp.int32, (2 * block_cols, block_cols), 0)
    col_out = lax.broadcasted_iota(jnp.int32, (2 * block_cols, block_cols), 1)
    range_taps = band_taps(col_in - block_cols // 2 - col_out - rg_off[0, 0], rg_frac[0, 0])
    resampled = jnp.einsum("kibm,mn->kibn", inputs, range_taps, preferred_element_type=jnp.float32)
    resampled = resampled.reshape(2, rows_n, cols_n).astype(jnp.bfloat16)
    prim = lax.all_gather(primary, "date", axis=2, tiled=True)[None]
    sec_f = resampled[None].astype(jnp.float32)
    prim_f = prim.astype(jnp.float32)
    ifg_re = prim_f[:, 0] * sec_f[:, 0] + prim_f[:, 1] * sec_f[:, 1]
    ifg_im = prim_f[:, 1] * sec_f[:, 0] - prim_f[:, 0] * sec_f[:, 1]
    interf = jnp.stack((ifg_re, ifg_im), axis=1)
    upcoming = passed_along(interf[:, :, :LAG, :], "tile", -1)
    later = jnp.concatenate([interf[:, :, LAG:, :], upcoming], axis=2)
    l_re = later[:, 0]
    l_im = later[:, 1]
    weight = margin_mask.astype(jnp.float32)[None, :, None]
    e_re = jnp.sum(weight * (ifg_re * l_re + ifg_im * l_im), axis=(1, 2))
    e_im = jnp.sum(weight * (ifg_im * l_re - ifg_re * l_im), axis=(1, 2))
    power = jnp.sum(
        weight * 0.5 * (ifg_re * ifg_re + ifg_im * ifg_im + l_re * l_re + l_im * l_im), axis=(1, 2)
    )
    count = jnp.zeros_like(e_re) + jnp.sum(margin_mask.astype(jnp.float32)) * interf.shape[3]
    stats = jnp.stack((e_re, e_im, power, count), axis=1)
    totals = lax.psum(stats, "tile")
    magnitude = jnp.sqrt(totals[:, 0] * totals[:, 0] + totals[:, 1] * totals[:, 1])
    floor_val = (totals[:, 2] + 1e-06) / jnp.sqrt(jnp.maximum(totals[:, 3], 1.0))
    denom = jnp.maximum(magnitude, floor_val)
    u_re = (totals[:, 0] / denom)[:, None, None]
    u_im = (totals[:, 1] / denom)[:, None, None]
    c_re = multilook(ifg_re * u_re + ifg_im * u_im)
    c_im = multilook(ifg_im * u_re - ifg_re * u_im)
    return jnp.stack((c_re, c_im), axis=1)


def shards(secondary, primary, *rest):
    rows_n, width = primary.shape[1:]
    fits = rows_n % BAND == 0 and rows_n > 2 * LAG + BAND and width % LANE == 0
    tiles_n = lax.axis_size("tile")
    fits = fits and lax.axis_size("date") == 4 and tiles_n & (tiles_n - 1) == 0
    return (fused if fits else plain)(secondary, primary, *rest)


def solution(mesh):
    return jax.shard_map(
        shards,
        mesh=mesh,
        in_specs=(
            P("date", None, "tile", None),
            P(None, "tile", "date"),
            P("tile"),
            P("date", "tile"),
            P("date", "tile"),
            P("date", "tile"),
            P("date", "tile"),
        ),
        out_specs=P("date", None, "tile", None),
        check_vma=False,
    )
```

```python
import functools

import jax
import jax.numpy as jnp
from jax import lax
from jax.experimental import pallas as pl
from jax.experimental.pallas import tpu as pltpu
from jax.sharding import PartitionSpec as P

KA = 16
LAG = 64
LA = 2
LR = 8
LANE = 128
BAND = 128
HALO = 32
VMEM_LIMIT = 40 * 1024 * 1024


def passed_along(value, axis, steps):
    count = lax.axis_size(axis)
    initial, last = (max(0, -steps), min(count, count - steps))
    return lax.ppermute(value, axis, [(source, source + steps) for source in range(initial, last)])


def window(dist):
    return jnp.sinc(dist) * (0.5 + 0.5 * jnp.cos(jnp.pi * dist / 4.0))


def tap_rows(frac):
    dist = lax.broadcasted_iota(jnp.int32, (8, LANE), 0).astype(jnp.float32) - 3.0 - frac
    angle = jnp.pi * dist
    sinc = jnp.where(dist == 0.0, 1.0, jnp.sin(angle) / jnp.where(dist == 0.0, 1.0, angle))
    taps = sinc * (0.5 + 0.5 * jnp.cos(jnp.pi * dist / 4.0))
    return taps.astype(jnp.bfloat16).astype(jnp.float32)


def band(shape, distance, taps):
    total = jnp.zeros(shape, jnp.float32)
    for j in range(8):
        total = jnp.where(distance == j - 3, taps[j : j + 1, :1], total)
    return total.astype(jnp.bfloat16)


def cut_halo_kernel(sec_ref, down_ref, up_ref):
    rows_n = sec_ref.shape[2]
    down_ref[...] = sec_ref[0, :, rows_n - HALO :]
    up_ref[...] = sec_ref[0, :, :HALO]


def cut_middle_kernel(prim_ref, *refs):
    cut_ref = refs[-1]
    cut_ref[...] = prim_ref[:, LAG : LAG + cut_ref.shape[1]]


def relay_kernel(block_ref, awaited_ref, out_ref):
    del awaited_ref
    out_ref[...] = block_ref[:, : out_ref.shape[1]]


def bands_kernel(ao_ref, ro_ref, af_ref, rf_ref, az_ref, rg_ref):
    shape = az_ref.shape
    offset = lax.broadcasted_iota(jnp.int32, shape, 1) - lax.broadcasted_iota(jnp.int32, shape, 0)
    az_ref[...] = band(shape, offset - HALO - ao_ref[...], tap_rows(af_ref[...]))
    square = rg_ref.shape[1:]
    offset = lax.broadcasted_iota(jnp.int32, square, 0) - lax.broadcasted_iota(jnp.int32, square, 1)
    taps = tap_rows(rf_ref[...])
    for at, shift in enumerate((-LANE, 0, LANE)):
        rg_ref[at] = band(square, offset + shift - ro_ref[...], taps)


def resample_kernel(sec_ref, low_ref, high_ref, az_ref, rg_ref, out_ref, azim_ref):
    rows_n, cols_n = sec_ref.shape[2:]
    az_band = az_ref[...]
    here, tiles_n = lax.axis_index("tile"), lax.axis_size("tile")
    none = jnp.zeros(low_ref.shape[1:], jnp.bfloat16)
    for part in range(2):
        for start in range(0, rows_n, BAND):
            pieces = []
            if start == 0:
                pieces.append(jnp.where(here == 0, none, low_ref[part]))
            pieces.append(sec_ref[0, part, max(0, start - HALO) : min(rows_n, start + BAND + HALO)])
            if start + BAND == rows_n:
                pieces.append(jnp.where(here == tiles_n - 1, none, high_ref[part]))
            rows = jnp.concatenate(pieces, axis=0) if len(pieces) > 1 else pieces[0]
            azim_ref[part, start : start + BAND] = jnp.dot(
                az_band, rows, preferred_element_type=jnp.float32
            ).astype(jnp.bfloat16)

    before, same, after = [rg_ref[at] for at in range(3)]
    none = jnp.zeros((LANE, LANE), jnp.bfloat16)
    blocks_n, _, _, width = out_ref.shape
    lanes_n = width // LANE
    columns = []
    for lane in range(lanes_n):
        column = [none] * (lanes_n + 2)
        column[lane], column[lane + 1], column[lane + 2] = before, same, after
        columns.append(jnp.concatenate(column, axis=0))
    rg_band = jnp.concatenate(columns, axis=1)
    for block in range(blocks_n):
        first = block * width - LANE
        last = (block + 1) * width + LANE
        taken = slice(max(first, 0), min(last, cols_n))
        used = rg_band[taken.start - first : taken.stop - first]
        for part in range(2):
            out_ref[block, part] = jnp.dot(
                azim_ref[part, :, taken], used, preferred_element_type=jnp.float32
            ).astype(jnp.bfloat16)


def interfere(prim_re, prim_im, sec_re, sec_im):
    p_re, p_im = prim_re.astype(jnp.float32), prim_im.astype(jnp.float32)
    s_re, s_im = sec_re.astype(jnp.float32), sec_im.astype(jnp.float32)
    return p_re * s_re + p_im * s_im, p_im * s_re - p_re * s_im


def look_columns(width, block, looks_n):
    shape = (width, looks_n)
    col = lax.broadcasted_iota(jnp.int32, shape, 0) + block * width
    look = lax.broadcasted_iota(jnp.int32, shape, 1) * LR
    return jnp.where((col >= look) & (col < look + LR), 1.0, 0.0).astype(jnp.bfloat16)


def look_rows(sums_ref, part, start, rows_n):
    count = rows_n // LA
    total = sums_ref[part, pl.ds(start, count, LA)]
    for row in range(1, LA):
        total = total + sums_ref[part, pl.ds(start + row, count, LA)]
    return total


def margin_kernel(
    own_ref, one_ref, two_ref, three_ref, res_ref, first_ref, last_ref, looks_ref, sums_ref
):
    here = lax.axis_index("date")
    _, _, rows_n, width = res_ref.shape
    whole, edges = (0, rows_n - LAG), (0, LAG)
    looks_n = looks_ref.shape[2]
    totals = [None, None]
    for step, (prim_ref, starts) in enumerate(
        ((own_ref, whole), (one_ref, whole), (two_ref, edges), (three_ref, edges))
    ):
        block = jnp.bitwise_xor(here, step)
        select = look_columns(width, block, looks_n)
        columns = pl.ds(pl.multiple_of(block * width, width), width)
        halves = []
        for held, start, target in zip(starts, whole, (first_ref, last_ref)):
            pair = interfere(
                prim_ref[0, held : held + LAG],
                prim_ref[1, held : held + LAG],
                res_ref[block, 0, start : start + LAG],
                res_ref[block, 1, start : start + LAG],
            )
            pair = [value.astype(jnp.bfloat16) for value in pair]
            for part in range(2):
                target[part, :, columns] = pair[part]
            halves.append(pair)
        for part in range(2):
            both = jnp.concatenate([halves[0][part], halves[1][part]], axis=0)
            summed = jnp.dot(both, select, preferred_element_type=jnp.float32)
            totals[part] = summed if step == 0 else totals[part] + summed
    for part in range(2):
        sums_ref[part] = totals[part]
        looks_ref[part] = look_rows(sums_ref, part, 0, 2 * LAG)


def stats_kernel(last_ref, later_ref, weight_ref, stats_ref):
    cols_n = last_ref.shape[2]
    weight = weight_ref[...]
    i_re, i_im = last_ref[0].astype(jnp.float32), last_ref[1].astype(jnp.float32)
    inside = jnp.where(lax.axis_index("tile") == lax.axis_size("tile") - 1, 0.0, 1.0)
    l_re, l_im = [later_ref[part].astype(jnp.float32) * inside for part in range(2)]
    values = (
        i_re * l_re + i_im * l_im,
        i_im * l_re - i_re * l_im,
        0.5 * (i_re * i_re + i_im * i_im + l_re * l_re + l_im * l_im),
    )
    rows = []
    for value in values:
        folded = value[:, :LANE]
        for start in range(LANE, cols_n, LANE):
            folded = folded + value[:, start : start + LANE]
        rows.append(jnp.sum(folded * weight, axis=0, keepdims=True))
    rows.append(jnp.sum(weight, axis=0, keepdims=True) * (cols_n // LANE))
    rows.append(jnp.zeros((4, LANE), jnp.float32))
    stats_ref[...] = jnp.concatenate(rows, axis=0)


def look_sums(pieces, res_ref, looks_n):
    here = lax.axis_index("date")
    _, _, rows_n, width = res_ref.shape
    middle_n = rows_n - 2 * LAG
    totals = [None, None]
    for at, (step, prim_ref) in enumerate(pieces):
        block = jnp.bitwise_xor(here, step)
        first = LAG if prim_ref.shape[1] == rows_n else 0
        select = look_columns(width, block, looks_n)
        pair = interfere(
            prim_ref[0, first : first + middle_n],
            prim_ref[1, first : first + middle_n],
            res_ref[block, 0, LAG : rows_n - LAG],
            res_ref[block, 1, LAG : rows_n - LAG],
        )
        for part in range(2):
            summed = jnp.dot(
                pair[part].astype(jnp.bfloat16), select, preferred_element_type=jnp.float32
            )
            totals[part] = summed if at == 0 else totals[part] + summed
    return totals


def middle_kernel(own_ref, one_ref, two_ref, res_ref, out_ref):
    pieces = ((0, own_ref), (1, one_ref), (2, two_ref))
    for part, total in enumerate(look_sums(pieces, res_ref, out_ref.shape[2])):
        out_ref[part] = total


def last_kernel(three_ref, res_ref, before_ref, looks_ref, out_ref, sums_ref):
    middle_n = before_ref.shape[1]
    edge = LAG // LA
    totals = look_sums(((3, three_ref),), res_ref, out_ref.shape[2])
    for part, total in enumerate(totals):
        sums_ref[part] = total + before_ref[part]
        out_ref[part, :edge] = looks_ref[part, :edge]
        out_ref[part, edge : edge + middle_n // LA] = look_rows(sums_ref, part, 0, middle_n)
        out_ref[part, edge + middle_n // LA :] = looks_ref[part, edge:]


def scale_kernel(looks_ref, mine_ref, other_ref, out_ref):
    stats = jnp.sum(mine_ref[...] + other_ref[...], axis=1, keepdims=True)
    e_re, e_im, power, count = [stats[row : row + 1] for row in range(4)]
    magnitude = jnp.sqrt(e_re * e_re + e_im * e_im)
    floor_val = (power + 1e-06) / jnp.sqrt(jnp.maximum(count, 1.0))
    denom = jnp.maximum(magnitude, floor_val)
    u_re = e_re / denom * (1.0 / (LA * LR))
    u_im = e_im / denom * (1.0 / (LA * LR))
    out_ref[0, 0] = looks_ref[0] * u_re + looks_ref[1] * u_im
    out_ref[0, 1] = looks_ref[1] * u_re - looks_ref[0] * u_im


def call(kernel, outs, scratch, cost, *args):
    vmem = pl.BlockSpec(memory_space=pltpu.VMEM)
    return pl.pallas_call(
        kernel,
        out_shape=outs,
        in_specs=[vmem] * len(args),
        out_specs=jax.tree.map(lambda _: vmem, outs),
        scratch_shapes=scratch,
        compiler_params=pltpu.CompilerParams(vmem_limit_bytes=VMEM_LIMIT),
        cost_estimate=pl.CostEstimate(flops=cost[0], bytes_accessed=cost[1], transcendentals=0),
    )(*args)


def ring(value, axis, step):
    count = lax.axis_size(axis)
    return lax.ppermute(value, axis, [(at, (at + step) % count) for at in range(count)])


def swap(value, axis, step):
    return lax.ppermute(value, axis, [(at, at ^ step) for at in range(lax.axis_size(axis))])


def fused(secondary, primary, margin_mask, az_off, rg_off, az_frac, rg_frac):
    _, _, rows_n, cols_n = secondary.shape
    width = primary.shape[2]
    dates_n = lax.axis_size("date")
    tiles_n = lax.axis_size("tile")
    bf16, f32 = jnp.bfloat16, jnp.float32
    shape = jax.ShapeDtypeStruct
    looks_n = cols_n // LR
    middle_n = rows_n - 2 * LAG
    edges = jnp.concatenate([primary[:, :LAG], primary[:, rows_n - LAG :]], axis=1)
    edges_two = swap(edges, "date", 2)
    one = swap(primary, "date", 1)
    halo = shape((2, HALO, cols_n), bf16)
    down, up = call(cut_halo_kernel, (halo, halo), [], (0, 0), secondary)
    low = ring(down, "tile", 1)
    high = ring(up, "tile", -1)
    az_band, rg_band = call(
        bands_kernel,
        (shape((BAND, BAND + 2 * HALO), bf16), shape((3, LANE, LANE), bf16)),
        [],
        (0, 0),
        az_off, rg_off, az_frac, rg_frac,
    )
    relayed = call(relay_kernel, edges, [], (0, 0), edges_two, az_band)
    edges_three = swap(relayed, "date", 1)
    middle = call(
        cut_middle_kernel,
        shape((2, middle_n + 16, width), bf16),
        [],
        (0, 0),
        primary, low, high,
    )
    weight = jnp.broadcast_to(margin_mask[rows_n - LAG :].astype(f32)[:, None], (LAG, LANE))
    res = call(
        resample_kernel,
        shape((dates_n, 2, rows_n, width), bf16),
        [pltpu.VMEM((2, rows_n, cols_n), bf16)],
        (0, 0),
        secondary, low, high, az_band, rg_band,
    )
    two = swap(middle, "date", 2)
    margin = shape((2, LAG, cols_n), bf16)
    first, last, looks = call(
        margin_kernel,
        (margin, margin, shape((2, 2 * LAG // LA, looks_n), f32)),
        [pltpu.VMEM((2, 2 * LAG, looks_n), f32)],
        (0, 0),
        primary, one, edges_two, edges_three, res,
    )
    later = ring(first, "tile", -1)
    stats = call(
        stats_kernel,
        shape((8, LANE), f32),
        [],
        (0, 0),
        last, later, weight,
    )
    before = call(
        middle_kernel,
        shape((2, middle_n, looks_n), f32),
        [],
        (2 * 2 * middle_n * cols_n * looks_n, 8 * rows_n * cols_n),
        primary, one, two, res,
    )
    other = swap(stats, "tile", 1)
    block = shape((2, middle_n, width), bf16)
    relayed = call(relay_kernel, block, [], (0, 0), two, other)
    three = swap(relayed, "date", 1)
    stride = 2
    while stride < tiles_n:
        stats = stats + other
        other = swap(stats, "tile", stride)
        stride *= 2
    looks = call(
        last_kernel,
        shape((2, rows_n // LA, looks_n), f32),
        [pltpu.VMEM((2, middle_n, looks_n), f32)],
        (2 * middle_n * cols_n * looks_n, 4 * rows_n * cols_n),
        three, res, before, looks,
    )
    return call(
        scale_kernel,
        shape((1, 2, rows_n // LA, looks_n), f32),
        [],
        (8 * rows_n * looks_n, 8 * rows_n * looks_n),
        looks, stats, other,
    )


def padded(block, sides, width):
    for axis, dim in sides:
        low = passed_along(
            lax.slice_in_dim(block, block.shape[dim] - width, None, axis=dim), axis, 1
        )
        high = passed_along(lax.slice_in_dim(block, 0, width, axis=dim), axis, -1)
        block = jnp.concatenate([low, block, high], axis=dim)
    return block


def band_taps(offset, frac):
    inside = (offset >= -3) & (offset <= 4)
    return jnp.where(inside, window(offset.astype(jnp.float32) - frac), 0.0).astype(jnp.bfloat16)


def multilook(values):
    depth, rows_n, cols_n = values.shape
    return values.reshape(depth, rows_n // LA, LA, cols_n // LR, LR).mean(axis=(2, 4))


def plain(secondary, primary, margin_mask, az_off, rg_off, az_frac, rg_frac):
    rim_rows = KA + 4
    block_cols = 256
    image = secondary[0]
    rows_n = image.shape[1]
    cols_n = image.shape[2]
    extended = padded(image, (("tile", 1),), rim_rows)
    row_out = lax.broadcasted_iota(jnp.int32, (rows_n, rows_n + 2 * rim_rows), 0)
    row_in = lax.broadcasted_iota(jnp.int32, (rows_n, rows_n + 2 * rim_rows), 1)
    azim_taps = band_taps(row_in - row_out - az_off[0, 0] - rim_rows, az_frac[0, 0])
    azim = jnp.einsum(
        "im,kmc->kic", azim_taps, extended, preferred_element_type=jnp.float32
    ).astype(jnp.bfloat16)
    blocks_n = cols_n // block_cols
    col_pad = jnp.pad(azim, ((0, 0), (0, 0), (block_cols // 2, block_cols // 2)))
    pieces = col_pad.reshape(2, rows_n, blocks_n + 1, block_cols)
    inputs = jnp.concatenate([pieces[:, :, :-1], pieces[:, :, 1:]], axis=3)
    col_in = lax.broadcasted_iota(jnp.int32, (2 * block_cols, block_cols), 0)
    col_out = lax.broadcasted_iota(jnp.int32, (2 * block_cols, block_cols), 1)
    range_taps = band_taps(col_in - block_cols // 2 - col_out - rg_off[0, 0], rg_frac[0, 0])
    resampled = jnp.einsum("kibm,mn->kibn", inputs, range_taps, preferred_element_type=jnp.float32)
    resampled = resampled.reshape(2, rows_n, cols_n).astype(jnp.bfloat16)
    prim = lax.all_gather(primary, "date", axis=2, tiled=True)[None]
    sec_f = resampled[None].astype(jnp.float32)
    prim_f = prim.astype(jnp.float32)
    ifg_re = prim_f[:, 0] * sec_f[:, 0] + prim_f[:, 1] * sec_f[:, 1]
    ifg_im = prim_f[:, 1] * sec_f[:, 0] - prim_f[:, 0] * sec_f[:, 1]
    interf = jnp.stack((ifg_re, ifg_im), axis=1)
    upcoming = passed_along(interf[:, :, :LAG, :], "tile", -1)
    later = jnp.concatenate([interf[:, :, LAG:, :], upcoming], axis=2)
    l_re = later[:, 0]
    l_im = later[:, 1]
    weight = margin_mask.astype(jnp.float32)[None, :, None]
    e_re = jnp.sum(weight * (ifg_re * l_re + ifg_im * l_im), axis=(1, 2))
    e_im = jnp.sum(weight * (ifg_im * l_re - ifg_re * l_im), axis=(1, 2))
    power = jnp.sum(
        weight * 0.5 * (ifg_re * ifg_re + ifg_im * ifg_im + l_re * l_re + l_im * l_im), axis=(1, 2)
    )
    count = jnp.zeros_like(e_re) + jnp.sum(margin_mask.astype(jnp.float32)) * interf.shape[3]
    stats = jnp.stack((e_re, e_im, power, count), axis=1)
    totals = lax.psum(stats, "tile")
    magnitude = jnp.sqrt(totals[:, 0] * totals[:, 0] + totals[:, 1] * totals[:, 1])
    floor_val = (totals[:, 2] + 1e-06) / jnp.sqrt(jnp.maximum(totals[:, 3], 1.0))
    denom = jnp.maximum(magnitude, floor_val)
    u_re = (totals[:, 0] / denom)[:, None, None]
    u_im = (totals[:, 1] / denom)[:, None, None]
    c_re = multilook(ifg_re * u_re + ifg_im * u_im)
    c_im = multilook(ifg_im * u_re - ifg_re * u_im)
    return jnp.stack((c_re, c_im), axis=1)


def shards(secondary, primary, *rest):
    rows_n, width = primary.shape[1:]
    fits = rows_n % BAND == 0 and rows_n > 2 * LAG + BAND and width % LANE == 0
    tiles_n = lax.axis_size("tile")
    fits = fits and lax.axis_size("date") == 4 and tiles_n & (tiles_n - 1) == 0
    return (fused if fits else plain)(secondary, primary, *rest)


def solution(mesh):
    return jax.shard_map(
        shards,
        mesh=mesh,
        in_specs=(
            P("date", None, "tile", None),
            P(None, "tile", "date"),
            P("tile"),
            P("date", "tile"),
            P("date", "tile"),
            P("date", "tile"),
            P("date", "tile"),
        ),
        out_specs=P("date", None, "tile", None),
        check_vma=False,
    )
```

```python
import functools

import jax
import jax.numpy as jnp
from jax import lax
from jax.experimental import pallas as pl
from jax.experimental.pallas import tpu as pltpu
from jax.sharding import PartitionSpec as P

KA = 16
LAG = 64
LA = 2
LR = 8
LANE = 128
BAND = 128
HALO = 32
VMEM_LIMIT = 40 * 1024 * 1024


def passed_along(value, axis, steps):
    count = lax.axis_size(axis)
    initial, last = (max(0, -steps), min(count, count - steps))
    return lax.ppermute(value, axis, [(source, source + steps) for source in range(initial, last)])


def window(dist):
    return jnp.sinc(dist) * (0.5 + 0.5 * jnp.cos(jnp.pi * dist / 4.0))


def tap_rows(frac):
    dist = lax.broadcasted_iota(jnp.int32, (8, LANE), 0).astype(jnp.float32) - 3.0 - frac
    angle = jnp.pi * dist
    sinc = jnp.where(dist == 0.0, 1.0, jnp.sin(angle) / jnp.where(dist == 0.0, 1.0, angle))
    taps = sinc * (0.5 + 0.5 * jnp.cos(jnp.pi * dist / 4.0))
    return taps.astype(jnp.bfloat16).astype(jnp.float32)


def band(shape, distance, taps):
    total = jnp.zeros(shape, jnp.float32)
    for j in range(8):
        total = jnp.where(distance == j - 3, taps[j : j + 1, :1], total)
    return total.astype(jnp.bfloat16)


def cut_halo_kernel(sec_ref, down_ref, up_ref):
    rows_n = sec_ref.shape[2]
    down_ref[...] = sec_ref[0, :, rows_n - HALO :]
    up_ref[...] = sec_ref[0, :, :HALO]


def cut_middle_kernel(prim_ref, *refs):
    cut_ref = refs[-1]
    cut_ref[...] = prim_ref[:, LAG : LAG + cut_ref.shape[1]]


def relay_kernel(block_ref, awaited_ref, out_ref):
    del awaited_ref
    out_ref[...] = block_ref[:, : out_ref.shape[1]]


def bands_kernel(ao_ref, ro_ref, af_ref, rf_ref, az_ref, rg_ref):
    shape = az_ref.shape
    offset = lax.broadcasted_iota(jnp.int32, shape, 1) - lax.broadcasted_iota(jnp.int32, shape, 0)
    az_ref[...] = band(shape, offset - HALO - ao_ref[...], tap_rows(af_ref[...]))
    square = rg_ref.shape[1:]
    offset = lax.broadcasted_iota(jnp.int32, square, 0) - lax.broadcasted_iota(jnp.int32, square, 1)
    taps = tap_rows(rf_ref[...])
    for at, shift in enumerate((-LANE, 0, LANE)):
        rg_ref[at] = band(square, offset + shift - ro_ref[...], taps)


def resample_kernel(sec_ref, low_ref, high_ref, az_ref, rg_ref, out_ref, azim_ref):
    rows_n, cols_n = sec_ref.shape[2:]
    az_band = az_ref[...]
    here, tiles_n = lax.axis_index("tile"), lax.axis_size("tile")
    none = jnp.zeros(low_ref.shape[1:], jnp.bfloat16)
    for part in range(2):
        for start in range(0, rows_n, BAND):
            pieces = []
            if start == 0:
                pieces.append(jnp.where(here == 0, none, low_ref[part]))
            pieces.append(sec_ref[0, part, max(0, start - HALO) : min(rows_n, start + BAND + HALO)])
            if start + BAND == rows_n:
                pieces.append(jnp.where(here == tiles_n - 1, none, high_ref[part]))
            rows = jnp.concatenate(pieces, axis=0) if len(pieces) > 1 else pieces[0]
            azim_ref[part, start : start + BAND] = jnp.dot(
                az_band, rows, preferred_element_type=jnp.float32
            ).astype(jnp.bfloat16)

    before, same, after = [rg_ref[at] for at in range(3)]
    none = jnp.zeros((LANE, LANE), jnp.bfloat16)
    blocks_n, _, _, width = out_ref.shape
    lanes_n = width // LANE
    columns = []
    for lane in range(lanes_n):
        column = [none] * (lanes_n + 2)
        column[lane], column[lane + 1], column[lane + 2] = before, same, after
        columns.append(jnp.concatenate(column, axis=0))
    rg_band = jnp.concatenate(columns, axis=1)
    for block in range(blocks_n):
        first = block * width - LANE
        last = (block + 1) * width + LANE
        taken = slice(max(first, 0), min(last, cols_n))
        used = rg_band[taken.start - first : taken.stop - first]
        for part in range(2):
            out_ref[block, part] = jnp.dot(
                azim_ref[part, :, taken], used, preferred_element_type=jnp.float32
            ).astype(jnp.bfloat16)


def interfere(prim_re, prim_im, sec_re, sec_im):
    p_re, p_im = prim_re.astype(jnp.float32), prim_im.astype(jnp.float32)
    s_re, s_im = sec_re.astype(jnp.float32), sec_im.astype(jnp.float32)
    return p_re * s_re + p_im * s_im, p_im * s_re - p_re * s_im


def look_columns(width, block, looks_n):
    shape = (width, looks_n)
    col = lax.broadcasted_iota(jnp.int32, shape, 0) + block * width
    look = lax.broadcasted_iota(jnp.int32, shape, 1) * LR
    return jnp.where((col >= look) & (col < look + LR), 1.0, 0.0).astype(jnp.bfloat16)


def look_rows(sums_ref, part, start, rows_n):
    count = rows_n // LA
    total = sums_ref[part, pl.ds(start, count, LA)]
    for row in range(1, LA):
        total = total + sums_ref[part, pl.ds(start + row, count, LA)]
    return total


def margin_kernel(
    own_ref, one_ref, two_ref, three_ref, res_ref, first_ref, last_ref, looks_ref, sums_ref
):
    here = lax.axis_index("date")
    _, _, rows_n, width = res_ref.shape
    whole, edges = (0, rows_n - LAG), (0, LAG)
    looks_n = looks_ref.shape[2]
    totals = [None, None]
    for step, (prim_ref, starts) in enumerate(
        ((own_ref, whole), (one_ref, edges), (two_ref, edges), (three_ref, edges))
    ):
        block = jnp.bitwise_xor(here, step)
        select = look_columns(width, block, looks_n)
        columns = pl.ds(pl.multiple_of(block * width, width), width)
        halves = []
        for held, start, target in zip(starts, whole, (first_ref, last_ref)):
            pair = interfere(
                prim_ref[0, held : held + LAG],
                prim_ref[1, held : held + LAG],
                res_ref[block, 0, start : start + LAG],
                res_ref[block, 1, start : start + LAG],
            )
            pair = [value.astype(jnp.bfloat16) for value in pair]
            for part in range(2):
                target[part, :, columns] = pair[part]
            halves.append(pair)
        for part in range(2):
            both = jnp.concatenate([halves[0][part], halves[1][part]], axis=0)
            summed = jnp.dot(both, select, preferred_element_type=jnp.float32)
            totals[part] = summed if step == 0 else totals[part] + summed
    for part in range(2):
        sums_ref[part] = totals[part]
        looks_ref[part] = look_rows(sums_ref, part, 0, 2 * LAG)


def stats_kernel(last_ref, later_ref, weight_ref, stats_ref):
    cols_n = last_ref.shape[2]
    weight = weight_ref[...]
    i_re, i_im = last_ref[0].astype(jnp.float32), last_ref[1].astype(jnp.float32)
    inside = jnp.where(lax.axis_index("tile") == lax.axis_size("tile") - 1, 0.0, 1.0)
    l_re, l_im = [later_ref[part].astype(jnp.float32) * inside for part in range(2)]
    values = (
        i_re * l_re + i_im * l_im,
        i_im * l_re - i_re * l_im,
        0.5 * (i_re * i_re + i_im * i_im + l_re * l_re + l_im * l_im),
    )
    rows = []
    for value in values:
        folded = value[:, :LANE]
        for start in range(LANE, cols_n, LANE):
            folded = folded + value[:, start : start + LANE]
        rows.append(jnp.sum(folded * weight, axis=0, keepdims=True))
    rows.append(jnp.sum(weight, axis=0, keepdims=True) * (cols_n // LANE))
    rows.append(jnp.zeros((4, LANE), jnp.float32))
    stats_ref[...] = jnp.concatenate(rows, axis=0)


def look_sums(pieces, res_ref, looks_n):
    here = lax.axis_index("date")
    _, _, rows_n, width = res_ref.shape
    middle_n = rows_n - 2 * LAG
    totals = [None, None]
    for at, (step, prim_ref) in enumerate(pieces):
        block = jnp.bitwise_xor(here, step)
        first = LAG if prim_ref.shape[1] == rows_n else 0
        select = look_columns(width, block, looks_n)
        pair = interfere(
            prim_ref[0, first : first + middle_n],
            prim_ref[1, first : first + middle_n],
            res_ref[block, 0, LAG : rows_n - LAG],
            res_ref[block, 1, LAG : rows_n - LAG],
        )
        for part in range(2):
            summed = jnp.dot(
                pair[part].astype(jnp.bfloat16), select, preferred_element_type=jnp.float32
            )
            totals[part] = summed if at == 0 else totals[part] + summed
    return totals


def middle_kernel(own_ref, one_ref, two_ref, res_ref, out_ref):
    pieces = ((0, own_ref), (1, one_ref), (2, two_ref))
    for part, total in enumerate(look_sums(pieces, res_ref, out_ref.shape[2])):
        out_ref[part] = total


def last_kernel(three_ref, res_ref, before_ref, looks_ref, out_ref, sums_ref):
    middle_n = before_ref.shape[1]
    edge = LAG // LA
    totals = look_sums(((3, three_ref),), res_ref, out_ref.shape[2])
    for part, total in enumerate(totals):
        sums_ref[part] = total + before_ref[part]
        out_ref[part, :edge] = looks_ref[part, :edge]
        out_ref[part, edge : edge + middle_n // LA] = look_rows(sums_ref, part, 0, middle_n)
        out_ref[part, edge + middle_n // LA :] = looks_ref[part, edge:]


def scale_kernel(looks_ref, mine_ref, other_ref, out_ref):
    stats = jnp.sum(mine_ref[...] + other_ref[...], axis=1, keepdims=True)
    e_re, e_im, power, count = [stats[row : row + 1] for row in range(4)]
    magnitude = jnp.sqrt(e_re * e_re + e_im * e_im)
    floor_val = (power + 1e-06) / jnp.sqrt(jnp.maximum(count, 1.0))
    denom = jnp.maximum(magnitude, floor_val)
    u_re = e_re / denom * (1.0 / (LA * LR))
    u_im = e_im / denom * (1.0 / (LA * LR))
    out_ref[0, 0] = looks_ref[0] * u_re + looks_ref[1] * u_im
    out_ref[0, 1] = looks_ref[1] * u_re - looks_ref[0] * u_im


def call(kernel, outs, scratch, cost, *args):
    vmem = pl.BlockSpec(memory_space=pltpu.VMEM)
    return pl.pallas_call(
        kernel,
        out_shape=outs,
        in_specs=[vmem] * len(args),
        out_specs=jax.tree.map(lambda _: vmem, outs),
        scratch_shapes=scratch,
        compiler_params=pltpu.CompilerParams(vmem_limit_bytes=VMEM_LIMIT),
        cost_estimate=pl.CostEstimate(flops=cost[0], bytes_accessed=cost[1], transcendentals=0),
    )(*args)


def ring(value, axis, step):
    count = lax.axis_size(axis)
    return lax.ppermute(value, axis, [(at, (at + step) % count) for at in range(count)])


def swap(value, axis, step):
    return lax.ppermute(value, axis, [(at, at ^ step) for at in range(lax.axis_size(axis))])


def fused(secondary, primary, margin_mask, az_off, rg_off, az_frac, rg_frac):
    _, _, rows_n, cols_n = secondary.shape
    width = primary.shape[2]
    dates_n = lax.axis_size("date")
    tiles_n = lax.axis_size("tile")
    bf16, f32 = jnp.bfloat16, jnp.float32
    shape = jax.ShapeDtypeStruct
    looks_n = cols_n // LR
    middle_n = rows_n - 2 * LAG
    edges = jnp.concatenate([primary[:, :LAG], primary[:, rows_n - LAG :]], axis=1)
    edges_two = swap(edges, "date", 2)
    edges_one = swap(edges, "date", 1)
    halo = shape((2, HALO, cols_n), bf16)
    down, up = call(cut_halo_kernel, (halo, halo), [], (0, 0), secondary)
    low = ring(down, "tile", 1)
    high = ring(up, "tile", -1)
    az_band, rg_band = call(
        bands_kernel,
        (shape((BAND, BAND + 2 * HALO), bf16), shape((3, LANE, LANE), bf16)),
        [],
        (0, 0),
        az_off, rg_off, az_frac, rg_frac,
    )
    relayed = call(relay_kernel, edges, [], (0, 0), edges_two, az_band)
    edges_three = swap(relayed, "date", 1)
    middle = call(
        cut_middle_kernel,
        shape((2, middle_n + 16, width), bf16),
        [],
        (0, 0),
        primary, edges_two,
    )
    weight = jnp.broadcast_to(margin_mask[rows_n - LAG :].astype(f32)[:, None], (LAG, LANE))
    res = call(
        resample_kernel,
        shape((dates_n, 2, rows_n, width), bf16),
        [pltpu.VMEM((2, rows_n, cols_n), bf16)],
        (0, 0),
        secondary, low, high, az_band, rg_band,
    )
    two, one = [swap(middle, "date", step) for step in (2, 1)]
    margin = shape((2, LAG, cols_n), bf16)
    first, last, looks = call(
        margin_kernel,
        (margin, margin, shape((2, 2 * LAG // LA, looks_n), f32)),
        [pltpu.VMEM((2, 2 * LAG, looks_n), f32)],
        (0, 0),
        primary, edges_one, edges_two, edges_three, res,
    )
    later = ring(first, "tile", -1)
    stats = call(
        stats_kernel,
        shape((8, LANE), f32),
        [],
        (0, 0),
        last, later, weight,
    )
    before = call(
        middle_kernel,
        shape((2, middle_n, looks_n), f32),
        [],
        (2 * 2 * middle_n * cols_n * looks_n, 8 * rows_n * cols_n),
        primary, one, two, res,
    )
    other = swap(stats, "tile", 1)
    block = shape((2, middle_n, width), bf16)
    relayed = call(relay_kernel, block, [], (0, 0), two, other)
    three = swap(relayed, "date", 1)
    stride = 2
    while stride < tiles_n:
        stats = stats + other
        other = swap(stats, "tile", stride)
        stride *= 2
    looks = call(
        last_kernel,
        shape((2, rows_n // LA, looks_n), f32),
        [pltpu.VMEM((2, middle_n, looks_n), f32)],
        (2 * middle_n * cols_n * looks_n, 4 * rows_n * cols_n),
        three, res, before, looks,
    )
    return call(
        scale_kernel,
        shape((1, 2, rows_n // LA, looks_n), f32),
        [],
        (8 * rows_n * looks_n, 8 * rows_n * looks_n),
        looks, stats, other,
    )


def padded(block, sides, width):
    for axis, dim in sides:
        low = passed_along(
            lax.slice_in_dim(block, block.shape[dim] - width, None, axis=dim), axis, 1
        )
        high = passed_along(lax.slice_in_dim(block, 0, width, axis=dim), axis, -1)
        block = jnp.concatenate([low, block, high], axis=dim)
    return block


def band_taps(offset, frac):
    inside = (offset >= -3) & (offset <= 4)
    return jnp.where(inside, window(offset.astype(jnp.float32) - frac), 0.0).astype(jnp.bfloat16)


def multilook(values):
    depth, rows_n, cols_n = values.shape
    return values.reshape(depth, rows_n // LA, LA, cols_n // LR, LR).mean(axis=(2, 4))


def plain(secondary, primary, margin_mask, az_off, rg_off, az_frac, rg_frac):
    rim_rows = KA + 4
    block_cols = 256
    image = secondary[0]
    rows_n = image.shape[1]
    cols_n = image.shape[2]
    extended = padded(image, (("tile", 1),), rim_rows)
    row_out = lax.broadcasted_iota(jnp.int32, (rows_n, rows_n + 2 * rim_rows), 0)
    row_in = lax.broadcasted_iota(jnp.int32, (rows_n, rows_n + 2 * rim_rows), 1)
    azim_taps = band_taps(row_in - row_out - az_off[0, 0] - rim_rows, az_frac[0, 0])
    azim = jnp.einsum(
        "im,kmc->kic", azim_taps, extended, preferred_element_type=jnp.float32
    ).astype(jnp.bfloat16)
    blocks_n = cols_n // block_cols
    col_pad = jnp.pad(azim, ((0, 0), (0, 0), (block_cols // 2, block_cols // 2)))
    pieces = col_pad.reshape(2, rows_n, blocks_n + 1, block_cols)
    inputs = jnp.concatenate([pieces[:, :, :-1], pieces[:, :, 1:]], axis=3)
    col_in = lax.broadcasted_iota(jnp.int32, (2 * block_cols, block_cols), 0)
    col_out = lax.broadcasted_iota(jnp.int32, (2 * block_cols, block_cols), 1)
    range_taps = band_taps(col_in - block_cols // 2 - col_out - rg_off[0, 0], rg_frac[0, 0])
    resampled = jnp.einsum("kibm,mn->kibn", inputs, range_taps, preferred_element_type=jnp.float32)
    resampled = resampled.reshape(2, rows_n, cols_n).astype(jnp.bfloat16)
    prim = lax.all_gather(primary, "date", axis=2, tiled=True)[None]
    sec_f = resampled[None].astype(jnp.float32)
    prim_f = prim.astype(jnp.float32)
    ifg_re = prim_f[:, 0] * sec_f[:, 0] + prim_f[:, 1] * sec_f[:, 1]
    ifg_im = prim_f[:, 1] * sec_f[:, 0] - prim_f[:, 0] * sec_f[:, 1]
    interf = jnp.stack((ifg_re, ifg_im), axis=1)
    upcoming = passed_along(interf[:, :, :LAG, :], "tile", -1)
    later = jnp.concatenate([interf[:, :, LAG:, :], upcoming], axis=2)
    l_re = later[:, 0]
    l_im = later[:, 1]
    weight = margin_mask.astype(jnp.float32)[None, :, None]
    e_re = jnp.sum(weight * (ifg_re * l_re + ifg_im * l_im), axis=(1, 2))
    e_im = jnp.sum(weight * (ifg_im * l_re - ifg_re * l_im), axis=(1, 2))
    power = jnp.sum(
        weight * 0.5 * (ifg_re * ifg_re + ifg_im * ifg_im + l_re * l_re + l_im * l_im), axis=(1, 2)
    )
    count = jnp.zeros_like(e_re) + jnp.sum(margin_mask.astype(jnp.float32)) * interf.shape[3]
    stats = jnp.stack((e_re, e_im, power, count), axis=1)
    totals = lax.psum(stats, "tile")
    magnitude = jnp.sqrt(totals[:, 0] * totals[:, 0] + totals[:, 1] * totals[:, 1])
    floor_val = (totals[:, 2] + 1e-06) / jnp.sqrt(jnp.maximum(totals[:, 3], 1.0))
    denom = jnp.maximum(magnitude, floor_val)
    u_re = (totals[:, 0] / denom)[:, None, None]
    u_im = (totals[:, 1] / denom)[:, None, None]
    c_re = multilook(ifg_re * u_re + ifg_im * u_im)
    c_im = multilook(ifg_im * u_re - ifg_re * u_im)
    return jnp.stack((c_re, c_im), axis=1)


def shards(secondary, primary, *rest):
    rows_n, width = primary.shape[1:]
    fits = rows_n % BAND == 0 and rows_n > 2 * LAG + BAND and width % LANE == 0
    tiles_n = lax.axis_size("tile")
    fits = fits and lax.axis_size("date") == 4 and tiles_n & (tiles_n - 1) == 0
    return (fused if fits else plain)(secondary, primary, *rest)


def solution(mesh):
    return jax.shard_map(
        shards,
        mesh=mesh,
        in_specs=(
            P("date", None, "tile", None),
            P(None, "tile", "date"),
            P("tile"),
            P("date", "tile"),
            P("date", "tile"),
            P("date", "tile"),
            P("date", "tile"),
        ),
        out_specs=P("date", None, "tile", None),
        check_vma=False,
    )
```

```python
import functools

import jax
import jax.numpy as jnp
from jax import lax
from jax.experimental import pallas as pl
from jax.experimental.pallas import tpu as pltpu
from jax.sharding import PartitionSpec as P

KA = 16
LAG = 64
LA = 2
LR = 8
LANE = 128
BAND = 128
HALO = 32
VMEM_LIMIT = 40 * 1024 * 1024


def passed_along(value, axis, steps):
    count = lax.axis_size(axis)
    initial, last = (max(0, -steps), min(count, count - steps))
    return lax.ppermute(value, axis, [(source, source + steps) for source in range(initial, last)])


def window(dist):
    return jnp.sinc(dist) * (0.5 + 0.5 * jnp.cos(jnp.pi * dist / 4.0))


def tap_rows(frac):
    dist = lax.broadcasted_iota(jnp.int32, (8, LANE), 0).astype(jnp.float32) - 3.0 - frac
    angle = jnp.pi * dist
    sinc = jnp.where(dist == 0.0, 1.0, jnp.sin(angle) / jnp.where(dist == 0.0, 1.0, angle))
    taps = sinc * (0.5 + 0.5 * jnp.cos(jnp.pi * dist / 4.0))
    return taps.astype(jnp.bfloat16).astype(jnp.float32)


def band(shape, distance, taps):
    total = jnp.zeros(shape, jnp.float32)
    for j in range(8):
        total = jnp.where(distance == j - 3, taps[j : j + 1, :1], total)
    return total.astype(jnp.bfloat16)


def cut_halo_kernel(sec_ref, down_ref, up_ref):
    rows_n = sec_ref.shape[2]
    down_ref[...] = sec_ref[0, :, rows_n - HALO :]
    up_ref[...] = sec_ref[0, :, :HALO]


def cut_kernel(prim_ref, edges_ref, middle_ref):
    rows_n = prim_ref.shape[1]
    edges_ref[:, :LAG] = prim_ref[:, :LAG]
    edges_ref[:, LAG:] = prim_ref[:, rows_n - LAG :]
    middle_ref[...] = prim_ref[:, LAG : LAG + middle_ref.shape[1]]


def relay_kernel(block_ref, awaited_ref, out_ref):
    del awaited_ref
    out_ref[...] = block_ref[:, : out_ref.shape[1]]


def bands_kernel(ao_ref, ro_ref, af_ref, rf_ref, az_ref, rg_ref):
    shape = az_ref.shape
    offset = lax.broadcasted_iota(jnp.int32, shape, 1) - lax.broadcasted_iota(jnp.int32, shape, 0)
    az_ref[...] = band(shape, offset - HALO - ao_ref[...], tap_rows(af_ref[...]))
    square = rg_ref.shape[1:]
    offset = lax.broadcasted_iota(jnp.int32, square, 0) - lax.broadcasted_iota(jnp.int32, square, 1)
    taps = tap_rows(rf_ref[...])
    for at, shift in enumerate((-LANE, 0, LANE)):
        rg_ref[at] = band(square, offset + shift - ro_ref[...], taps)


def resample_kernel(sec_ref, low_ref, high_ref, az_ref, rg_ref, out_ref, azim_ref):
    rows_n, cols_n = sec_ref.shape[2:]
    az_band = az_ref[...]
    here, tiles_n = lax.axis_index("tile"), lax.axis_size("tile")
    none = jnp.zeros(low_ref.shape[1:], jnp.bfloat16)
    for part in range(2):
        for start in range(0, rows_n, BAND):
            pieces = []
            if start == 0:
                pieces.append(jnp.where(here == 0, none, low_ref[part]))
            pieces.append(sec_ref[0, part, max(0, start - HALO) : min(rows_n, start + BAND + HALO)])
            if start + BAND == rows_n:
                pieces.append(jnp.where(here == tiles_n - 1, none, high_ref[part]))
            rows = jnp.concatenate(pieces, axis=0) if len(pieces) > 1 else pieces[0]
            azim_ref[part, start : start + BAND] = jnp.dot(
                az_band, rows, preferred_element_type=jnp.float32
            ).astype(jnp.bfloat16)

    before, same, after = [rg_ref[at] for at in range(3)]
    none = jnp.zeros((LANE, LANE), jnp.bfloat16)
    blocks_n, _, _, width = out_ref.shape
    lanes_n = width // LANE
    columns = []
    for lane in range(lanes_n):
        column = [none] * (lanes_n + 2)
        column[lane], column[lane + 1], column[lane + 2] = before, same, after
        columns.append(jnp.concatenate(column, axis=0))
    rg_band = jnp.concatenate(columns, axis=1)
    for block in range(blocks_n):
        first = block * width - LANE
        last = (block + 1) * width + LANE
        taken = slice(max(first, 0), min(last, cols_n))
        used = rg_band[taken.start - first : taken.stop - first]
        for part in range(2):
            out_ref[block, part] = jnp.dot(
                azim_ref[part, :, taken], used, preferred_element_type=jnp.float32
            ).astype(jnp.bfloat16)


def interfere(prim_re, prim_im, sec_re, sec_im):
    p_re, p_im = prim_re.astype(jnp.float32), prim_im.astype(jnp.float32)
    s_re, s_im = sec_re.astype(jnp.float32), sec_im.astype(jnp.float32)
    return p_re * s_re + p_im * s_im, p_im * s_re - p_re * s_im


def look_columns(width, block, looks_n):
    shape = (width, looks_n)
    col = lax.broadcasted_iota(jnp.int32, shape, 0) + block * width
    look = lax.broadcasted_iota(jnp.int32, shape, 1) * LR
    return jnp.where((col >= look) & (col < look + LR), 1.0, 0.0).astype(jnp.bfloat16)


def look_rows(sums_ref, part, start, rows_n):
    count = rows_n // LA
    total = sums_ref[part, pl.ds(start, count, LA)]
    for row in range(1, LA):
        total = total + sums_ref[part, pl.ds(start + row, count, LA)]
    return total


def margin_kernel(
    own_ref, one_ref, two_ref, three_ref, res_ref, first_ref, last_ref, looks_ref, sums_ref
):
    here = lax.axis_index("date")
    _, _, rows_n, width = res_ref.shape
    whole, edges = (0, rows_n - LAG), (0, LAG)
    looks_n = looks_ref.shape[2]
    totals = [None, None]
    for step, (prim_ref, starts) in enumerate(
        ((own_ref, whole), (one_ref, edges), (two_ref, edges), (three_ref, edges))
    ):
        block = jnp.bitwise_xor(here, step)
        select = look_columns(width, block, looks_n)
        columns = pl.ds(pl.multiple_of(block * width, width), width)
        halves = []
        for held, start, target in zip(starts, whole, (first_ref, last_ref)):
            pair = interfere(
                prim_ref[0, held : held + LAG],
                prim_ref[1, held : held + LAG],
                res_ref[block, 0, start : start + LAG],
                res_ref[block, 1, start : start + LAG],
            )
            pair = [value.astype(jnp.bfloat16) for value in pair]
            for part in range(2):
                target[part, :, columns] = pair[part]
            halves.append(pair)
        for part in range(2):
            both = jnp.concatenate([halves[0][part], halves[1][part]], axis=0)
            summed = jnp.dot(both, select, preferred_element_type=jnp.float32)
            totals[part] = summed if step == 0 else totals[part] + summed
    for part in range(2):
        sums_ref[part] = totals[part]
        looks_ref[part] = look_rows(sums_ref, part, 0, 2 * LAG)


def stats_kernel(last_ref, later_ref, weight_ref, stats_ref):
    cols_n = last_ref.shape[2]
    weight = weight_ref[...]
    i_re, i_im = last_ref[0].astype(jnp.float32), last_ref[1].astype(jnp.float32)
    inside = jnp.where(lax.axis_index("tile") == lax.axis_size("tile") - 1, 0.0, 1.0)
    l_re, l_im = [later_ref[part].astype(jnp.float32) * inside for part in range(2)]
    values = (
        i_re * l_re + i_im * l_im,
        i_im * l_re - i_re * l_im,
        0.5 * (i_re * i_re + i_im * i_im + l_re * l_re + l_im * l_im),
    )
    rows = []
    for value in values:
        folded = value[:, :LANE]
        for start in range(LANE, cols_n, LANE):
            folded = folded + value[:, start : start + LANE]
        rows.append(jnp.sum(folded * weight, axis=0, keepdims=True))
    rows.append(jnp.sum(weight, axis=0, keepdims=True) * (cols_n // LANE))
    rows.append(jnp.zeros((4, LANE), jnp.float32))
    stats_ref[...] = jnp.concatenate(rows, axis=0)


def look_sums(pieces, res_ref, looks_n):
    here = lax.axis_index("date")
    _, _, rows_n, width = res_ref.shape
    middle_n = rows_n - 2 * LAG
    totals = [None, None]
    for at, (step, prim_ref) in enumerate(pieces):
        block = jnp.bitwise_xor(here, step)
        first = LAG if prim_ref.shape[1] == rows_n else 0
        select = look_columns(width, block, looks_n)
        pair = interfere(
            prim_ref[0, first : first + middle_n],
            prim_ref[1, first : first + middle_n],
            res_ref[block, 0, LAG : rows_n - LAG],
            res_ref[block, 1, LAG : rows_n - LAG],
        )
        for part in range(2):
            summed = jnp.dot(
                pair[part].astype(jnp.bfloat16), select, preferred_element_type=jnp.float32
            )
            totals[part] = summed if at == 0 else totals[part] + summed
    return totals


def middle_kernel(own_ref, one_ref, two_ref, res_ref, out_ref):
    pieces = ((0, own_ref), (1, one_ref), (2, two_ref))
    for part, total in enumerate(look_sums(pieces, res_ref, out_ref.shape[2])):
        out_ref[part] = total


def last_kernel(three_ref, res_ref, before_ref, looks_ref, out_ref, sums_ref):
    middle_n = before_ref.shape[1]
    edge = LAG // LA
    totals = look_sums(((3, three_ref),), res_ref, out_ref.shape[2])
    for part, total in enumerate(totals):
        sums_ref[part] = total + before_ref[part]
        out_ref[part, :edge] = looks_ref[part, :edge]
        out_ref[part, edge : edge + middle_n // LA] = look_rows(sums_ref, part, 0, middle_n)
        out_ref[part, edge + middle_n // LA :] = looks_ref[part, edge:]


def scale_kernel(looks_ref, mine_ref, other_ref, out_ref):
    stats = jnp.sum(mine_ref[...] + other_ref[...], axis=1, keepdims=True)
    e_re, e_im, power, count = [stats[row : row + 1] for row in range(4)]
    magnitude = jnp.sqrt(e_re * e_re + e_im * e_im)
    floor_val = (power + 1e-06) / jnp.sqrt(jnp.maximum(count, 1.0))
    denom = jnp.maximum(magnitude, floor_val)
    u_re = e_re / denom * (1.0 / (LA * LR))
    u_im = e_im / denom * (1.0 / (LA * LR))
    out_ref[0, 0] = looks_ref[0] * u_re + looks_ref[1] * u_im
    out_ref[0, 1] = looks_ref[1] * u_re - looks_ref[0] * u_im


def call(kernel, outs, scratch, cost, *args):
    vmem = pl.BlockSpec(memory_space=pltpu.VMEM)
    return pl.pallas_call(
        kernel,
        out_shape=outs,
        in_specs=[vmem] * len(args),
        out_specs=jax.tree.map(lambda _: vmem, outs),
        scratch_shapes=scratch,
        compiler_params=pltpu.CompilerParams(vmem_limit_bytes=VMEM_LIMIT),
        cost_estimate=pl.CostEstimate(flops=cost[0], bytes_accessed=cost[1], transcendentals=0),
    )(*args)


def ring(value, axis, step):
    count = lax.axis_size(axis)
    return lax.ppermute(value, axis, [(at, (at + step) % count) for at in range(count)])


def swap(value, axis, step):
    return lax.ppermute(value, axis, [(at, at ^ step) for at in range(lax.axis_size(axis))])


def fused(secondary, primary, margin_mask, az_off, rg_off, az_frac, rg_frac):
    _, _, rows_n, cols_n = secondary.shape
    width = primary.shape[2]
    dates_n = lax.axis_size("date")
    tiles_n = lax.axis_size("tile")
    bf16, f32 = jnp.bfloat16, jnp.float32
    shape = jax.ShapeDtypeStruct
    looks_n = cols_n // LR
    middle_n = rows_n - 2 * LAG
    edges, middle = call(
        cut_kernel,
        (shape((2, 2 * LAG, width), bf16), shape((2, middle_n + 0, width), bf16)),
        [],
        (0, 0),
        primary,
    )
    edges_two = swap(edges, "date", 2)
    edges_one = swap(edges, "date", 1)
    halo = shape((2, HALO, cols_n), bf16)
    down, up = call(cut_halo_kernel, (halo, halo), [], (0, 0), secondary)
    low = ring(down, "tile", 1)
    high = ring(up, "tile", -1)
    az_band, rg_band = call(
        bands_kernel,
        (shape((BAND, BAND + 2 * HALO), bf16), shape((3, LANE, LANE), bf16)),
        [],
        (0, 0),
        az_off, rg_off, az_frac, rg_frac,
    )
    relayed = call(
        relay_kernel, shape(edges.shape, bf16), [], (0, 0), edges_two, az_band
    )
    edges_three = swap(relayed, "date", 1)
    weight = jnp.broadcast_to(margin_mask[rows_n - LAG :].astype(f32)[:, None], (LAG, LANE))
    res = call(
        resample_kernel,
        shape((dates_n, 2, rows_n, width), bf16),
        [pltpu.VMEM((2, rows_n, cols_n), bf16)],
        (0, 0),
        secondary, low, high, az_band, rg_band,
    )
    two, one = [swap(middle, "date", step) for step in (2, 1)]
    margin = shape((2, LAG, cols_n), bf16)
    first, last, looks = call(
        margin_kernel,
        (margin, margin, shape((2, 2 * LAG // LA, looks_n), f32)),
        [pltpu.VMEM((2, 2 * LAG, looks_n), f32)],
        (0, 0),
        primary, edges_one, edges_two, edges_three, res,
    )
    later = ring(first, "tile", -1)
    stats = call(
        stats_kernel,
        shape((8, LANE), f32),
        [],
        (0, 0),
        last, later, weight,
    )
    before = call(
        middle_kernel,
        shape((2, middle_n, looks_n), f32),
        [],
        (2 * 2 * middle_n * cols_n * looks_n, 8 * rows_n * cols_n),
        primary, one, two, res,
    )
    other = swap(stats, "tile", 1)
    block = shape((2, middle_n, width), bf16)
    relayed = call(relay_kernel, block, [], (0, 0), two, first)
    three = swap(relayed, "date", 1)
    stride = 2
    while stride < tiles_n:
        stats = stats + other
        other = swap(stats, "tile", stride)
        stride *= 2
    looks = call(
        last_kernel,
        shape((2, rows_n // LA, looks_n), f32),
        [pltpu.VMEM((2, middle_n, looks_n), f32)],
        (2 * middle_n * cols_n * looks_n, 4 * rows_n * cols_n),
        three, res, before, looks,
    )
    return call(
        scale_kernel,
        shape((1, 2, rows_n // LA, looks_n), f32),
        [],
        (8 * rows_n * looks_n, 8 * rows_n * looks_n),
        looks, stats, other,
    )


def padded(block, sides, width):
    for axis, dim in sides:
        low = passed_along(
            lax.slice_in_dim(block, block.shape[dim] - width, None, axis=dim), axis, 1
        )
        high = passed_along(lax.slice_in_dim(block, 0, width, axis=dim), axis, -1)
        block = jnp.concatenate([low, block, high], axis=dim)
    return block


def band_taps(offset, frac):
    inside = (offset >= -3) & (offset <= 4)
    return jnp.where(inside, window(offset.astype(jnp.float32) - frac), 0.0).astype(jnp.bfloat16)


def multilook(values):
    depth, rows_n, cols_n = values.shape
    return values.reshape(depth, rows_n // LA, LA, cols_n // LR, LR).mean(axis=(2, 4))


def plain(secondary, primary, margin_mask, az_off, rg_off, az_frac, rg_frac):
    rim_rows = KA + 4
    block_cols = 256
    image = secondary[0]
    rows_n = image.shape[1]
    cols_n = image.shape[2]
    extended = padded(image, (("tile", 1),), rim_rows)
    row_out = lax.broadcasted_iota(jnp.int32, (rows_n, rows_n + 2 * rim_rows), 0)
    row_in = lax.broadcasted_iota(jnp.int32, (rows_n, rows_n + 2 * rim_rows), 1)
    azim_taps = band_taps(row_in - row_out - az_off[0, 0] - rim_rows, az_frac[0, 0])
    azim = jnp.einsum(
        "im,kmc->kic", azim_taps, extended, preferred_element_type=jnp.float32
    ).astype(jnp.bfloat16)
    blocks_n = cols_n // block_cols
    col_pad = jnp.pad(azim, ((0, 0), (0, 0), (block_cols // 2, block_cols // 2)))
    pieces = col_pad.reshape(2, rows_n, blocks_n + 1, block_cols)
    inputs = jnp.concatenate([pieces[:, :, :-1], pieces[:, :, 1:]], axis=3)
    col_in = lax.broadcasted_iota(jnp.int32, (2 * block_cols, block_cols), 0)
    col_out = lax.broadcasted_iota(jnp.int32, (2 * block_cols, block_cols), 1)
    range_taps = band_taps(col_in - block_cols // 2 - col_out - rg_off[0, 0], rg_frac[0, 0])
    resampled = jnp.einsum("kibm,mn->kibn", inputs, range_taps, preferred_element_type=jnp.float32)
    resampled = resampled.reshape(2, rows_n, cols_n).astype(jnp.bfloat16)
    prim = lax.all_gather(primary, "date", axis=2, tiled=True)[None]
    sec_f = resampled[None].astype(jnp.float32)
    prim_f = prim.astype(jnp.float32)
    ifg_re = prim_f[:, 0] * sec_f[:, 0] + prim_f[:, 1] * sec_f[:, 1]
    ifg_im = prim_f[:, 1] * sec_f[:, 0] - prim_f[:, 0] * sec_f[:, 1]
    interf = jnp.stack((ifg_re, ifg_im), axis=1)
    upcoming = passed_along(interf[:, :, :LAG, :], "tile", -1)
    later = jnp.concatenate([interf[:, :, LAG:, :], upcoming], axis=2)
    l_re = later[:, 0]
    l_im = later[:, 1]
    weight = margin_mask.astype(jnp.float32)[None, :, None]
    e_re = jnp.sum(weight * (ifg_re * l_re + ifg_im * l_im), axis=(1, 2))
    e_im = jnp.sum(weight * (ifg_im * l_re - ifg_re * l_im), axis=(1, 2))
    power = jnp.sum(
        weight * 0.5 * (ifg_re * ifg_re + ifg_im * ifg_im + l_re * l_re + l_im * l_im), axis=(1, 2)
    )
    count = jnp.zeros_like(e_re) + jnp.sum(margin_mask.astype(jnp.float32)) * interf.shape[3]
    stats = jnp.stack((e_re, e_im, power, count), axis=1)
    totals = lax.psum(stats, "tile")
    magnitude = jnp.sqrt(totals[:, 0] * totals[:, 0] + totals[:, 1] * totals[:, 1])
    floor_val = (totals[:, 2] + 1e-06) / jnp.sqrt(jnp.maximum(totals[:, 3], 1.0))
    denom = jnp.maximum(magnitude, floor_val)
    u_re = (totals[:, 0] / denom)[:, None, None]
    u_im = (totals[:, 1] / denom)[:, None, None]
    c_re = multilook(ifg_re * u_re + ifg_im * u_im)
    c_im = multilook(ifg_im * u_re - ifg_re * u_im)
    return jnp.stack((c_re, c_im), axis=1)


def shards(secondary, primary, *rest):
    rows_n, width = primary.shape[1:]
    fits = rows_n % BAND == 0 and rows_n > 2 * LAG + BAND and width % LANE == 0
    tiles_n = lax.axis_size("tile")
    fits = fits and lax.axis_size("date") == 4 and tiles_n & (tiles_n - 1) == 0
    return (fused if fits else plain)(secondary, primary, *rest)


def solution(mesh):
    return jax.shard_map(
        shards,
        mesh=mesh,
        in_specs=(
            P("date", None, "tile", None),
            P(None, "tile", "date"),
            P("tile"),
            P("date", "tile"),
            P("date", "tile"),
            P("date", "tile"),
            P("date", "tile"),
        ),
        out_specs=P("date", None, "tile", None),
        check_vma=False,
    )
```

```python
import functools

import jax
import jax.numpy as jnp
from jax import lax
from jax.experimental import pallas as pl
from jax.experimental.pallas import tpu as pltpu
from jax.sharding import PartitionSpec as P

KA = 16
LAG = 64
LA = 2
LR = 8
LANE = 128
BAND = 128
HALO = 32
VMEM_LIMIT = 40 * 1024 * 1024


def passed_along(value, axis, steps):
    count = lax.axis_size(axis)
    initial, last = (max(0, -steps), min(count, count - steps))
    return lax.ppermute(value, axis, [(source, source + steps) for source in range(initial, last)])


def window(dist):
    return jnp.sinc(dist) * (0.5 + 0.5 * jnp.cos(jnp.pi * dist / 4.0))


def tap_rows(frac):
    dist = lax.broadcasted_iota(jnp.int32, (8, LANE), 0).astype(jnp.float32) - 3.0 - frac
    angle = jnp.pi * dist
    sinc = jnp.where(dist == 0.0, 1.0, jnp.sin(angle) / jnp.where(dist == 0.0, 1.0, angle))
    taps = sinc * (0.5 + 0.5 * jnp.cos(jnp.pi * dist / 4.0))
    return taps.astype(jnp.bfloat16).astype(jnp.float32)


def band(shape, distance, taps):
    total = jnp.zeros(shape, jnp.float32)
    for j in range(8):
        total = jnp.where(distance == j - 3, taps[j : j + 1, :1], total)
    return total.astype(jnp.bfloat16)


def cut_halo_kernel(sec_ref, down_ref, up_ref):
    rows_n = sec_ref.shape[2]
    down_ref[...] = sec_ref[0, :, rows_n - HALO :]
    up_ref[...] = sec_ref[0, :, :HALO]


def cut_middle_kernel(prim_ref, *refs):
    cut_ref = refs[-1]
    cut_ref[...] = prim_ref[:, LAG : LAG + cut_ref.shape[1]]


def relay_kernel(block_ref, *refs):
    out_ref = refs[-1]
    out_ref[...] = block_ref[:, : out_ref.shape[1]]


def bands_kernel(ao_ref, ro_ref, af_ref, rf_ref, az_ref, rg_ref):
    shape = az_ref.shape
    offset = lax.broadcasted_iota(jnp.int32, shape, 1) - lax.broadcasted_iota(jnp.int32, shape, 0)
    az_ref[...] = band(shape, offset - HALO - ao_ref[...], tap_rows(af_ref[...]))
    square = rg_ref.shape[1:]
    offset = lax.broadcasted_iota(jnp.int32, square, 0) - lax.broadcasted_iota(jnp.int32, square, 1)
    taps = tap_rows(rf_ref[...])
    for at, shift in enumerate((-LANE, 0, LANE)):
        rg_ref[at] = band(square, offset + shift - ro_ref[...], taps)


def resample_kernel(sec_ref, low_ref, high_ref, az_ref, rg_ref, out_ref, azim_ref):
    rows_n, cols_n = sec_ref.shape[2:]
    az_band = az_ref[...]
    here, tiles_n = lax.axis_index("tile"), lax.axis_size("tile")
    none = jnp.zeros(low_ref.shape[1:], jnp.bfloat16)
    for part in range(2):
        for start in range(0, rows_n, BAND):
            pieces = []
            if start == 0:
                pieces.append(jnp.where(here == 0, none, low_ref[part]))
            pieces.append(sec_ref[0, part, max(0, start - HALO) : min(rows_n, start + BAND + HALO)])
            if start + BAND == rows_n:
                pieces.append(jnp.where(here == tiles_n - 1, none, high_ref[part]))
            rows = jnp.concatenate(pieces, axis=0) if len(pieces) > 1 else pieces[0]
            azim_ref[part, start : start + BAND] = jnp.dot(
                az_band, rows, preferred_element_type=jnp.float32
            ).astype(jnp.bfloat16)

    before, same, after = [rg_ref[at] for at in range(3)]
    none = jnp.zeros((LANE, LANE), jnp.bfloat16)
    blocks_n, _, _, width = out_ref.shape
    lanes_n = width // LANE
    columns = []
    for lane in range(lanes_n):
        column = [none] * (lanes_n + 2)
        column[lane], column[lane + 1], column[lane + 2] = before, same, after
        columns.append(jnp.concatenate(column, axis=0))
    rg_band = jnp.concatenate(columns, axis=1)
    for block in range(blocks_n):
        first = block * width - LANE
        last = (block + 1) * width + LANE
        taken = slice(max(first, 0), min(last, cols_n))
        used = rg_band[taken.start - first : taken.stop - first]
        for part in range(2):
            out_ref[block, part] = jnp.dot(
                azim_ref[part, :, taken], used, preferred_element_type=jnp.float32
            ).astype(jnp.bfloat16)


def interfere(prim_re, prim_im, sec_re, sec_im):
    p_re, p_im = prim_re.astype(jnp.float32), prim_im.astype(jnp.float32)
    s_re, s_im = sec_re.astype(jnp.float32), sec_im.astype(jnp.float32)
    return p_re * s_re + p_im * s_im, p_im * s_re - p_re * s_im


def look_columns(width, block, looks_n):
    shape = (width, looks_n)
    col = lax.broadcasted_iota(jnp.int32, shape, 0) + block * width
    look = lax.broadcasted_iota(jnp.int32, shape, 1) * LR
    return jnp.where((col >= look) & (col < look + LR), 1.0, 0.0).astype(jnp.bfloat16)


def look_rows(sums_ref, part, start, rows_n):
    count = rows_n // LA
    total = sums_ref[part, pl.ds(start, count, LA)]
    for row in range(1, LA):
        total = total + sums_ref[part, pl.ds(start + row, count, LA)]
    return total


def margin_kernel(
    own_ref, one_ref, two_ref, three_ref, res_ref, first_ref, last_ref, looks_ref, sums_ref
):
    here = lax.axis_index("date")
    _, _, rows_n, width = res_ref.shape
    whole, edges = (0, rows_n - LAG), (0, LAG)
    looks_n = looks_ref.shape[2]
    totals = [None, None]
    for step, (prim_ref, starts) in enumerate(
        ((own_ref, whole), (one_ref, edges), (two_ref, edges), (three_ref, edges))
    ):
        block = jnp.bitwise_xor(here, step)
        select = look_columns(width, block, looks_n)
        columns = pl.ds(pl.multiple_of(block * width, width), width)
        halves = []
        for held, start, target in zip(starts, whole, (first_ref, last_ref)):
            pair = interfere(
                prim_ref[0, held : held + LAG],
                prim_ref[1, held : held + LAG],
                res_ref[block, 0, start : start + LAG],
                res_ref[block, 1, start : start + LAG],
            )
            pair = [value.astype(jnp.bfloat16) for value in pair]
            for part in range(2):
                target[part, :, columns] = pair[part]
            halves.append(pair)
        for part in range(2):
            both = jnp.concatenate([halves[0][part], halves[1][part]], axis=0)
            summed = jnp.dot(both, select, preferred_element_type=jnp.float32)
            totals[part] = summed if step == 0 else totals[part] + summed
    for part in range(2):
        sums_ref[part] = totals[part]
        looks_ref[part] = look_rows(sums_ref, part, 0, 2 * LAG)


def stats_kernel(last_ref, later_ref, weight_ref, stats_ref):
    cols_n = last_ref.shape[2]
    weight = weight_ref[...]
    i_re, i_im = last_ref[0].astype(jnp.float32), last_ref[1].astype(jnp.float32)
    inside = jnp.where(lax.axis_index("tile") == lax.axis_size("tile") - 1, 0.0, 1.0)
    l_re, l_im = [later_ref[part].astype(jnp.float32) * inside for part in range(2)]
    values = (
        i_re * l_re + i_im * l_im,
        i_im * l_re - i_re * l_im,
        0.5 * (i_re * i_re + i_im * i_im + l_re * l_re + l_im * l_im),
    )
    rows = []
    for value in values:
        folded = value[:, :LANE]
        for start in range(LANE, cols_n, LANE):
            folded = folded + value[:, start : start + LANE]
        rows.append(jnp.sum(folded * weight, axis=0, keepdims=True))
    rows.append(jnp.sum(weight, axis=0, keepdims=True) * (cols_n // LANE))
    rows.append(jnp.zeros((4, LANE), jnp.float32))
    stats_ref[...] = jnp.concatenate(rows, axis=0)


def look_sums(pieces, res_ref, looks_n):
    here = lax.axis_index("date")
    _, _, rows_n, width = res_ref.shape
    middle_n = rows_n - 2 * LAG
    totals = [None, None]
    for at, (step, prim_ref) in enumerate(pieces):
        block = jnp.bitwise_xor(here, step)
        first = LAG if prim_ref.shape[1] == rows_n else 0
        select = look_columns(width, block, looks_n)
        pair = interfere(
            prim_ref[0, first : first + middle_n],
            prim_ref[1, first : first + middle_n],
            res_ref[block, 0, LAG : rows_n - LAG],
            res_ref[block, 1, LAG : rows_n - LAG],
        )
        for part in range(2):
            summed = jnp.dot(
                pair[part].astype(jnp.bfloat16), select, preferred_element_type=jnp.float32
            )
            totals[part] = summed if at == 0 else totals[part] + summed
    return totals


def middle_kernel(own_ref, one_ref, two_ref, res_ref, out_ref):
    pieces = ((0, own_ref), (1, one_ref), (2, two_ref))
    for part, total in enumerate(look_sums(pieces, res_ref, out_ref.shape[2])):
        out_ref[part] = total


def last_kernel(three_ref, res_ref, before_ref, looks_ref, out_ref, sums_ref):
    middle_n = before_ref.shape[1]
    edge = LAG // LA
    totals = look_sums(((3, three_ref),), res_ref, out_ref.shape[2])
    for part, total in enumerate(totals):
        sums_ref[part] = total + before_ref[part]
        out_ref[part, :edge] = looks_ref[part, :edge]
        out_ref[part, edge : edge + middle_n // LA] = look_rows(sums_ref, part, 0, middle_n)
        out_ref[part, edge + middle_n // LA :] = looks_ref[part, edge:]


def scale_kernel(looks_ref, mine_ref, other_ref, out_ref):
    stats = jnp.sum(mine_ref[...] + other_ref[...], axis=1, keepdims=True)
    e_re, e_im, power, count = [stats[row : row + 1] for row in range(4)]
    magnitude = jnp.sqrt(e_re * e_re + e_im * e_im)
    floor_val = (power + 1e-06) / jnp.sqrt(jnp.maximum(count, 1.0))
    denom = jnp.maximum(magnitude, floor_val)
    u_re = e_re / denom * (1.0 / (LA * LR))
    u_im = e_im / denom * (1.0 / (LA * LR))
    out_ref[0, 0] = looks_ref[0] * u_re + looks_ref[1] * u_im
    out_ref[0, 1] = looks_ref[1] * u_re - looks_ref[0] * u_im


def call(kernel, outs, scratch, cost, *args):
    vmem = pl.BlockSpec(memory_space=pltpu.VMEM)
    return pl.pallas_call(
        kernel,
        out_shape=outs,
        in_specs=[vmem] * len(args),
        out_specs=jax.tree.map(lambda _: vmem, outs),
        scratch_shapes=scratch,
        compiler_params=pltpu.CompilerParams(vmem_limit_bytes=VMEM_LIMIT),
        cost_estimate=pl.CostEstimate(flops=cost[0], bytes_accessed=cost[1], transcendentals=0),
    )(*args)


def ring(value, axis, step):
    count = lax.axis_size(axis)
    return lax.ppermute(value, axis, [(at, (at + step) % count) for at in range(count)])


def swap(value, axis, step):
    return lax.ppermute(value, axis, [(at, at ^ step) for at in range(lax.axis_size(axis))])


def fused(secondary, primary, margin_mask, az_off, rg_off, az_frac, rg_frac):
    _, _, rows_n, cols_n = secondary.shape
    width = primary.shape[2]
    dates_n = lax.axis_size("date")
    tiles_n = lax.axis_size("tile")
    bf16, f32 = jnp.bfloat16, jnp.float32
    shape = jax.ShapeDtypeStruct
    looks_n = cols_n // LR
    middle_n = rows_n - 2 * LAG
    edges = jnp.concatenate([primary[:, :LAG], primary[:, rows_n - LAG :]], axis=1)
    edges_two, edges_three, edges_one = [swap(edges, "date", step) for step in (2, 3, 1)]
    halo = shape((2, HALO, cols_n), bf16)
    down, up = call(cut_halo_kernel, (halo, halo), [], (0, 0), secondary)
    low = ring(down, "tile", 1)
    high = ring(up, "tile", -1)
    az_band, rg_band = call(
        bands_kernel,
        (shape((BAND, BAND + 2 * HALO), bf16), shape((3, LANE, LANE), bf16)),
        [],
        (0, 0),
        az_off, rg_off, az_frac, rg_frac,
    )
    middle = call(
        cut_middle_kernel,
        shape((2, middle_n + 16, width), bf16),
        [],
        (0, 0),
        primary, edges_two,edges_three,az_band,
    )
    weight = jnp.broadcast_to(margin_mask[rows_n - LAG :].astype(f32)[:, None], (LAG, LANE))
    res = call(
        resample_kernel,
        shape((dates_n, 2, rows_n, width), bf16),
        [pltpu.VMEM((2, rows_n, cols_n), bf16)],
        (0, 0),
        secondary, low, high, az_band, rg_band,
    )
    two, one = [swap(middle, "date", step) for step in (2, 1)]
    margin = shape((2, LAG, cols_n), bf16)
    first, last, looks = call(
        margin_kernel,
        (margin, margin, shape((2, 2 * LAG // LA, looks_n), f32)),
        [pltpu.VMEM((2, 2 * LAG, looks_n), f32)],
        (0, 0),
        primary, edges_one, edges_two, edges_three, res,
    )
    later = ring(first, "tile", -1)
    stats = call(
        stats_kernel,
        shape((8, LANE), f32),
        [],
        (0, 0),
        last, later, weight,
    )
    before = call(
        middle_kernel,
        shape((2, middle_n, looks_n), f32),
        [],
        (2 * 2 * middle_n * cols_n * looks_n, 8 * rows_n * cols_n),
        primary, one, two, res,
    )
    other = swap(stats, "tile", 1)
    block = shape((2, middle_n, width), bf16)
    relayed = call(relay_kernel, block, [], (0, 0), two, other,one)
    three = swap(relayed, "date", 1)
    stride = 2
    while stride < tiles_n:
        stats = stats + other
        other = swap(stats, "tile", stride)
        stride *= 2
    looks = call(
        last_kernel,
        shape((2, rows_n // LA, looks_n), f32),
        [pltpu.VMEM((2, middle_n, looks_n), f32)],
        (2 * middle_n * cols_n * looks_n, 4 * rows_n * cols_n),
        three, res, before, looks,
    )
    return call(
        scale_kernel,
        shape((1, 2, rows_n // LA, looks_n), f32),
        [],
        (8 * rows_n * looks_n, 8 * rows_n * looks_n),
        looks, stats, other,
    )


def padded(block, sides, width):
    for axis, dim in sides:
        low = passed_along(
            lax.slice_in_dim(block, block.shape[dim] - width, None, axis=dim), axis, 1
        )
        high = passed_along(lax.slice_in_dim(block, 0, width, axis=dim), axis, -1)
        block = jnp.concatenate([low, block, high], axis=dim)
    return block


def band_taps(offset, frac):
    inside = (offset >= -3) & (offset <= 4)
    return jnp.where(inside, window(offset.astype(jnp.float32) - frac), 0.0).astype(jnp.bfloat16)


def multilook(values):
    depth, rows_n, cols_n = values.shape
    return values.reshape(depth, rows_n // LA, LA, cols_n // LR, LR).mean(axis=(2, 4))


def plain(secondary, primary, margin_mask, az_off, rg_off, az_frac, rg_frac):
    rim_rows = KA + 4
    block_cols = 256
    image = secondary[0]
    rows_n = image.shape[1]
    cols_n = image.shape[2]
    extended = padded(image, (("tile", 1),), rim_rows)
    row_out = lax.broadcasted_iota(jnp.int32, (rows_n, rows_n + 2 * rim_rows), 0)
    row_in = lax.broadcasted_iota(jnp.int32, (rows_n, rows_n + 2 * rim_rows), 1)
    azim_taps = band_taps(row_in - row_out - az_off[0, 0] - rim_rows, az_frac[0, 0])
    azim = jnp.einsum(
        "im,kmc->kic", azim_taps, extended, preferred_element_type=jnp.float32
    ).astype(jnp.bfloat16)
    blocks_n = cols_n // block_cols
    col_pad = jnp.pad(azim, ((0, 0), (0, 0), (block_cols // 2, block_cols // 2)))
    pieces = col_pad.reshape(2, rows_n, blocks_n + 1, block_cols)
    inputs = jnp.concatenate([pieces[:, :, :-1], pieces[:, :, 1:]], axis=3)
    col_in = lax.broadcasted_iota(jnp.int32, (2 * block_cols, block_cols), 0)
    col_out = lax.broadcasted_iota(jnp.int32, (2 * block_cols, block_cols), 1)
    range_taps = band_taps(col_in - block_cols // 2 - col_out - rg_off[0, 0], rg_frac[0, 0])
    resampled = jnp.einsum("kibm,mn->kibn", inputs, range_taps, preferred_element_type=jnp.float32)
    resampled = resampled.reshape(2, rows_n, cols_n).astype(jnp.bfloat16)
    prim = lax.all_gather(primary, "date", axis=2, tiled=True)[None]
    sec_f = resampled[None].astype(jnp.float32)
    prim_f = prim.astype(jnp.float32)
    ifg_re = prim_f[:, 0] * sec_f[:, 0] + prim_f[:, 1] * sec_f[:, 1]
    ifg_im = prim_f[:, 1] * sec_f[:, 0] - prim_f[:, 0] * sec_f[:, 1]
    interf = jnp.stack((ifg_re, ifg_im), axis=1)
    upcoming = passed_along(interf[:, :, :LAG, :], "tile", -1)
    later = jnp.concatenate([interf[:, :, LAG:, :], upcoming], axis=2)
    l_re = later[:, 0]
    l_im = later[:, 1]
    weight = margin_mask.astype(jnp.float32)[None, :, None]
    e_re = jnp.sum(weight * (ifg_re * l_re + ifg_im * l_im), axis=(1, 2))
    e_im = jnp.sum(weight * (ifg_im * l_re - ifg_re * l_im), axis=(1, 2))
    power = jnp.sum(
        weight * 0.5 * (ifg_re * ifg_re + ifg_im * ifg_im + l_re * l_re + l_im * l_im), axis=(1, 2)
    )
    count = jnp.zeros_like(e_re) + jnp.sum(margin_mask.astype(jnp.float32)) * interf.shape[3]
    stats = jnp.stack((e_re, e_im, power, count), axis=1)
    totals = lax.psum(stats, "tile")
    magnitude = jnp.sqrt(totals[:, 0] * totals[:, 0] + totals[:, 1] * totals[:, 1])
    floor_val = (totals[:, 2] + 1e-06) / jnp.sqrt(jnp.maximum(totals[:, 3], 1.0))
    denom = jnp.maximum(magnitude, floor_val)
    u_re = (totals[:, 0] / denom)[:, None, None]
    u_im = (totals[:, 1] / denom)[:, None, None]
    c_re = multilook(ifg_re * u_re + ifg_im * u_im)
    c_im = multilook(ifg_im * u_re - ifg_re * u_im)
    return jnp.stack((c_re, c_im), axis=1)


def shards(secondary, primary, *rest):
    rows_n, width = primary.shape[1:]
    fits = rows_n % BAND == 0 and rows_n > 2 * LAG + BAND and width % LANE == 0
    tiles_n = lax.axis_size("tile")
    fits = fits and lax.axis_size("date") == 4 and tiles_n & (tiles_n - 1) == 0
    return (fused if fits else plain)(secondary, primary, *rest)


def solution(mesh):
    return jax.shard_map(
        shards,
        mesh=mesh,
        in_specs=(
            P("date", None, "tile", None),
            P(None, "tile", "date"),
            P("tile"),
            P("date", "tile"),
            P("date", "tile"),
            P("date", "tile"),
            P("date", "tile"),
        ),
        out_specs=P("date", None, "tile", None),
        check_vma=False,
    )
```

```python
import functools

import jax
import jax.numpy as jnp
from jax import lax
from jax.experimental import pallas as pl
from jax.experimental.pallas import tpu as pltpu
from jax.sharding import PartitionSpec as P

KA = 16
LAG = 64
LA = 2
LR = 8
LANE = 128
BAND = 128
HALO = 32
VMEM_LIMIT = 40 * 1024 * 1024


def passed_along(value, axis, steps):
    count = lax.axis_size(axis)
    initial, last = (max(0, -steps), min(count, count - steps))
    return lax.ppermute(value, axis, [(source, source + steps) for source in range(initial, last)])


def window(dist):
    return jnp.sinc(dist) * (0.5 + 0.5 * jnp.cos(jnp.pi * dist / 4.0))


def tap_rows(frac):
    dist = lax.broadcasted_iota(jnp.int32, (8, LANE), 0).astype(jnp.float32) - 3.0 - frac
    angle = jnp.pi * dist
    sinc = jnp.where(dist == 0.0, 1.0, jnp.sin(angle) / jnp.where(dist == 0.0, 1.0, angle))
    taps = sinc * (0.5 + 0.5 * jnp.cos(jnp.pi * dist / 4.0))
    return taps.astype(jnp.bfloat16).astype(jnp.float32)


def band(shape, distance, taps):
    total = jnp.zeros(shape, jnp.float32)
    for j in range(8):
        total = jnp.where(distance == j - 3, taps[j : j + 1, :1], total)
    return total.astype(jnp.bfloat16)


def cut_halo_kernel(sec_ref, down_ref, up_ref):
    rows_n = sec_ref.shape[2]
    down_ref[...] = sec_ref[0, :, rows_n - HALO :]
    up_ref[...] = sec_ref[0, :, :HALO]


def cut_middle_kernel(prim_ref, *refs):
    cut_ref = refs[-1]
    cut_ref[...] = prim_ref[:, LAG : LAG + cut_ref.shape[1]]


def relay_kernel(block_ref, *refs):
    out_ref = refs[-1]
    out_ref[...] = block_ref[:, : out_ref.shape[1]]


def bands_kernel(ao_ref, ro_ref, af_ref, rf_ref, az_ref, rg_ref):
    shape = az_ref.shape
    offset = lax.broadcasted_iota(jnp.int32, shape, 1) - lax.broadcasted_iota(jnp.int32, shape, 0)
    az_ref[...] = band(shape, offset - HALO - ao_ref[...], tap_rows(af_ref[...]))
    square = rg_ref.shape[1:]
    offset = lax.broadcasted_iota(jnp.int32, square, 0) - lax.broadcasted_iota(jnp.int32, square, 1)
    taps = tap_rows(rf_ref[...])
    for at, shift in enumerate((-LANE, 0, LANE)):
        rg_ref[at] = band(square, offset + shift - ro_ref[...], taps)


def resample_kernel(sec_ref, low_ref, high_ref, az_ref, rg_ref, out_ref, azim_ref):
    rows_n, cols_n = sec_ref.shape[2:]
    az_band = az_ref[...]
    here, tiles_n = lax.axis_index("tile"), lax.axis_size("tile")
    none = jnp.zeros(low_ref.shape[1:], jnp.bfloat16)
    for part in range(2):
        for start in range(0, rows_n, BAND):
            pieces = []
            if start == 0:
                pieces.append(jnp.where(here == 0, none, low_ref[part]))
            pieces.append(sec_ref[0, part, max(0, start - HALO) : min(rows_n, start + BAND + HALO)])
            if start + BAND == rows_n:
                pieces.append(jnp.where(here == tiles_n - 1, none, high_ref[part]))
            rows = jnp.concatenate(pieces, axis=0) if len(pieces) > 1 else pieces[0]
            azim_ref[part, start : start + BAND] = jnp.dot(
                az_band, rows, preferred_element_type=jnp.float32
            ).astype(jnp.bfloat16)

    before, same, after = [rg_ref[at] for at in range(3)]
    none = jnp.zeros((LANE, LANE), jnp.bfloat16)
    blocks_n, _, _, width = out_ref.shape
    lanes_n = width // LANE
    columns = []
    for lane in range(lanes_n):
        column = [none] * (lanes_n + 2)
        column[lane], column[lane + 1], column[lane + 2] = before, same, after
        columns.append(jnp.concatenate(column, axis=0))
    rg_band = jnp.concatenate(columns, axis=1)
    for block in range(blocks_n):
        first = block * width - LANE
        last = (block + 1) * width + LANE
        taken = slice(max(first, 0), min(last, cols_n))
        used = rg_band[taken.start - first : taken.stop - first]
        for part in range(2):
            out_ref[block, part] = jnp.dot(
                azim_ref[part, :, taken], used, preferred_element_type=jnp.float32
            ).astype(jnp.bfloat16)


def interfere(prim_re, prim_im, sec_re, sec_im):
    p_re, p_im = prim_re.astype(jnp.float32), prim_im.astype(jnp.float32)
    s_re, s_im = sec_re.astype(jnp.float32), sec_im.astype(jnp.float32)
    return p_re * s_re + p_im * s_im, p_im * s_re - p_re * s_im


def look_columns(width, block, looks_n):
    shape = (width, looks_n)
    col = lax.broadcasted_iota(jnp.int32, shape, 0) + block * width
    look = lax.broadcasted_iota(jnp.int32, shape, 1) * LR
    return jnp.where((col >= look) & (col < look + LR), 1.0, 0.0).astype(jnp.bfloat16)


def look_rows(sums_ref, part, start, rows_n):
    count = rows_n // LA
    total = sums_ref[part, pl.ds(start, count, LA)]
    for row in range(1, LA):
        total = total + sums_ref[part, pl.ds(start + row, count, LA)]
    return total


def margin_kernel(
    own_ref, one_ref, two_ref, three_ref, res_ref, first_ref, last_ref, looks_ref, sums_ref
):
    here = lax.axis_index("date")
    _, _, rows_n, width = res_ref.shape
    whole, edges = (0, rows_n - LAG), (0, LAG)
    looks_n = looks_ref.shape[2]
    totals = [None, None]
    for step, (prim_ref, starts) in enumerate(
        ((own_ref, whole), (one_ref, edges), (two_ref, edges), (three_ref, edges))
    ):
        block = jnp.bitwise_xor(here, step)
        select = look_columns(width, block, looks_n)
        columns = pl.ds(pl.multiple_of(block * width, width), width)
        halves = []
        for held, start, target in zip(starts, whole, (first_ref, last_ref)):
            pair = interfere(
                prim_ref[0, held : held + LAG],
                prim_ref[1, held : held + LAG],
                res_ref[block, 0, start : start + LAG],
                res_ref[block, 1, start : start + LAG],
            )
            pair = [value.astype(jnp.bfloat16) for value in pair]
            for part in range(2):
                target[part, :, columns] = pair[part]
            halves.append(pair)
        for part in range(2):
            both = jnp.concatenate([halves[0][part], halves[1][part]], axis=0)
            summed = jnp.dot(both, select, preferred_element_type=jnp.float32)
            totals[part] = summed if step == 0 else totals[part] + summed
    for part in range(2):
        sums_ref[part] = totals[part]
        looks_ref[part] = look_rows(sums_ref, part, 0, 2 * LAG)


def stats_kernel(last_ref, later_ref, weight_ref, stats_ref):
    cols_n = last_ref.shape[2]
    weight = weight_ref[...]
    i_re, i_im = last_ref[0].astype(jnp.float32), last_ref[1].astype(jnp.float32)
    inside = jnp.where(lax.axis_index("tile") == lax.axis_size("tile") - 1, 0.0, 1.0)
    l_re, l_im = [later_ref[part].astype(jnp.float32) * inside for part in range(2)]
    values = (
        i_re * l_re + i_im * l_im,
        i_im * l_re - i_re * l_im,
        0.5 * (i_re * i_re + i_im * i_im + l_re * l_re + l_im * l_im),
    )
    rows = []
    for value in values:
        folded = value[:, :LANE]
        for start in range(LANE, cols_n, LANE):
            folded = folded + value[:, start : start + LANE]
        rows.append(jnp.sum(folded * weight, axis=0, keepdims=True))
    rows.append(jnp.sum(weight, axis=0, keepdims=True) * (cols_n // LANE))
    rows.append(jnp.zeros((4, LANE), jnp.float32))
    stats_ref[...] = jnp.concatenate(rows, axis=0)


def look_sums(pieces, res_ref, looks_n):
    here = lax.axis_index("date")
    _, _, rows_n, width = res_ref.shape
    middle_n = rows_n - 2 * LAG
    totals = [None, None]
    for at, (step, prim_ref) in enumerate(pieces):
        block = jnp.bitwise_xor(here, step)
        first = LAG if prim_ref.shape[1] == rows_n else 0
        select = look_columns(width, block, looks_n)
        pair = interfere(
            prim_ref[0, first : first + middle_n],
            prim_ref[1, first : first + middle_n],
            res_ref[block, 0, LAG : rows_n - LAG],
            res_ref[block, 1, LAG : rows_n - LAG],
        )
        for part in range(2):
            summed = jnp.dot(
                pair[part].astype(jnp.bfloat16), select, preferred_element_type=jnp.float32
            )
            totals[part] = summed if at == 0 else totals[part] + summed
    return totals


def middle_kernel(own_ref, one_ref, two_ref, res_ref, out_ref):
    pieces = ((0, own_ref), (1, one_ref), (2, two_ref))
    for part, total in enumerate(look_sums(pieces, res_ref, out_ref.shape[2])):
        out_ref[part] = total


def last_kernel(three_ref, res_ref, before_ref, looks_ref, out_ref, sums_ref):
    middle_n = before_ref.shape[1]
    edge = LAG // LA
    totals = look_sums(((3, three_ref),), res_ref, out_ref.shape[2])
    for part, total in enumerate(totals):
        sums_ref[part] = total + before_ref[part]
        out_ref[part, :edge] = looks_ref[part, :edge]
        out_ref[part, edge : edge + middle_n // LA] = look_rows(sums_ref, part, 0, middle_n)
        out_ref[part, edge + middle_n // LA :] = looks_ref[part, edge:]


def scale_kernel(looks_ref, mine_ref, other_ref, out_ref):
    stats = jnp.sum(mine_ref[...] + other_ref[...], axis=1, keepdims=True)
    e_re, e_im, power, count = [stats[row : row + 1] for row in range(4)]
    magnitude = jnp.sqrt(e_re * e_re + e_im * e_im)
    floor_val = (power + 1e-06) / jnp.sqrt(jnp.maximum(count, 1.0))
    denom = jnp.maximum(magnitude, floor_val)
    u_re = e_re / denom * (1.0 / (LA * LR))
    u_im = e_im / denom * (1.0 / (LA * LR))
    out_ref[0, 0] = looks_ref[0] * u_re + looks_ref[1] * u_im
    out_ref[0, 1] = looks_ref[1] * u_re - looks_ref[0] * u_im


def call(kernel, outs, scratch, cost, *args):
    vmem = pl.BlockSpec(memory_space=pltpu.VMEM)
    return pl.pallas_call(
        kernel,
        out_shape=outs,
        in_specs=[vmem] * len(args),
        out_specs=jax.tree.map(lambda _: vmem, outs),
        scratch_shapes=scratch,
        compiler_params=pltpu.CompilerParams(vmem_limit_bytes=VMEM_LIMIT),
        cost_estimate=pl.CostEstimate(flops=cost[0], bytes_accessed=cost[1], transcendentals=0),
    )(*args)


def ring(value, axis, step):
    count = lax.axis_size(axis)
    return lax.ppermute(value, axis, [(at, (at + step) % count) for at in range(count)])


def swap(value, axis, step):
    return lax.ppermute(value, axis, [(at, at ^ step) for at in range(lax.axis_size(axis))])


def fused(secondary, primary, margin_mask, az_off, rg_off, az_frac, rg_frac):
    _, _, rows_n, cols_n = secondary.shape
    width = primary.shape[2]
    dates_n = lax.axis_size("date")
    tiles_n = lax.axis_size("tile")
    bf16, f32 = jnp.bfloat16, jnp.float32
    shape = jax.ShapeDtypeStruct
    looks_n = cols_n // LR
    middle_n = rows_n - 2 * LAG
    edges = jnp.concatenate([primary[:, :LAG], primary[:, rows_n - LAG :]], axis=1)
    edges_two = swap(edges, "date", 2)
    edges_one = swap(edges, "date", 1)
    halo = shape((2, HALO, cols_n), bf16)
    down, up = call(cut_halo_kernel, (halo, halo), [], (0, 0), secondary)
    low = ring(down, "tile", 1)
    high = ring(up, "tile", -1)
    az_band, rg_band = call(
        bands_kernel,
        (shape((BAND, BAND + 2 * HALO), bf16), shape((3, LANE, LANE), bf16)),
        [],
        (0, 0),
        az_off, rg_off, az_frac, rg_frac,
    )
    edges_three = swap(edges_two, "date", 1)
    middle = call(
        cut_middle_kernel,
        shape((2, middle_n + 16, width), bf16),
        [],
        (0, 0),
        primary, edges_two,
    )
    weight = jnp.broadcast_to(margin_mask[rows_n - LAG :].astype(f32)[:, None], (LAG, LANE))
    res = call(
        resample_kernel,
        shape((dates_n, 2, rows_n, width), bf16),
        [pltpu.VMEM((2, rows_n, cols_n), bf16)],
        (0, 0),
        secondary, low, high, az_band, rg_band,
    )
    two, one = [swap(middle, "date", step) for step in (2, 1)]
    margin = shape((2, LAG, cols_n), bf16)
    first, last, looks = call(
        margin_kernel,
        (margin, margin, shape((2, 2 * LAG // LA, looks_n), f32)),
        [pltpu.VMEM((2, 2 * LAG, looks_n), f32)],
        (0, 0),
        primary, edges_one, edges_two, edges_three, res,
    )
    later = ring(first, "tile", -1)
    stats = call(
        stats_kernel,
        shape((8, LANE), f32),
        [],
        (0, 0),
        last, later, weight,
    )
    before = call(
        middle_kernel,
        shape((2, middle_n, looks_n), f32),
        [],
        (2 * 2 * middle_n * cols_n * looks_n, 8 * rows_n * cols_n),
        primary, one, two, res,
    )
    other = swap(stats, "tile", 1)
    block = shape((2, middle_n, width), bf16)
    relayed = call(relay_kernel, block, [], (0, 0), two, other)
    three = swap(relayed, "date", 1)
    stride = 2
    while stride < tiles_n:
        stats = stats + other
        other = swap(stats, "tile", stride)
        stride *= 2
    looks = call(
        last_kernel,
        shape((2, rows_n // LA, looks_n), f32),
        [pltpu.VMEM((2, middle_n, looks_n), f32)],
        (2 * middle_n * cols_n * looks_n, 4 * rows_n * cols_n),
        three, res, before, looks,
    )
    return call(
        scale_kernel,
        shape((1, 2, rows_n // LA, looks_n), f32),
        [],
        (8 * rows_n * looks_n, 8 * rows_n * looks_n),
        looks, stats, other,
    )


def padded(block, sides, width):
    for axis, dim in sides:
        low = passed_along(
            lax.slice_in_dim(block, block.shape[dim] - width, None, axis=dim), axis, 1
        )
        high = passed_along(lax.slice_in_dim(block, 0, width, axis=dim), axis, -1)
        block = jnp.concatenate([low, block, high], axis=dim)
    return block


def band_taps(offset, frac):
    inside = (offset >= -3) & (offset <= 4)
    return jnp.where(inside, window(offset.astype(jnp.float32) - frac), 0.0).astype(jnp.bfloat16)


def multilook(values):
    depth, rows_n, cols_n = values.shape
    return values.reshape(depth, rows_n // LA, LA, cols_n // LR, LR).mean(axis=(2, 4))


def plain(secondary, primary, margin_mask, az_off, rg_off, az_frac, rg_frac):
    rim_rows = KA + 4
    block_cols = 256
    image = secondary[0]
    rows_n = image.shape[1]
    cols_n = image.shape[2]
    extended = padded(image, (("tile", 1),), rim_rows)
    row_out = lax.broadcasted_iota(jnp.int32, (rows_n, rows_n + 2 * rim_rows), 0)
    row_in = lax.broadcasted_iota(jnp.int32, (rows_n, rows_n + 2 * rim_rows), 1)
    azim_taps = band_taps(row_in - row_out - az_off[0, 0] - rim_rows, az_frac[0, 0])
    azim = jnp.einsum(
        "im,kmc->kic", azim_taps, extended, preferred_element_type=jnp.float32
    ).astype(jnp.bfloat16)
    blocks_n = cols_n // block_cols
    col_pad = jnp.pad(azim, ((0, 0), (0, 0), (block_cols // 2, block_cols // 2)))
    pieces = col_pad.reshape(2, rows_n, blocks_n + 1, block_cols)
    inputs = jnp.concatenate([pieces[:, :, :-1], pieces[:, :, 1:]], axis=3)
    col_in = lax.broadcasted_iota(jnp.int32, (2 * block_cols, block_cols), 0)
    col_out = lax.broadcasted_iota(jnp.int32, (2 * block_cols, block_cols), 1)
    range_taps = band_taps(col_in - block_cols // 2 - col_out - rg_off[0, 0], rg_frac[0, 0])
    resampled = jnp.einsum("kibm,mn->kibn", inputs, range_taps, preferred_element_type=jnp.float32)
    resampled = resampled.reshape(2, rows_n, cols_n).astype(jnp.bfloat16)
    prim = lax.all_gather(primary, "date", axis=2, tiled=True)[None]
    sec_f = resampled[None].astype(jnp.float32)
    prim_f = prim.astype(jnp.float32)
    ifg_re = prim_f[:, 0] * sec_f[:, 0] + prim_f[:, 1] * sec_f[:, 1]
    ifg_im = prim_f[:, 1] * sec_f[:, 0] - prim_f[:, 0] * sec_f[:, 1]
    interf = jnp.stack((ifg_re, ifg_im), axis=1)
    upcoming = passed_along(interf[:, :, :LAG, :], "tile", -1)
    later = jnp.concatenate([interf[:, :, LAG:, :], upcoming], axis=2)
    l_re = later[:, 0]
    l_im = later[:, 1]
    weight = margin_mask.astype(jnp.float32)[None, :, None]
    e_re = jnp.sum(weight * (ifg_re * l_re + ifg_im * l_im), axis=(1, 2))
    e_im = jnp.sum(weight * (ifg_im * l_re - ifg_re * l_im), axis=(1, 2))
    power = jnp.sum(
        weight * 0.5 * (ifg_re * ifg_re + ifg_im * ifg_im + l_re * l_re + l_im * l_im), axis=(1, 2)
    )
    count = jnp.zeros_like(e_re) + jnp.sum(margin_mask.astype(jnp.float32)) * interf.shape[3]
    stats = jnp.stack((e_re, e_im, power, count), axis=1)
    totals = lax.psum(stats, "tile")
    magnitude = jnp.sqrt(totals[:, 0] * totals[:, 0] + totals[:, 1] * totals[:, 1])
    floor_val = (totals[:, 2] + 1e-06) / jnp.sqrt(jnp.maximum(totals[:, 3], 1.0))
    denom = jnp.maximum(magnitude, floor_val)
    u_re = (totals[:, 0] / denom)[:, None, None]
    u_im = (totals[:, 1] / denom)[:, None, None]
    c_re = multilook(ifg_re * u_re + ifg_im * u_im)
    c_im = multilook(ifg_im * u_re - ifg_re * u_im)
    return jnp.stack((c_re, c_im), axis=1)


def shards(secondary, primary, *rest):
    rows_n, width = primary.shape[1:]
    fits = rows_n % BAND == 0 and rows_n > 2 * LAG + BAND and width % LANE == 0
    tiles_n = lax.axis_size("tile")
    fits = fits and lax.axis_size("date") == 4 and tiles_n & (tiles_n - 1) == 0
    return (fused if fits else plain)(secondary, primary, *rest)


def solution(mesh):
    return jax.shard_map(
        shards,
        mesh=mesh,
        in_specs=(
            P("date", None, "tile", None),
            P(None, "tile", "date"),
            P("tile"),
            P("date", "tile"),
            P("date", "tile"),
            P("date", "tile"),
            P("date", "tile"),
        ),
        out_specs=P("date", None, "tile", None),
        check_vma=False,
    )
```

```python
import functools

import jax
import jax.numpy as jnp
from jax import lax
from jax.experimental import pallas as pl
from jax.experimental.pallas import tpu as pltpu
from jax.sharding import PartitionSpec as P

KA = 16
LAG = 64
LA = 2
LR = 8
LANE = 128
BAND = 128
HALO = 32
VMEM_LIMIT = 40 * 1024 * 1024


def passed_along(value, axis, steps):
    count = lax.axis_size(axis)
    initial, last = (max(0, -steps), min(count, count - steps))
    return lax.ppermute(value, axis, [(source, source + steps) for source in range(initial, last)])


def window(dist):
    return jnp.sinc(dist) * (0.5 + 0.5 * jnp.cos(jnp.pi * dist / 4.0))


def tap_rows(frac):
    dist = lax.broadcasted_iota(jnp.int32, (8, LANE), 0).astype(jnp.float32) - 3.0 - frac
    angle = jnp.pi * dist
    sinc = jnp.where(dist == 0.0, 1.0, jnp.sin(angle) / jnp.where(dist == 0.0, 1.0, angle))
    taps = sinc * (0.5 + 0.5 * jnp.cos(jnp.pi * dist / 4.0))
    return taps.astype(jnp.bfloat16).astype(jnp.float32)


def band(shape, distance, taps):
    total = jnp.zeros(shape, jnp.float32)
    for j in range(8):
        total = jnp.where(distance == j - 3, taps[j : j + 1, :1], total)
    return total.astype(jnp.bfloat16)


def cut_halo_kernel(sec_ref, down_ref, up_ref):
    rows_n = sec_ref.shape[2]
    down_ref[...] = sec_ref[0, :, rows_n - HALO :]
    up_ref[...] = sec_ref[0, :, :HALO]


def cut_middle_kernel(prim_ref, *refs):
    cut_ref = refs[-1]
    cut_ref[...] = prim_ref[:, LAG : LAG + cut_ref.shape[1]]


def relay_kernel(block_ref, *refs):
    out_ref = refs[-1]
    out_ref[...] = block_ref[:, : out_ref.shape[1]]


def bands_kernel(ao_ref, ro_ref, af_ref, rf_ref, az_ref, rg_ref):
    shape = az_ref.shape
    offset = lax.broadcasted_iota(jnp.int32, shape, 1) - lax.broadcasted_iota(jnp.int32, shape, 0)
    az_ref[...] = band(shape, offset - HALO - ao_ref[...], tap_rows(af_ref[...]))
    square = rg_ref.shape[1:]
    offset = lax.broadcasted_iota(jnp.int32, square, 0) - lax.broadcasted_iota(jnp.int32, square, 1)
    taps = tap_rows(rf_ref[...])
    for at, shift in enumerate((-LANE, 0, LANE)):
        rg_ref[at] = band(square, offset + shift - ro_ref[...], taps)


def resample_kernel(sec_ref, low_ref, high_ref, az_ref, rg_ref, out_ref, azim_ref):
    rows_n, cols_n = sec_ref.shape[2:]
    az_band = az_ref[...]
    here, tiles_n = lax.axis_index("tile"), lax.axis_size("tile")
    none = jnp.zeros(low_ref.shape[1:], jnp.bfloat16)
    for part in range(2):
        for start in range(0, rows_n, BAND):
            pieces = []
            if start == 0:
                pieces.append(jnp.where(here == 0, none, low_ref[part]))
            pieces.append(sec_ref[0, part, max(0, start - HALO) : min(rows_n, start + BAND + HALO)])
            if start + BAND == rows_n:
                pieces.append(jnp.where(here == tiles_n - 1, none, high_ref[part]))
            rows = jnp.concatenate(pieces, axis=0) if len(pieces) > 1 else pieces[0]
            azim_ref[part, start : start + BAND] = jnp.dot(
                az_band, rows, preferred_element_type=jnp.float32
            ).astype(jnp.bfloat16)

    before, same, after = [rg_ref[at] for at in range(3)]
    none = jnp.zeros((LANE, LANE), jnp.bfloat16)
    blocks_n, _, _, width = out_ref.shape
    lanes_n = width // LANE
    columns = []
    for lane in range(lanes_n):
        column = [none] * (lanes_n + 2)
        column[lane], column[lane + 1], column[lane + 2] = before, same, after
        columns.append(jnp.concatenate(column, axis=0))
    rg_band = jnp.concatenate(columns, axis=1)
    for block in range(blocks_n):
        first = block * width - LANE
        last = (block + 1) * width + LANE
        taken = slice(max(first, 0), min(last, cols_n))
        used = rg_band[taken.start - first : taken.stop - first]
        for part in range(2):
            out_ref[block, part] = jnp.dot(
                azim_ref[part, :, taken], used, preferred_element_type=jnp.float32
            ).astype(jnp.bfloat16)


def interfere(prim_re, prim_im, sec_re, sec_im):
    p_re, p_im = prim_re.astype(jnp.float32), prim_im.astype(jnp.float32)
    s_re, s_im = sec_re.astype(jnp.float32), sec_im.astype(jnp.float32)
    return p_re * s_re + p_im * s_im, p_im * s_re - p_re * s_im


def look_columns(width, block, looks_n):
    shape = (width, looks_n)
    col = lax.broadcasted_iota(jnp.int32, shape, 0) + block * width
    look = lax.broadcasted_iota(jnp.int32, shape, 1) * LR
    return jnp.where((col >= look) & (col < look + LR), 1.0, 0.0).astype(jnp.bfloat16)


def look_rows(sums_ref, part, start, rows_n):
    count = rows_n // LA
    total = sums_ref[part, pl.ds(start, count, LA)]
    for row in range(1, LA):
        total = total + sums_ref[part, pl.ds(start + row, count, LA)]
    return total


def margin_kernel(
    own_ref, one_ref, two_ref, three_ref, res_ref, first_ref, last_ref, looks_ref, sums_ref
):
    here = lax.axis_index("date")
    _, _, rows_n, width = res_ref.shape
    whole, edges = (0, rows_n - LAG), (0, LAG)
    looks_n = looks_ref.shape[2]
    totals = [None, None]
    for step, (prim_ref, starts) in enumerate(
        ((own_ref, whole), (one_ref, edges), (two_ref, edges), (three_ref, edges))
    ):
        block = jnp.bitwise_xor(here, step)
        select = look_columns(width, block, looks_n)
        columns = pl.ds(pl.multiple_of(block * width, width), width)
        halves = []
        for held, start, target in zip(starts, whole, (first_ref, last_ref)):
            pair = interfere(
                prim_ref[0, held : held + LAG],
                prim_ref[1, held : held + LAG],
                res_ref[block, 0, start : start + LAG],
                res_ref[block, 1, start : start + LAG],
            )
            pair = [value.astype(jnp.bfloat16) for value in pair]
            for part in range(2):
                target[part, :, columns] = pair[part]
            halves.append(pair)
        for part in range(2):
            both = jnp.concatenate([halves[0][part], halves[1][part]], axis=0)
            summed = jnp.dot(both, select, preferred_element_type=jnp.float32)
            totals[part] = summed if step == 0 else totals[part] + summed
    for part in range(2):
        sums_ref[part] = totals[part]
        looks_ref[part] = look_rows(sums_ref, part, 0, 2 * LAG)


def stats_kernel(last_ref, later_ref, weight_ref, stats_ref):
    cols_n = last_ref.shape[2]
    weight = weight_ref[...]
    i_re, i_im = last_ref[0].astype(jnp.float32), last_ref[1].astype(jnp.float32)
    inside = jnp.where(lax.axis_index("tile") == lax.axis_size("tile") - 1, 0.0, 1.0)
    l_re, l_im = [later_ref[part].astype(jnp.float32) * inside for part in range(2)]
    values = (
        i_re * l_re + i_im * l_im,
        i_im * l_re - i_re * l_im,
        0.5 * (i_re * i_re + i_im * i_im + l_re * l_re + l_im * l_im),
    )
    rows = []
    for value in values:
        folded = value[:, :LANE]
        for start in range(LANE, cols_n, LANE):
            folded = folded + value[:, start : start + LANE]
        rows.append(jnp.sum(folded * weight, axis=0, keepdims=True))
    rows.append(jnp.sum(weight, axis=0, keepdims=True) * (cols_n // LANE))
    rows.append(jnp.zeros((4, LANE), jnp.float32))
    stats_ref[...] = jnp.concatenate(rows, axis=0)


def look_sums(pieces, res_ref, looks_n):
    here = lax.axis_index("date")
    _, _, rows_n, width = res_ref.shape
    middle_n = rows_n - 2 * LAG
    totals = [None, None]
    for at, (step, prim_ref) in enumerate(pieces):
        block = jnp.bitwise_xor(here, step)
        first = LAG if prim_ref.shape[1] == rows_n else 0
        select = look_columns(width, block, looks_n)
        pair = interfere(
            prim_ref[0, first : first + middle_n],
            prim_ref[1, first : first + middle_n],
            res_ref[block, 0, LAG : rows_n - LAG],
            res_ref[block, 1, LAG : rows_n - LAG],
        )
        for part in range(2):
            summed = jnp.dot(
                pair[part].astype(jnp.bfloat16), select, preferred_element_type=jnp.float32
            )
            totals[part] = summed if at == 0 else totals[part] + summed
    return totals


def middle_kernel(own_ref, one_ref, two_ref, res_ref, out_ref):
    pieces = ((0, own_ref), (1, one_ref), (2, two_ref))
    for part, total in enumerate(look_sums(pieces, res_ref, out_ref.shape[2])):
        out_ref[part] = total


def last_kernel(three_ref, res_ref, before_ref, looks_ref, out_ref, sums_ref):
    middle_n = before_ref.shape[1]
    edge = LAG // LA
    totals = look_sums(((3, three_ref),), res_ref, out_ref.shape[2])
    for part, total in enumerate(totals):
        sums_ref[part] = total + before_ref[part]
        out_ref[part, :edge] = looks_ref[part, :edge]
        out_ref[part, edge : edge + middle_n // LA] = look_rows(sums_ref, part, 0, middle_n)
        out_ref[part, edge + middle_n // LA :] = looks_ref[part, edge:]


def scale_kernel(looks_ref, mine_ref, other_ref, out_ref):
    stats = jnp.sum(mine_ref[...] + other_ref[...], axis=1, keepdims=True)
    e_re, e_im, power, count = [stats[row : row + 1] for row in range(4)]
    magnitude = jnp.sqrt(e_re * e_re + e_im * e_im)
    floor_val = (power + 1e-06) / jnp.sqrt(jnp.maximum(count, 1.0))
    denom = jnp.maximum(magnitude, floor_val)
    u_re = e_re / denom * (1.0 / (LA * LR))
    u_im = e_im / denom * (1.0 / (LA * LR))
    out_ref[0, 0] = looks_ref[0] * u_re + looks_ref[1] * u_im
    out_ref[0, 1] = looks_ref[1] * u_re - looks_ref[0] * u_im


def call(kernel, outs, scratch, cost, *args):
    vmem = pl.BlockSpec(memory_space=pltpu.VMEM)
    return pl.pallas_call(
        kernel,
        out_shape=outs,
        in_specs=[vmem] * len(args),
        out_specs=jax.tree.map(lambda _: vmem, outs),
        scratch_shapes=scratch,
        compiler_params=pltpu.CompilerParams(vmem_limit_bytes=VMEM_LIMIT),
        cost_estimate=pl.CostEstimate(flops=cost[0], bytes_accessed=cost[1], transcendentals=0),
    )(*args)


def ring(value, axis, step):
    count = lax.axis_size(axis)
    return lax.ppermute(value, axis, [(at, (at + step) % count) for at in range(count)])


def swap(value, axis, step):
    return lax.ppermute(value, axis, [(at, at ^ step) for at in range(lax.axis_size(axis))])


def fused(secondary, primary, margin_mask, az_off, rg_off, az_frac, rg_frac):
    _, _, rows_n, cols_n = secondary.shape
    width = primary.shape[2]
    dates_n = lax.axis_size("date")
    tiles_n = lax.axis_size("tile")
    bf16, f32 = jnp.bfloat16, jnp.float32
    shape = jax.ShapeDtypeStruct
    looks_n = cols_n // LR
    middle_n = rows_n - 2 * LAG
    edges = jnp.concatenate([primary[:, :LAG], primary[:, rows_n - LAG :]], axis=1)
    edges_two = swap(edges, "date", 2)
    edges_one = swap(edges, "date", 1)
    halo = shape((2, HALO, cols_n), bf16)
    down, up = call(cut_halo_kernel, (halo, halo), [], (0, 0), secondary)
    low = ring(down, "tile", 1)
    high = ring(up, "tile", -1)
    az_band, rg_band = call(
        bands_kernel,
        (shape((BAND, BAND + 2 * HALO), bf16), shape((3, LANE, LANE), bf16)),
        [],
        (0, 0),
        az_off, rg_off, az_frac, rg_frac,
    )
    edges_three = swap(edges_two, "date", 1)
    middle = call(
        cut_middle_kernel,
        shape((2, middle_n + 16, width), bf16),
        [],
        (0, 0),
        primary, edges_two,
    )
    weight = jnp.broadcast_to(margin_mask[rows_n - LAG :].astype(f32)[:, None], (LAG, LANE))
    res = call(
        resample_kernel,
        shape((dates_n, 2, rows_n, width), bf16),
        [pltpu.VMEM((2, rows_n, cols_n), bf16)],
        (0, 0),
        secondary, low, high, az_band, rg_band,
    )
    two, one = [swap(middle, "date", step) for step in (2, 1)]
    margin = shape((2, LAG, cols_n), bf16)
    first, last, looks = call(
        margin_kernel,
        (margin, margin, shape((2, 2 * LAG // LA, looks_n), f32)),
        [pltpu.VMEM((2, 2 * LAG, looks_n), f32)],
        (0, 0),
        primary, edges_one, edges_two, edges_three, res,
    )
    later = ring(first, "tile", -1)
    stats = call(
        stats_kernel,
        shape((8, LANE), f32),
        [],
        (0, 0),
        last, later, weight,
    )
    before = call(
        middle_kernel,
        shape((2, middle_n, looks_n), f32),
        [],
        (2 * 2 * middle_n * cols_n * looks_n, 8 * rows_n * cols_n),
        primary, one, two, res,
    )
    other = swap(stats, "tile", 1)
    block = shape((2, middle_n, width), bf16)
    relayed = call(relay_kernel, block, [], (0, 0), two, other,one)
    three = swap(relayed, "date", 1)
    stride = 2
    while stride < tiles_n:
        stats = stats + other
        other = swap(stats, "tile", stride)
        stride *= 2
    looks = call(
        last_kernel,
        shape((2, rows_n // LA, looks_n), f32),
        [pltpu.VMEM((2, middle_n, looks_n), f32)],
        (2 * middle_n * cols_n * looks_n, 4 * rows_n * cols_n),
        three, res, before, looks,
    )
    return call(
        scale_kernel,
        shape((1, 2, rows_n // LA, looks_n), f32),
        [],
        (8 * rows_n * looks_n, 8 * rows_n * looks_n),
        looks, stats, other,
    )


def padded(block, sides, width):
    for axis, dim in sides:
        low = passed_along(
            lax.slice_in_dim(block, block.shape[dim] - width, None, axis=dim), axis, 1
        )
        high = passed_along(lax.slice_in_dim(block, 0, width, axis=dim), axis, -1)
        block = jnp.concatenate([low, block, high], axis=dim)
    return block


def band_taps(offset, frac):
    inside = (offset >= -3) & (offset <= 4)
    return jnp.where(inside, window(offset.astype(jnp.float32) - frac), 0.0).astype(jnp.bfloat16)


def multilook(values):
    depth, rows_n, cols_n = values.shape
    return values.reshape(depth, rows_n // LA, LA, cols_n // LR, LR).mean(axis=(2, 4))


def plain(secondary, primary, margin_mask, az_off, rg_off, az_frac, rg_frac):
    rim_rows = KA + 4
    block_cols = 256
    image = secondary[0]
    rows_n = image.shape[1]
    cols_n = image.shape[2]
    extended = padded(image, (("tile", 1),), rim_rows)
    row_out = lax.broadcasted_iota(jnp.int32, (rows_n, rows_n + 2 * rim_rows), 0)
    row_in = lax.broadcasted_iota(jnp.int32, (rows_n, rows_n + 2 * rim_rows), 1)
    azim_taps = band_taps(row_in - row_out - az_off[0, 0] - rim_rows, az_frac[0, 0])
    azim = jnp.einsum(
        "im,kmc->kic", azim_taps, extended, preferred_element_type=jnp.float32
    ).astype(jnp.bfloat16)
    blocks_n = cols_n // block_cols
    col_pad = jnp.pad(azim, ((0, 0), (0, 0), (block_cols // 2, block_cols // 2)))
    pieces = col_pad.reshape(2, rows_n, blocks_n + 1, block_cols)
    inputs = jnp.concatenate([pieces[:, :, :-1], pieces[:, :, 1:]], axis=3)
    col_in = lax.broadcasted_iota(jnp.int32, (2 * block_cols, block_cols), 0)
    col_out = lax.broadcasted_iota(jnp.int32, (2 * block_cols, block_cols), 1)
    range_taps = band_taps(col_in - block_cols // 2 - col_out - rg_off[0, 0], rg_frac[0, 0])
    resampled = jnp.einsum("kibm,mn->kibn", inputs, range_taps, preferred_element_type=jnp.float32)
    resampled = resampled.reshape(2, rows_n, cols_n).astype(jnp.bfloat16)
    prim = lax.all_gather(primary, "date", axis=2, tiled=True)[None]
    sec_f = resampled[None].astype(jnp.float32)
    prim_f = prim.astype(jnp.float32)
    ifg_re = prim_f[:, 0] * sec_f[:, 0] + prim_f[:, 1] * sec_f[:, 1]
    ifg_im = prim_f[:, 1] * sec_f[:, 0] - prim_f[:, 0] * sec_f[:, 1]
    interf = jnp.stack((ifg_re, ifg_im), axis=1)
    upcoming = passed_along(interf[:, :, :LAG, :], "tile", -1)
    later = jnp.concatenate([interf[:, :, LAG:, :], upcoming], axis=2)
    l_re = later[:, 0]
    l_im = later[:, 1]
    weight = margin_mask.astype(jnp.float32)[None, :, None]
    e_re = jnp.sum(weight * (ifg_re * l_re + ifg_im * l_im), axis=(1, 2))
    e_im = jnp.sum(weight * (ifg_im * l_re - ifg_re * l_im), axis=(1, 2))
    power = jnp.sum(
        weight * 0.5 * (ifg_re * ifg_re + ifg_im * ifg_im + l_re * l_re + l_im * l_im), axis=(1, 2)
    )
    count = jnp.zeros_like(e_re) + jnp.sum(margin_mask.astype(jnp.float32)) * interf.shape[3]
    stats = jnp.stack((e_re, e_im, power, count), axis=1)
    totals = lax.psum(stats, "tile")
    magnitude = jnp.sqrt(totals[:, 0] * totals[:, 0] + totals[:, 1] * totals[:, 1])
    floor_val = (totals[:, 2] + 1e-06) / jnp.sqrt(jnp.maximum(totals[:, 3], 1.0))
    denom = jnp.maximum(magnitude, floor_val)
    u_re = (totals[:, 0] / denom)[:, None, None]
    u_im = (totals[:, 1] / denom)[:, None, None]
    c_re = multilook(ifg_re * u_re + ifg_im * u_im)
    c_im = multilook(ifg_im * u_re - ifg_re * u_im)
    return jnp.stack((c_re, c_im), axis=1)


def shards(secondary, primary, *rest):
    rows_n, width = primary.shape[1:]
    fits = rows_n % BAND == 0 and rows_n > 2 * LAG + BAND and width % LANE == 0
    tiles_n = lax.axis_size("tile")
    fits = fits and lax.axis_size("date") == 4 and tiles_n & (tiles_n - 1) == 0
    return (fused if fits else plain)(secondary, primary, *rest)


def solution(mesh):
    return jax.shard_map(
        shards,
        mesh=mesh,
        in_specs=(
            P("date", None, "tile", None),
            P(None, "tile", "date"),
            P("tile"),
            P("date", "tile"),
            P("date", "tile"),
            P("date", "tile"),
            P("date", "tile"),
        ),
        out_specs=P("date", None, "tile", None),
        check_vma=False,
    )
```

```python
import functools

import jax
import jax.numpy as jnp
from jax import lax
from jax.experimental import pallas as pl
from jax.experimental.pallas import tpu as pltpu
from jax.sharding import PartitionSpec as P

KA = 16
LAG = 64
LA = 2
LR = 8
LANE = 128
BAND = 128
HALO = 32
HOP_ROUND = 4
VMEM_LIMIT = 40 * 1024 * 1024


def passed_along(value, axis, steps):
    count = lax.axis_size(axis)
    initial, last = (max(0, -steps), min(count, count - steps))
    return lax.ppermute(value, axis, [(source, source + steps) for source in range(initial, last)])


def window(dist):
    return jnp.sinc(dist) * (0.5 + 0.5 * jnp.cos(jnp.pi * dist / 4.0))


def tap_rows(frac):
    dist = lax.broadcasted_iota(jnp.int32, (8, LANE), 0).astype(jnp.float32) - 3.0 - frac
    angle = jnp.pi * dist
    sinc = jnp.where(dist == 0.0, 1.0, jnp.sin(angle) / jnp.where(dist == 0.0, 1.0, angle))
    taps = sinc * (0.5 + 0.5 * jnp.cos(jnp.pi * dist / 4.0))
    return taps.astype(jnp.bfloat16).astype(jnp.float32)


def band(shape, distance, taps):
    total = jnp.zeros(shape, jnp.float32)
    for j in range(8):
        total = jnp.where(distance == j - 3, taps[j : j + 1, :1], total)
    return total.astype(jnp.bfloat16)


def cut_halo_kernel(sec_ref, down_ref, up_ref):
    rows_n = sec_ref.shape[2]
    down_ref[...] = sec_ref[0, :, rows_n - HALO :]
    up_ref[...] = sec_ref[0, :, :HALO]


def cut_middle_kernel(prim_ref, *refs):
    cut_ref = refs[-1]
    cut_ref[...] = prim_ref[:, LAG : LAG + cut_ref.shape[1]]


def relay_kernel(block_ref, *refs):
    out_ref = refs[-1]
    out_ref[...] = block_ref[:, : out_ref.shape[1]]


def bands_kernel(ao_ref, ro_ref, af_ref, rf_ref, az_ref, rg_ref):
    shape = az_ref.shape
    offset = lax.broadcasted_iota(jnp.int32, shape, 1) - lax.broadcasted_iota(jnp.int32, shape, 0)
    az_ref[...] = band(shape, offset - HALO - ao_ref[...], tap_rows(af_ref[...]))
    square = rg_ref.shape[1:]
    offset = lax.broadcasted_iota(jnp.int32, square, 0) - lax.broadcasted_iota(jnp.int32, square, 1)
    taps = tap_rows(rf_ref[...])
    for at, shift in enumerate((-LANE, 0, LANE)):
        rg_ref[at] = band(square, offset + shift - ro_ref[...], taps)


def resample_kernel(sec_ref, low_ref, high_ref, az_ref, rg_ref, out_ref, azim_ref):
    rows_n, cols_n = sec_ref.shape[2:]
    az_band = az_ref[...]
    here, tiles_n = lax.axis_index("tile"), lax.axis_size("tile")
    none = jnp.zeros(low_ref.shape[1:], jnp.bfloat16)
    for part in range(2):
        for start in range(0, rows_n, BAND):
            pieces = []
            if start == 0:
                pieces.append(jnp.where(here == 0, none, low_ref[part]))
            pieces.append(sec_ref[0, part, max(0, start - HALO) : min(rows_n, start + BAND + HALO)])
            if start + BAND == rows_n:
                pieces.append(jnp.where(here == tiles_n - 1, none, high_ref[part]))
            rows = jnp.concatenate(pieces, axis=0) if len(pieces) > 1 else pieces[0]
            azim_ref[part, start : start + BAND] = jnp.dot(
                az_band, rows, preferred_element_type=jnp.float32
            ).astype(jnp.bfloat16)

    before, same, after = [rg_ref[at] for at in range(3)]
    none = jnp.zeros((LANE, LANE), jnp.bfloat16)
    blocks_n, _, _, width = out_ref.shape
    lanes_n = width // LANE
    columns = []
    for lane in range(lanes_n):
        column = [none] * (lanes_n + 2)
        column[lane], column[lane + 1], column[lane + 2] = before, same, after
        columns.append(jnp.concatenate(column, axis=0))
    rg_band = jnp.concatenate(columns, axis=1)
    for block in range(blocks_n):
        first = block * width - LANE
        last = (block + 1) * width + LANE
        taken = slice(max(first, 0), min(last, cols_n))
        used = rg_band[taken.start - first : taken.stop - first]
        for part in range(2):
            out_ref[block, part] = jnp.dot(
                azim_ref[part, :, taken], used, preferred_element_type=jnp.float32
            ).astype(jnp.bfloat16)


def interfere(prim_re, prim_im, sec_re, sec_im):
    p_re, p_im = prim_re.astype(jnp.float32), prim_im.astype(jnp.float32)
    s_re, s_im = sec_re.astype(jnp.float32), sec_im.astype(jnp.float32)
    return p_re * s_re + p_im * s_im, p_im * s_re - p_re * s_im


def look_columns(width, block, looks_n):
    shape = (width, looks_n)
    col = lax.broadcasted_iota(jnp.int32, shape, 0) + block * width
    look = lax.broadcasted_iota(jnp.int32, shape, 1) * LR
    return jnp.where((col >= look) & (col < look + LR), 1.0, 0.0).astype(jnp.bfloat16)


def look_rows(sums_ref, part, start, rows_n):
    count = rows_n // LA
    total = sums_ref[part, pl.ds(start, count, LA)]
    for row in range(1, LA):
        total = total + sums_ref[part, pl.ds(start + row, count, LA)]
    return total


def margin_kernel(
    own_ref, one_ref, two_ref, three_ref, res_ref, first_ref, last_ref, looks_ref, sums_ref
):
    here = lax.axis_index("date")
    _, _, rows_n, width = res_ref.shape
    whole, edges = (0, rows_n - LAG), (0, LAG)
    looks_n = looks_ref.shape[2]
    totals = [None, None]
    for step, (prim_ref, starts) in enumerate(
        ((own_ref, whole), (one_ref, edges), (two_ref, edges), (three_ref, edges))
    ):
        block = jnp.bitwise_xor(here, step)
        select = look_columns(width, block, looks_n)
        columns = pl.ds(pl.multiple_of(block * width, width), width)
        halves = []
        for held, start, target in zip(starts, whole, (first_ref, last_ref)):
            pair = interfere(
                prim_ref[0, held : held + LAG],
                prim_ref[1, held : held + LAG],
                res_ref[block, 0, start : start + LAG],
                res_ref[block, 1, start : start + LAG],
            )
            pair = [value.astype(jnp.bfloat16) for value in pair]
            for part in range(2):
                target[part, :, columns] = pair[part]
            halves.append(pair)
        for part in range(2):
            both = jnp.concatenate([halves[0][part], halves[1][part]], axis=0)
            summed = jnp.dot(both, select, preferred_element_type=jnp.float32)
            totals[part] = summed if step == 0 else totals[part] + summed
    for part in range(2):
        sums_ref[part] = totals[part]
        looks_ref[part] = look_rows(sums_ref, part, 0, 2 * LAG)


def stats_kernel(last_ref, later_ref, weight_ref, stats_ref):
    cols_n = last_ref.shape[2]
    weight = weight_ref[...]
    i_re, i_im = last_ref[0].astype(jnp.float32), last_ref[1].astype(jnp.float32)
    inside = jnp.where(lax.axis_index("tile") == lax.axis_size("tile") - 1, 0.0, 1.0)
    l_re, l_im = [later_ref[part].astype(jnp.float32) * inside for part in range(2)]
    values = (
        i_re * l_re + i_im * l_im,
        i_im * l_re - i_re * l_im,
        0.5 * (i_re * i_re + i_im * i_im + l_re * l_re + l_im * l_im),
    )
    rows = []
    for value in values:
        folded = value[:, :LANE]
        for start in range(LANE, cols_n, LANE):
            folded = folded + value[:, start : start + LANE]
        rows.append(jnp.sum(folded * weight, axis=0, keepdims=True))
    rows.append(jnp.sum(weight, axis=0, keepdims=True) * (cols_n // LANE))
    rows.append(jnp.zeros((4, LANE), jnp.float32))
    stats_ref[...] = jnp.concatenate(rows, axis=0)


def look_sums(pieces, res_ref, looks_n):
    here = lax.axis_index("date")
    _, _, rows_n, width = res_ref.shape
    middle_n = rows_n - 2 * LAG
    totals = [None, None]
    for at, (step, prim_ref) in enumerate(pieces):
        block = jnp.bitwise_xor(here, step)
        first = LAG if prim_ref.shape[1] == rows_n else 0
        select = look_columns(width, block, looks_n)
        pair = interfere(
            prim_ref[0, first : first + middle_n],
            prim_ref[1, first : first + middle_n],
            res_ref[block, 0, LAG : rows_n - LAG],
            res_ref[block, 1, LAG : rows_n - LAG],
        )
        for part in range(2):
            summed = jnp.dot(
                pair[part].astype(jnp.bfloat16), select, preferred_element_type=jnp.float32
            )
            totals[part] = summed if at == 0 else totals[part] + summed
    return totals


def middle_kernel(own_ref, one_ref, two_ref, res_ref, out_ref):
    pieces = ((0, own_ref), (1, one_ref), (2, two_ref))
    for part, total in enumerate(look_sums(pieces, res_ref, out_ref.shape[2])):
        out_ref[part] = total


def unit_kernel(mine_ref, other_ref, unit_ref):
    stats = jnp.sum(mine_ref[...] + other_ref[...], axis=1, keepdims=True)
    e_re, e_im, power, count = [stats[row : row + 1] for row in range(4)]
    magnitude = jnp.sqrt(e_re * e_re + e_im * e_im)
    floor_val = (power + 1e-06) / jnp.sqrt(jnp.maximum(count, 1.0))
    denom = jnp.maximum(magnitude, floor_val)
    row = lax.broadcasted_iota(jnp.int32, unit_ref.shape, 0)
    unit_ref[...] = jnp.where(row == 0, e_re / denom, e_im / denom) * (1.0 / (LA * LR))


def finish_kernel(three_ref, res_ref, before_ref, looks_ref, unit_ref, out_ref, sums_ref):
    middle_n = before_ref.shape[1]
    edge = LAG // LA
    u_re, u_im = unit_ref[0:1], unit_ref[1:2]
    totals = look_sums(((3, three_ref),), res_ref, out_ref.shape[3])
    for part, total in enumerate(totals):
        sums_ref[part] = total + before_ref[part]
    for at, held in (
        (0, looks_ref[:, :edge]),
        (edge, [look_rows(sums_ref, part, 0, middle_n) for part in range(2)]),
        (edge + middle_n // LA, looks_ref[:, edge:]),
    ):
        rows = slice(at, at + held[0].shape[0])
        out_ref[0, 0, rows] = held[0] * u_re + held[1] * u_im
        out_ref[0, 1, rows] = held[1] * u_re - held[0] * u_im


def call(kernel, outs, scratch, cost, *args):
    vmem = pl.BlockSpec(memory_space=pltpu.VMEM)
    return pl.pallas_call(
        kernel,
        out_shape=outs,
        in_specs=[vmem] * len(args),
        out_specs=jax.tree.map(lambda _: vmem, outs),
        scratch_shapes=scratch,
        compiler_params=pltpu.CompilerParams(vmem_limit_bytes=VMEM_LIMIT),
        cost_estimate=pl.CostEstimate(flops=cost[0], bytes_accessed=cost[1], transcendentals=0),
    )(*args)


def ring(value, axis, step):
    count = lax.axis_size(axis)
    return lax.ppermute(value, axis, [(at, (at + step) % count) for at in range(count)])


def swap(value, axis, step):
    return lax.ppermute(value, axis, [(at, at ^ step) for at in range(lax.axis_size(axis))])


def fused(secondary, primary, margin_mask, az_off, rg_off, az_frac, rg_frac):
    _, _, rows_n, cols_n = secondary.shape
    width = primary.shape[2]
    dates_n = lax.axis_size("date")
    tiles_n = lax.axis_size("tile")
    bf16, f32 = jnp.bfloat16, jnp.float32
    shape = jax.ShapeDtypeStruct
    looks_n = cols_n // LR
    middle_n = rows_n - 2 * LAG
    edges = jnp.concatenate([primary[:, :LAG], primary[:, rows_n - LAG :]], axis=1)
    edges_two = swap(edges, "date", 2)
    edges_one = swap(edges, "date", 1)
    halo = shape((2, HALO, cols_n), bf16)
    down, up = call(cut_halo_kernel, (halo, halo), [], (0, 0), secondary)
    low = ring(down, "tile", 1)
    high = ring(up, "tile", -1)
    az_band, rg_band = call(
        bands_kernel,
        (shape((BAND, BAND + 2 * HALO), bf16), shape((3, LANE, LANE), bf16)),
        [],
        (0, 0),
        az_off, rg_off, az_frac, rg_frac,
    )
    edges_three = swap(edges_two, "date", 1)
    weight = jnp.broadcast_to(margin_mask[rows_n - LAG :].astype(f32)[:, None], (LAG, LANE))
    res = call(
        resample_kernel,
        shape((dates_n, 2, rows_n, width), bf16),
        [pltpu.VMEM((2, rows_n, cols_n), bf16)],
        (0, 0),
        secondary, low, high, az_band, rg_band,
    )
    middle = call(
        cut_middle_kernel,
        shape((2, middle_n + 16, width), bf16),
        [],
        (0, 0),
        primary, edges_two,res,
    )
    two, one = [swap(middle, "date", step) for step in (2, 1)]
    margin = shape((2, LAG, cols_n), bf16)
    first, last, looks = call(
        margin_kernel,
        (margin, margin, shape((2, 2 * LAG // LA, looks_n), f32)),
        [pltpu.VMEM((2, 2 * LAG, looks_n), f32)],
        (0, 0),
        primary, edges_one, edges_two, edges_three, res,
    )
    later = ring(first, "tile", -1)
    stats = call(
        stats_kernel,
        shape((8, LANE), f32),
        [],
        (0, 0),
        last, later, weight,
    )
    before = call(
        middle_kernel,
        shape((2, middle_n, looks_n), f32),
        [],
        (2 * 2 * middle_n * cols_n * looks_n, 8 * rows_n * cols_n),
        primary, one, two, res,
    )
    awaited = other = swap(stats, "tile", 1)
    stride = 2
    while stride < tiles_n:
        if stride == HOP_ROUND:
            awaited = other
        stats = stats + other
        other = swap(stats, "tile", stride)
        stride *= 2
    relayed = call(
        relay_kernel, shape((2, middle_n, width), bf16), [], (0, 0), two, awaited, one
    )
    three = swap(relayed, "date", 1)
    unit = call(unit_kernel, shape((8, LANE), f32), [], (0, 0), stats, other)
    return call(
        finish_kernel,
        shape((1, 2, rows_n // LA, looks_n), f32),
        [pltpu.VMEM((2, middle_n, looks_n), f32)],
        (2 * middle_n * cols_n * looks_n, 4 * rows_n * cols_n),
        three, res, before, looks, unit,
    )


def padded(block, sides, width):
    for axis, dim in sides:
        low = passed_along(
            lax.slice_in_dim(block, block.shape[dim] - width, None, axis=dim), axis, 1
        )
        high = passed_along(lax.slice_in_dim(block, 0, width, axis=dim), axis, -1)
        block = jnp.concatenate([low, block, high], axis=dim)
    return block


def band_taps(offset, frac):
    inside = (offset >= -3) & (offset <= 4)
    return jnp.where(inside, window(offset.astype(jnp.float32) - frac), 0.0).astype(jnp.bfloat16)


def multilook(values):
    depth, rows_n, cols_n = values.shape
    return values.reshape(depth, rows_n // LA, LA, cols_n // LR, LR).mean(axis=(2, 4))


def plain(secondary, primary, margin_mask, az_off, rg_off, az_frac, rg_frac):
    rim_rows = KA + 4
    block_cols = 256
    image = secondary[0]
    rows_n = image.shape[1]
    cols_n = image.shape[2]
    extended = padded(image, (("tile", 1),), rim_rows)
    row_out = lax.broadcasted_iota(jnp.int32, (rows_n, rows_n + 2 * rim_rows), 0)
    row_in = lax.broadcasted_iota(jnp.int32, (rows_n, rows_n + 2 * rim_rows), 1)
    azim_taps = band_taps(row_in - row_out - az_off[0, 0] - rim_rows, az_frac[0, 0])
    azim = jnp.einsum(
        "im,kmc->kic", azim_taps, extended, preferred_element_type=jnp.float32
    ).astype(jnp.bfloat16)
    blocks_n = cols_n // block_cols
    col_pad = jnp.pad(azim, ((0, 0), (0, 0), (block_cols // 2, block_cols // 2)))
    pieces = col_pad.reshape(2, rows_n, blocks_n + 1, block_cols)
    inputs = jnp.concatenate([pieces[:, :, :-1], pieces[:, :, 1:]], axis=3)
    col_in = lax.broadcasted_iota(jnp.int32, (2 * block_cols, block_cols), 0)
    col_out = lax.broadcasted_iota(jnp.int32, (2 * block_cols, block_cols), 1)
    range_taps = band_taps(col_in - block_cols // 2 - col_out - rg_off[0, 0], rg_frac[0, 0])
    resampled = jnp.einsum("kibm,mn->kibn", inputs, range_taps, preferred_element_type=jnp.float32)
    resampled = resampled.reshape(2, rows_n, cols_n).astype(jnp.bfloat16)
    prim = lax.all_gather(primary, "date", axis=2, tiled=True)[None]
    sec_f = resampled[None].astype(jnp.float32)
    prim_f = prim.astype(jnp.float32)
    ifg_re = prim_f[:, 0] * sec_f[:, 0] + prim_f[:, 1] * sec_f[:, 1]
    ifg_im = prim_f[:, 1] * sec_f[:, 0] - prim_f[:, 0] * sec_f[:, 1]
    interf = jnp.stack((ifg_re, ifg_im), axis=1)
    upcoming = passed_along(interf[:, :, :LAG, :], "tile", -1)
    later = jnp.concatenate([interf[:, :, LAG:, :], upcoming], axis=2)
    l_re = later[:, 0]
    l_im = later[:, 1]
    weight = margin_mask.astype(jnp.float32)[None, :, None]
    e_re = jnp.sum(weight * (ifg_re * l_re + ifg_im * l_im), axis=(1, 2))
    e_im = jnp.sum(weight * (ifg_im * l_re - ifg_re * l_im), axis=(1, 2))
    power = jnp.sum(
        weight * 0.5 * (ifg_re * ifg_re + ifg_im * ifg_im + l_re * l_re + l_im * l_im), axis=(1, 2)
    )
    count = jnp.zeros_like(e_re) + jnp.sum(margin_mask.astype(jnp.float32)) * interf.shape[3]
    stats = jnp.stack((e_re, e_im, power, count), axis=1)
    totals = lax.psum(stats, "tile")
    magnitude = jnp.sqrt(totals[:, 0] * totals[:, 0] + totals[:, 1] * totals[:, 1])
    floor_val = (totals[:, 2] + 1e-06) / jnp.sqrt(jnp.maximum(totals[:, 3], 1.0))
    denom = jnp.maximum(magnitude, floor_val)
    u_re = (totals[:, 0] / denom)[:, None, None]
    u_im = (totals[:, 1] / denom)[:, None, None]
    c_re = multilook(ifg_re * u_re + ifg_im * u_im)
    c_im = multilook(ifg_im * u_re - ifg_re * u_im)
    return jnp.stack((c_re, c_im), axis=1)


def shards(secondary, primary, *rest):
    rows_n, width = primary.shape[1:]
    fits = rows_n % BAND == 0 and rows_n > 2 * LAG + BAND and width % LANE == 0
    tiles_n = lax.axis_size("tile")
    fits = fits and lax.axis_size("date") == 4 and tiles_n & (tiles_n - 1) == 0
    return (fused if fits else plain)(secondary, primary, *rest)


def solution(mesh):
    return jax.shard_map(
        shards,
        mesh=mesh,
        in_specs=(
            P("date", None, "tile", None),
            P(None, "tile", "date"),
            P("tile"),
            P("date", "tile"),
            P("date", "tile"),
            P("date", "tile"),
            P("date", "tile"),
        ),
        out_specs=P("date", None, "tile", None),
        check_vma=False,
    )
```

```python
import functools

import jax
import jax.numpy as jnp
from jax import lax
from jax.experimental import pallas as pl
from jax.experimental.pallas import tpu as pltpu
from jax.sharding import PartitionSpec as P

KA = 16
LAG = 64
LA = 2
LR = 8
LANE = 128
BAND = 128
HALO = 32
VMEM_LIMIT = 40 * 1024 * 1024


def passed_along(value, axis, steps):
    count = lax.axis_size(axis)
    initial, last = (max(0, -steps), min(count, count - steps))
    return lax.ppermute(value, axis, [(source, source + steps) for source in range(initial, last)])


def window(dist):
    return jnp.sinc(dist) * (0.5 + 0.5 * jnp.cos(jnp.pi * dist / 4.0))


def tap_rows(frac):
    dist = lax.broadcasted_iota(jnp.int32, (8, LANE), 0).astype(jnp.float32) - 3.0 - frac
    angle = jnp.pi * dist
    sinc = jnp.where(dist == 0.0, 1.0, jnp.sin(angle) / jnp.where(dist == 0.0, 1.0, angle))
    taps = sinc * (0.5 + 0.5 * jnp.cos(jnp.pi * dist / 4.0))
    return taps.astype(jnp.bfloat16).astype(jnp.float32)


def band(shape, distance, taps):
    total = jnp.zeros(shape, jnp.float32)
    for j in range(8):
        total = jnp.where(distance == j - 3, taps[j : j + 1, :1], total)
    return total.astype(jnp.bfloat16)


def cut_halo_kernel(sec_ref, down_ref, up_ref):
    rows_n = sec_ref.shape[2]
    down_ref[...] = sec_ref[0, :, rows_n - HALO :]
    up_ref[...] = sec_ref[0, :, :HALO]


def cut_middle_kernel(prim_ref, *refs):
    cut_ref = refs[-1]
    cut_ref[...] = prim_ref[:, LAG : LAG + cut_ref.shape[1]]


def relay_kernel(block_ref, *refs):
    out_ref = refs[-1]
    out_ref[...] = block_ref[:, : out_ref.shape[1]]


def bands_kernel(ao_ref, ro_ref, af_ref, rf_ref, az_ref, rg_ref):
    shape = az_ref.shape
    offset = lax.broadcasted_iota(jnp.int32, shape, 1) - lax.broadcasted_iota(jnp.int32, shape, 0)
    az_ref[...] = band(shape, offset - HALO - ao_ref[...], tap_rows(af_ref[...]))
    square = rg_ref.shape[1:]
    offset = lax.broadcasted_iota(jnp.int32, square, 0) - lax.broadcasted_iota(jnp.int32, square, 1)
    taps = tap_rows(rf_ref[...])
    for at, shift in enumerate((-LANE, 0, LANE)):
        rg_ref[at] = band(square, offset + shift - ro_ref[...], taps)


def resample_kernel(sec_ref, low_ref, high_ref, az_ref, rg_ref, out_ref, azim_ref):
    rows_n, cols_n = sec_ref.shape[2:]
    az_band = az_ref[...]
    here, tiles_n = lax.axis_index("tile"), lax.axis_size("tile")
    none = jnp.zeros(low_ref.shape[1:], jnp.bfloat16)
    for part in range(2):
        for start in range(0, rows_n, BAND):
            pieces = []
            if start == 0:
                pieces.append(jnp.where(here == 0, none, low_ref[part]))
            pieces.append(sec_ref[0, part, max(0, start - HALO) : min(rows_n, start + BAND + HALO)])
            if start + BAND == rows_n:
                pieces.append(jnp.where(here == tiles_n - 1, none, high_ref[part]))
            rows = jnp.concatenate(pieces, axis=0) if len(pieces) > 1 else pieces[0]
            azim_ref[part, start : start + BAND] = jnp.dot(
                az_band, rows, preferred_element_type=jnp.float32
            ).astype(jnp.bfloat16)

    before, same, after = [rg_ref[at] for at in range(3)]
    none = jnp.zeros((LANE, LANE), jnp.bfloat16)
    blocks_n, _, _, width = out_ref.shape
    lanes_n = width // LANE
    columns = []
    for lane in range(lanes_n):
        column = [none] * (lanes_n + 2)
        column[lane], column[lane + 1], column[lane + 2] = before, same, after
        columns.append(jnp.concatenate(column, axis=0))
    rg_band = jnp.concatenate(columns, axis=1)
    for block in range(blocks_n):
        first = block * width - LANE
        last = (block + 1) * width + LANE
        taken = slice(max(first, 0), min(last, cols_n))
        used = rg_band[taken.start - first : taken.stop - first]
        for part in range(2):
            out_ref[block, part] = jnp.dot(
                azim_ref[part, :, taken], used, preferred_element_type=jnp.float32
            ).astype(jnp.bfloat16)


def interfere(prim_re, prim_im, sec_re, sec_im):
    p_re, p_im = prim_re.astype(jnp.float32), prim_im.astype(jnp.float32)
    s_re, s_im = sec_re.astype(jnp.float32), sec_im.astype(jnp.float32)
    return p_re * s_re + p_im * s_im, p_im * s_re - p_re * s_im


def look_columns(width, block, looks_n):
    shape = (width, looks_n)
    col = lax.broadcasted_iota(jnp.int32, shape, 0) + block * width
    look = lax.broadcasted_iota(jnp.int32, shape, 1) * LR
    return jnp.where((col >= look) & (col < look + LR), 1.0, 0.0).astype(jnp.bfloat16)


def look_rows(sums_ref, part, start, rows_n):
    count = rows_n // LA
    total = sums_ref[part, pl.ds(start, count, LA)]
    for row in range(1, LA):
        total = total + sums_ref[part, pl.ds(start + row, count, LA)]
    return total


def margin_kernel(
    own_ref, one_ref, two_ref, three_ref, res_ref, first_ref, last_ref, looks_ref, sums_ref
):
    here = lax.axis_index("date")
    _, _, rows_n, width = res_ref.shape
    whole, edges = (0, rows_n - LAG), (0, LAG)
    looks_n = looks_ref.shape[2]
    totals = [None, None]
    for step, (prim_ref, starts) in enumerate(
        ((own_ref, whole), (one_ref, edges), (two_ref, edges), (three_ref, edges))
    ):
        block = jnp.bitwise_xor(here, step)
        select = look_columns(width, block, looks_n)
        columns = pl.ds(pl.multiple_of(block * width, width), width)
        halves = []
        for held, start, target in zip(starts, whole, (first_ref, last_ref)):
            pair = interfere(
                prim_ref[0, held : held + LAG],
                prim_ref[1, held : held + LAG],
                res_ref[block, 0, start : start + LAG],
                res_ref[block, 1, start : start + LAG],
            )
            pair = [value.astype(jnp.bfloat16) for value in pair]
            for part in range(2):
                target[part, :, columns] = pair[part]
            halves.append(pair)
        for part in range(2):
            both = jnp.concatenate([halves[0][part], halves[1][part]], axis=0)
            summed = jnp.dot(both, select, preferred_element_type=jnp.float32)
            totals[part] = summed if step == 0 else totals[part] + summed
    for part in range(2):
        sums_ref[part] = totals[part]
        looks_ref[part] = look_rows(sums_ref, part, 0, 2 * LAG)


def stats_kernel(last_ref, later_ref, weight_ref, stats_ref):
    cols_n = last_ref.shape[2]
    weight = weight_ref[...]
    i_re, i_im = last_ref[0].astype(jnp.float32), last_ref[1].astype(jnp.float32)
    inside = jnp.where(lax.axis_index("tile") == lax.axis_size("tile") - 1, 0.0, 1.0)
    l_re, l_im = [later_ref[part].astype(jnp.float32) * inside for part in range(2)]
    values = (
        i_re * l_re + i_im * l_im,
        i_im * l_re - i_re * l_im,
        0.5 * (i_re * i_re + i_im * i_im + l_re * l_re + l_im * l_im),
    )
    rows = []
    for value in values:
        folded = value[:, :LANE]
        for start in range(LANE, cols_n, LANE):
            folded = folded + value[:, start : start + LANE]
        rows.append(jnp.sum(folded * weight, axis=0, keepdims=True))
    rows.append(jnp.sum(weight, axis=0, keepdims=True) * (cols_n // LANE))
    rows.append(jnp.zeros((4, LANE), jnp.float32))
    stats_ref[...] = jnp.concatenate(rows, axis=0)


def look_sums(pieces, res_ref, looks_n):
    here = lax.axis_index("date")
    _, _, rows_n, width = res_ref.shape
    middle_n = rows_n - 2 * LAG
    totals = [None, None]
    for at, (step, prim_ref) in enumerate(pieces):
        block = jnp.bitwise_xor(here, step)
        first = LAG if prim_ref.shape[1] == rows_n else 0
        select = look_columns(width, block, looks_n)
        pair = interfere(
            prim_ref[0, first : first + middle_n],
            prim_ref[1, first : first + middle_n],
            res_ref[block, 0, LAG : rows_n - LAG],
            res_ref[block, 1, LAG : rows_n - LAG],
        )
        for part in range(2):
            summed = jnp.dot(
                pair[part].astype(jnp.bfloat16), select, preferred_element_type=jnp.float32
            )
            totals[part] = summed if at == 0 else totals[part] + summed
    return totals


def middle_kernel(own_ref, one_ref, two_ref, res_ref, out_ref):
    pieces = ((0, own_ref), (1, one_ref), (2, two_ref))
    for part, total in enumerate(look_sums(pieces, res_ref, out_ref.shape[2])):
        out_ref[part] = total


def unit_kernel(*refs):
    *sums, unit_ref = refs
    total = sums[0][...]
    for other_ref in sums[1:]:
        total = total + other_ref[...]
    stats = jnp.sum(total, axis=1, keepdims=True)
    e_re, e_im, power, count = [stats[row : row + 1] for row in range(4)]
    magnitude = jnp.sqrt(e_re * e_re + e_im * e_im)
    floor_val = (power + 1e-06) / jnp.sqrt(jnp.maximum(count, 1.0))
    denom = jnp.maximum(magnitude, floor_val)
    row = lax.broadcasted_iota(jnp.int32, unit_ref.shape, 0)
    unit_ref[...] = jnp.where(row == 0, e_re / denom, e_im / denom) * (1.0 / (LA * LR))


def finish_kernel(three_ref, res_ref, before_ref, looks_ref, unit_ref, out_ref, sums_ref):
    middle_n = before_ref.shape[1]
    edge = LAG // LA
    u_re, u_im = unit_ref[0:1], unit_ref[1:2]
    totals = look_sums(((3, three_ref),), res_ref, out_ref.shape[3])
    for part, total in enumerate(totals):
        sums_ref[part] = total + before_ref[part]
    for at, held in (
        (0, looks_ref[:, :edge]),
        (edge, [look_rows(sums_ref, part, 0, middle_n) for part in range(2)]),
        (edge + middle_n // LA, looks_ref[:, edge:]),
    ):
        rows = slice(at, at + held[0].shape[0])
        out_ref[0, 0, rows] = held[0] * u_re + held[1] * u_im
        out_ref[0, 1, rows] = held[1] * u_re - held[0] * u_im


def call(kernel, outs, scratch, cost, *args):
    vmem = pl.BlockSpec(memory_space=pltpu.VMEM)
    return pl.pallas_call(
        kernel,
        out_shape=outs,
        in_specs=[vmem] * len(args),
        out_specs=jax.tree.map(lambda _: vmem, outs),
        scratch_shapes=scratch,
        compiler_params=pltpu.CompilerParams(vmem_limit_bytes=VMEM_LIMIT),
        cost_estimate=pl.CostEstimate(flops=cost[0], bytes_accessed=cost[1], transcendentals=0),
    )(*args)


def ring(value, axis, step):
    count = lax.axis_size(axis)
    return lax.ppermute(value, axis, [(at, (at + step) % count) for at in range(count)])


def swap(value, axis, step):
    return lax.ppermute(value, axis, [(at, at ^ step) for at in range(lax.axis_size(axis))])


def fused(secondary, primary, margin_mask, az_off, rg_off, az_frac, rg_frac):
    _, _, rows_n, cols_n = secondary.shape
    width = primary.shape[2]
    dates_n = lax.axis_size("date")
    tiles_n = lax.axis_size("tile")
    bf16, f32 = jnp.bfloat16, jnp.float32
    shape = jax.ShapeDtypeStruct
    looks_n = cols_n // LR
    middle_n = rows_n - 2 * LAG
    edges = jnp.concatenate([primary[:, :LAG], primary[:, rows_n - LAG :]], axis=1)
    edges_two = swap(edges, "date", 2)
    edges_one = swap(edges, "date", 1)
    halo = shape((2, HALO, cols_n), bf16)
    down, up = call(cut_halo_kernel, (halo, halo), [], (0, 0), secondary)
    low = ring(down, "tile", 1)
    high = ring(up, "tile", -1)
    az_band, rg_band = call(
        bands_kernel,
        (shape((BAND, BAND + 2 * HALO), bf16), shape((3, LANE, LANE), bf16)),
        [],
        (0, 0),
        az_off, rg_off, az_frac, rg_frac,
    )
    passed = call(
        relay_kernel, shape(edges.shape, bf16), [], (0, 0), edges_two, edges_one
    )
    edges_three = swap(passed, "date", 1)
    middle = call(
        cut_middle_kernel,
        shape((2, middle_n + 16, width), bf16),
        [],
        (0, 0),
        primary, edges_two,
    )
    weight = jnp.broadcast_to(margin_mask[rows_n - LAG :].astype(f32)[:, None], (LAG, LANE))
    res = call(
        resample_kernel,
        shape((dates_n, 2, rows_n, width), bf16),
        [pltpu.VMEM((2, rows_n, cols_n), bf16)],
        (0, 0),
        secondary, low, high, az_band, rg_band,
    )
    two, one = [swap(middle, "date", step) for step in (2, 1)]
    margin = shape((2, LAG, cols_n), bf16)
    first, last, looks = call(
        margin_kernel,
        (margin, margin, shape((2, 2 * LAG // LA, looks_n), f32)),
        [pltpu.VMEM((2, 2 * LAG, looks_n), f32)],
        (0, 0),
        primary, edges_one, edges_two, edges_three, res,
    )
    later = ring(first, "tile", -1)
    stats = call(
        stats_kernel,
        shape((8, LANE), f32),
        [],
        (0, 0),
        last, later, weight,
    )
    before = call(
        middle_kernel,
        shape((2, middle_n, looks_n), f32),
        [],
        (2 * 2 * middle_n * cols_n * looks_n, 8 * rows_n * cols_n),
        primary, one, two, res,
    )
    other = swap(stats, "tile", 1)
    block = shape((2, middle_n, width), bf16)
    relayed = call(relay_kernel, block, [], (0, 0), two, other,one)
    three = swap(relayed, "date", 1)
    stats = stats + other
    others = [swap(stats, "tile", step) for step in range(2, tiles_n, 2)]
    unit = call(unit_kernel, shape((8, LANE), f32), [], (0, 0), stats, *others)
    return call(
        finish_kernel,
        shape((1, 2, rows_n // LA, looks_n), f32),
        [pltpu.VMEM((2, middle_n, looks_n), f32)],
        (2 * middle_n * cols_n * looks_n, 4 * rows_n * cols_n),
        three, res, before, looks, unit,
    )


def padded(block, sides, width):
    for axis, dim in sides:
        low = passed_along(
            lax.slice_in_dim(block, block.shape[dim] - width, None, axis=dim), axis, 1
        )
        high = passed_along(lax.slice_in_dim(block, 0, width, axis=dim), axis, -1)
        block = jnp.concatenate([low, block, high], axis=dim)
    return block


def band_taps(offset, frac):
    inside = (offset >= -3) & (offset <= 4)
    return jnp.where(inside, window(offset.astype(jnp.float32) - frac), 0.0).astype(jnp.bfloat16)


def multilook(values):
    depth, rows_n, cols_n = values.shape
    return values.reshape(depth, rows_n // LA, LA, cols_n // LR, LR).mean(axis=(2, 4))


def plain(secondary, primary, margin_mask, az_off, rg_off, az_frac, rg_frac):
    rim_rows = KA + 4
    block_cols = 256
    image = secondary[0]
    rows_n = image.shape[1]
    cols_n = image.shape[2]
    extended = padded(image, (("tile", 1),), rim_rows)
    row_out = lax.broadcasted_iota(jnp.int32, (rows_n, rows_n + 2 * rim_rows), 0)
    row_in = lax.broadcasted_iota(jnp.int32, (rows_n, rows_n + 2 * rim_rows), 1)
    azim_taps = band_taps(row_in - row_out - az_off[0, 0] - rim_rows, az_frac[0, 0])
    azim = jnp.einsum(
        "im,kmc->kic", azim_taps, extended, preferred_element_type=jnp.float32
    ).astype(jnp.bfloat16)
    blocks_n = cols_n // block_cols
    col_pad = jnp.pad(azim, ((0, 0), (0, 0), (block_cols // 2, block_cols // 2)))
    pieces = col_pad.reshape(2, rows_n, blocks_n + 1, block_cols)
    inputs = jnp.concatenate([pieces[:, :, :-1], pieces[:, :, 1:]], axis=3)
    col_in = lax.broadcasted_iota(jnp.int32, (2 * block_cols, block_cols), 0)
    col_out = lax.broadcasted_iota(jnp.int32, (2 * block_cols, block_cols), 1)
    range_taps = band_taps(col_in - block_cols // 2 - col_out - rg_off[0, 0], rg_frac[0, 0])
    resampled = jnp.einsum("kibm,mn->kibn", inputs, range_taps, preferred_element_type=jnp.float32)
    resampled = resampled.reshape(2, rows_n, cols_n).astype(jnp.bfloat16)
    prim = lax.all_gather(primary, "date", axis=2, tiled=True)[None]
    sec_f = resampled[None].astype(jnp.float32)
    prim_f = prim.astype(jnp.float32)
    ifg_re = prim_f[:, 0] * sec_f[:, 0] + prim_f[:, 1] * sec_f[:, 1]
    ifg_im = prim_f[:, 1] * sec_f[:, 0] - prim_f[:, 0] * sec_f[:, 1]
    interf = jnp.stack((ifg_re, ifg_im), axis=1)
    upcoming = passed_along(interf[:, :, :LAG, :], "tile", -1)
    later = jnp.concatenate([interf[:, :, LAG:, :], upcoming], axis=2)
    l_re = later[:, 0]
    l_im = later[:, 1]
    weight = margin_mask.astype(jnp.float32)[None, :, None]
    e_re = jnp.sum(weight * (ifg_re * l_re + ifg_im * l_im), axis=(1, 2))
    e_im = jnp.sum(weight * (ifg_im * l_re - ifg_re * l_im), axis=(1, 2))
    power = jnp.sum(
        weight * 0.5 * (ifg_re * ifg_re + ifg_im * ifg_im + l_re * l_re + l_im * l_im), axis=(1, 2)
    )
    count = jnp.zeros_like(e_re) + jnp.sum(margin_mask.astype(jnp.float32)) * interf.shape[3]
    stats = jnp.stack((e_re, e_im, power, count), axis=1)
    totals = lax.psum(stats, "tile")
    magnitude = jnp.sqrt(totals[:, 0] * totals[:, 0] + totals[:, 1] * totals[:, 1])
    floor_val = (totals[:, 2] + 1e-06) / jnp.sqrt(jnp.maximum(totals[:, 3], 1.0))
    denom = jnp.maximum(magnitude, floor_val)
    u_re = (totals[:, 0] / denom)[:, None, None]
    u_im = (totals[:, 1] / denom)[:, None, None]
    c_re = multilook(ifg_re * u_re + ifg_im * u_im)
    c_im = multilook(ifg_im * u_re - ifg_re * u_im)
    return jnp.stack((c_re, c_im), axis=1)


def shards(secondary, primary, *rest):
    rows_n, width = primary.shape[1:]
    fits = rows_n % BAND == 0 and rows_n > 2 * LAG + BAND and width % LANE == 0
    tiles_n = lax.axis_size("tile")
    fits = fits and lax.axis_size("date") == 4 and tiles_n & (tiles_n - 1) == 0
    return (fused if fits else plain)(secondary, primary, *rest)


def solution(mesh):
    return jax.shard_map(
        shards,
        mesh=mesh,
        in_specs=(
            P("date", None, "tile", None),
            P(None, "tile", "date"),
            P("tile"),
            P("date", "tile"),
            P("date", "tile"),
            P("date", "tile"),
            P("date", "tile"),
        ),
        out_specs=P("date", None, "tile", None),
        check_vma=False,
    )
```

```python
import functools

import jax
import jax.numpy as jnp
from jax import lax
from jax.experimental import pallas as pl
from jax.experimental.pallas import tpu as pltpu
from jax.sharding import PartitionSpec as P

KA = 16
LAG = 64
LA = 2
LR = 8
LANE = 128
BAND = 128
HALO = 32
VMEM_LIMIT = 40 * 1024 * 1024


def passed_along(value, axis, steps):
    count = lax.axis_size(axis)
    initial, last = (max(0, -steps), min(count, count - steps))
    return lax.ppermute(value, axis, [(source, source + steps) for source in range(initial, last)])


def window(dist):
    return jnp.sinc(dist) * (0.5 + 0.5 * jnp.cos(jnp.pi * dist / 4.0))


def tap_rows(frac):
    dist = lax.broadcasted_iota(jnp.int32, (8, LANE), 0).astype(jnp.float32) - 3.0 - frac
    angle = jnp.pi * dist
    sinc = jnp.where(dist == 0.0, 1.0, jnp.sin(angle) / jnp.where(dist == 0.0, 1.0, angle))
    taps = sinc * (0.5 + 0.5 * jnp.cos(jnp.pi * dist / 4.0))
    return taps.astype(jnp.bfloat16).astype(jnp.float32)


def band(shape, distance, taps):
    total = jnp.zeros(shape, jnp.float32)
    for j in range(8):
        total = jnp.where(distance == j - 3, taps[j : j + 1, :1], total)
    return total.astype(jnp.bfloat16)


def cut_halo_kernel(sec_ref, down_ref, up_ref):
    rows_n = sec_ref.shape[2]
    down_ref[...] = sec_ref[0, :, rows_n - HALO :]
    up_ref[...] = sec_ref[0, :, :HALO]


def cut_middle_kernel(prim_ref, *refs):
    cut_ref = refs[-1]
    cut_ref[...] = prim_ref[:, LAG : LAG + cut_ref.shape[1]]


def relay_kernel(block_ref, *refs):
    out_ref = refs[-1]
    out_ref[...] = block_ref[:, : out_ref.shape[1]]


def bands_kernel(ao_ref, ro_ref, af_ref, rf_ref, az_ref, rg_ref):
    shape = az_ref.shape
    offset = lax.broadcasted_iota(jnp.int32, shape, 1) - lax.broadcasted_iota(jnp.int32, shape, 0)
    az_ref[...] = band(shape, offset - HALO - ao_ref[...], tap_rows(af_ref[...]))
    square = rg_ref.shape[1:]
    offset = lax.broadcasted_iota(jnp.int32, square, 0) - lax.broadcasted_iota(jnp.int32, square, 1)
    taps = tap_rows(rf_ref[...])
    for at, shift in enumerate((-LANE, 0, LANE)):
        rg_ref[at] = band(square, offset + shift - ro_ref[...], taps)


def resample_kernel(sec_ref, low_ref, high_ref, az_ref, rg_ref, out_ref, azim_ref):
    rows_n, cols_n = sec_ref.shape[2:]
    az_band = az_ref[...]
    here, tiles_n = lax.axis_index("tile"), lax.axis_size("tile")
    none = jnp.zeros(low_ref.shape[1:], jnp.bfloat16)
    for part in range(2):
        for start in range(0, rows_n, BAND):
            pieces = []
            if start == 0:
                pieces.append(jnp.where(here == 0, none, low_ref[part]))
            pieces.append(sec_ref[0, part, max(0, start - HALO) : min(rows_n, start + BAND + HALO)])
            if start + BAND == rows_n:
                pieces.append(jnp.where(here == tiles_n - 1, none, high_ref[part]))
            rows = jnp.concatenate(pieces, axis=0) if len(pieces) > 1 else pieces[0]
            azim_ref[part, start : start + BAND] = jnp.dot(
                az_band, rows, preferred_element_type=jnp.float32
            ).astype(jnp.bfloat16)

    before, same, after = [rg_ref[at] for at in range(3)]
    none = jnp.zeros((LANE, LANE), jnp.bfloat16)
    blocks_n, _, _, width = out_ref.shape
    lanes_n = width // LANE
    columns = []
    for lane in range(lanes_n):
        column = [none] * (lanes_n + 2)
        column[lane], column[lane + 1], column[lane + 2] = before, same, after
        columns.append(jnp.concatenate(column, axis=0))
    rg_band = jnp.concatenate(columns, axis=1)
    for block in range(blocks_n):
        first = block * width - LANE
        last = (block + 1) * width + LANE
        taken = slice(max(first, 0), min(last, cols_n))
        used = rg_band[taken.start - first : taken.stop - first]
        for part in range(2):
            out_ref[block, part] = jnp.dot(
                azim_ref[part, :, taken], used, preferred_element_type=jnp.float32
            ).astype(jnp.bfloat16)


def interfere(prim_re, prim_im, sec_re, sec_im):
    p_re, p_im = prim_re.astype(jnp.float32), prim_im.astype(jnp.float32)
    s_re, s_im = sec_re.astype(jnp.float32), sec_im.astype(jnp.float32)
    return p_re * s_re + p_im * s_im, p_im * s_re - p_re * s_im


def look_columns(width, block, looks_n):
    shape = (width, looks_n)
    col = lax.broadcasted_iota(jnp.int32, shape, 0) + block * width
    look = lax.broadcasted_iota(jnp.int32, shape, 1) * LR
    return jnp.where((col >= look) & (col < look + LR), 1.0, 0.0).astype(jnp.bfloat16)


def look_rows(sums_ref, part, start, rows_n):
    count = rows_n // LA
    total = sums_ref[part, pl.ds(start, count, LA)]
    for row in range(1, LA):
        total = total + sums_ref[part, pl.ds(start + row, count, LA)]
    return total


def margin_kernel(
    own_ref, one_ref, two_ref, three_ref, res_ref, first_ref, last_ref, looks_ref, sums_ref
):
    here = lax.axis_index("date")
    _, _, rows_n, width = res_ref.shape
    whole, edges = (0, rows_n - LAG), (0, LAG)
    looks_n = looks_ref.shape[2]
    totals = [None, None]
    for step, (prim_ref, starts) in enumerate(
        ((own_ref, whole), (one_ref, edges), (two_ref, edges), (three_ref, edges))
    ):
        block = jnp.bitwise_xor(here, step)
        select = look_columns(width, block, looks_n)
        columns = pl.ds(pl.multiple_of(block * width, width), width)
        halves = []
        for held, start, target in zip(starts, whole, (first_ref, last_ref)):
            pair = interfere(
                prim_ref[0, held : held + LAG],
                prim_ref[1, held : held + LAG],
                res_ref[block, 0, start : start + LAG],
                res_ref[block, 1, start : start + LAG],
            )
            pair = [value.astype(jnp.bfloat16) for value in pair]
            for part in range(2):
                target[part, :, columns] = pair[part]
            halves.append(pair)
        for part in range(2):
            both = jnp.concatenate([halves[0][part], halves[1][part]], axis=0)
            summed = jnp.dot(both, select, preferred_element_type=jnp.float32)
            totals[part] = summed if step == 0 else totals[part] + summed
    for part in range(2):
        sums_ref[part] = totals[part]
        looks_ref[part] = look_rows(sums_ref, part, 0, 2 * LAG)


def stats_kernel(last_ref, later_ref, weight_ref, stats_ref):
    cols_n = last_ref.shape[2]
    weight = weight_ref[...]
    i_re, i_im = last_ref[0].astype(jnp.float32), last_ref[1].astype(jnp.float32)
    inside = jnp.where(lax.axis_index("tile") == lax.axis_size("tile") - 1, 0.0, 1.0)
    l_re, l_im = [later_ref[part].astype(jnp.float32) * inside for part in range(2)]
    values = (
        i_re * l_re + i_im * l_im,
        i_im * l_re - i_re * l_im,
        0.5 * (i_re * i_re + i_im * i_im + l_re * l_re + l_im * l_im),
    )
    rows = []
    for value in values:
        folded = value[:, :LANE]
        for start in range(LANE, cols_n, LANE):
            folded = folded + value[:, start : start + LANE]
        rows.append(jnp.sum(folded * weight, axis=0, keepdims=True))
    rows.append(jnp.sum(weight, axis=0, keepdims=True) * (cols_n // LANE))
    rows.append(jnp.zeros((4, LANE), jnp.float32))
    stats_ref[...] = jnp.concatenate(rows, axis=0)


def look_sums(pieces, res_ref, looks_n):
    here = lax.axis_index("date")
    _, _, rows_n, width = res_ref.shape
    middle_n = rows_n - 2 * LAG
    totals = [None, None]
    for at, (step, prim_ref) in enumerate(pieces):
        block = jnp.bitwise_xor(here, step)
        first = LAG if prim_ref.shape[1] == rows_n else 0
        select = look_columns(width, block, looks_n)
        pair = interfere(
            prim_ref[0, first : first + middle_n],
            prim_ref[1, first : first + middle_n],
            res_ref[block, 0, LAG : rows_n - LAG],
            res_ref[block, 1, LAG : rows_n - LAG],
        )
        for part in range(2):
            summed = jnp.dot(
                pair[part].astype(jnp.bfloat16), select, preferred_element_type=jnp.float32
            )
            totals[part] = summed if at == 0 else totals[part] + summed
    return totals


def middle_kernel(own_ref, one_ref, two_ref, res_ref, out_ref):
    pieces = ((0, own_ref), (1, one_ref), (2, two_ref))
    for part, total in enumerate(look_sums(pieces, res_ref, out_ref.shape[2])):
        out_ref[part] = total


def unit_kernel(mine_ref, other_ref, unit_ref):
    stats = jnp.sum(mine_ref[...] + other_ref[...], axis=1, keepdims=True)
    e_re, e_im, power, count = [stats[row : row + 1] for row in range(4)]
    magnitude = jnp.sqrt(e_re * e_re + e_im * e_im)
    floor_val = (power + 1e-06) / jnp.sqrt(jnp.maximum(count, 1.0))
    denom = jnp.maximum(magnitude, floor_val)
    row = lax.broadcasted_iota(jnp.int32, unit_ref.shape, 0)
    unit_ref[...] = jnp.where(row == 0, e_re / denom, e_im / denom) * (1.0 / (LA * LR))


def finish_kernel(three_ref, res_ref, before_ref, looks_ref, unit_ref, out_ref, sums_ref):
    middle_n = before_ref.shape[1]
    edge = LAG // LA
    u_re, u_im = unit_ref[0:1], unit_ref[1:2]
    totals = look_sums(((3, three_ref),), res_ref, out_ref.shape[3])
    for part, total in enumerate(totals):
        sums_ref[part] = total + before_ref[part]
    for at, held in (
        (0, looks_ref[:, :edge]),
        (edge, [look_rows(sums_ref, part, 0, middle_n) for part in range(2)]),
        (edge + middle_n // LA, looks_ref[:, edge:]),
    ):
        rows = slice(at, at + held[0].shape[0])
        out_ref[0, 0, rows] = held[0] * u_re + held[1] * u_im
        out_ref[0, 1, rows] = held[1] * u_re - held[0] * u_im


def call(kernel, outs, scratch, cost, *args):
    vmem = pl.BlockSpec(memory_space=pltpu.VMEM)
    return pl.pallas_call(
        kernel,
        out_shape=outs,
        in_specs=[vmem] * len(args),
        out_specs=jax.tree.map(lambda _: vmem, outs),
        scratch_shapes=scratch,
        compiler_params=pltpu.CompilerParams(vmem_limit_bytes=VMEM_LIMIT),
        cost_estimate=pl.CostEstimate(flops=cost[0], bytes_accessed=cost[1], transcendentals=0),
    )(*args)


def ring(value, axis, step):
    count = lax.axis_size(axis)
    return lax.ppermute(value, axis, [(at, (at + step) % count) for at in range(count)])


def swap(value, axis, step):
    return lax.ppermute(value, axis, [(at, at ^ step) for at in range(lax.axis_size(axis))])


def fused(secondary, primary, margin_mask, az_off, rg_off, az_frac, rg_frac):
    _, _, rows_n, cols_n = secondary.shape
    width = primary.shape[2]
    dates_n = lax.axis_size("date")
    tiles_n = lax.axis_size("tile")
    bf16, f32 = jnp.bfloat16, jnp.float32
    shape = jax.ShapeDtypeStruct
    looks_n = cols_n // LR
    middle_n = rows_n - 2 * LAG
    edges = jnp.concatenate([primary[:, :LAG], primary[:, rows_n - LAG :]], axis=1)
    edges_two = swap(edges, "date", 2)
    edges_one = swap(edges, "date", 1)
    halo = shape((2, HALO, cols_n), bf16)
    down, up = call(cut_halo_kernel, (halo, halo), [], (0, 0), secondary)
    low = ring(down, "tile", 1)
    high = ring(up, "tile", -1)
    az_band, rg_band = call(
        bands_kernel,
        (shape((BAND, BAND + 2 * HALO), bf16), shape((3, LANE, LANE), bf16)),
        [],
        (0, 0),
        az_off, rg_off, az_frac, rg_frac,
    )
    passed = call(
        relay_kernel, shape(edges.shape, bf16), [], (0, 0), edges_two, edges_one
    )
    edges_three = swap(passed, "date", 1)
    middle = call(
        cut_middle_kernel,
        shape((2, middle_n + 16, width), bf16),
        [],
        (0, 0),
        primary, edges_two,
    )
    weight = jnp.broadcast_to(margin_mask[rows_n - LAG :].astype(f32)[:, None], (LAG, LANE))
    res = call(
        resample_kernel,
        shape((dates_n, 2, rows_n, width), bf16),
        [pltpu.VMEM((2, rows_n, cols_n), bf16)],
        (0, 0),
        secondary, low, high, az_band, rg_band,
    )
    two, one = [swap(middle, "date", step) for step in (2, 1)]
    margin = shape((2, LAG, cols_n), bf16)
    first, last, looks = call(
        margin_kernel,
        (margin, margin, shape((2, 2 * LAG // LA, looks_n), f32)),
        [pltpu.VMEM((2, 2 * LAG, looks_n), f32)],
        (0, 0),
        primary, edges_one, edges_two, edges_three, res,
    )
    later = ring(first, "tile", -1)
    stats = call(
        stats_kernel,
        shape((8, LANE), f32),
        [],
        (0, 0),
        last, later, weight,
    )
    before = call(
        middle_kernel,
        shape((2, middle_n, looks_n), f32),
        [],
        (2 * 2 * middle_n * cols_n * looks_n, 8 * rows_n * cols_n),
        primary, one, two, res,
    )
    other = swap(stats, "tile", 1)
    block = shape((2, middle_n, width), bf16)
    relayed = call(relay_kernel, block, [], (0, 0), two, other,one)
    three = swap(relayed, "date", 1)
    stride = 2
    while stride < tiles_n:
        stats = stats + other
        other = swap(stats, "tile", stride)
        stride *= 2
    unit = call(unit_kernel, shape((8, LANE), f32), [], (0, 0), stats, other)
    return call(
        finish_kernel,
        shape((1, 2, rows_n // LA, looks_n), f32),
        [pltpu.VMEM((2, middle_n, looks_n), f32)],
        (2 * middle_n * cols_n * looks_n, 4 * rows_n * cols_n),
        three, res, before, looks, unit,
    )


def padded(block, sides, width):
    for axis, dim in sides:
        low = passed_along(
            lax.slice_in_dim(block, block.shape[dim] - width, None, axis=dim), axis, 1
        )
        high = passed_along(lax.slice_in_dim(block, 0, width, axis=dim), axis, -1)
        block = jnp.concatenate([low, block, high], axis=dim)
    return block


def band_taps(offset, frac):
    inside = (offset >= -3) & (offset <= 4)
    return jnp.where(inside, window(offset.astype(jnp.float32) - frac), 0.0).astype(jnp.bfloat16)


def multilook(values):
    depth, rows_n, cols_n = values.shape
    return values.reshape(depth, rows_n // LA, LA, cols_n // LR, LR).mean(axis=(2, 4))


def plain(secondary, primary, margin_mask, az_off, rg_off, az_frac, rg_frac):
    rim_rows = KA + 4
    block_cols = 256
    image = secondary[0]
    rows_n = image.shape[1]
    cols_n = image.shape[2]
    extended = padded(image, (("tile", 1),), rim_rows)
    row_out = lax.broadcasted_iota(jnp.int32, (rows_n, rows_n + 2 * rim_rows), 0)
    row_in = lax.broadcasted_iota(jnp.int32, (rows_n, rows_n + 2 * rim_rows), 1)
    azim_taps = band_taps(row_in - row_out - az_off[0, 0] - rim_rows, az_frac[0, 0])
    azim = jnp.einsum(
        "im,kmc->kic", azim_taps, extended, preferred_element_type=jnp.float32
    ).astype(jnp.bfloat16)
    blocks_n = cols_n // block_cols
    col_pad = jnp.pad(azim, ((0, 0), (0, 0), (block_cols // 2, block_cols // 2)))
    pieces = col_pad.reshape(2, rows_n, blocks_n + 1, block_cols)
    inputs = jnp.concatenate([pieces[:, :, :-1], pieces[:, :, 1:]], axis=3)
    col_in = lax.broadcasted_iota(jnp.int32, (2 * block_cols, block_cols), 0)
    col_out = lax.broadcasted_iota(jnp.int32, (2 * block_cols, block_cols), 1)
    range_taps = band_taps(col_in - block_cols // 2 - col_out - rg_off[0, 0], rg_frac[0, 0])
    resampled = jnp.einsum("kibm,mn->kibn", inputs, range_taps, preferred_element_type=jnp.float32)
    resampled = resampled.reshape(2, rows_n, cols_n).astype(jnp.bfloat16)
    prim = lax.all_gather(primary, "date", axis=2, tiled=True)[None]
    sec_f = resampled[None].astype(jnp.float32)
    prim_f = prim.astype(jnp.float32)
    ifg_re = prim_f[:, 0] * sec_f[:, 0] + prim_f[:, 1] * sec_f[:, 1]
    ifg_im = prim_f[:, 1] * sec_f[:, 0] - prim_f[:, 0] * sec_f[:, 1]
    interf = jnp.stack((ifg_re, ifg_im), axis=1)
    upcoming = passed_along(interf[:, :, :LAG, :], "tile", -1)
    later = jnp.concatenate([interf[:, :, LAG:, :], upcoming], axis=2)
    l_re = later[:, 0]
    l_im = later[:, 1]
    weight = margin_mask.astype(jnp.float32)[None, :, None]
    e_re = jnp.sum(weight * (ifg_re * l_re + ifg_im * l_im), axis=(1, 2))
    e_im = jnp.sum(weight * (ifg_im * l_re - ifg_re * l_im), axis=(1, 2))
    power = jnp.sum(
        weight * 0.5 * (ifg_re * ifg_re + ifg_im * ifg_im + l_re * l_re + l_im * l_im), axis=(1, 2)
    )
    count = jnp.zeros_like(e_re) + jnp.sum(margin_mask.astype(jnp.float32)) * interf.shape[3]
    stats = jnp.stack((e_re, e_im, power, count), axis=1)
    totals = lax.psum(stats, "tile")
    magnitude = jnp.sqrt(totals[:, 0] * totals[:, 0] + totals[:, 1] * totals[:, 1])
    floor_val = (totals[:, 2] + 1e-06) / jnp.sqrt(jnp.maximum(totals[:, 3], 1.0))
    denom = jnp.maximum(magnitude, floor_val)
    u_re = (totals[:, 0] / denom)[:, None, None]
    u_im = (totals[:, 1] / denom)[:, None, None]
    c_re = multilook(ifg_re * u_re + ifg_im * u_im)
    c_im = multilook(ifg_im * u_re - ifg_re * u_im)
    return jnp.stack((c_re, c_im), axis=1)


def shards(secondary, primary, *rest):
    rows_n, width = primary.shape[1:]
    fits = rows_n % BAND == 0 and rows_n > 2 * LAG + BAND and width % LANE == 0
    tiles_n = lax.axis_size("tile")
    fits = fits and lax.axis_size("date") == 4 and tiles_n & (tiles_n - 1) == 0
    return (fused if fits else plain)(secondary, primary, *rest)


def solution(mesh):
    return jax.shard_map(
        shards,
        mesh=mesh,
        in_specs=(
            P("date", None, "tile", None),
            P(None, "tile", "date"),
            P("tile"),
            P("date", "tile"),
            P("date", "tile"),
            P("date", "tile"),
            P("date", "tile"),
        ),
        out_specs=P("date", None, "tile", None),
        check_vma=False,
    )
```

```python
import functools

import jax
import jax.numpy as jnp
from jax import lax
from jax.experimental import pallas as pl
from jax.experimental.pallas import tpu as pltpu
from jax.sharding import PartitionSpec as P

KA = 16
LAG = 64
LA = 2
LR = 8
LANE = 128
BAND = 128
HALO = 32
VMEM_LIMIT = 40 * 1024 * 1024


def passed_along(value, axis, steps):
    count = lax.axis_size(axis)
    initial, last = (max(0, -steps), min(count, count - steps))
    return lax.ppermute(value, axis, [(source, source + steps) for source in range(initial, last)])


def window(dist):
    return jnp.sinc(dist) * (0.5 + 0.5 * jnp.cos(jnp.pi * dist / 4.0))


def tap_rows(frac):
    dist = lax.broadcasted_iota(jnp.int32, (8, LANE), 0).astype(jnp.float32) - 3.0 - frac
    angle = jnp.pi * dist
    sinc = jnp.where(dist == 0.0, 1.0, jnp.sin(angle) / jnp.where(dist == 0.0, 1.0, angle))
    taps = sinc * (0.5 + 0.5 * jnp.cos(jnp.pi * dist / 4.0))
    return taps.astype(jnp.bfloat16).astype(jnp.float32)


def band(shape, distance, taps):
    total = jnp.zeros(shape, jnp.float32)
    for j in range(8):
        total = jnp.where(distance == j - 3, taps[j : j + 1, :1], total)
    return total.astype(jnp.bfloat16)


def cut_halo_kernel(sec_ref, down_ref, up_ref):
    rows_n = sec_ref.shape[2]
    down_ref[...] = sec_ref[0, :, rows_n - HALO :]
    up_ref[...] = sec_ref[0, :, :HALO]


def cut_middle_kernel(prim_ref, *refs):
    cut_ref = refs[-1]
    cut_ref[...] = prim_ref[:, LAG : LAG + cut_ref.shape[1]]


def relay_kernel(block_ref, *refs):
    out_ref = refs[-1]
    out_ref[...] = block_ref[:, : out_ref.shape[1]]


def bands_kernel(ao_ref, ro_ref, af_ref, rf_ref, az_ref, rg_ref):
    shape = az_ref.shape
    offset = lax.broadcasted_iota(jnp.int32, shape, 1) - lax.broadcasted_iota(jnp.int32, shape, 0)
    az_ref[...] = band(shape, offset - HALO - ao_ref[...], tap_rows(af_ref[...]))
    square = rg_ref.shape[1:]
    offset = lax.broadcasted_iota(jnp.int32, square, 0) - lax.broadcasted_iota(jnp.int32, square, 1)
    taps = tap_rows(rf_ref[...])
    for at, shift in enumerate((-LANE, 0, LANE)):
        rg_ref[at] = band(square, offset + shift - ro_ref[...], taps)


def resample_kernel(sec_ref, low_ref, high_ref, az_ref, rg_ref, out_ref, azim_ref):
    rows_n, cols_n = sec_ref.shape[2:]
    az_band = az_ref[...]
    here, tiles_n = lax.axis_index("tile"), lax.axis_size("tile")
    none = jnp.zeros(low_ref.shape[1:], jnp.bfloat16)
    for part in range(2):
        for start in range(0, rows_n, BAND):
            pieces = []
            if start == 0:
                pieces.append(jnp.where(here == 0, none, low_ref[part]))
            pieces.append(sec_ref[0, part, max(0, start - HALO) : min(rows_n, start + BAND + HALO)])
            if start + BAND == rows_n:
                pieces.append(jnp.where(here == tiles_n - 1, none, high_ref[part]))
            rows = jnp.concatenate(pieces, axis=0) if len(pieces) > 1 else pieces[0]
            azim_ref[part, start : start + BAND] = jnp.dot(
                az_band, rows, preferred_element_type=jnp.float32
            ).astype(jnp.bfloat16)

    before, same, after = [rg_ref[at] for at in range(3)]
    none = jnp.zeros((LANE, LANE), jnp.bfloat16)
    blocks_n, _, _, width = out_ref.shape
    lanes_n = width // LANE
    columns = []
    for lane in range(lanes_n):
        column = [none] * (lanes_n + 2)
        column[lane], column[lane + 1], column[lane + 2] = before, same, after
        columns.append(jnp.concatenate(column, axis=0))
    rg_band = jnp.concatenate(columns, axis=1)
    for block in range(blocks_n):
        first = block * width - LANE
        last = (block + 1) * width + LANE
        taken = slice(max(first, 0), min(last, cols_n))
        used = rg_band[taken.start - first : taken.stop - first]
        for part in range(2):
            out_ref[block, part] = jnp.dot(
                azim_ref[part, :, taken], used, preferred_element_type=jnp.float32
            ).astype(jnp.bfloat16)


def interfere(prim_re, prim_im, sec_re, sec_im):
    p_re, p_im = prim_re.astype(jnp.float32), prim_im.astype(jnp.float32)
    s_re, s_im = sec_re.astype(jnp.float32), sec_im.astype(jnp.float32)
    return p_re * s_re + p_im * s_im, p_im * s_re - p_re * s_im


def look_columns(width, block, looks_n):
    shape = (width, looks_n)
    col = lax.broadcasted_iota(jnp.int32, shape, 0) + block * width
    look = lax.broadcasted_iota(jnp.int32, shape, 1) * LR
    return jnp.where((col >= look) & (col < look + LR), 1.0, 0.0).astype(jnp.bfloat16)


def look_rows(sums_ref, part, start, rows_n):
    count = rows_n // LA
    total = sums_ref[part, pl.ds(start, count, LA)]
    for row in range(1, LA):
        total = total + sums_ref[part, pl.ds(start + row, count, LA)]
    return total


def margin_kernel(
    own_ref, one_ref, two_ref, three_ref, res_ref, first_ref, last_ref, looks_ref, sums_ref
):
    here = lax.axis_index("date")
    _, _, rows_n, width = res_ref.shape
    whole, edges = (0, rows_n - LAG), (0, LAG)
    looks_n = looks_ref.shape[2]
    totals = [None, None]
    for step, (prim_ref, starts) in enumerate(
        ((own_ref, whole), (one_ref, whole), (two_ref, edges), (three_ref, edges))
    ):
        block = jnp.bitwise_xor(here, step)
        select = look_columns(width, block, looks_n)
        columns = pl.ds(pl.multiple_of(block * width, width), width)
        halves = []
        for held, start, target in zip(starts, whole, (first_ref, last_ref)):
            pair = interfere(
                prim_ref[0, held : held + LAG],
                prim_ref[1, held : held + LAG],
                res_ref[block, 0, start : start + LAG],
                res_ref[block, 1, start : start + LAG],
            )
            pair = [value.astype(jnp.bfloat16) for value in pair]
            for part in range(2):
                target[part, :, columns] = pair[part]
            halves.append(pair)
        for part in range(2):
            both = jnp.concatenate([halves[0][part], halves[1][part]], axis=0)
            summed = jnp.dot(both, select, preferred_element_type=jnp.float32)
            totals[part] = summed if step == 0 else totals[part] + summed
    for part in range(2):
        sums_ref[part] = totals[part]
        looks_ref[part] = look_rows(sums_ref, part, 0, 2 * LAG)


def stats_kernel(last_ref, later_ref, weight_ref, stats_ref):
    cols_n = last_ref.shape[2]
    weight = weight_ref[...]
    i_re, i_im = last_ref[0].astype(jnp.float32), last_ref[1].astype(jnp.float32)
    inside = jnp.where(lax.axis_index("tile") == lax.axis_size("tile") - 1, 0.0, 1.0)
    l_re, l_im = [later_ref[part].astype(jnp.float32) * inside for part in range(2)]
    values = (
        i_re * l_re + i_im * l_im,
        i_im * l_re - i_re * l_im,
        0.5 * (i_re * i_re + i_im * i_im + l_re * l_re + l_im * l_im),
    )
    rows = []
    for value in values:
        folded = value[:, :LANE]
        for start in range(LANE, cols_n, LANE):
            folded = folded + value[:, start : start + LANE]
        rows.append(jnp.sum(folded * weight, axis=0, keepdims=True))
    rows.append(jnp.sum(weight, axis=0, keepdims=True) * (cols_n // LANE))
    rows.append(jnp.zeros((4, LANE), jnp.float32))
    stats_ref[...] = jnp.concatenate(rows, axis=0)


def look_sums(pieces, res_ref, looks_n):
    here = lax.axis_index("date")
    _, _, rows_n, width = res_ref.shape
    middle_n = rows_n - 2 * LAG
    totals = [None, None]
    for at, (step, prim_ref) in enumerate(pieces):
        block = jnp.bitwise_xor(here, step)
        first = LAG if prim_ref.shape[1] == rows_n else 0
        select = look_columns(width, block, looks_n)
        pair = interfere(
            prim_ref[0, first : first + middle_n],
            prim_ref[1, first : first + middle_n],
            res_ref[block, 0, LAG : rows_n - LAG],
            res_ref[block, 1, LAG : rows_n - LAG],
        )
        for part in range(2):
            summed = jnp.dot(
                pair[part].astype(jnp.bfloat16), select, preferred_element_type=jnp.float32
            )
            totals[part] = summed if at == 0 else totals[part] + summed
    return totals


def middle_kernel(own_ref, one_ref, two_ref, res_ref, out_ref):
    pieces = ((0, own_ref), (1, one_ref), (2, two_ref))
    for part, total in enumerate(look_sums(pieces, res_ref, out_ref.shape[2])):
        out_ref[part] = total


def unit_kernel(mine_ref, other_ref, unit_ref):
    stats = jnp.sum(mine_ref[...] + other_ref[...], axis=1, keepdims=True)
    e_re, e_im, power, count = [stats[row : row + 1] for row in range(4)]
    magnitude = jnp.sqrt(e_re * e_re + e_im * e_im)
    floor_val = (power + 1e-06) / jnp.sqrt(jnp.maximum(count, 1.0))
    denom = jnp.maximum(magnitude, floor_val)
    row = lax.broadcasted_iota(jnp.int32, unit_ref.shape, 0)
    unit_ref[...] = jnp.where(row == 0, e_re / denom, e_im / denom) * (1.0 / (LA * LR))


def finish_kernel(three_ref, res_ref, before_ref, looks_ref, unit_ref, out_ref, sums_ref):
    middle_n = before_ref.shape[1]
    edge = LAG // LA
    u_re, u_im = unit_ref[0:1], unit_ref[1:2]
    totals = look_sums(((3, three_ref),), res_ref, out_ref.shape[3])
    for part, total in enumerate(totals):
        sums_ref[part] = total + before_ref[part]
    for at, held in (
        (0, looks_ref[:, :edge]),
        (edge, [look_rows(sums_ref, part, 0, middle_n) for part in range(2)]),
        (edge + middle_n // LA, looks_ref[:, edge:]),
    ):
        rows = slice(at, at + held[0].shape[0])
        out_ref[0, 0, rows] = held[0] * u_re + held[1] * u_im
        out_ref[0, 1, rows] = held[1] * u_re - held[0] * u_im


def call(kernel, outs, scratch, cost, *args):
    vmem = pl.BlockSpec(memory_space=pltpu.VMEM)
    return pl.pallas_call(
        kernel,
        out_shape=outs,
        in_specs=[vmem] * len(args),
        out_specs=jax.tree.map(lambda _: vmem, outs),
        scratch_shapes=scratch,
        compiler_params=pltpu.CompilerParams(vmem_limit_bytes=VMEM_LIMIT),
        cost_estimate=pl.CostEstimate(flops=cost[0], bytes_accessed=cost[1], transcendentals=0),
    )(*args)


def ring(value, axis, step):
    count = lax.axis_size(axis)
    return lax.ppermute(value, axis, [(at, (at + step) % count) for at in range(count)])


def swap(value, axis, step):
    return lax.ppermute(value, axis, [(at, at ^ step) for at in range(lax.axis_size(axis))])


def fused(secondary, primary, margin_mask, az_off, rg_off, az_frac, rg_frac):
    _, _, rows_n, cols_n = secondary.shape
    width = primary.shape[2]
    dates_n = lax.axis_size("date")
    tiles_n = lax.axis_size("tile")
    bf16, f32 = jnp.bfloat16, jnp.float32
    shape = jax.ShapeDtypeStruct
    looks_n = cols_n // LR
    middle_n = rows_n - 2 * LAG
    edges = jnp.concatenate([primary[:, :LAG], primary[:, rows_n - LAG :]], axis=1)
    edges_two = swap(edges, "date", 2)
    one = swap(primary, "date", 1)
    halo = shape((2, HALO, cols_n), bf16)
    down, up = call(cut_halo_kernel, (halo, halo), [], (0, 0), secondary)
    low = ring(down, "tile", 1)
    high = ring(up, "tile", -1)
    az_band, rg_band = call(
        bands_kernel,
        (shape((BAND, BAND + 2 * HALO), bf16), shape((3, LANE, LANE), bf16)),
        [],
        (0, 0),
        az_off, rg_off, az_frac, rg_frac,
    )
    passed = call(
        relay_kernel, shape(edges.shape, bf16), [], (2 * 10**9, 0), edges_two, edges
    )
    edges_three = swap(passed, "date", 1)
    middle = call(
        cut_middle_kernel,
        shape((2, middle_n + 16, width), bf16),
        [],
        (0, 0),
        primary, edges_two,
    )
    weight = jnp.broadcast_to(margin_mask[rows_n - LAG :].astype(f32)[:, None], (LAG, LANE))
    res = call(
        resample_kernel,
        shape((dates_n, 2, rows_n, width), bf16),
        [pltpu.VMEM((2, rows_n, cols_n), bf16)],
        (0, 0),
        secondary, low, high, az_band, rg_band,
    )
    two = swap(middle, "date", 2)
    margin = shape((2, LAG, cols_n), bf16)
    first, last, looks = call(
        margin_kernel,
        (margin, margin, shape((2, 2 * LAG // LA, looks_n), f32)),
        [pltpu.VMEM((2, 2 * LAG, looks_n), f32)],
        (0, 0),
        primary, one, edges_two, edges_three, res,
    )
    later = ring(first, "tile", -1)
    stats = call(
        stats_kernel,
        shape((8, LANE), f32),
        [],
        (0, 0),
        last, later, weight,
    )
    before = call(
        middle_kernel,
        shape((2, middle_n, looks_n), f32),
        [],
        (2 * 2 * middle_n * cols_n * looks_n, 8 * rows_n * cols_n),
        primary, one, two, res,
    )
    other = swap(stats, "tile", 1)
    block = shape((2, middle_n, width), bf16)
    relayed = call(relay_kernel, block, [], (0, 0), two, other)
    three = swap(relayed, "date", 1)
    stride = 2
    while stride < tiles_n:
        stats = stats + other
        other = swap(stats, "tile", stride)
        stride *= 2
    unit = call(unit_kernel, shape((8, LANE), f32), [], (0, 0), stats, other)
    return call(
        finish_kernel,
        shape((1, 2, rows_n // LA, looks_n), f32),
        [pltpu.VMEM((2, middle_n, looks_n), f32)],
        (2 * middle_n * cols_n * looks_n, 4 * rows_n * cols_n),
        three, res, before, looks, unit,
    )


def padded(block, sides, width):
    for axis, dim in sides:
        low = passed_along(
            lax.slice_in_dim(block, block.shape[dim] - width, None, axis=dim), axis, 1
        )
        high = passed_along(lax.slice_in_dim(block, 0, width, axis=dim), axis, -1)
        block = jnp.concatenate([low, block, high], axis=dim)
    return block


def band_taps(offset, frac):
    inside = (offset >= -3) & (offset <= 4)
    return jnp.where(inside, window(offset.astype(jnp.float32) - frac), 0.0).astype(jnp.bfloat16)


def multilook(values):
    depth, rows_n, cols_n = values.shape
    return values.reshape(depth, rows_n // LA, LA, cols_n // LR, LR).mean(axis=(2, 4))


def plain(secondary, primary, margin_mask, az_off, rg_off, az_frac, rg_frac):
    rim_rows = KA + 4
    block_cols = 256
    image = secondary[0]
    rows_n = image.shape[1]
    cols_n = image.shape[2]
    extended = padded(image, (("tile", 1),), rim_rows)
    row_out = lax.broadcasted_iota(jnp.int32, (rows_n, rows_n + 2 * rim_rows), 0)
    row_in = lax.broadcasted_iota(jnp.int32, (rows_n, rows_n + 2 * rim_rows), 1)
    azim_taps = band_taps(row_in - row_out - az_off[0, 0] - rim_rows, az_frac[0, 0])
    azim = jnp.einsum(
        "im,kmc->kic", azim_taps, extended, preferred_element_type=jnp.float32
    ).astype(jnp.bfloat16)
    blocks_n = cols_n // block_cols
    col_pad = jnp.pad(azim, ((0, 0), (0, 0), (block_cols // 2, block_cols // 2)))
    pieces = col_pad.reshape(2, rows_n, blocks_n + 1, block_cols)
    inputs = jnp.concatenate([pieces[:, :, :-1], pieces[:, :, 1:]], axis=3)
    col_in = lax.broadcasted_iota(jnp.int32, (2 * block_cols, block_cols), 0)
    col_out = lax.broadcasted_iota(jnp.int32, (2 * block_cols, block_cols), 1)
    range_taps = band_taps(col_in - block_cols // 2 - col_out - rg_off[0, 0], rg_frac[0, 0])
    resampled = jnp.einsum("kibm,mn->kibn", inputs, range_taps, preferred_element_type=jnp.float32)
    resampled = resampled.reshape(2, rows_n, cols_n).astype(jnp.bfloat16)
    prim = lax.all_gather(primary, "date", axis=2, tiled=True)[None]
    sec_f = resampled[None].astype(jnp.float32)
    prim_f = prim.astype(jnp.float32)
    ifg_re = prim_f[:, 0] * sec_f[:, 0] + prim_f[:, 1] * sec_f[:, 1]
    ifg_im = prim_f[:, 1] * sec_f[:, 0] - prim_f[:, 0] * sec_f[:, 1]
    interf = jnp.stack((ifg_re, ifg_im), axis=1)
    upcoming = passed_along(interf[:, :, :LAG, :], "tile", -1)
    later = jnp.concatenate([interf[:, :, LAG:, :], upcoming], axis=2)
    l_re = later[:, 0]
    l_im = later[:, 1]
    weight = margin_mask.astype(jnp.float32)[None, :, None]
    e_re = jnp.sum(weight * (ifg_re * l_re + ifg_im * l_im), axis=(1, 2))
    e_im = jnp.sum(weight * (ifg_im * l_re - ifg_re * l_im), axis=(1, 2))
    power = jnp.sum(
        weight * 0.5 * (ifg_re * ifg_re + ifg_im * ifg_im + l_re * l_re + l_im * l_im), axis=(1, 2)
    )
    count = jnp.zeros_like(e_re) + jnp.sum(margin_mask.astype(jnp.float32)) * interf.shape[3]
    stats = jnp.stack((e_re, e_im, power, count), axis=1)
    totals = lax.psum(stats, "tile")
    magnitude = jnp.sqrt(totals[:, 0] * totals[:, 0] + totals[:, 1] * totals[:, 1])
    floor_val = (totals[:, 2] + 1e-06) / jnp.sqrt(jnp.maximum(totals[:, 3], 1.0))
    denom = jnp.maximum(magnitude, floor_val)
    u_re = (totals[:, 0] / denom)[:, None, None]
    u_im = (totals[:, 1] / denom)[:, None, None]
    c_re = multilook(ifg_re * u_re + ifg_im * u_im)
    c_im = multilook(ifg_im * u_re - ifg_re * u_im)
    return jnp.stack((c_re, c_im), axis=1)


def shards(secondary, primary, *rest):
    rows_n, width = primary.shape[1:]
    fits = rows_n % BAND == 0 and rows_n > 2 * LAG + BAND and width % LANE == 0
    tiles_n = lax.axis_size("tile")
    fits = fits and lax.axis_size("date") == 4 and tiles_n & (tiles_n - 1) == 0
    return (fused if fits else plain)(secondary, primary, *rest)


def solution(mesh):
    return jax.shard_map(
        shards,
        mesh=mesh,
        in_specs=(
            P("date", None, "tile", None),
            P(None, "tile", "date"),
            P("tile"),
            P("date", "tile"),
            P("date", "tile"),
            P("date", "tile"),
            P("date", "tile"),
        ),
        out_specs=P("date", None, "tile", None),
        check_vma=False,
    )
```

```python
import functools

import jax
import jax.numpy as jnp
from jax import lax
from jax.experimental import pallas as pl
from jax.experimental.pallas import tpu as pltpu
from jax.sharding import PartitionSpec as P

KA = 16
LAG = 64
LA = 2
LR = 8
LANE = 128
BAND = 128
HALO = 32
VMEM_LIMIT = 40 * 1024 * 1024


def passed_along(value, axis, steps):
    count = lax.axis_size(axis)
    initial, last = (max(0, -steps), min(count, count - steps))
    return lax.ppermute(value, axis, [(source, source + steps) for source in range(initial, last)])


def window(dist):
    return jnp.sinc(dist) * (0.5 + 0.5 * jnp.cos(jnp.pi * dist / 4.0))


def tap_rows(frac):
    dist = lax.broadcasted_iota(jnp.int32, (8, LANE), 0).astype(jnp.float32) - 3.0 - frac
    angle = jnp.pi * dist
    sinc = jnp.where(dist == 0.0, 1.0, jnp.sin(angle) / jnp.where(dist == 0.0, 1.0, angle))
    taps = sinc * (0.5 + 0.5 * jnp.cos(jnp.pi * dist / 4.0))
    return taps.astype(jnp.bfloat16).astype(jnp.float32)


def band(shape, distance, taps):
    total = jnp.zeros(shape, jnp.float32)
    for j in range(8):
        total = jnp.where(distance == j - 3, taps[j : j + 1, :1], total)
    return total.astype(jnp.bfloat16)


def cut_halo_kernel(sec_ref, down_ref, up_ref):
    rows_n = sec_ref.shape[2]
    down_ref[...] = sec_ref[0, :, rows_n - HALO :]
    up_ref[...] = sec_ref[0, :, :HALO]


def cut_middle_kernel(prim_ref, *refs):
    cut_ref = refs[-1]
    cut_ref[...] = prim_ref[:, LAG : LAG + cut_ref.shape[1]]


def relay_kernel(block_ref, *refs):
    out_ref = refs[-1]
    out_ref[...] = block_ref[:, : out_ref.shape[1]]


def bands_kernel(ao_ref, ro_ref, af_ref, rf_ref, az_ref, rg_ref):
    shape = az_ref.shape
    offset = lax.broadcasted_iota(jnp.int32, shape, 1) - lax.broadcasted_iota(jnp.int32, shape, 0)
    az_ref[...] = band(shape, offset - HALO - ao_ref[...], tap_rows(af_ref[...]))
    square = rg_ref.shape[1:]
    offset = lax.broadcasted_iota(jnp.int32, square, 0) - lax.broadcasted_iota(jnp.int32, square, 1)
    taps = tap_rows(rf_ref[...])
    for at, shift in enumerate((-LANE, 0, LANE)):
        rg_ref[at] = band(square, offset + shift - ro_ref[...], taps)


def resample_kernel(sec_ref, low_ref, high_ref, az_ref, rg_ref, out_ref, azim_ref):
    rows_n, cols_n = sec_ref.shape[2:]
    az_band = az_ref[...]
    here, tiles_n = lax.axis_index("tile"), lax.axis_size("tile")
    none = jnp.zeros(low_ref.shape[1:], jnp.bfloat16)
    for part in range(2):
        for start in range(0, rows_n, BAND):
            pieces = []
            if start == 0:
                pieces.append(jnp.where(here == 0, none, low_ref[part]))
            pieces.append(sec_ref[0, part, max(0, start - HALO) : min(rows_n, start + BAND + HALO)])
            if start + BAND == rows_n:
                pieces.append(jnp.where(here == tiles_n - 1, none, high_ref[part]))
            rows = jnp.concatenate(pieces, axis=0) if len(pieces) > 1 else pieces[0]
            azim_ref[part, start : start + BAND] = jnp.dot(
                az_band, rows, preferred_element_type=jnp.float32
            ).astype(jnp.bfloat16)

    before, same, after = [rg_ref[at] for at in range(3)]
    none = jnp.zeros((LANE, LANE), jnp.bfloat16)
    blocks_n, _, _, width = out_ref.shape
    lanes_n = width // LANE
    columns = []
    for lane in range(lanes_n):
        column = [none] * (lanes_n + 2)
        column[lane], column[lane + 1], column[lane + 2] = before, same, after
        columns.append(jnp.concatenate(column, axis=0))
    rg_band = jnp.concatenate(columns, axis=1)
    for block in range(blocks_n):
        first = block * width - LANE
        last = (block + 1) * width + LANE
        taken = slice(max(first, 0), min(last, cols_n))
        used = rg_band[taken.start - first : taken.stop - first]
        for part in range(2):
            out_ref[block, part] = jnp.dot(
                azim_ref[part, :, taken], used, preferred_element_type=jnp.float32
            ).astype(jnp.bfloat16)


def interfere(prim_re, prim_im, sec_re, sec_im):
    p_re, p_im = prim_re.astype(jnp.float32), prim_im.astype(jnp.float32)
    s_re, s_im = sec_re.astype(jnp.float32), sec_im.astype(jnp.float32)
    return p_re * s_re + p_im * s_im, p_im * s_re - p_re * s_im


def look_columns(width, block, looks_n):
    shape = (width, looks_n)
    col = lax.broadcasted_iota(jnp.int32, shape, 0) + block * width
    look = lax.broadcasted_iota(jnp.int32, shape, 1) * LR
    return jnp.where((col >= look) & (col < look + LR), 1.0, 0.0).astype(jnp.bfloat16)


def look_rows(sums_ref, part, start, rows_n):
    count = rows_n // LA
    total = sums_ref[part, pl.ds(start, count, LA)]
    for row in range(1, LA):
        total = total + sums_ref[part, pl.ds(start + row, count, LA)]
    return total


def margin_kernel(
    own_ref, one_ref, two_ref, three_ref, res_ref, first_ref, last_ref, looks_ref, sums_ref
):
    here = lax.axis_index("date")
    _, _, rows_n, width = res_ref.shape
    whole, edges = (0, rows_n - LAG), (0, LAG)
    looks_n = looks_ref.shape[2]
    totals = [None, None]
    for step, (prim_ref, starts) in enumerate(
        ((own_ref, whole), (one_ref, edges), (two_ref, edges), (three_ref, edges))
    ):
        block = jnp.bitwise_xor(here, step)
        select = look_columns(width, block, looks_n)
        columns = pl.ds(pl.multiple_of(block * width, width), width)
        halves = []
        for held, start, target in zip(starts, whole, (first_ref, last_ref)):
            pair = interfere(
                prim_ref[0, held : held + LAG],
                prim_ref[1, held : held + LAG],
                res_ref[block, 0, start : start + LAG],
                res_ref[block, 1, start : start + LAG],
            )
            pair = [value.astype(jnp.bfloat16) for value in pair]
            for part in range(2):
                target[part, :, columns] = pair[part]
            halves.append(pair)
        for part in range(2):
            both = jnp.concatenate([halves[0][part], halves[1][part]], axis=0)
            summed = jnp.dot(both, select, preferred_element_type=jnp.float32)
            totals[part] = summed if step == 0 else totals[part] + summed
    for part in range(2):
        sums_ref[part] = totals[part]
        looks_ref[part] = look_rows(sums_ref, part, 0, 2 * LAG)


def stats_kernel(last_ref, later_ref, weight_ref, stats_ref):
    cols_n = last_ref.shape[2]
    weight = weight_ref[...]
    i_re, i_im = last_ref[0].astype(jnp.float32), last_ref[1].astype(jnp.float32)
    inside = jnp.where(lax.axis_index("tile") == lax.axis_size("tile") - 1, 0.0, 1.0)
    l_re, l_im = [later_ref[part].astype(jnp.float32) * inside for part in range(2)]
    values = (
        i_re * l_re + i_im * l_im,
        i_im * l_re - i_re * l_im,
        0.5 * (i_re * i_re + i_im * i_im + l_re * l_re + l_im * l_im),
    )
    rows = []
    for value in values:
        folded = value[:, :LANE]
        for start in range(LANE, cols_n, LANE):
            folded = folded + value[:, start : start + LANE]
        rows.append(jnp.sum(folded * weight, axis=0, keepdims=True))
    rows.append(jnp.sum(weight, axis=0, keepdims=True) * (cols_n // LANE))
    rows.append(jnp.zeros((4, LANE), jnp.float32))
    stats_ref[...] = jnp.concatenate(rows, axis=0)


def look_sums(pieces, res_ref, looks_n):
    here = lax.axis_index("date")
    _, _, rows_n, width = res_ref.shape
    middle_n = rows_n - 2 * LAG
    totals = [None, None]
    for at, (step, prim_ref) in enumerate(pieces):
        block = jnp.bitwise_xor(here, step)
        first = LAG if prim_ref.shape[1] == rows_n else 0
        select = look_columns(width, block, looks_n)
        pair = interfere(
            prim_ref[0, first : first + middle_n],
            prim_ref[1, first : first + middle_n],
            res_ref[block, 0, LAG : rows_n - LAG],
            res_ref[block, 1, LAG : rows_n - LAG],
        )
        for part in range(2):
            summed = jnp.dot(
                pair[part].astype(jnp.bfloat16), select, preferred_element_type=jnp.float32
            )
            totals[part] = summed if at == 0 else totals[part] + summed
    return totals


def middle_kernel(own_ref, one_ref, two_ref, res_ref, out_ref):
    pieces = ((0, own_ref), (1, one_ref), (2, two_ref))
    for part, total in enumerate(look_sums(pieces, res_ref, out_ref.shape[2])):
        out_ref[part] = total


def add_kernel(mine_ref, other_ref, *refs):
    refs[-1][...] = mine_ref[...] + other_ref[...]


def unit_kernel(mine_ref, other_ref, unit_ref):
    stats = jnp.sum(mine_ref[...] + other_ref[...], axis=1, keepdims=True)
    e_re, e_im, power, count = [stats[row : row + 1] for row in range(4)]
    magnitude = jnp.sqrt(e_re * e_re + e_im * e_im)
    floor_val = (power + 1e-06) / jnp.sqrt(jnp.maximum(count, 1.0))
    denom = jnp.maximum(magnitude, floor_val)
    row = lax.broadcasted_iota(jnp.int32, unit_ref.shape, 0)
    unit_ref[...] = jnp.where(row == 0, e_re / denom, e_im / denom) * (1.0 / (LA * LR))


def finish_kernel(three_ref, res_ref, before_ref, looks_ref, unit_ref, out_ref, sums_ref):
    middle_n = before_ref.shape[1]
    edge = LAG // LA
    u_re, u_im = unit_ref[0:1], unit_ref[1:2]
    totals = look_sums(((3, three_ref),), res_ref, out_ref.shape[3])
    for part, total in enumerate(totals):
        sums_ref[part] = total + before_ref[part]
    for at, held in (
        (0, looks_ref[:, :edge]),
        (edge, [look_rows(sums_ref, part, 0, middle_n) for part in range(2)]),
        (edge + middle_n // LA, looks_ref[:, edge:]),
    ):
        rows = slice(at, at + held[0].shape[0])
        out_ref[0, 0, rows] = held[0] * u_re + held[1] * u_im
        out_ref[0, 1, rows] = held[1] * u_re - held[0] * u_im


def call(kernel, outs, scratch, cost, *args):
    vmem = pl.BlockSpec(memory_space=pltpu.VMEM)
    return pl.pallas_call(
        kernel,
        out_shape=outs,
        in_specs=[vmem] * len(args),
        out_specs=jax.tree.map(lambda _: vmem, outs),
        scratch_shapes=scratch,
        compiler_params=pltpu.CompilerParams(vmem_limit_bytes=VMEM_LIMIT),
        cost_estimate=pl.CostEstimate(flops=cost[0], bytes_accessed=cost[1], transcendentals=0),
    )(*args)


def ring(value, axis, step):
    count = lax.axis_size(axis)
    return lax.ppermute(value, axis, [(at, (at + step) % count) for at in range(count)])


def swap(value, axis, step):
    return lax.ppermute(value, axis, [(at, at ^ step) for at in range(lax.axis_size(axis))])


def fused(secondary, primary, margin_mask, az_off, rg_off, az_frac, rg_frac):
    _, _, rows_n, cols_n = secondary.shape
    width = primary.shape[2]
    dates_n = lax.axis_size("date")
    tiles_n = lax.axis_size("tile")
    bf16, f32 = jnp.bfloat16, jnp.float32
    shape = jax.ShapeDtypeStruct
    looks_n = cols_n // LR
    middle_n = rows_n - 2 * LAG
    edges = jnp.concatenate([primary[:, :LAG], primary[:, rows_n - LAG :]], axis=1)
    edges_two = swap(edges, "date", 2)
    edges_one = swap(edges, "date", 1)
    down, up = secondary[0, :, rows_n - HALO :], secondary[0, :, :HALO]
    low = ring(down, "tile", 1)
    high = ring(up, "tile", -1)
    az_band, rg_band = call(
        bands_kernel,
        (shape((BAND, BAND + 2 * HALO), bf16), shape((3, LANE, LANE), bf16)),
        [],
        (0, 0),
        az_off, rg_off, az_frac, rg_frac,
    )
    passed = call(
        relay_kernel, shape(edges.shape, bf16), [], (0, 0), edges_two, edges_one
    )
    edges_three = swap(passed, "date", 1)
    middle = call(
        cut_middle_kernel,
        shape((2, middle_n + 16, width), bf16),
        [],
        (0, 0),
        primary, edges_two,
    )
    weight = jnp.broadcast_to(margin_mask[rows_n - LAG :].astype(f32)[:, None], (LAG, LANE))
    res = call(
        resample_kernel,
        shape((dates_n, 2, rows_n, width), bf16),
        [pltpu.VMEM((2, rows_n, cols_n), bf16)],
        (0, 0),
        secondary, low, high, az_band, rg_band,
    )
    two, one = [swap(middle, "date", step) for step in (2, 1)]
    margin = shape((2, LAG, cols_n), bf16)
    first, last, looks = call(
        margin_kernel,
        (margin, margin, shape((2, 2 * LAG // LA, looks_n), f32)),
        [pltpu.VMEM((2, 2 * LAG, looks_n), f32)],
        (0, 0),
        primary, edges_one, edges_two, edges_three, res,
    )
    later = ring(first, "tile", -1)
    stats = call(
        stats_kernel,
        shape((8, LANE), f32),
        [],
        (0, 0),
        last, later, weight,
    )
    before = call(
        middle_kernel,
        shape((2, middle_n, looks_n), f32),
        [],
        (3 * 10**9, 8 * rows_n * cols_n),
        primary, one, two, res,
    )
    other = swap(stats, "tile", 1)
    block = shape((2, middle_n, width), bf16)
    relayed = call(relay_kernel, block, [], (0, 0), two, other)
    three = swap(relayed, "date", 1)
    stats = call(add_kernel, shape((8, LANE), f32), [], (0, 0), stats, other, one)
    other = swap(stats, "tile", 2)
    stride = 4
    while stride < tiles_n:
        stats = stats + other
        other = swap(stats, "tile", stride)
        stride *= 2
    unit = call(unit_kernel, shape((8, LANE), f32), [], (0, 0), stats, other)
    return call(
        finish_kernel,
        shape((1, 2, rows_n // LA, looks_n), f32),
        [pltpu.VMEM((2, middle_n, looks_n), f32)],
        (2 * middle_n * cols_n * looks_n, 4 * rows_n * cols_n),
        three, res, before, looks, unit,
    )


def padded(block, sides, width):
    for axis, dim in sides:
        low = passed_along(
            lax.slice_in_dim(block, block.shape[dim] - width, None, axis=dim), axis, 1
        )
        high = passed_along(lax.slice_in_dim(block, 0, width, axis=dim), axis, -1)
        block = jnp.concatenate([low, block, high], axis=dim)
    return block


def band_taps(offset, frac):
    inside = (offset >= -3) & (offset <= 4)
    return jnp.where(inside, window(offset.astype(jnp.float32) - frac), 0.0).astype(jnp.bfloat16)


def multilook(values):
    depth, rows_n, cols_n = values.shape
    return values.reshape(depth, rows_n // LA, LA, cols_n // LR, LR).mean(axis=(2, 4))


def plain(secondary, primary, margin_mask, az_off, rg_off, az_frac, rg_frac):
    rim_rows = KA + 4
    block_cols = 256
    image = secondary[0]
    rows_n = image.shape[1]
    cols_n = image.shape[2]
    extended = padded(image, (("tile", 1),), rim_rows)
    row_out = lax.broadcasted_iota(jnp.int32, (rows_n, rows_n + 2 * rim_rows), 0)
    row_in = lax.broadcasted_iota(jnp.int32, (rows_n, rows_n + 2 * rim_rows), 1)
    azim_taps = band_taps(row_in - row_out - az_off[0, 0] - rim_rows, az_frac[0, 0])
    azim = jnp.einsum(
        "im,kmc->kic", azim_taps, extended, preferred_element_type=jnp.float32
    ).astype(jnp.bfloat16)
    blocks_n = cols_n // block_cols
    col_pad = jnp.pad(azim, ((0, 0), (0, 0), (block_cols // 2, block_cols // 2)))
    pieces = col_pad.reshape(2, rows_n, blocks_n + 1, block_cols)
    inputs = jnp.concatenate([pieces[:, :, :-1], pieces[:, :, 1:]], axis=3)
    col_in = lax.broadcasted_iota(jnp.int32, (2 * block_cols, block_cols), 0)
    col_out = lax.broadcasted_iota(jnp.int32, (2 * block_cols, block_cols), 1)
    range_taps = band_taps(col_in - block_cols // 2 - col_out - rg_off[0, 0], rg_frac[0, 0])
    resampled = jnp.einsum("kibm,mn->kibn", inputs, range_taps, preferred_element_type=jnp.float32)
    resampled = resampled.reshape(2, rows_n, cols_n).astype(jnp.bfloat16)
    prim = lax.all_gather(primary, "date", axis=2, tiled=True)[None]
    sec_f = resampled[None].astype(jnp.float32)
    prim_f = prim.astype(jnp.float32)
    ifg_re = prim_f[:, 0] * sec_f[:, 0] + prim_f[:, 1] * sec_f[:, 1]
    ifg_im = prim_f[:, 1] * sec_f[:, 0] - prim_f[:, 0] * sec_f[:, 1]
    interf = jnp.stack((ifg_re, ifg_im), axis=1)
    upcoming = passed_along(interf[:, :, :LAG, :], "tile", -1)
    later = jnp.concatenate([interf[:, :, LAG:, :], upcoming], axis=2)
    l_re = later[:, 0]
    l_im = later[:, 1]
    weight = margin_mask.astype(jnp.float32)[None, :, None]
    e_re = jnp.sum(weight * (ifg_re * l_re + ifg_im * l_im), axis=(1, 2))
    e_im = jnp.sum(weight * (ifg_im * l_re - ifg_re * l_im), axis=(1, 2))
    power = jnp.sum(
        weight * 0.5 * (ifg_re * ifg_re + ifg_im * ifg_im + l_re * l_re + l_im * l_im), axis=(1, 2)
    )
    count = jnp.zeros_like(e_re) + jnp.sum(margin_mask.astype(jnp.float32)) * interf.shape[3]
    stats = jnp.stack((e_re, e_im, power, count), axis=1)
    totals = lax.psum(stats, "tile")
    magnitude = jnp.sqrt(totals[:, 0] * totals[:, 0] + totals[:, 1] * totals[:, 1])
    floor_val = (totals[:, 2] + 1e-06) / jnp.sqrt(jnp.maximum(totals[:, 3], 1.0))
    denom = jnp.maximum(magnitude, floor_val)
    u_re = (totals[:, 0] / denom)[:, None, None]
    u_im = (totals[:, 1] / denom)[:, None, None]
    c_re = multilook(ifg_re * u_re + ifg_im * u_im)
    c_im = multilook(ifg_im * u_re - ifg_re * u_im)
    return jnp.stack((c_re, c_im), axis=1)


def shards(secondary, primary, *rest):
    rows_n, width = primary.shape[1:]
    fits = rows_n % BAND == 0 and rows_n > 2 * LAG + BAND and width % LANE == 0
    tiles_n = lax.axis_size("tile")
    fits = fits and lax.axis_size("date") == 4 and tiles_n & (tiles_n - 1) == 0
    return (fused if fits else plain)(secondary, primary, *rest)


def solution(mesh):
    return jax.shard_map(
        shards,
        mesh=mesh,
        in_specs=(
            P("date", None, "tile", None),
            P(None, "tile", "date"),
            P("tile"),
            P("date", "tile"),
            P("date", "tile"),
            P("date", "tile"),
            P("date", "tile"),
        ),
        out_specs=P("date", None, "tile", None),
        check_vma=False,
    )
```

```python
import functools

import jax
import jax.numpy as jnp
from jax import lax
from jax.experimental import pallas as pl
from jax.experimental.pallas import tpu as pltpu
from jax.sharding import PartitionSpec as P

KA = 16
LAG = 64
LA = 2
LR = 8
LANE = 128
BAND = 128
HALO = 32
VMEM_LIMIT = 40 * 1024 * 1024


def passed_along(value, axis, steps):
    count = lax.axis_size(axis)
    initial, last = (max(0, -steps), min(count, count - steps))
    return lax.ppermute(value, axis, [(source, source + steps) for source in range(initial, last)])


def window(dist):
    return jnp.sinc(dist) * (0.5 + 0.5 * jnp.cos(jnp.pi * dist / 4.0))


def tap_rows(frac):
    dist = lax.broadcasted_iota(jnp.int32, (8, LANE), 0).astype(jnp.float32) - 3.0 - frac
    angle = jnp.pi * dist
    sinc = jnp.where(dist == 0.0, 1.0, jnp.sin(angle) / jnp.where(dist == 0.0, 1.0, angle))
    taps = sinc * (0.5 + 0.5 * jnp.cos(jnp.pi * dist / 4.0))
    return taps.astype(jnp.bfloat16).astype(jnp.float32)


def band(shape, distance, taps):
    total = jnp.zeros(shape, jnp.float32)
    for j in range(8):
        total = jnp.where(distance == j - 3, taps[j : j + 1, :1], total)
    return total.astype(jnp.bfloat16)


def cut_middle_kernel(prim_ref, *refs):
    cut_ref = refs[-1]
    cut_ref[...] = prim_ref[:, LAG : LAG + cut_ref.shape[1]]


def relay_kernel(block_ref, *refs):
    out_ref = refs[-1]
    out_ref[...] = block_ref[:, : out_ref.shape[1]]


def azimuth_kernel(off_ref, frac_ref, out_ref):
    shape = out_ref.shape
    offset = lax.broadcasted_iota(jnp.int32, shape, 1) - lax.broadcasted_iota(jnp.int32, shape, 0)
    out_ref[...] = band(shape, offset - HALO - off_ref[...], tap_rows(frac_ref[...]))


def range_kernel(off_ref, frac_ref, out_ref):
    square = out_ref.shape[1:]
    offset = lax.broadcasted_iota(jnp.int32, square, 0) - lax.broadcasted_iota(jnp.int32, square, 1)
    taps = tap_rows(frac_ref[...])
    for at, shift in enumerate((-LANE, 0, LANE)):
        out_ref[at] = band(square, offset + shift - off_ref[...], taps)


def resample_kernel(sec_ref, low_ref, high_ref, az_ref, rg_ref, out_ref, azim_ref):
    rows_n, cols_n = sec_ref.shape[2:]
    az_band = az_ref[...]
    here, tiles_n = lax.axis_index("tile"), lax.axis_size("tile")
    none = jnp.zeros(low_ref.shape[1:], jnp.bfloat16)
    for part in range(2):
        for start in range(0, rows_n, BAND):
            pieces = []
            if start == 0:
                pieces.append(jnp.where(here == 0, none, low_ref[part]))
            pieces.append(sec_ref[0, part, max(0, start - HALO) : min(rows_n, start + BAND + HALO)])
            if start + BAND == rows_n:
                pieces.append(jnp.where(here == tiles_n - 1, none, high_ref[part]))
            rows = jnp.concatenate(pieces, axis=0) if len(pieces) > 1 else pieces[0]
            azim_ref[part, start : start + BAND] = jnp.dot(
                az_band, rows, preferred_element_type=jnp.float32
            ).astype(jnp.bfloat16)

    before, same, after = [rg_ref[at] for at in range(3)]
    none = jnp.zeros((LANE, LANE), jnp.bfloat16)
    blocks_n, _, _, width = out_ref.shape
    lanes_n = width // LANE
    columns = []
    for lane in range(lanes_n):
        column = [none] * (lanes_n + 2)
        column[lane], column[lane + 1], column[lane + 2] = before, same, after
        columns.append(jnp.concatenate(column, axis=0))
    rg_band = jnp.concatenate(columns, axis=1)
    for block in range(blocks_n):
        first = block * width - LANE
        last = (block + 1) * width + LANE
        taken = slice(max(first, 0), min(last, cols_n))
        used = rg_band[taken.start - first : taken.stop - first]
        for part in range(2):
            out_ref[block, part] = jnp.dot(
                azim_ref[part, :, taken], used, preferred_element_type=jnp.float32
            ).astype(jnp.bfloat16)


def interfere(prim_re, prim_im, sec_re, sec_im):
    p_re, p_im = prim_re.astype(jnp.float32), prim_im.astype(jnp.float32)
    s_re, s_im = sec_re.astype(jnp.float32), sec_im.astype(jnp.float32)
    return p_re * s_re + p_im * s_im, p_im * s_re - p_re * s_im


def look_columns(width, block, looks_n):
    shape = (width, looks_n)
    col = lax.broadcasted_iota(jnp.int32, shape, 0) + block * width
    look = lax.broadcasted_iota(jnp.int32, shape, 1) * LR
    return jnp.where((col >= look) & (col < look + LR), 1.0, 0.0).astype(jnp.bfloat16)


def look_rows(sums_ref, part, start, rows_n):
    count = rows_n // LA
    total = sums_ref[part, pl.ds(start, count, LA)]
    for row in range(1, LA):
        total = total + sums_ref[part, pl.ds(start + row, count, LA)]
    return total


def margin_kernel(
    own_ref, one_ref, two_ref, three_ref, res_ref, first_ref, last_ref, looks_ref, sums_ref
):
    here = lax.axis_index("date")
    _, _, rows_n, width = res_ref.shape
    whole, edges = (0, rows_n - LAG), (0, LAG)
    looks_n = looks_ref.shape[2]
    totals = [None, None]
    for step, (prim_ref, starts) in enumerate(
        ((own_ref, whole), (one_ref, edges), (two_ref, edges), (three_ref, edges))
    ):
        block = jnp.bitwise_xor(here, step)
        select = look_columns(width, block, looks_n)
        columns = pl.ds(pl.multiple_of(block * width, width), width)
        halves = []
        for held, start, target in zip(starts, whole, (first_ref, last_ref)):
            pair = interfere(
                prim_ref[0, held : held + LAG],
                prim_ref[1, held : held + LAG],
                res_ref[block, 0, start : start + LAG],
                res_ref[block, 1, start : start + LAG],
            )
            pair = [value.astype(jnp.bfloat16) for value in pair]
            for part in range(2):
                target[part, :, columns] = pair[part]
            halves.append(pair)
        for part in range(2):
            both = jnp.concatenate([halves[0][part], halves[1][part]], axis=0)
            summed = jnp.dot(both, select, preferred_element_type=jnp.float32)
            totals[part] = summed if step == 0 else totals[part] + summed
    for part in range(2):
        sums_ref[part] = totals[part]
        looks_ref[part] = look_rows(sums_ref, part, 0, 2 * LAG)


def stats_kernel(last_ref, later_ref, weight_ref, stats_ref):
    cols_n = last_ref.shape[2]
    weight = weight_ref[...]
    i_re, i_im = last_ref[0].astype(jnp.float32), last_ref[1].astype(jnp.float32)
    inside = jnp.where(lax.axis_index("tile") == lax.axis_size("tile") - 1, 0.0, 1.0)
    l_re, l_im = [later_ref[part].astype(jnp.float32) * inside for part in range(2)]
    values = (
        i_re * l_re + i_im * l_im,
        i_im * l_re - i_re * l_im,
        0.5 * (i_re * i_re + i_im * i_im + l_re * l_re + l_im * l_im),
    )
    rows = []
    for value in values:
        folded = value[:, :LANE]
        for start in range(LANE, cols_n, LANE):
            folded = folded + value[:, start : start + LANE]
        rows.append(jnp.sum(folded * weight, axis=0, keepdims=True))
    rows.append(jnp.sum(weight, axis=0, keepdims=True) * (cols_n // LANE))
    rows.append(jnp.zeros((4, LANE), jnp.float32))
    stats_ref[...] = jnp.concatenate(rows, axis=0)


def look_sums(pieces, res_ref, looks_n):
    here = lax.axis_index("date")
    _, _, rows_n, width = res_ref.shape
    middle_n = rows_n - 2 * LAG
    totals = [None, None]
    for at, (step, prim_ref) in enumerate(pieces):
        block = jnp.bitwise_xor(here, step)
        first = LAG if prim_ref.shape[1] == rows_n else 0
        select = look_columns(width, block, looks_n)
        pair = interfere(
            prim_ref[0, first : first + middle_n],
            prim_ref[1, first : first + middle_n],
            res_ref[block, 0, LAG : rows_n - LAG],
            res_ref[block, 1, LAG : rows_n - LAG],
        )
        for part in range(2):
            summed = jnp.dot(
                pair[part].astype(jnp.bfloat16), select, preferred_element_type=jnp.float32
            )
            totals[part] = summed if at == 0 else totals[part] + summed
    return totals


def middle_kernel(own_ref, one_ref, two_ref, res_ref, out_ref):
    pieces = ((0, own_ref), (1, one_ref), (2, two_ref))
    for part, total in enumerate(look_sums(pieces, res_ref, out_ref.shape[2])):
        out_ref[part] = total


def unit_kernel(mine_ref, other_ref, unit_ref):
    stats = jnp.sum(mine_ref[...] + other_ref[...], axis=1, keepdims=True)
    e_re, e_im, power, count = [stats[row : row + 1] for row in range(4)]
    magnitude = jnp.sqrt(e_re * e_re + e_im * e_im)
    floor_val = (power + 1e-06) / jnp.sqrt(jnp.maximum(count, 1.0))
    denom = jnp.maximum(magnitude, floor_val)
    row = lax.broadcasted_iota(jnp.int32, unit_ref.shape, 0)
    unit_ref[...] = jnp.where(row == 0, e_re / denom, e_im / denom) * (1.0 / (LA * LR))


def finish_kernel(three_ref, res_ref, before_ref, looks_ref, unit_ref, out_ref, sums_ref):
    middle_n = before_ref.shape[1]
    edge = LAG // LA
    u_re, u_im = unit_ref[0:1], unit_ref[1:2]
    totals = look_sums(((3, three_ref),), res_ref, out_ref.shape[3])
    for part, total in enumerate(totals):
        sums_ref[part] = total + before_ref[part]
    for at, held in (
        (0, looks_ref[:, :edge]),
        (edge, [look_rows(sums_ref, part, 0, middle_n) for part in range(2)]),
        (edge + middle_n // LA, looks_ref[:, edge:]),
    ):
        rows = slice(at, at + held[0].shape[0])
        out_ref[0, 0, rows] = held[0] * u_re + held[1] * u_im
        out_ref[0, 1, rows] = held[1] * u_re - held[0] * u_im


def call(kernel, outs, scratch, cost, *args):
    vmem = pl.BlockSpec(memory_space=pltpu.VMEM)
    return pl.pallas_call(
        kernel,
        out_shape=outs,
        in_specs=[vmem] * len(args),
        out_specs=jax.tree.map(lambda _: vmem, outs),
        scratch_shapes=scratch,
        compiler_params=pltpu.CompilerParams(vmem_limit_bytes=VMEM_LIMIT),
        cost_estimate=pl.CostEstimate(flops=cost[0], bytes_accessed=cost[1], transcendentals=0),
    )(*args)


def ring(value, axis, step):
    count = lax.axis_size(axis)
    return lax.ppermute(value, axis, [(at, (at + step) % count) for at in range(count)])


def swap(value, axis, step):
    return lax.ppermute(value, axis, [(at, at ^ step) for at in range(lax.axis_size(axis))])


def fused(secondary, primary, margin_mask, az_off, rg_off, az_frac, rg_frac):
    _, _, rows_n, cols_n = secondary.shape
    width = primary.shape[2]
    dates_n = lax.axis_size("date")
    tiles_n = lax.axis_size("tile")
    bf16, f32 = jnp.bfloat16, jnp.float32
    shape = jax.ShapeDtypeStruct
    looks_n = cols_n // LR
    middle_n = rows_n - 2 * LAG
    edges = jnp.concatenate([primary[:, :LAG], primary[:, rows_n - LAG :]], axis=1)
    edges_two = swap(edges, "date", 2)
    edges_one = swap(edges, "date", 1)
    down, up = secondary[0, :, rows_n - HALO :], secondary[0, :, :HALO]
    low = ring(down, "tile", 1)
    high = ring(up, "tile", -1)
    az_band = call(
        azimuth_kernel, shape((BAND, BAND + 2 * HALO), bf16), [], (0, 0), az_off, az_frac
    )
    rg_band = call(range_kernel, shape((3, LANE, LANE), bf16), [], (0, 0), rg_off, rg_frac)
    passed = call(
        relay_kernel, shape(edges.shape, bf16), [], (0, 0), edges_two, edges_one, az_band
    )
    edges_three = swap(passed, "date", 1)
    middle = call(
        cut_middle_kernel,
        shape((2, middle_n + 16, width), bf16),
        [],
        (0, 0),
        primary, edges_two,
    )
    weight = jnp.broadcast_to(margin_mask[rows_n - LAG :].astype(f32)[:, None], (LAG, LANE))
    res = call(
        resample_kernel,
        shape((dates_n, 2, rows_n, width), bf16),
        [pltpu.VMEM((2, rows_n, cols_n), bf16)],
        (0, 0),
        secondary, low, high, az_band, rg_band,
    )
    two, one = [swap(middle, "date", step) for step in (2, 1)]
    margin = shape((2, LAG, cols_n), bf16)
    first, last, looks = call(
        margin_kernel,
        (margin, margin, shape((2, 2 * LAG // LA, looks_n), f32)),
        [pltpu.VMEM((2, 2 * LAG, looks_n), f32)],
        (0, 0),
        primary, edges_one, edges_two, edges_three, res,
    )
    later = ring(first, "tile", -1)
    stats = call(
        stats_kernel,
        shape((8, LANE), f32),
        [],
        (0, 0),
        last, later, weight,
    )
    before = call(
        middle_kernel,
        shape((2, middle_n, looks_n), f32),
        [],
        (2 * 2 * middle_n * cols_n * looks_n, 8 * rows_n * cols_n),
        primary, one, two, res,
    )
    other = swap(stats, "tile", 1)
    block = shape((2, middle_n, width), bf16)
    relayed = call(relay_kernel, block, [], (0, 0), two, other,one)
    three = swap(relayed, "date", 1)
    stride = 2
    while stride < tiles_n:
        stats = stats + other
        other = swap(stats, "tile", stride)
        stride *= 2
    unit = call(unit_kernel, shape((8, LANE), f32), [], (0, 0), stats, other)
    return call(
        finish_kernel,
        shape((1, 2, rows_n // LA, looks_n), f32),
        [pltpu.VMEM((2, middle_n, looks_n), f32)],
        (2 * middle_n * cols_n * looks_n, 4 * rows_n * cols_n),
        three, res, before, looks, unit,
    )


def padded(block, sides, width):
    for axis, dim in sides:
        low = passed_along(
            lax.slice_in_dim(block, block.shape[dim] - width, None, axis=dim), axis, 1
        )
        high = passed_along(lax.slice_in_dim(block, 0, width, axis=dim), axis, -1)
        block = jnp.concatenate([low, block, high], axis=dim)
    return block


def band_taps(offset, frac):
    inside = (offset >= -3) & (offset <= 4)
    return jnp.where(inside, window(offset.astype(jnp.float32) - frac), 0.0).astype(jnp.bfloat16)


def multilook(values):
    depth, rows_n, cols_n = values.shape
    return values.reshape(depth, rows_n // LA, LA, cols_n // LR, LR).mean(axis=(2, 4))


def plain(secondary, primary, margin_mask, az_off, rg_off, az_frac, rg_frac):
    rim_rows = KA + 4
    block_cols = 256
    image = secondary[0]
    rows_n = image.shape[1]
    cols_n = image.shape[2]
    extended = padded(image, (("tile", 1),), rim_rows)
    row_out = lax.broadcasted_iota(jnp.int32, (rows_n, rows_n + 2 * rim_rows), 0)
    row_in = lax.broadcasted_iota(jnp.int32, (rows_n, rows_n + 2 * rim_rows), 1)
    azim_taps = band_taps(row_in - row_out - az_off[0, 0] - rim_rows, az_frac[0, 0])
    azim = jnp.einsum(
        "im,kmc->kic", azim_taps, extended, preferred_element_type=jnp.float32
    ).astype(jnp.bfloat16)
    blocks_n = cols_n // block_cols
    col_pad = jnp.pad(azim, ((0, 0), (0, 0), (block_cols // 2, block_cols // 2)))
    pieces = col_pad.reshape(2, rows_n, blocks_n + 1, block_cols)
    inputs = jnp.concatenate([pieces[:, :, :-1], pieces[:, :, 1:]], axis=3)
    col_in = lax.broadcasted_iota(jnp.int32, (2 * block_cols, block_cols), 0)
    col_out = lax.broadcasted_iota(jnp.int32, (2 * block_cols, block_cols), 1)
    range_taps = band_taps(col_in - block_cols // 2 - col_out - rg_off[0, 0], rg_frac[0, 0])
    resampled = jnp.einsum("kibm,mn->kibn", inputs, range_taps, preferred_element_type=jnp.float32)
    resampled = resampled.reshape(2, rows_n, cols_n).astype(jnp.bfloat16)
    prim = lax.all_gather(primary, "date", axis=2, tiled=True)[None]
    sec_f = resampled[None].astype(jnp.float32)
    prim_f = prim.astype(jnp.float32)
    ifg_re = prim_f[:, 0] * sec_f[:, 0] + prim_f[:, 1] * sec_f[:, 1]
    ifg_im = prim_f[:, 1] * sec_f[:, 0] - prim_f[:, 0] * sec_f[:, 1]
    interf = jnp.stack((ifg_re, ifg_im), axis=1)
    upcoming = passed_along(interf[:, :, :LAG, :], "tile", -1)
    later = jnp.concatenate([interf[:, :, LAG:, :], upcoming], axis=2)
    l_re = later[:, 0]
    l_im = later[:, 1]
    weight = margin_mask.astype(jnp.float32)[None, :, None]
    e_re = jnp.sum(weight * (ifg_re * l_re + ifg_im * l_im), axis=(1, 2))
    e_im = jnp.sum(weight * (ifg_im * l_re - ifg_re * l_im), axis=(1, 2))
    power = jnp.sum(
        weight * 0.5 * (ifg_re * ifg_re + ifg_im * ifg_im + l_re * l_re + l_im * l_im), axis=(1, 2)
    )
    count = jnp.zeros_like(e_re) + jnp.sum(margin_mask.astype(jnp.float32)) * interf.shape[3]
    stats = jnp.stack((e_re, e_im, power, count), axis=1)
    totals = lax.psum(stats, "tile")
    magnitude = jnp.sqrt(totals[:, 0] * totals[:, 0] + totals[:, 1] * totals[:, 1])
    floor_val = (totals[:, 2] + 1e-06) / jnp.sqrt(jnp.maximum(totals[:, 3], 1.0))
    denom = jnp.maximum(magnitude, floor_val)
    u_re = (totals[:, 0] / denom)[:, None, None]
    u_im = (totals[:, 1] / denom)[:, None, None]
    c_re = multilook(ifg_re * u_re + ifg_im * u_im)
    c_im = multilook(ifg_im * u_re - ifg_re * u_im)
    return jnp.stack((c_re, c_im), axis=1)


def shards(secondary, primary, *rest):
    rows_n, width = primary.shape[1:]
    fits = rows_n % BAND == 0 and rows_n > 2 * LAG + BAND and width % LANE == 0
    tiles_n = lax.axis_size("tile")
    fits = fits and lax.axis_size("date") == 4 and tiles_n & (tiles_n - 1) == 0
    return (fused if fits else plain)(secondary, primary, *rest)


def solution(mesh):
    return jax.shard_map(
        shards,
        mesh=mesh,
        in_specs=(
            P("date", None, "tile", None),
            P(None, "tile", "date"),
            P("tile"),
            P("date", "tile"),
            P("date", "tile"),
            P("date", "tile"),
            P("date", "tile"),
        ),
        out_specs=P("date", None, "tile", None),
        check_vma=False,
    )
```

```python
import functools

import jax
import jax.numpy as jnp
from jax import lax
from jax.experimental import pallas as pl
from jax.experimental.pallas import tpu as pltpu
from jax.sharding import PartitionSpec as P

KA = 16
LAG = 64
LA = 2
LR = 8
LANE = 128
BAND = 128
HALO = 32
VMEM_LIMIT = 40 * 1024 * 1024


def passed_along(value, axis, steps):
    count = lax.axis_size(axis)
    initial, last = (max(0, -steps), min(count, count - steps))
    return lax.ppermute(value, axis, [(source, source + steps) for source in range(initial, last)])


def window(dist):
    return jnp.sinc(dist) * (0.5 + 0.5 * jnp.cos(jnp.pi * dist / 4.0))


def tap_rows(frac):
    dist = lax.broadcasted_iota(jnp.int32, (8, LANE), 0).astype(jnp.float32) - 3.0 - frac
    angle = jnp.pi * dist
    sinc = jnp.where(dist == 0.0, 1.0, jnp.sin(angle) / jnp.where(dist == 0.0, 1.0, angle))
    taps = sinc * (0.5 + 0.5 * jnp.cos(jnp.pi * dist / 4.0))
    return taps.astype(jnp.bfloat16).astype(jnp.float32)


def band(shape, distance, taps):
    total = jnp.zeros(shape, jnp.float32)
    for j in range(8):
        total = jnp.where(distance == j - 3, taps[j : j + 1, :1], total)
    return total.astype(jnp.bfloat16)


def cut_middle_kernel(prim_ref, *refs):
    cut_ref = refs[-1]
    cut_ref[...] = prim_ref[:, LAG : LAG + cut_ref.shape[1]]


def relay_kernel(block_ref, *refs):
    out_ref = refs[-1]
    out_ref[...] = block_ref[:, : out_ref.shape[1]]


def azimuth_kernel(off_ref, frac_ref, out_ref):
    shape = out_ref.shape
    offset = lax.broadcasted_iota(jnp.int32, shape, 1) - lax.broadcasted_iota(jnp.int32, shape, 0)
    out_ref[...] = band(shape, offset - HALO - off_ref[...], tap_rows(frac_ref[...]))


def range_kernel(off_ref, frac_ref, out_ref):
    square = out_ref.shape[1:]
    offset = lax.broadcasted_iota(jnp.int32, square, 0) - lax.broadcasted_iota(jnp.int32, square, 1)
    taps = tap_rows(frac_ref[...])
    for at, shift in enumerate((-LANE, 0, LANE)):
        out_ref[at] = band(square, offset + shift - off_ref[...], taps)


def resample_kernel(sec_ref, low_ref, high_ref, az_ref, rg_ref, out_ref, azim_ref):
    rows_n, cols_n = sec_ref.shape[2:]
    az_band = az_ref[...]
    here, tiles_n = lax.axis_index("tile"), lax.axis_size("tile")
    none = jnp.zeros(low_ref.shape[1:], jnp.bfloat16)
    for part in range(2):
        for start in range(0, rows_n, BAND):
            pieces = []
            if start == 0:
                pieces.append(jnp.where(here == 0, none, low_ref[part]))
            pieces.append(sec_ref[0, part, max(0, start - HALO) : min(rows_n, start + BAND + HALO)])
            if start + BAND == rows_n:
                pieces.append(jnp.where(here == tiles_n - 1, none, high_ref[part]))
            rows = jnp.concatenate(pieces, axis=0) if len(pieces) > 1 else pieces[0]
            azim_ref[part, start : start + BAND] = jnp.dot(
                az_band, rows, preferred_element_type=jnp.float32
            ).astype(jnp.bfloat16)

    before, same, after = [rg_ref[at] for at in range(3)]
    none = jnp.zeros((LANE, LANE), jnp.bfloat16)
    blocks_n, _, _, width = out_ref.shape
    lanes_n = width // LANE
    columns = []
    for lane in range(lanes_n):
        column = [none] * (lanes_n + 2)
        column[lane], column[lane + 1], column[lane + 2] = before, same, after
        columns.append(jnp.concatenate(column, axis=0))
    rg_band = jnp.concatenate(columns, axis=1)
    for block in range(blocks_n):
        first = block * width - LANE
        last = (block + 1) * width + LANE
        taken = slice(max(first, 0), min(last, cols_n))
        used = rg_band[taken.start - first : taken.stop - first]
        for part in range(2):
            out_ref[block, part] = jnp.dot(
                azim_ref[part, :, taken], used, preferred_element_type=jnp.float32
            ).astype(jnp.bfloat16)


def interfere(prim_re, prim_im, sec_re, sec_im):
    p_re, p_im = prim_re.astype(jnp.float32), prim_im.astype(jnp.float32)
    s_re, s_im = sec_re.astype(jnp.float32), sec_im.astype(jnp.float32)
    return p_re * s_re + p_im * s_im, p_im * s_re - p_re * s_im


def look_columns(width, block, looks_n):
    shape = (width, looks_n)
    col = lax.broadcasted_iota(jnp.int32, shape, 0) + block * width
    look = lax.broadcasted_iota(jnp.int32, shape, 1) * LR
    return jnp.where((col >= look) & (col < look + LR), 1.0, 0.0).astype(jnp.bfloat16)


def look_rows(sums_ref, part, start, rows_n):
    count = rows_n // LA
    total = sums_ref[part, pl.ds(start, count, LA)]
    for row in range(1, LA):
        total = total + sums_ref[part, pl.ds(start + row, count, LA)]
    return total


def margin_kernel(
    own_ref, one_ref, two_ref, three_ref, res_ref, first_ref, last_ref, looks_ref, sums_ref
):
    here = lax.axis_index("date")
    _, _, rows_n, width = res_ref.shape
    whole, edges = (0, rows_n - LAG), (0, LAG)
    looks_n = looks_ref.shape[2]
    totals = [None, None]
    for step, (prim_ref, starts) in enumerate(
        ((own_ref, whole), (one_ref, edges), (two_ref, edges), (three_ref, edges))
    ):
        block = jnp.bitwise_xor(here, step)
        select = look_columns(width, block, looks_n)
        columns = pl.ds(pl.multiple_of(block * width, width), width)
        halves = []
        for held, start, target in zip(starts, whole, (first_ref, last_ref)):
            pair = interfere(
                prim_ref[0, held : held + LAG],
                prim_ref[1, held : held + LAG],
                res_ref[block, 0, start : start + LAG],
                res_ref[block, 1, start : start + LAG],
            )
            pair = [value.astype(jnp.bfloat16) for value in pair]
            for part in range(2):
                target[part, :, columns] = pair[part]
            halves.append(pair)
        for part in range(2):
            both = jnp.concatenate([halves[0][part], halves[1][part]], axis=0)
            summed = jnp.dot(both, select, preferred_element_type=jnp.float32)
            totals[part] = summed if step == 0 else totals[part] + summed
    for part in range(2):
        sums_ref[part] = totals[part]
        looks_ref[part] = look_rows(sums_ref, part, 0, 2 * LAG)


def stats_kernel(last_ref, later_ref, weight_ref, stats_ref):
    cols_n = last_ref.shape[2]
    weight = weight_ref[...]
    i_re, i_im = last_ref[0].astype(jnp.float32), last_ref[1].astype(jnp.float32)
    inside = jnp.where(lax.axis_index("tile") == lax.axis_size("tile") - 1, 0.0, 1.0)
    l_re, l_im = [later_ref[part].astype(jnp.float32) * inside for part in range(2)]
    values = (
        i_re * l_re + i_im * l_im,
        i_im * l_re - i_re * l_im,
        0.5 * (i_re * i_re + i_im * i_im + l_re * l_re + l_im * l_im),
    )
    rows = []
    for value in values:
        folded = value[:, :LANE]
        for start in range(LANE, cols_n, LANE):
            folded = folded + value[:, start : start + LANE]
        rows.append(jnp.sum(folded * weight, axis=0, keepdims=True))
    rows.append(jnp.sum(weight, axis=0, keepdims=True) * (cols_n // LANE))
    rows.append(jnp.zeros((4, LANE), jnp.float32))
    stats_ref[...] = jnp.concatenate(rows, axis=0)


def look_sums(pieces, res_ref, looks_n):
    here = lax.axis_index("date")
    _, _, rows_n, width = res_ref.shape
    middle_n = rows_n - 2 * LAG
    totals = [None, None]
    for at, (step, prim_ref) in enumerate(pieces):
        block = jnp.bitwise_xor(here, step)
        first = LAG if prim_ref.shape[1] == rows_n else 0
        select = look_columns(width, block, looks_n)
        pair = interfere(
            prim_ref[0, first : first + middle_n],
            prim_ref[1, first : first + middle_n],
            res_ref[block, 0, LAG : rows_n - LAG],
            res_ref[block, 1, LAG : rows_n - LAG],
        )
        for part in range(2):
            summed = jnp.dot(
                pair[part].astype(jnp.bfloat16), select, preferred_element_type=jnp.float32
            )
            totals[part] = summed if at == 0 else totals[part] + summed
    return totals


def middle_kernel(own_ref, one_ref, two_ref, res_ref, out_ref):
    pieces = ((0, own_ref), (1, one_ref), (2, two_ref))
    for part, total in enumerate(look_sums(pieces, res_ref, out_ref.shape[2])):
        out_ref[part] = total


def unit_kernel(mine_ref, other_ref, unit_ref):
    stats = jnp.sum(mine_ref[...] + other_ref[...], axis=1, keepdims=True)
    e_re, e_im, power, count = [stats[row : row + 1] for row in range(4)]
    magnitude = jnp.sqrt(e_re * e_re + e_im * e_im)
    floor_val = (power + 1e-06) / jnp.sqrt(jnp.maximum(count, 1.0))
    denom = jnp.maximum(magnitude, floor_val)
    row = lax.broadcasted_iota(jnp.int32, unit_ref.shape, 0)
    unit_ref[...] = jnp.where(row == 0, e_re / denom, e_im / denom) * (1.0 / (LA * LR))


def finish_kernel(three_ref, res_ref, before_ref, looks_ref, unit_ref, out_ref, sums_ref):
    middle_n = before_ref.shape[1]
    edge = LAG // LA
    u_re, u_im = unit_ref[0:1], unit_ref[1:2]
    totals = look_sums(((3, three_ref),), res_ref, out_ref.shape[3])
    for part, total in enumerate(totals):
        sums_ref[part] = total + before_ref[part]
    for at, held in (
        (0, looks_ref[:, :edge]),
        (edge, [look_rows(sums_ref, part, 0, middle_n) for part in range(2)]),
        (edge + middle_n // LA, looks_ref[:, edge:]),
    ):
        rows = slice(at, at + held[0].shape[0])
        out_ref[0, 0, rows] = held[0] * u_re + held[1] * u_im
        out_ref[0, 1, rows] = held[1] * u_re - held[0] * u_im


def call(kernel, outs, scratch, cost, *args):
    vmem = pl.BlockSpec(memory_space=pltpu.VMEM)
    return pl.pallas_call(
        kernel,
        out_shape=outs,
        in_specs=[vmem] * len(args),
        out_specs=jax.tree.map(lambda _: vmem, outs),
        scratch_shapes=scratch,
        compiler_params=pltpu.CompilerParams(vmem_limit_bytes=VMEM_LIMIT),
        cost_estimate=pl.CostEstimate(flops=cost[0], bytes_accessed=cost[1], transcendentals=0),
    )(*args)


def ring(value, axis, step):
    count = lax.axis_size(axis)
    return lax.ppermute(value, axis, [(at, (at + step) % count) for at in range(count)])


def swap(value, axis, step):
    return lax.ppermute(value, axis, [(at, at ^ step) for at in range(lax.axis_size(axis))])


def fused(secondary, primary, margin_mask, az_off, rg_off, az_frac, rg_frac):
    _, _, rows_n, cols_n = secondary.shape
    width = primary.shape[2]
    dates_n = lax.axis_size("date")
    tiles_n = lax.axis_size("tile")
    bf16, f32 = jnp.bfloat16, jnp.float32
    shape = jax.ShapeDtypeStruct
    looks_n = cols_n // LR
    middle_n = rows_n - 2 * LAG
    edges = jnp.concatenate([primary[:, :LAG], primary[:, rows_n - LAG :]], axis=1)
    edges_two = swap(edges, "date", 2)
    edges_one = swap(edges, "date", 1)
    down, up = secondary[0, :, rows_n - HALO :], secondary[0, :, :HALO]
    low = ring(down, "tile", 1)
    high = ring(up, "tile", -1)
    az_band = call(
        azimuth_kernel, shape((BAND, BAND + 2 * HALO), bf16), [], (0, 0), az_off, az_frac
    )
    rg_band = call(range_kernel, shape((3, LANE, LANE), bf16), [], (0, 0), rg_off, rg_frac)
    passed = call(
        relay_kernel, shape(edges.shape, bf16), [], (0, 0), edges_two, edges_one, az_band
    )
    edges_three = swap(passed, "date", 1)
    middle = call(
        cut_middle_kernel,
        shape((2, middle_n + 16, width), bf16),
        [],
        (0, 0),
        primary, edges_two,
    )
    weight = jnp.broadcast_to(margin_mask[rows_n - LAG :].astype(f32)[:, None], (LAG, LANE))
    res = call(
        resample_kernel,
        shape((dates_n, 2, rows_n, width), bf16),
        [pltpu.VMEM((2, rows_n, cols_n), bf16)],
        (0, 0),
        secondary, low, high, az_band, rg_band,
    )
    two, one = [swap(middle, "date", step) for step in (2, 1)]
    margin = shape((2, LAG, cols_n), bf16)
    first, last, looks = call(
        margin_kernel,
        (margin, margin, shape((2, 2 * LAG // LA, looks_n), f32)),
        [pltpu.VMEM((2, 2 * LAG, looks_n), f32)],
        (0, 0),
        primary, edges_one, edges_two, edges_three, res,
    )
    later = ring(first, "tile", -1)
    stats = call(
        stats_kernel,
        shape((8, LANE), f32),
        [],
        (0, 0),
        last, later, weight,
    )
    before = call(
        middle_kernel,
        shape((2, middle_n, looks_n), f32),
        [],
        (3 * 10**9, 8 * rows_n * cols_n),
        primary, one, two, res,
    )
    other = swap(stats, "tile", 1)
    block = shape((2, middle_n, width), bf16)
    relayed = call(relay_kernel, block, [], (0, 0), two, other,one)
    three = swap(relayed, "date", 1)
    stride = 2
    while stride < tiles_n:
        stats = stats + other
        other = swap(stats, "tile", stride)
        stride *= 2
    unit = call(unit_kernel, shape((8, LANE), f32), [], (0, 0), stats, other)
    return call(
        finish_kernel,
        shape((1, 2, rows_n // LA, looks_n), f32),
        [pltpu.VMEM((2, middle_n, looks_n), f32)],
        (2 * middle_n * cols_n * looks_n, 4 * rows_n * cols_n),
        three, res, before, looks, unit,
    )


def padded(block, sides, width):
    for axis, dim in sides:
        low = passed_along(
            lax.slice_in_dim(block, block.shape[dim] - width, None, axis=dim), axis, 1
        )
        high = passed_along(lax.slice_in_dim(block, 0, width, axis=dim), axis, -1)
        block = jnp.concatenate([low, block, high], axis=dim)
    return block


def band_taps(offset, frac):
    inside = (offset >= -3) & (offset <= 4)
    return jnp.where(inside, window(offset.astype(jnp.float32) - frac), 0.0).astype(jnp.bfloat16)


def multilook(values):
    depth, rows_n, cols_n = values.shape
    return values.reshape(depth, rows_n // LA, LA, cols_n // LR, LR).mean(axis=(2, 4))


def plain(secondary, primary, margin_mask, az_off, rg_off, az_frac, rg_frac):
    rim_rows = KA + 4
    block_cols = 256
    image = secondary[0]
    rows_n = image.shape[1]
    cols_n = image.shape[2]
    extended = padded(image, (("tile", 1),), rim_rows)
    row_out = lax.broadcasted_iota(jnp.int32, (rows_n, rows_n + 2 * rim_rows), 0)
    row_in = lax.broadcasted_iota(jnp.int32, (rows_n, rows_n + 2 * rim_rows), 1)
    azim_taps = band_taps(row_in - row_out - az_off[0, 0] - rim_rows, az_frac[0, 0])
    azim = jnp.einsum(
        "im,kmc->kic", azim_taps, extended, preferred_element_type=jnp.float32
    ).astype(jnp.bfloat16)
    blocks_n = cols_n // block_cols
    col_pad = jnp.pad(azim, ((0, 0), (0, 0), (block_cols // 2, block_cols // 2)))
    pieces = col_pad.reshape(2, rows_n, blocks_n + 1, block_cols)
    inputs = jnp.concatenate([pieces[:, :, :-1], pieces[:, :, 1:]], axis=3)
    col_in = lax.broadcasted_iota(jnp.int32, (2 * block_cols, block_cols), 0)
    col_out = lax.broadcasted_iota(jnp.int32, (2 * block_cols, block_cols), 1)
    range_taps = band_taps(col_in - block_cols // 2 - col_out - rg_off[0, 0], rg_frac[0, 0])
    resampled = jnp.einsum("kibm,mn->kibn", inputs, range_taps, preferred_element_type=jnp.float32)
    resampled = resampled.reshape(2, rows_n, cols_n).astype(jnp.bfloat16)
    prim = lax.all_gather(primary, "date", axis=2, tiled=True)[None]
    sec_f = resampled[None].astype(jnp.float32)
    prim_f = prim.astype(jnp.float32)
    ifg_re = prim_f[:, 0] * sec_f[:, 0] + prim_f[:, 1] * sec_f[:, 1]
    ifg_im = prim_f[:, 1] * sec_f[:, 0] - prim_f[:, 0] * sec_f[:, 1]
    interf = jnp.stack((ifg_re, ifg_im), axis=1)
    upcoming = passed_along(interf[:, :, :LAG, :], "tile", -1)
    later = jnp.concatenate([interf[:, :, LAG:, :], upcoming], axis=2)
    l_re = later[:, 0]
    l_im = later[:, 1]
    weight = margin_mask.astype(jnp.float32)[None, :, None]
    e_re = jnp.sum(weight * (ifg_re * l_re + ifg_im * l_im), axis=(1, 2))
    e_im = jnp.sum(weight * (ifg_im * l_re - ifg_re * l_im), axis=(1, 2))
    power = jnp.sum(
        weight * 0.5 * (ifg_re * ifg_re + ifg_im * ifg_im + l_re * l_re + l_im * l_im), axis=(1, 2)
    )
    count = jnp.zeros_like(e_re) + jnp.sum(margin_mask.astype(jnp.float32)) * interf.shape[3]
    stats = jnp.stack((e_re, e_im, power, count), axis=1)
    totals = lax.psum(stats, "tile")
    magnitude = jnp.sqrt(totals[:, 0] * totals[:, 0] + totals[:, 1] * totals[:, 1])
    floor_val = (totals[:, 2] + 1e-06) / jnp.sqrt(jnp.maximum(totals[:, 3], 1.0))
    denom = jnp.maximum(magnitude, floor_val)
    u_re = (totals[:, 0] / denom)[:, None, None]
    u_im = (totals[:, 1] / denom)[:, None, None]
    c_re = multilook(ifg_re * u_re + ifg_im * u_im)
    c_im = multilook(ifg_im * u_re - ifg_re * u_im)
    return jnp.stack((c_re, c_im), axis=1)


def shards(secondary, primary, *rest):
    rows_n, width = primary.shape[1:]
    fits = rows_n % BAND == 0 and rows_n > 2 * LAG + BAND and width % LANE == 0
    tiles_n = lax.axis_size("tile")
    fits = fits and lax.axis_size("date") == 4 and tiles_n & (tiles_n - 1) == 0
    return (fused if fits else plain)(secondary, primary, *rest)


def solution(mesh):
    return jax.shard_map(
        shards,
        mesh=mesh,
        in_specs=(
            P("date", None, "tile", None),
            P(None, "tile", "date"),
            P("tile"),
            P("date", "tile"),
            P("date", "tile"),
            P("date", "tile"),
            P("date", "tile"),
        ),
        out_specs=P("date", None, "tile", None),
        check_vma=False,
    )
```

```python
import functools

import jax
import jax.numpy as jnp
from jax import lax
from jax.experimental import pallas as pl
from jax.experimental.pallas import tpu as pltpu
from jax.sharding import PartitionSpec as P

KA = 16
LAG = 64
LA = 2
LR = 8
LANE = 128
BAND = 128
HALO = 32
VMEM_LIMIT = 40 * 1024 * 1024


def passed_along(value, axis, steps):
    count = lax.axis_size(axis)
    initial, last = (max(0, -steps), min(count, count - steps))
    return lax.ppermute(value, axis, [(source, source + steps) for source in range(initial, last)])


def window(dist):
    return jnp.sinc(dist) * (0.5 + 0.5 * jnp.cos(jnp.pi * dist / 4.0))


def tap_rows(frac):
    dist = lax.broadcasted_iota(jnp.int32, (8, LANE), 0).astype(jnp.float32) - 3.0 - frac
    angle = jnp.pi * dist
    sinc = jnp.where(dist == 0.0, 1.0, jnp.sin(angle) / jnp.where(dist == 0.0, 1.0, angle))
    taps = sinc * (0.5 + 0.5 * jnp.cos(jnp.pi * dist / 4.0))
    return taps.astype(jnp.bfloat16).astype(jnp.float32)


def band(shape, distance, taps):
    total = jnp.zeros(shape, jnp.float32)
    for j in range(8):
        total = jnp.where(distance == j - 3, taps[j : j + 1, :1], total)
    return total.astype(jnp.bfloat16)


def cut_middle_kernel(prim_ref, *refs):
    cut_ref = refs[-1]
    cut_ref[...] = prim_ref[:, LAG : LAG + cut_ref.shape[1]]


def relay_kernel(block_ref, *refs):
    out_ref = refs[-1]
    out_ref[...] = block_ref[:, : out_ref.shape[1]]


def bands_kernel(ao_ref, ro_ref, af_ref, rf_ref, az_ref, rg_ref):
    shape = az_ref.shape
    offset = lax.broadcasted_iota(jnp.int32, shape, 1) - lax.broadcasted_iota(jnp.int32, shape, 0)
    az_ref[...] = band(shape, offset - HALO - ao_ref[...], tap_rows(af_ref[...]))
    square = rg_ref.shape[1:]
    offset = lax.broadcasted_iota(jnp.int32, square, 0) - lax.broadcasted_iota(jnp.int32, square, 1)
    taps = tap_rows(rf_ref[...])
    for at, shift in enumerate((-LANE, 0, LANE)):
        rg_ref[at] = band(square, offset + shift - ro_ref[...], taps)


def resample_kernel(sec_ref, low_ref, high_ref, az_ref, rg_ref, out_ref, azim_ref):
    rows_n, cols_n = sec_ref.shape[2:]
    az_band = az_ref[...]
    here, tiles_n = lax.axis_index("tile"), lax.axis_size("tile")
    none = jnp.zeros(low_ref.shape[1:], jnp.bfloat16)
    for part in range(2):
        for start in range(0, rows_n, BAND):
            pieces = []
            if start == 0:
                pieces.append(jnp.where(here == 0, none, low_ref[part]))
            pieces.append(sec_ref[0, part, max(0, start - HALO) : min(rows_n, start + BAND + HALO)])
            if start + BAND == rows_n:
                pieces.append(jnp.where(here == tiles_n - 1, none, high_ref[part]))
            rows = jnp.concatenate(pieces, axis=0) if len(pieces) > 1 else pieces[0]
            azim_ref[part, start : start + BAND] = jnp.dot(
                az_band, rows, preferred_element_type=jnp.float32
            ).astype(jnp.bfloat16)

    before, same, after = [rg_ref[at] for at in range(3)]
    none = jnp.zeros((LANE, LANE), jnp.bfloat16)
    blocks_n, _, _, width = out_ref.shape
    lanes_n = width // LANE
    columns = []
    for lane in range(lanes_n):
        column = [none] * (lanes_n + 2)
        column[lane], column[lane + 1], column[lane + 2] = before, same, after
        columns.append(jnp.concatenate(column, axis=0))
    rg_band = jnp.concatenate(columns, axis=1)
    for block in range(blocks_n):
        first = block * width - LANE
        last = (block + 1) * width + LANE
        taken = slice(max(first, 0), min(last, cols_n))
        used = rg_band[taken.start - first : taken.stop - first]
        for part in range(2):
            out_ref[block, part] = jnp.dot(
                azim_ref[part, :, taken], used, preferred_element_type=jnp.float32
            ).astype(jnp.bfloat16)


def interfere(prim_re, prim_im, sec_re, sec_im):
    p_re, p_im = prim_re.astype(jnp.float32), prim_im.astype(jnp.float32)
    s_re, s_im = sec_re.astype(jnp.float32), sec_im.astype(jnp.float32)
    return p_re * s_re + p_im * s_im, p_im * s_re - p_re * s_im


def look_columns(width, block, looks_n):
    shape = (width, looks_n)
    col = lax.broadcasted_iota(jnp.int32, shape, 0) + block * width
    look = lax.broadcasted_iota(jnp.int32, shape, 1) * LR
    return jnp.where((col >= look) & (col < look + LR), 1.0, 0.0).astype(jnp.bfloat16)


def look_rows(sums_ref, part, start, rows_n):
    count = rows_n // LA
    total = sums_ref[part, pl.ds(start, count, LA)]
    for row in range(1, LA):
        total = total + sums_ref[part, pl.ds(start + row, count, LA)]
    return total


def margin_kernel(
    own_ref, one_ref, two_ref, three_ref, res_ref, first_ref, last_ref, looks_ref, sums_ref
):
    here = lax.axis_index("date")
    _, _, rows_n, width = res_ref.shape
    whole, edges = (0, rows_n - LAG), (0, LAG)
    looks_n = looks_ref.shape[2]
    totals = [None, None]
    for step, (prim_ref, starts) in enumerate(
        ((own_ref, whole), (one_ref, edges), (two_ref, edges), (three_ref, edges))
    ):
        block = jnp.bitwise_xor(here, step)
        select = look_columns(width, block, looks_n)
        columns = pl.ds(pl.multiple_of(block * width, width), width)
        halves = []
        for held, start, target in zip(starts, whole, (first_ref, last_ref)):
            pair = interfere(
                prim_ref[0, held : held + LAG],
                prim_ref[1, held : held + LAG],
                res_ref[block, 0, start : start + LAG],
                res_ref[block, 1, start : start + LAG],
            )
            pair = [value.astype(jnp.bfloat16) for value in pair]
            for part in range(2):
                target[part, :, columns] = pair[part]
            halves.append(pair)
        for part in range(2):
            both = jnp.concatenate([halves[0][part], halves[1][part]], axis=0)
            summed = jnp.dot(both, select, preferred_element_type=jnp.float32)
            totals[part] = summed if step == 0 else totals[part] + summed
    for part in range(2):
        sums_ref[part] = totals[part]
        looks_ref[part] = look_rows(sums_ref, part, 0, 2 * LAG)


def stats_kernel(last_ref, later_ref, weight_ref, stats_ref):
    cols_n = last_ref.shape[2]
    weight = weight_ref[...]
    i_re, i_im = last_ref[0].astype(jnp.float32), last_ref[1].astype(jnp.float32)
    inside = jnp.where(lax.axis_index("tile") == lax.axis_size("tile") - 1, 0.0, 1.0)
    l_re, l_im = [later_ref[part].astype(jnp.float32) * inside for part in range(2)]
    values = (
        i_re * l_re + i_im * l_im,
        i_im * l_re - i_re * l_im,
        0.5 * (i_re * i_re + i_im * i_im + l_re * l_re + l_im * l_im),
    )
    rows = []
    for value in values:
        folded = value[:, :LANE]
        for start in range(LANE, cols_n, LANE):
            folded = folded + value[:, start : start + LANE]
        rows.append(jnp.sum(folded * weight, axis=0, keepdims=True))
    rows.append(jnp.sum(weight, axis=0, keepdims=True) * (cols_n // LANE))
    rows.append(jnp.zeros((4, LANE), jnp.float32))
    stats_ref[...] = jnp.concatenate(rows, axis=0)


def look_sums(pieces, res_ref, looks_n):
    here = lax.axis_index("date")
    _, _, rows_n, width = res_ref.shape
    middle_n = rows_n - 2 * LAG
    totals = [None, None]
    for at, (step, prim_ref) in enumerate(pieces):
        block = jnp.bitwise_xor(here, step)
        first = LAG if prim_ref.shape[1] == rows_n else 0
        select = look_columns(width, block, looks_n)
        pair = interfere(
            prim_ref[0, first : first + middle_n],
            prim_ref[1, first : first + middle_n],
            res_ref[block, 0, LAG : rows_n - LAG],
            res_ref[block, 1, LAG : rows_n - LAG],
        )
        for part in range(2):
            summed = jnp.dot(
                pair[part].astype(jnp.bfloat16), select, preferred_element_type=jnp.float32
            )
            totals[part] = summed if at == 0 else totals[part] + summed
    return totals


def middle_kernel(own_ref, one_ref, two_ref, res_ref, out_ref):
    pieces = ((0, own_ref), (1, one_ref), (2, two_ref))
    for part, total in enumerate(look_sums(pieces, res_ref, out_ref.shape[2])):
        out_ref[part] = total


def unit_kernel(mine_ref, other_ref, unit_ref):
    stats = jnp.sum(mine_ref[...] + other_ref[...], axis=1, keepdims=True)
    e_re, e_im, power, count = [stats[row : row + 1] for row in range(4)]
    magnitude = jnp.sqrt(e_re * e_re + e_im * e_im)
    floor_val = (power + 1e-06) / jnp.sqrt(jnp.maximum(count, 1.0))
    denom = jnp.maximum(magnitude, floor_val)
    row = lax.broadcasted_iota(jnp.int32, unit_ref.shape, 0)
    unit_ref[...] = jnp.where(row == 0, e_re / denom, e_im / denom) * (1.0 / (LA * LR))


def finish_kernel(three_ref, res_ref, before_ref, looks_ref, unit_ref, out_ref, sums_ref):
    middle_n = before_ref.shape[1]
    edge = LAG // LA
    u_re, u_im = unit_ref[0:1], unit_ref[1:2]
    totals = look_sums(((3, three_ref),), res_ref, out_ref.shape[3])
    for part, total in enumerate(totals):
        sums_ref[part] = total + before_ref[part]
    for at, held in (
        (0, looks_ref[:, :edge]),
        (edge, [look_rows(sums_ref, part, 0, middle_n) for part in range(2)]),
        (edge + middle_n // LA, looks_ref[:, edge:]),
    ):
        rows = slice(at, at + held[0].shape[0])
        out_ref[0, 0, rows] = held[0] * u_re + held[1] * u_im
        out_ref[0, 1, rows] = held[1] * u_re - held[0] * u_im


def call(kernel, outs, scratch, cost, *args):
    vmem = pl.BlockSpec(memory_space=pltpu.VMEM)
    return pl.pallas_call(
        kernel,
        out_shape=outs,
        in_specs=[vmem] * len(args),
        out_specs=jax.tree.map(lambda _: vmem, outs),
        scratch_shapes=scratch,
        compiler_params=pltpu.CompilerParams(vmem_limit_bytes=VMEM_LIMIT),
        cost_estimate=pl.CostEstimate(flops=cost[0], bytes_accessed=cost[1], transcendentals=0),
    )(*args)


def ring(value, axis, step):
    count = lax.axis_size(axis)
    return lax.ppermute(value, axis, [(at, (at + step) % count) for at in range(count)])


def swap(value, axis, step):
    return lax.ppermute(value, axis, [(at, at ^ step) for at in range(lax.axis_size(axis))])


def fused(secondary, primary, margin_mask, az_off, rg_off, az_frac, rg_frac):
    _, _, rows_n, cols_n = secondary.shape
    width = primary.shape[2]
    dates_n = lax.axis_size("date")
    tiles_n = lax.axis_size("tile")
    bf16, f32 = jnp.bfloat16, jnp.float32
    shape = jax.ShapeDtypeStruct
    looks_n = cols_n // LR
    middle_n = rows_n - 2 * LAG
    edges = jnp.concatenate([primary[:, :LAG], primary[:, rows_n - LAG :]], axis=1)
    edges_two = swap(edges, "date", 2)
    edges_one = swap(edges, "date", 1)
    down, up = secondary[0, :, rows_n - HALO :], secondary[0, :, :HALO]
    low = ring(down, "tile", 1)
    high = ring(up, "tile", -1)
    az_band, rg_band = call(
        bands_kernel,
        (shape((BAND, BAND + 2 * HALO), bf16), shape((3, LANE, LANE), bf16)),
        [],
        (0, 0),
        az_off, rg_off, az_frac, rg_frac,
    )
    passed = call(
        relay_kernel, shape(edges.shape, bf16), [], (0, 0), edges_two, edges_one
    )
    edges_three = swap(passed, "date", 1)
    middle = call(
        cut_middle_kernel,
        shape((2, middle_n + 16, width), bf16),
        [],
        (0, 0),
        primary, edges_two,
    )
    weight = jnp.broadcast_to(margin_mask[rows_n - LAG :].astype(f32)[:, None], (LAG, LANE))
    res = call(
        resample_kernel,
        shape((dates_n, 2, rows_n, width), bf16),
        [pltpu.VMEM((2, rows_n, cols_n), bf16)],
        (0, 0),
        secondary, low, high, az_band, rg_band,
    )
    two, one = [swap(middle, "date", step) for step in (2, 1)]
    margin = shape((2, LAG, cols_n), bf16)
    first, last, looks = call(
        margin_kernel,
        (margin, margin, shape((2, 2 * LAG // LA, looks_n), f32)),
        [pltpu.VMEM((2, 2 * LAG, looks_n), f32)],
        (0, 0),
        primary, edges_one, edges_two, edges_three, res,
    )
    later = ring(first, "tile", -1)
    stats = call(
        stats_kernel,
        shape((8, LANE), f32),
        [],
        (0, 0),
        last, later, weight,
    )
    before = call(
        middle_kernel,
        shape((2, middle_n, looks_n), f32),
        [],
        (2 * 2 * middle_n * cols_n * looks_n, 8 * rows_n * cols_n),
        primary, one, two, res,
    )
    other = swap(stats, "tile", 1)
    block = shape((2, middle_n, width), bf16)
    relayed = call(relay_kernel, block, [], (0, 0), two, other,one)
    three = swap(relayed, "date", 1)
    stride = 2
    while stride < tiles_n:
        stats = stats + other
        other = swap(stats, "tile", stride)
        stride *= 2
    unit = call(unit_kernel, shape((8, LANE), f32), [], (0, 0), stats, other)
    return call(
        finish_kernel,
        shape((1, 2, rows_n // LA, looks_n), f32),
        [pltpu.VMEM((2, middle_n, looks_n), f32)],
        (2 * middle_n * cols_n * looks_n, 4 * rows_n * cols_n),
        three, res, before, looks, unit,
    )


def padded(block, sides, width):
    for axis, dim in sides:
        low = passed_along(
            lax.slice_in_dim(block, block.shape[dim] - width, None, axis=dim), axis, 1
        )
        high = passed_along(lax.slice_in_dim(block, 0, width, axis=dim), axis, -1)
        block = jnp.concatenate([low, block, high], axis=dim)
    return block


def band_taps(offset, frac):
    inside = (offset >= -3) & (offset <= 4)
    return jnp.where(inside, window(offset.astype(jnp.float32) - frac), 0.0).astype(jnp.bfloat16)


def multilook(values):
    depth, rows_n, cols_n = values.shape
    return values.reshape(depth, rows_n // LA, LA, cols_n // LR, LR).mean(axis=(2, 4))


def plain(secondary, primary, margin_mask, az_off, rg_off, az_frac, rg_frac):
    rim_rows = KA + 4
    block_cols = 256
    image = secondary[0]
    rows_n = image.shape[1]
    cols_n = image.shape[2]
    extended = padded(image, (("tile", 1),), rim_rows)
    row_out = lax.broadcasted_iota(jnp.int32, (rows_n, rows_n + 2 * rim_rows), 0)
    row_in = lax.broadcasted_iota(jnp.int32, (rows_n, rows_n + 2 * rim_rows), 1)
    azim_taps = band_taps(row_in - row_out - az_off[0, 0] - rim_rows, az_frac[0, 0])
    azim = jnp.einsum(
        "im,kmc->kic", azim_taps, extended, preferred_element_type=jnp.float32
    ).astype(jnp.bfloat16)
    blocks_n = cols_n // block_cols
    col_pad = jnp.pad(azim, ((0, 0), (0, 0), (block_cols // 2, block_cols // 2)))
    pieces = col_pad.reshape(2, rows_n, blocks_n + 1, block_cols)
    inputs = jnp.concatenate([pieces[:, :, :-1], pieces[:, :, 1:]], axis=3)
    col_in = lax.broadcasted_iota(jnp.int32, (2 * block_cols, block_cols), 0)
    col_out = lax.broadcasted_iota(jnp.int32, (2 * block_cols, block_cols), 1)
    range_taps = band_taps(col_in - block_cols // 2 - col_out - rg_off[0, 0], rg_frac[0, 0])
    resampled = jnp.einsum("kibm,mn->kibn", inputs, range_taps, preferred_element_type=jnp.float32)
    resampled = resampled.reshape(2, rows_n, cols_n).astype(jnp.bfloat16)
    prim = lax.all_gather(primary, "date", axis=2, tiled=True)[None]
    sec_f = resampled[None].astype(jnp.float32)
    prim_f = prim.astype(jnp.float32)
    ifg_re = prim_f[:, 0] * sec_f[:, 0] + prim_f[:, 1] * sec_f[:, 1]
    ifg_im = prim_f[:, 1] * sec_f[:, 0] - prim_f[:, 0] * sec_f[:, 1]
    interf = jnp.stack((ifg_re, ifg_im), axis=1)
    upcoming = passed_along(interf[:, :, :LAG, :], "tile", -1)
    later = jnp.concatenate([interf[:, :, LAG:, :], upcoming], axis=2)
    l_re = later[:, 0]
    l_im = later[:, 1]
    weight = margin_mask.astype(jnp.float32)[None, :, None]
    e_re = jnp.sum(weight * (ifg_re * l_re + ifg_im * l_im), axis=(1, 2))
    e_im = jnp.sum(weight * (ifg_im * l_re - ifg_re * l_im), axis=(1, 2))
    power = jnp.sum(
        weight * 0.5 * (ifg_re * ifg_re + ifg_im * ifg_im + l_re * l_re + l_im * l_im), axis=(1, 2)
    )
    count = jnp.zeros_like(e_re) + jnp.sum(margin_mask.astype(jnp.float32)) * interf.shape[3]
    stats = jnp.stack((e_re, e_im, power, count), axis=1)
    totals = lax.psum(stats, "tile")
    magnitude = jnp.sqrt(totals[:, 0] * totals[:, 0] + totals[:, 1] * totals[:, 1])
    floor_val = (totals[:, 2] + 1e-06) / jnp.sqrt(jnp.maximum(totals[:, 3], 1.0))
    denom = jnp.maximum(magnitude, floor_val)
    u_re = (totals[:, 0] / denom)[:, None, None]
    u_im = (totals[:, 1] / denom)[:, None, None]
    c_re = multilook(ifg_re * u_re + ifg_im * u_im)
    c_im = multilook(ifg_im * u_re - ifg_re * u_im)
    return jnp.stack((c_re, c_im), axis=1)


def shards(secondary, primary, *rest):
    rows_n, width = primary.shape[1:]
    fits = rows_n % BAND == 0 and rows_n > 2 * LAG + BAND and width % LANE == 0
    tiles_n = lax.axis_size("tile")
    fits = fits and lax.axis_size("date") == 4 and tiles_n & (tiles_n - 1) == 0
    return (fused if fits else plain)(secondary, primary, *rest)


def solution(mesh):
    return jax.shard_map(
        shards,
        mesh=mesh,
        in_specs=(
            P("date", None, "tile", None),
            P(None, "tile", "date"),
            P("tile"),
            P("date", "tile"),
            P("date", "tile"),
            P("date", "tile"),
            P("date", "tile"),
        ),
        out_specs=P("date", None, "tile", None),
        check_vma=False,
    )
```

```python
import functools

import jax
import jax.numpy as jnp
from jax import lax
from jax.experimental import pallas as pl
from jax.experimental.pallas import tpu as pltpu
from jax.sharding import PartitionSpec as P

KA = 16
LAG = 64
LA = 2
LR = 8
LANE = 128
BAND = 128
HALO = 32
VMEM_LIMIT = 40 * 1024 * 1024


def passed_along(value, axis, steps):
    count = lax.axis_size(axis)
    initial, last = (max(0, -steps), min(count, count - steps))
    return lax.ppermute(value, axis, [(source, source + steps) for source in range(initial, last)])


def window(dist):
    return jnp.sinc(dist) * (0.5 + 0.5 * jnp.cos(jnp.pi * dist / 4.0))


def tap_rows(frac):
    dist = lax.broadcasted_iota(jnp.int32, (8, LANE), 0).astype(jnp.float32) - 3.0 - frac
    angle = jnp.pi * dist
    sinc = jnp.where(dist == 0.0, 1.0, jnp.sin(angle) / jnp.where(dist == 0.0, 1.0, angle))
    taps = sinc * (0.5 + 0.5 * jnp.cos(jnp.pi * dist / 4.0))
    return taps.astype(jnp.bfloat16).astype(jnp.float32)


def band(shape, distance, taps):
    total = jnp.zeros(shape, jnp.float32)
    for j in range(8):
        total = jnp.where(distance == j - 3, taps[j : j + 1, :1], total)
    return total.astype(jnp.bfloat16)


def cut_middle_kernel(prim_ref, *refs):
    cut_ref = refs[-1]
    cut_ref[...] = prim_ref[:, LAG : LAG + cut_ref.shape[1]]


def relay_kernel(block_ref, *refs):
    out_ref = refs[-1]
    out_ref[...] = block_ref[:, : out_ref.shape[1]]


def bands_kernel(ao_ref, ro_ref, af_ref, rf_ref, az_ref, rg_ref):
    shape = az_ref.shape
    offset = lax.broadcasted_iota(jnp.int32, shape, 1) - lax.broadcasted_iota(jnp.int32, shape, 0)
    az_ref[...] = band(shape, offset - HALO - ao_ref[...], tap_rows(af_ref[...]))
    square = rg_ref.shape[1:]
    offset = lax.broadcasted_iota(jnp.int32, square, 0) - lax.broadcasted_iota(jnp.int32, square, 1)
    taps = tap_rows(rf_ref[...])
    for at, shift in enumerate((-LANE, 0, LANE)):
        rg_ref[at] = band(square, offset + shift - ro_ref[...], taps)


def resample_kernel(sec_ref, low_ref, high_ref, az_ref, rg_ref, out_ref, azim_ref):
    rows_n, cols_n = sec_ref.shape[2:]
    az_band = az_ref[...]
    here, tiles_n = lax.axis_index("tile"), lax.axis_size("tile")
    none = jnp.zeros(low_ref.shape[1:], jnp.bfloat16)
    for part in range(2):
        for start in range(0, rows_n, BAND):
            pieces = []
            if start == 0:
                pieces.append(jnp.where(here == 0, none, low_ref[part]))
            pieces.append(sec_ref[0, part, max(0, start - HALO) : min(rows_n, start + BAND + HALO)])
            if start + BAND == rows_n:
                pieces.append(jnp.where(here == tiles_n - 1, none, high_ref[part]))
            rows = jnp.concatenate(pieces, axis=0) if len(pieces) > 1 else pieces[0]
            azim_ref[part, start : start + BAND] = jnp.dot(
                az_band, rows, preferred_element_type=jnp.float32
            ).astype(jnp.bfloat16)

    before, same, after = [rg_ref[at] for at in range(3)]
    none = jnp.zeros((LANE, LANE), jnp.bfloat16)
    blocks_n, _, _, width = out_ref.shape
    lanes_n = width // LANE
    columns = []
    for lane in range(lanes_n):
        column = [none] * (lanes_n + 2)
        column[lane], column[lane + 1], column[lane + 2] = before, same, after
        columns.append(jnp.concatenate(column, axis=0))
    rg_band = jnp.concatenate(columns, axis=1)
    for block in range(blocks_n):
        first = block * width - LANE
        last = (block + 1) * width + LANE
        taken = slice(max(first, 0), min(last, cols_n))
        used = rg_band[taken.start - first : taken.stop - first]
        for part in range(2):
            out_ref[block, part] = jnp.dot(
                azim_ref[part, :, taken], used, preferred_element_type=jnp.float32
            ).astype(jnp.bfloat16)


def interfere(prim_re, prim_im, sec_re, sec_im):
    p_re, p_im = prim_re.astype(jnp.float32), prim_im.astype(jnp.float32)
    s_re, s_im = sec_re.astype(jnp.float32), sec_im.astype(jnp.float32)
    return p_re * s_re + p_im * s_im, p_im * s_re - p_re * s_im


def look_columns(width, block, looks_n):
    shape = (width, looks_n)
    col = lax.broadcasted_iota(jnp.int32, shape, 0) + block * width
    look = lax.broadcasted_iota(jnp.int32, shape, 1) * LR
    return jnp.where((col >= look) & (col < look + LR), 1.0, 0.0).astype(jnp.bfloat16)


def look_rows(sums_ref, part, start, rows_n):
    count = rows_n // LA
    total = sums_ref[part, pl.ds(start, count, LA)]
    for row in range(1, LA):
        total = total + sums_ref[part, pl.ds(start + row, count, LA)]
    return total


def margin_kernel(
    own_ref, one_ref, two_ref, three_ref, res_ref, first_ref, last_ref, looks_ref, sums_ref
):
    here = lax.axis_index("date")
    _, _, rows_n, width = res_ref.shape
    whole, edges = (0, rows_n - LAG), (0, LAG)
    looks_n = looks_ref.shape[2]
    totals = [None, None]
    for step, (prim_ref, starts) in enumerate(
        ((own_ref, whole), (one_ref, edges), (two_ref, edges), (three_ref, edges))
    ):
        block = jnp.bitwise_xor(here, step)
        select = look_columns(width, block, looks_n)
        columns = pl.ds(pl.multiple_of(block * width, width), width)
        halves = []
        for held, start, target in zip(starts, whole, (first_ref, last_ref)):
            pair = interfere(
                prim_ref[0, held : held + LAG],
                prim_ref[1, held : held + LAG],
                res_ref[block, 0, start : start + LAG],
                res_ref[block, 1, start : start + LAG],
            )
            pair = [value.astype(jnp.bfloat16) for value in pair]
            for part in range(2):
                target[part, :, columns] = pair[part]
            halves.append(pair)
        for part in range(2):
            both = jnp.concatenate([halves[0][part], halves[1][part]], axis=0)
            summed = jnp.dot(both, select, preferred_element_type=jnp.float32)
            totals[part] = summed if step == 0 else totals[part] + summed
    for part in range(2):
        sums_ref[part] = totals[part]
        looks_ref[part] = look_rows(sums_ref, part, 0, 2 * LAG)


def stats_kernel(last_ref, later_ref, weight_ref, stats_ref):
    cols_n = last_ref.shape[2]
    weight = weight_ref[...]
    i_re, i_im = last_ref[0].astype(jnp.float32), last_ref[1].astype(jnp.float32)
    inside = jnp.where(lax.axis_index("tile") == lax.axis_size("tile") - 1, 0.0, 1.0)
    l_re, l_im = [later_ref[part].astype(jnp.float32) * inside for part in range(2)]
    values = (
        i_re * l_re + i_im * l_im,
        i_im * l_re - i_re * l_im,
        0.5 * (i_re * i_re + i_im * i_im + l_re * l_re + l_im * l_im),
    )
    rows = []
    for value in values:
        folded = value[:, :LANE]
        for start in range(LANE, cols_n, LANE):
            folded = folded + value[:, start : start + LANE]
        rows.append(jnp.sum(folded * weight, axis=0, keepdims=True))
    rows.append(jnp.sum(weight, axis=0, keepdims=True) * (cols_n // LANE))
    rows.append(jnp.zeros((4, LANE), jnp.float32))
    stats_ref[...] = jnp.concatenate(rows, axis=0)


def look_sums(pieces, res_ref, looks_n):
    here = lax.axis_index("date")
    _, _, rows_n, width = res_ref.shape
    middle_n = rows_n - 2 * LAG
    totals = [None, None]
    for at, (step, prim_ref) in enumerate(pieces):
        block = jnp.bitwise_xor(here, step)
        first = LAG if prim_ref.shape[1] == rows_n else 0
        select = look_columns(width, block, looks_n)
        pair = interfere(
            prim_ref[0, first : first + middle_n],
            prim_ref[1, first : first + middle_n],
            res_ref[block, 0, LAG : rows_n - LAG],
            res_ref[block, 1, LAG : rows_n - LAG],
        )
        for part in range(2):
            summed = jnp.dot(
                pair[part].astype(jnp.bfloat16), select, preferred_element_type=jnp.float32
            )
            totals[part] = summed if at == 0 else totals[part] + summed
    return totals


def middle_kernel(own_ref, one_ref, two_ref, res_ref, out_ref):
    pieces = ((0, own_ref), (1, one_ref), (2, two_ref))
    for part, total in enumerate(look_sums(pieces, res_ref, out_ref.shape[2])):
        out_ref[part] = total


def unit_kernel(mine_ref, other_ref, unit_ref):
    stats = jnp.sum(mine_ref[...] + other_ref[...], axis=1, keepdims=True)
    e_re, e_im, power, count = [stats[row : row + 1] for row in range(4)]
    magnitude = jnp.sqrt(e_re * e_re + e_im * e_im)
    floor_val = (power + 1e-06) / jnp.sqrt(jnp.maximum(count, 1.0))
    denom = jnp.maximum(magnitude, floor_val)
    row = lax.broadcasted_iota(jnp.int32, unit_ref.shape, 0)
    unit_ref[...] = jnp.where(row == 0, e_re / denom, e_im / denom) * (1.0 / (LA * LR))


def finish_kernel(three_ref, res_ref, before_ref, looks_ref, unit_ref, out_ref, sums_ref):
    middle_n = before_ref.shape[1]
    edge = LAG // LA
    u_re, u_im = unit_ref[0:1], unit_ref[1:2]
    totals = look_sums(((3, three_ref),), res_ref, out_ref.shape[3])
    for part, total in enumerate(totals):
        sums_ref[part] = total + before_ref[part]
    for at, held in (
        (0, looks_ref[:, :edge]),
        (edge, [look_rows(sums_ref, part, 0, middle_n) for part in range(2)]),
        (edge + middle_n // LA, looks_ref[:, edge:]),
    ):
        rows = slice(at, at + held[0].shape[0])
        out_ref[0, 0, rows] = held[0] * u_re + held[1] * u_im
        out_ref[0, 1, rows] = held[1] * u_re - held[0] * u_im


def call(kernel, outs, scratch, cost, *args):
    vmem = pl.BlockSpec(memory_space=pltpu.VMEM)
    return pl.pallas_call(
        kernel,
        out_shape=outs,
        in_specs=[vmem] * len(args),
        out_specs=jax.tree.map(lambda _: vmem, outs),
        scratch_shapes=scratch,
        compiler_params=pltpu.CompilerParams(vmem_limit_bytes=VMEM_LIMIT),
        cost_estimate=pl.CostEstimate(flops=cost[0], bytes_accessed=cost[1], transcendentals=0),
    )(*args)


def ring(value, axis, step):
    count = lax.axis_size(axis)
    return lax.ppermute(value, axis, [(at, (at + step) % count) for at in range(count)])


def swap(value, axis, step):
    return lax.ppermute(value, axis, [(at, at ^ step) for at in range(lax.axis_size(axis))])


def fused(secondary, primary, margin_mask, az_off, rg_off, az_frac, rg_frac):
    _, _, rows_n, cols_n = secondary.shape
    width = primary.shape[2]
    dates_n = lax.axis_size("date")
    tiles_n = lax.axis_size("tile")
    bf16, f32 = jnp.bfloat16, jnp.float32
    shape = jax.ShapeDtypeStruct
    looks_n = cols_n // LR
    middle_n = rows_n - 2 * LAG
    edges = jnp.concatenate([primary[:, :LAG], primary[:, rows_n - LAG :]], axis=1)
    edges_two = swap(edges, "date", 2)
    edges_one = swap(edges, "date", 1)
    down, up = secondary[0, :, rows_n - HALO :], secondary[0, :, :HALO]
    low = ring(down, "tile", 1)
    high = ring(up, "tile", -1)
    az_band, rg_band = call(
        bands_kernel,
        (shape((BAND, BAND + 2 * HALO), bf16), shape((3, LANE, LANE), bf16)),
        [],
        (0, 0),
        az_off, rg_off, az_frac, rg_frac,
    )
    passed = call(
        relay_kernel, shape(edges.shape, bf16), [], (0, 0), edges_two
    )
    edges_three = swap(passed, "date", 1)
    middle = call(
        cut_middle_kernel,
        shape((2, middle_n + 16, width), bf16),
        [],
        (0, 0),
        primary, edges_two, edges_one,
    )
    weight = jnp.broadcast_to(margin_mask[rows_n - LAG :].astype(f32)[:, None], (LAG, LANE))
    res = call(
        resample_kernel,
        shape((dates_n, 2, rows_n, width), bf16),
        [pltpu.VMEM((2, rows_n, cols_n), bf16)],
        (0, 0),
        secondary, low, high, az_band, rg_band,
    )
    two, one = [swap(middle, "date", step) for step in (2, 1)]
    margin = shape((2, LAG, cols_n), bf16)
    first, last, looks = call(
        margin_kernel,
        (margin, margin, shape((2, 2 * LAG // LA, looks_n), f32)),
        [pltpu.VMEM((2, 2 * LAG, looks_n), f32)],
        (0, 0),
        primary, edges_one, edges_two, edges_three, res,
    )
    later = ring(first, "tile", -1)
    stats = call(
        stats_kernel,
        shape((8, LANE), f32),
        [],
        (0, 0),
        last, later, weight,
    )
    before = call(
        middle_kernel,
        shape((2, middle_n, looks_n), f32),
        [],
        (2 * 2 * middle_n * cols_n * looks_n, 8 * rows_n * cols_n),
        primary, one, two, res,
    )
    other = swap(stats, "tile", 1)
    block = shape((2, middle_n, width), bf16)
    relayed = call(relay_kernel, block, [], (0, 0), two, other,one)
    three = swap(relayed, "date", 1)
    stride = 2
    while stride < tiles_n:
        stats = stats + other
        other = swap(stats, "tile", stride)
        stride *= 2
    unit = call(unit_kernel, shape((8, LANE), f32), [], (0, 0), stats, other)
    return call(
        finish_kernel,
        shape((1, 2, rows_n // LA, looks_n), f32),
        [pltpu.VMEM((2, middle_n, looks_n), f32)],
        (2 * middle_n * cols_n * looks_n, 4 * rows_n * cols_n),
        three, res, before, looks, unit,
    )


def padded(block, sides, width):
    for axis, dim in sides:
        low = passed_along(
            lax.slice_in_dim(block, block.shape[dim] - width, None, axis=dim), axis, 1
        )
        high = passed_along(lax.slice_in_dim(block, 0, width, axis=dim), axis, -1)
        block = jnp.concatenate([low, block, high], axis=dim)
    return block


def band_taps(offset, frac):
    inside = (offset >= -3) & (offset <= 4)
    return jnp.where(inside, window(offset.astype(jnp.float32) - frac), 0.0).astype(jnp.bfloat16)


def multilook(values):
    depth, rows_n, cols_n = values.shape
    return values.reshape(depth, rows_n // LA, LA, cols_n // LR, LR).mean(axis=(2, 4))


def plain(secondary, primary, margin_mask, az_off, rg_off, az_frac, rg_frac):
    rim_rows = KA + 4
    block_cols = 256
    image = secondary[0]
    rows_n = image.shape[1]
    cols_n = image.shape[2]
    extended = padded(image, (("tile", 1),), rim_rows)
    row_out = lax.broadcasted_iota(jnp.int32, (rows_n, rows_n + 2 * rim_rows), 0)
    row_in = lax.broadcasted_iota(jnp.int32, (rows_n, rows_n + 2 * rim_rows), 1)
    azim_taps = band_taps(row_in - row_out - az_off[0, 0] - rim_rows, az_frac[0, 0])
    azim = jnp.einsum(
        "im,kmc->kic", azim_taps, extended, preferred_element_type=jnp.float32
    ).astype(jnp.bfloat16)
    blocks_n = cols_n // block_cols
    col_pad = jnp.pad(azim, ((0, 0), (0, 0), (block_cols // 2, block_cols // 2)))
    pieces = col_pad.reshape(2, rows_n, blocks_n + 1, block_cols)
    inputs = jnp.concatenate([pieces[:, :, :-1], pieces[:, :, 1:]], axis=3)
    col_in = lax.broadcasted_iota(jnp.int32, (2 * block_cols, block_cols), 0)
    col_out = lax.broadcasted_iota(jnp.int32, (2 * block_cols, block_cols), 1)
    range_taps = band_taps(col_in - block_cols // 2 - col_out - rg_off[0, 0], rg_frac[0, 0])
    resampled = jnp.einsum("kibm,mn->kibn", inputs, range_taps, preferred_element_type=jnp.float32)
    resampled = resampled.reshape(2, rows_n, cols_n).astype(jnp.bfloat16)
    prim = lax.all_gather(primary, "date", axis=2, tiled=True)[None]
    sec_f = resampled[None].astype(jnp.float32)
    prim_f = prim.astype(jnp.float32)
    ifg_re = prim_f[:, 0] * sec_f[:, 0] + prim_f[:, 1] * sec_f[:, 1]
    ifg_im = prim_f[:, 1] * sec_f[:, 0] - prim_f[:, 0] * sec_f[:, 1]
    interf = jnp.stack((ifg_re, ifg_im), axis=1)
    upcoming = passed_along(interf[:, :, :LAG, :], "tile", -1)
    later = jnp.concatenate([interf[:, :, LAG:, :], upcoming], axis=2)
    l_re = later[:, 0]
    l_im = later[:, 1]
    weight = margin_mask.astype(jnp.float32)[None, :, None]
    e_re = jnp.sum(weight * (ifg_re * l_re + ifg_im * l_im), axis=(1, 2))
    e_im = jnp.sum(weight * (ifg_im * l_re - ifg_re * l_im), axis=(1, 2))
    power = jnp.sum(
        weight * 0.5 * (ifg_re * ifg_re + ifg_im * ifg_im + l_re * l_re + l_im * l_im), axis=(1, 2)
    )
    count = jnp.zeros_like(e_re) + jnp.sum(margin_mask.astype(jnp.float32)) * interf.shape[3]
    stats = jnp.stack((e_re, e_im, power, count), axis=1)
    totals = lax.psum(stats, "tile")
    magnitude = jnp.sqrt(totals[:, 0] * totals[:, 0] + totals[:, 1] * totals[:, 1])
    floor_val = (totals[:, 2] + 1e-06) / jnp.sqrt(jnp.maximum(totals[:, 3], 1.0))
    denom = jnp.maximum(magnitude, floor_val)
    u_re = (totals[:, 0] / denom)[:, None, None]
    u_im = (totals[:, 1] / denom)[:, None, None]
    c_re = multilook(ifg_re * u_re + ifg_im * u_im)
    c_im = multilook(ifg_im * u_re - ifg_re * u_im)
    return jnp.stack((c_re, c_im), axis=1)


def shards(secondary, primary, *rest):
    rows_n, width = primary.shape[1:]
    fits = rows_n % BAND == 0 and rows_n > 2 * LAG + BAND and width % LANE == 0
    tiles_n = lax.axis_size("tile")
    fits = fits and lax.axis_size("date") == 4 and tiles_n & (tiles_n - 1) == 0
    return (fused if fits else plain)(secondary, primary, *rest)


def solution(mesh):
    return jax.shard_map(
        shards,
        mesh=mesh,
        in_specs=(
            P("date", None, "tile", None),
            P(None, "tile", "date"),
            P("tile"),
            P("date", "tile"),
            P("date", "tile"),
            P("date", "tile"),
            P("date", "tile"),
        ),
        out_specs=P("date", None, "tile", None),
        check_vma=False,
    )
```

```python
import functools

import jax
import jax.numpy as jnp
from jax import lax
from jax.experimental import pallas as pl
from jax.experimental.pallas import tpu as pltpu
from jax.sharding import PartitionSpec as P

KA = 16
LAG = 64
LA = 2
LR = 8
LANE = 128
BAND = 128
HALO = 32
VMEM_LIMIT = 40 * 1024 * 1024


def passed_along(value, axis, steps):
    count = lax.axis_size(axis)
    initial, last = (max(0, -steps), min(count, count - steps))
    return lax.ppermute(value, axis, [(source, source + steps) for source in range(initial, last)])


def window(dist):
    return jnp.sinc(dist) * (0.5 + 0.5 * jnp.cos(jnp.pi * dist / 4.0))


def tap_rows(frac):
    dist = lax.broadcasted_iota(jnp.int32, (8, LANE), 0).astype(jnp.float32) - 3.0 - frac
    angle = jnp.pi * dist
    sinc = jnp.where(dist == 0.0, 1.0, jnp.sin(angle) / jnp.where(dist == 0.0, 1.0, angle))
    taps = sinc * (0.5 + 0.5 * jnp.cos(jnp.pi * dist / 4.0))
    return taps.astype(jnp.bfloat16).astype(jnp.float32)


def band(shape, distance, taps):
    total = jnp.zeros(shape, jnp.float32)
    for j in range(8):
        total = jnp.where(distance == j - 3, taps[j : j + 1, :1], total)
    return total.astype(jnp.bfloat16)


def cut_middle_kernel(prim_ref, *refs):
    cut_ref = refs[-1]
    cut_ref[...] = prim_ref[:, LAG : LAG + cut_ref.shape[1]]


def relay_kernel(block_ref, *refs):
    out_ref = refs[-1]
    out_ref[...] = block_ref[:, : out_ref.shape[1]]


def bands_kernel(ao_ref, ro_ref, af_ref, rf_ref, az_ref, rg_ref):
    shape = az_ref.shape
    offset = lax.broadcasted_iota(jnp.int32, shape, 1) - lax.broadcasted_iota(jnp.int32, shape, 0)
    az_ref[...] = band(shape, offset - HALO - ao_ref[...], tap_rows(af_ref[...]))
    square = rg_ref.shape[1:]
    offset = lax.broadcasted_iota(jnp.int32, square, 0) - lax.broadcasted_iota(jnp.int32, square, 1)
    taps = tap_rows(rf_ref[...])
    for at, shift in enumerate((-LANE, 0, LANE)):
        rg_ref[at] = band(square, offset + shift - ro_ref[...], taps)


def resample_kernel(sec_ref, low_ref, high_ref, az_ref, rg_ref, out_ref, azim_ref):
    rows_n, cols_n = sec_ref.shape[2:]
    az_band = az_ref[...]
    here, tiles_n = lax.axis_index("tile"), lax.axis_size("tile")
    none = jnp.zeros(low_ref.shape[1:], jnp.bfloat16)
    for part in range(2):
        for start in range(0, rows_n, BAND):
            pieces = []
            if start == 0:
                pieces.append(jnp.where(here == 0, none, low_ref[part]))
            pieces.append(sec_ref[0, part, max(0, start - HALO) : min(rows_n, start + BAND + HALO)])
            if start + BAND == rows_n:
                pieces.append(jnp.where(here == tiles_n - 1, none, high_ref[part]))
            rows = jnp.concatenate(pieces, axis=0) if len(pieces) > 1 else pieces[0]
            azim_ref[part, start : start + BAND] = jnp.dot(
                az_band, rows, preferred_element_type=jnp.float32
            ).astype(jnp.bfloat16)

    before, same, after = [rg_ref[at] for at in range(3)]
    none = jnp.zeros((LANE, LANE), jnp.bfloat16)
    blocks_n, _, _, width = out_ref.shape
    lanes_n = width // LANE
    columns = []
    for lane in range(lanes_n):
        column = [none] * (lanes_n + 2)
        column[lane], column[lane + 1], column[lane + 2] = before, same, after
        columns.append(jnp.concatenate(column, axis=0))
    rg_band = jnp.concatenate(columns, axis=1)
    for block in range(blocks_n):
        first = block * width - LANE
        last = (block + 1) * width + LANE
        taken = slice(max(first, 0), min(last, cols_n))
        used = rg_band[taken.start - first : taken.stop - first]
        for part in range(2):
            out_ref[block, part] = jnp.dot(
                azim_ref[part, :, taken], used, preferred_element_type=jnp.float32
            ).astype(jnp.bfloat16)


def interfere(prim_re, prim_im, sec_re, sec_im):
    p_re, p_im = prim_re.astype(jnp.float32), prim_im.astype(jnp.float32)
    s_re, s_im = sec_re.astype(jnp.float32), sec_im.astype(jnp.float32)
    return p_re * s_re + p_im * s_im, p_im * s_re - p_re * s_im


def look_columns(width, block, looks_n):
    shape = (width, looks_n)
    col = lax.broadcasted_iota(jnp.int32, shape, 0) + block * width
    look = lax.broadcasted_iota(jnp.int32, shape, 1) * LR
    return jnp.where((col >= look) & (col < look + LR), 1.0, 0.0).astype(jnp.bfloat16)


def look_rows(sums_ref, part, start, rows_n):
    count = rows_n // LA
    total = sums_ref[part, pl.ds(start, count, LA)]
    for row in range(1, LA):
        total = total + sums_ref[part, pl.ds(start + row, count, LA)]
    return total


def margin_kernel(
    own_ref, one_ref, two_ref, three_ref, res_ref, first_ref, last_ref, looks_ref, sums_ref
):
    here = lax.axis_index("date")
    _, _, rows_n, width = res_ref.shape
    whole, edges = (0, rows_n - LAG), (0, LAG)
    looks_n = looks_ref.shape[2]
    totals = [None, None]
    for step, (prim_ref, starts) in enumerate(
        ((own_ref, whole), (one_ref, edges), (two_ref, edges), (three_ref, edges))
    ):
        block = jnp.bitwise_xor(here, step)
        select = look_columns(width, block, looks_n)
        columns = pl.ds(pl.multiple_of(block * width, width), width)
        halves = []
        for held, start, target in zip(starts, whole, (first_ref, last_ref)):
            pair = interfere(
                prim_ref[0, held : held + LAG],
                prim_ref[1, held : held + LAG],
                res_ref[block, 0, start : start + LAG],
                res_ref[block, 1, start : start + LAG],
            )
            pair = [value.astype(jnp.bfloat16) for value in pair]
            for part in range(2):
                target[part, :, columns] = pair[part]
            halves.append(pair)
        for part in range(2):
            both = jnp.concatenate([halves[0][part], halves[1][part]], axis=0)
            summed = jnp.dot(both, select, preferred_element_type=jnp.float32)
            totals[part] = summed if step == 0 else totals[part] + summed
    for part in range(2):
        sums_ref[part] = totals[part]
        looks_ref[part] = look_rows(sums_ref, part, 0, 2 * LAG)


def stats_kernel(last_ref, later_ref, weight_ref, stats_ref):
    cols_n = last_ref.shape[2]
    weight = weight_ref[...]
    i_re, i_im = last_ref[0].astype(jnp.float32), last_ref[1].astype(jnp.float32)
    inside = jnp.where(lax.axis_index("tile") == lax.axis_size("tile") - 1, 0.0, 1.0)
    l_re, l_im = [later_ref[part].astype(jnp.float32) * inside for part in range(2)]
    values = (
        i_re * l_re + i_im * l_im,
        i_im * l_re - i_re * l_im,
        0.5 * (i_re * i_re + i_im * i_im + l_re * l_re + l_im * l_im),
    )
    rows = []
    for value in values:
        folded = value[:, :LANE]
        for start in range(LANE, cols_n, LANE):
            folded = folded + value[:, start : start + LANE]
        rows.append(jnp.sum(folded * weight, axis=0, keepdims=True))
    rows.append(jnp.sum(weight, axis=0, keepdims=True) * (cols_n // LANE))
    rows.append(jnp.zeros((4, LANE), jnp.float32))
    stats_ref[...] = jnp.concatenate(rows, axis=0)


def look_sums(pieces, res_ref, looks_n):
    here = lax.axis_index("date")
    _, _, rows_n, width = res_ref.shape
    middle_n = rows_n - 2 * LAG
    totals = [None, None]
    for at, (step, prim_ref) in enumerate(pieces):
        block = jnp.bitwise_xor(here, step)
        first = LAG if prim_ref.shape[1] == rows_n else 0
        select = look_columns(width, block, looks_n)
        pair = interfere(
            prim_ref[0, first : first + middle_n],
            prim_ref[1, first : first + middle_n],
            res_ref[block, 0, LAG : rows_n - LAG],
            res_ref[block, 1, LAG : rows_n - LAG],
        )
        for part in range(2):
            summed = jnp.dot(
                pair[part].astype(jnp.bfloat16), select, preferred_element_type=jnp.float32
            )
            totals[part] = summed if at == 0 else totals[part] + summed
    return totals


def middle_kernel(own_ref, one_ref, two_ref, res_ref, out_ref):
    pieces = ((0, own_ref), (1, one_ref), (2, two_ref))
    for part, total in enumerate(look_sums(pieces, res_ref, out_ref.shape[2])):
        out_ref[part] = total


def unit_kernel(mine_ref, other_ref, unit_ref):
    stats = jnp.sum(mine_ref[...] + other_ref[...], axis=1, keepdims=True)
    e_re, e_im, power, count = [stats[row : row + 1] for row in range(4)]
    magnitude = jnp.sqrt(e_re * e_re + e_im * e_im)
    floor_val = (power + 1e-06) / jnp.sqrt(jnp.maximum(count, 1.0))
    denom = jnp.maximum(magnitude, floor_val)
    row = lax.broadcasted_iota(jnp.int32, unit_ref.shape, 0)
    unit_ref[...] = jnp.where(row == 0, e_re / denom, e_im / denom) * (1.0 / (LA * LR))


def finish_kernel(
    three_ref, res_ref, before_ref, looks_ref, unit_ref, out_hbm, sums_ref, held_ref, sems
):
    middle_n = before_ref.shape[1]
    edge = LAG // LA
    u_re, u_im = unit_ref[0:1], unit_ref[1:2]
    copies = []

    def leave(at, held):
        rows = slice(at, at + held[0].shape[0])
        held_ref[0, rows] = held[0] * u_re + held[1] * u_im
        held_ref[1, rows] = held[1] * u_re - held[0] * u_im
        copy = pltpu.make_async_copy(
            held_ref.at[:, rows], out_hbm.at[0, :, rows], sems.at[len(copies)]
        )
        copy.start()
        copies.append(copy)

    leave(0, looks_ref[:, :edge])
    leave(edge + middle_n // LA, looks_ref[:, edge:])
    totals = look_sums(((3, three_ref),), res_ref, out_hbm.shape[3])
    for part, total in enumerate(totals):
        sums_ref[part] = total + before_ref[part]
    half = middle_n // 2
    for start in (0, half):
        leave(edge + start // LA, [look_rows(sums_ref, part, start, half) for part in range(2)])
    for copy in copies:
        copy.wait()


def call(kernel, outs, scratch, cost, *args, out_place=pltpu.VMEM):
    vmem = pl.BlockSpec(memory_space=pltpu.VMEM)
    out_spec = pl.BlockSpec(memory_space=out_place)
    return pl.pallas_call(
        kernel,
        out_shape=outs,
        in_specs=[vmem] * len(args),
        out_specs=jax.tree.map(lambda _: out_spec, outs),
        scratch_shapes=scratch,
        compiler_params=pltpu.CompilerParams(vmem_limit_bytes=VMEM_LIMIT),
        cost_estimate=pl.CostEstimate(flops=cost[0], bytes_accessed=cost[1], transcendentals=0),
    )(*args)


def ring(value, axis, step):
    count = lax.axis_size(axis)
    return lax.ppermute(value, axis, [(at, (at + step) % count) for at in range(count)])


def swap(value, axis, step):
    return lax.ppermute(value, axis, [(at, at ^ step) for at in range(lax.axis_size(axis))])


def fused(secondary, primary, margin_mask, az_off, rg_off, az_frac, rg_frac):
    _, _, rows_n, cols_n = secondary.shape
    width = primary.shape[2]
    dates_n = lax.axis_size("date")
    tiles_n = lax.axis_size("tile")
    bf16, f32 = jnp.bfloat16, jnp.float32
    shape = jax.ShapeDtypeStruct
    looks_n = cols_n // LR
    middle_n = rows_n - 2 * LAG
    edges = jnp.concatenate([primary[:, :LAG], primary[:, rows_n - LAG :]], axis=1)
    edges_two = swap(edges, "date", 2)
    edges_one = swap(edges, "date", 1)
    down, up = secondary[0, :, rows_n - HALO :], secondary[0, :, :HALO]
    low = ring(down, "tile", 1)
    high = ring(up, "tile", -1)
    az_band, rg_band = call(
        bands_kernel,
        (shape((BAND, BAND + 2 * HALO), bf16), shape((3, LANE, LANE), bf16)),
        [],
        (0, 0),
        az_off, rg_off, az_frac, rg_frac,
    )
    passed = call(
        relay_kernel, shape(edges.shape, bf16), [], (0, 0), edges_two
    )
    edges_three = swap(passed, "date", 1)
    middle = call(
        cut_middle_kernel,
        shape((2, middle_n + 16, width), bf16),
        [],
        (0, 0),
        primary, edges_two, edges_one,
    )
    weight = jnp.broadcast_to(margin_mask[rows_n - LAG :].astype(f32)[:, None], (LAG, LANE))
    res = call(
        resample_kernel,
        shape((dates_n, 2, rows_n, width), bf16),
        [pltpu.VMEM((2, rows_n, cols_n), bf16)],
        (0, 0),
        secondary, low, high, az_band, rg_band,
    )
    two, one = [swap(middle, "date", step) for step in (2, 1)]
    margin = shape((2, LAG, cols_n), bf16)
    first, last, looks = call(
        margin_kernel,
        (margin, margin, shape((2, 2 * LAG // LA, looks_n), f32)),
        [pltpu.VMEM((2, 2 * LAG, looks_n), f32)],
        (0, 0),
        primary, edges_one, edges_two, edges_three, res,
    )
    later = ring(first, "tile", -1)
    stats = call(
        stats_kernel,
        shape((8, LANE), f32),
        [],
        (0, 0),
        last, later, weight,
    )
    before = call(
        middle_kernel,
        shape((2, middle_n, looks_n), f32),
        [],
        (2 * 2 * middle_n * cols_n * looks_n, 8 * rows_n * cols_n),
        primary, one, two, res,
    )
    other = swap(stats, "tile", 1)
    block = shape((2, middle_n, width), bf16)
    relayed = call(relay_kernel, block, [], (0, 0), two, other,one)
    three = swap(relayed, "date", 1)
    stride = 2
    while stride < tiles_n:
        stats = stats + other
        other = swap(stats, "tile", stride)
        stride *= 2
    unit = call(unit_kernel, shape((8, LANE), f32), [], (0, 0), stats, other)
    return call(
        finish_kernel,
        shape((1, 2, rows_n // LA, looks_n), f32),
        [
            pltpu.VMEM((2, middle_n, looks_n), f32),
            pltpu.VMEM((2, rows_n // LA, looks_n), f32),
            pltpu.SemaphoreType.DMA((4,)),
        ],
        (2 * middle_n * cols_n * looks_n, 4 * rows_n * cols_n),
        three, res, before, looks, unit,
        out_place=pl.ANY,
    )


def padded(block, sides, width):
    for axis, dim in sides:
        low = passed_along(
            lax.slice_in_dim(block, block.shape[dim] - width, None, axis=dim), axis, 1
        )
        high = passed_along(lax.slice_in_dim(block, 0, width, axis=dim), axis, -1)
        block = jnp.concatenate([low, block, high], axis=dim)
    return block


def band_taps(offset, frac):
    inside = (offset >= -3) & (offset <= 4)
    return jnp.where(inside, window(offset.astype(jnp.float32) - frac), 0.0).astype(jnp.bfloat16)


def multilook(values):
    depth, rows_n, cols_n = values.shape
    return values.reshape(depth, rows_n // LA, LA, cols_n // LR, LR).mean(axis=(2, 4))


def plain(secondary, primary, margin_mask, az_off, rg_off, az_frac, rg_frac):
    rim_rows = KA + 4
    block_cols = 256
    image = secondary[0]
    rows_n = image.shape[1]
    cols_n = image.shape[2]
    extended = padded(image, (("tile", 1),), rim_rows)
    row_out = lax.broadcasted_iota(jnp.int32, (rows_n, rows_n + 2 * rim_rows), 0)
    row_in = lax.broadcasted_iota(jnp.int32, (rows_n, rows_n + 2 * rim_rows), 1)
    azim_taps = band_taps(row_in - row_out - az_off[0, 0] - rim_rows, az_frac[0, 0])
    azim = jnp.einsum(
        "im,kmc->kic", azim_taps, extended, preferred_element_type=jnp.float32
    ).astype(jnp.bfloat16)
    blocks_n = cols_n // block_cols
    col_pad = jnp.pad(azim, ((0, 0), (0, 0), (block_cols // 2, block_cols // 2)))
    pieces = col_pad.reshape(2, rows_n, blocks_n + 1, block_cols)
    inputs = jnp.concatenate([pieces[:, :, :-1], pieces[:, :, 1:]], axis=3)
    col_in = lax.broadcasted_iota(jnp.int32, (2 * block_cols, block_cols), 0)
    col_out = lax.broadcasted_iota(jnp.int32, (2 * block_cols, block_cols), 1)
    range_taps = band_taps(col_in - block_cols // 2 - col_out - rg_off[0, 0], rg_frac[0, 0])
    resampled = jnp.einsum("kibm,mn->kibn", inputs, range_taps, preferred_element_type=jnp.float32)
    resampled = resampled.reshape(2, rows_n, cols_n).astype(jnp.bfloat16)
    prim = lax.all_gather(primary, "date", axis=2, tiled=True)[None]
    sec_f = resampled[None].astype(jnp.float32)
    prim_f = prim.astype(jnp.float32)
    ifg_re = prim_f[:, 0] * sec_f[:, 0] + prim_f[:, 1] * sec_f[:, 1]
    ifg_im = prim_f[:, 1] * sec_f[:, 0] - prim_f[:, 0] * sec_f[:, 1]
    interf = jnp.stack((ifg_re, ifg_im), axis=1)
    upcoming = passed_along(interf[:, :, :LAG, :], "tile", -1)
    later = jnp.concatenate([interf[:, :, LAG:, :], upcoming], axis=2)
    l_re = later[:, 0]
    l_im = later[:, 1]
    weight = margin_mask.astype(jnp.float32)[None, :, None]
    e_re = jnp.sum(weight * (ifg_re * l_re + ifg_im * l_im), axis=(1, 2))
    e_im = jnp.sum(weight * (ifg_im * l_re - ifg_re * l_im), axis=(1, 2))
    power = jnp.sum(
        weight * 0.5 * (ifg_re * ifg_re + ifg_im * ifg_im + l_re * l_re + l_im * l_im), axis=(1, 2)
    )
    count = jnp.zeros_like(e_re) + jnp.sum(margin_mask.astype(jnp.float32)) * interf.shape[3]
    stats = jnp.stack((e_re, e_im, power, count), axis=1)
    totals = lax.psum(stats, "tile")
    magnitude = jnp.sqrt(totals[:, 0] * totals[:, 0] + totals[:, 1] * totals[:, 1])
    floor_val = (totals[:, 2] + 1e-06) / jnp.sqrt(jnp.maximum(totals[:, 3], 1.0))
    denom = jnp.maximum(magnitude, floor_val)
    u_re = (totals[:, 0] / denom)[:, None, None]
    u_im = (totals[:, 1] / denom)[:, None, None]
    c_re = multilook(ifg_re * u_re + ifg_im * u_im)
    c_im = multilook(ifg_im * u_re - ifg_re * u_im)
    return jnp.stack((c_re, c_im), axis=1)


def shards(secondary, primary, *rest):
    rows_n, width = primary.shape[1:]
    fits = rows_n % BAND == 0 and rows_n > 2 * LAG + BAND and width % LANE == 0
    tiles_n = lax.axis_size("tile")
    fits = fits and lax.axis_size("date") == 4 and tiles_n & (tiles_n - 1) == 0
    return (fused if fits else plain)(secondary, primary, *rest)


def solution(mesh):
    return jax.shard_map(
        shards,
        mesh=mesh,
        in_specs=(
            P("date", None, "tile", None),
            P(None, "tile", "date"),
            P("tile"),
            P("date", "tile"),
            P("date", "tile"),
            P("date", "tile"),
            P("date", "tile"),
        ),
        out_specs=P("date", None, "tile", None),
        check_vma=False,
    )
```

```python
import functools

import jax
import jax.numpy as jnp
from jax import lax
from jax.experimental import pallas as pl
from jax.experimental.pallas import tpu as pltpu
from jax.sharding import PartitionSpec as P

KA = 16
LAG = 64
LA = 2
LR = 8
LANE = 128
BAND = 128
CHUNK = 64
HALO = 32
VMEM_LIMIT = 40 * 1024 * 1024


def passed_along(value, axis, steps):
    count = lax.axis_size(axis)
    initial, last = (max(0, -steps), min(count, count - steps))
    return lax.ppermute(value, axis, [(source, source + steps) for source in range(initial, last)])


def window(dist):
    return jnp.sinc(dist) * (0.5 + 0.5 * jnp.cos(jnp.pi * dist / 4.0))


def tap_rows(frac):
    dist = lax.broadcasted_iota(jnp.int32, (8, LANE), 0).astype(jnp.float32) - 3.0 - frac
    angle = jnp.pi * dist
    sinc = jnp.where(dist == 0.0, 1.0, jnp.sin(angle) / jnp.where(dist == 0.0, 1.0, angle))
    taps = sinc * (0.5 + 0.5 * jnp.cos(jnp.pi * dist / 4.0))
    return taps.astype(jnp.bfloat16).astype(jnp.float32)


def band(shape, distance, taps):
    total = jnp.zeros(shape, jnp.float32)
    for j in range(8):
        total = jnp.where(distance == j - 3, taps[j : j + 1, :1], total)
    return total.astype(jnp.bfloat16)


def cut_middle_kernel(prim_ref, *refs):
    cut_ref = refs[-1]
    cut_ref[...] = prim_ref[:, LAG : LAG + cut_ref.shape[1]]


def relay_kernel(block_ref, *refs):
    out_ref = refs[-1]
    out_ref[...] = block_ref[:, : out_ref.shape[1]]


def bands_kernel(ao_ref, ro_ref, af_ref, rf_ref, az_ref, rg_ref):
    shape = az_ref.shape
    offset = lax.broadcasted_iota(jnp.int32, shape, 1) - lax.broadcasted_iota(jnp.int32, shape, 0)
    az_ref[...] = band(shape, offset - HALO - ao_ref[...], tap_rows(af_ref[...]))
    square = rg_ref.shape[1:]
    offset = lax.broadcasted_iota(jnp.int32, square, 0) - lax.broadcasted_iota(jnp.int32, square, 1)
    taps = tap_rows(rf_ref[...])
    for at, shift in enumerate((-LANE, 0, LANE)):
        rg_ref[at] = band(square, offset + shift - ro_ref[...], taps)


def resample_kernel(sec_ref, low_ref, high_ref, az_ref, rg_ref, out_ref, azim_ref):
    rows_n, cols_n = sec_ref.shape[2:]
    az_band = az_ref[...]
    here, tiles_n = lax.axis_index("tile"), lax.axis_size("tile")
    none = jnp.zeros(low_ref.shape[1:], jnp.bfloat16)
    for part in range(2):
        for start in range(0, rows_n, BAND):
            pieces = []
            if start == 0:
                pieces.append(jnp.where(here == 0, none, low_ref[part]))
            pieces.append(sec_ref[0, part, max(0, start - HALO) : min(rows_n, start + BAND + HALO)])
            if start + BAND == rows_n:
                pieces.append(jnp.where(here == tiles_n - 1, none, high_ref[part]))
            rows = jnp.concatenate(pieces, axis=0) if len(pieces) > 1 else pieces[0]
            azim_ref[part, start : start + BAND] = jnp.dot(
                az_band, rows, preferred_element_type=jnp.float32
            ).astype(jnp.bfloat16)

    before, same, after = [rg_ref[at] for at in range(3)]
    none = jnp.zeros((LANE, LANE), jnp.bfloat16)
    blocks_n, _, _, width = out_ref.shape
    lanes_n = width // LANE
    columns = []
    for lane in range(lanes_n):
        column = [none] * (lanes_n + 2)
        column[lane], column[lane + 1], column[lane + 2] = before, same, after
        columns.append(jnp.concatenate(column, axis=0))
    rg_band = jnp.concatenate(columns, axis=1)
    for block in range(blocks_n):
        first = block * width - LANE
        last = (block + 1) * width + LANE
        taken = slice(max(first, 0), min(last, cols_n))
        used = rg_band[taken.start - first : taken.stop - first]
        for part in range(2):
            out_ref[block, part] = jnp.dot(
                azim_ref[part, :, taken], used, preferred_element_type=jnp.float32
            ).astype(jnp.bfloat16)


def interfere(prim_re, prim_im, sec_re, sec_im):
    p_re, p_im = prim_re.astype(jnp.float32), prim_im.astype(jnp.float32)
    s_re, s_im = sec_re.astype(jnp.float32), sec_im.astype(jnp.float32)
    return p_re * s_re + p_im * s_im, p_im * s_re - p_re * s_im


def look_columns(width, block, looks_n):
    shape = (width, looks_n)
    col = lax.broadcasted_iota(jnp.int32, shape, 0) + block * width
    look = lax.broadcasted_iota(jnp.int32, shape, 1) * LR
    return jnp.where((col >= look) & (col < look + LR), 1.0, 0.0).astype(jnp.bfloat16)


def look_rows(sums_ref, part, start, rows_n):
    count = rows_n // LA
    total = sums_ref[part, pl.ds(start, count, LA)]
    for row in range(1, LA):
        total = total + sums_ref[part, pl.ds(start + row, count, LA)]
    return total


def margin_kernel(
    own_ref, one_ref, two_ref, three_ref, res_ref, first_ref, last_ref, looks_ref, sums_ref
):
    here = lax.axis_index("date")
    _, _, rows_n, width = res_ref.shape
    whole, edges = (0, rows_n - LAG), (0, LAG)
    looks_n = looks_ref.shape[2]
    totals = [None, None]
    for step, (prim_ref, starts) in enumerate(
        ((own_ref, whole), (one_ref, edges), (two_ref, edges), (three_ref, edges))
    ):
        block = jnp.bitwise_xor(here, step)
        select = look_columns(width, block, looks_n)
        columns = pl.ds(pl.multiple_of(block * width, width), width)
        halves = []
        for held, start, target in zip(starts, whole, (first_ref, last_ref)):
            pair = interfere(
                prim_ref[0, held : held + LAG],
                prim_ref[1, held : held + LAG],
                res_ref[block, 0, start : start + LAG],
                res_ref[block, 1, start : start + LAG],
            )
            pair = [value.astype(jnp.bfloat16) for value in pair]
            for part in range(2):
                target[part, :, columns] = pair[part]
            halves.append(pair)
        for part in range(2):
            both = jnp.concatenate([halves[0][part], halves[1][part]], axis=0)
            summed = jnp.dot(both, select, preferred_element_type=jnp.float32)
            totals[part] = summed if step == 0 else totals[part] + summed
    for part in range(2):
        sums_ref[part] = totals[part]
        looks_ref[part] = look_rows(sums_ref, part, 0, 2 * LAG)


def stats_kernel(last_ref, later_ref, weight_ref, stats_ref):
    cols_n = last_ref.shape[2]
    weight = weight_ref[...]
    i_re, i_im = last_ref[0].astype(jnp.float32), last_ref[1].astype(jnp.float32)
    inside = jnp.where(lax.axis_index("tile") == lax.axis_size("tile") - 1, 0.0, 1.0)
    l_re, l_im = [later_ref[part].astype(jnp.float32) * inside for part in range(2)]
    values = (
        i_re * l_re + i_im * l_im,
        i_im * l_re - i_re * l_im,
        0.5 * (i_re * i_re + i_im * i_im + l_re * l_re + l_im * l_im),
    )
    rows = []
    for value in values:
        folded = value[:, :LANE]
        for start in range(LANE, cols_n, LANE):
            folded = folded + value[:, start : start + LANE]
        rows.append(jnp.sum(folded * weight, axis=0, keepdims=True))
    rows.append(jnp.sum(weight, axis=0, keepdims=True) * (cols_n // LANE))
    rows.append(jnp.zeros((4, LANE), jnp.float32))
    stats_ref[...] = jnp.concatenate(rows, axis=0)


def look_sums(pieces, res_ref, out_ref, before_ref=None):
    here = lax.axis_index("date")
    _, _, rows_n, width = res_ref.shape
    plan = []
    for step, prim_ref in pieces:
        block = jnp.bitwise_xor(here, step)
        first = LAG if prim_ref.shape[1] == rows_n else 0
        plan.append((block, prim_ref, first, look_columns(width, block, out_ref.shape[2])))

    def chunk(at, carry):
        start = pl.multiple_of(at * CHUNK, CHUNK)
        rows = pl.ds(start, CHUNK)
        totals = [None, None] if before_ref is None else [before_ref[part, rows] for part in range(2)]
        for block, prim_ref, first, select in plan:
            held = pl.ds(pl.multiple_of(start + first, CHUNK), CHUNK)
            taken = pl.ds(pl.multiple_of(start + LAG, CHUNK), CHUNK)
            pair = interfere(
                prim_ref[0, held], prim_ref[1, held],
                res_ref[block, 0, taken], res_ref[block, 1, taken],
            )
            for part in range(2):
                summed = jnp.dot(
                    pair[part].astype(jnp.bfloat16), select, preferred_element_type=jnp.float32
                )
                totals[part] = summed if totals[part] is None else totals[part] + summed
        for part in range(2):
            out_ref[part, rows] = totals[part]
        return carry

    lax.fori_loop(0, (rows_n - 2 * LAG) // CHUNK, chunk, 0)


def middle_kernel(own_ref, one_ref, two_ref, res_ref, out_ref):
    look_sums(((0, own_ref), (1, one_ref), (2, two_ref)), res_ref, out_ref)


def unit_kernel(mine_ref, other_ref, unit_ref):
    stats = jnp.sum(mine_ref[...] + other_ref[...], axis=1, keepdims=True)
    e_re, e_im, power, count = [stats[row : row + 1] for row in range(4)]
    magnitude = jnp.sqrt(e_re * e_re + e_im * e_im)
    floor_val = (power + 1e-06) / jnp.sqrt(jnp.maximum(count, 1.0))
    denom = jnp.maximum(magnitude, floor_val)
    row = lax.broadcasted_iota(jnp.int32, unit_ref.shape, 0)
    unit_ref[...] = jnp.where(row == 0, e_re / denom, e_im / denom) * (1.0 / (LA * LR))


def finish_kernel(three_ref, res_ref, before_ref, looks_ref, unit_ref, out_ref, sums_ref):
    middle_n = before_ref.shape[1]
    edge = LAG // LA
    u_re, u_im = unit_ref[0:1], unit_ref[1:2]
    look_sums(((3, three_ref),), res_ref, sums_ref, before_ref)
    for at, held in (
        (0, looks_ref[:, :edge]),
        (edge, [look_rows(sums_ref, part, 0, middle_n) for part in range(2)]),
        (edge + middle_n // LA, looks_ref[:, edge:]),
    ):
        rows = slice(at, at + held[0].shape[0])
        out_ref[0, 0, rows] = held[0] * u_re + held[1] * u_im
        out_ref[0, 1, rows] = held[1] * u_re - held[0] * u_im


def call(kernel, outs, scratch, cost, *args):
    vmem = pl.BlockSpec(memory_space=pltpu.VMEM)
    return pl.pallas_call(
        kernel,
        out_shape=outs,
        in_specs=[vmem] * len(args),
        out_specs=jax.tree.map(lambda _: vmem, outs),
        scratch_shapes=scratch,
        compiler_params=pltpu.CompilerParams(vmem_limit_bytes=VMEM_LIMIT),
        cost_estimate=pl.CostEstimate(flops=cost[0], bytes_accessed=cost[1], transcendentals=0),
    )(*args)


def ring(value, axis, step):
    count = lax.axis_size(axis)
    return lax.ppermute(value, axis, [(at, (at + step) % count) for at in range(count)])


def swap(value, axis, step):
    return lax.ppermute(value, axis, [(at, at ^ step) for at in range(lax.axis_size(axis))])


def fused(secondary, primary, margin_mask, az_off, rg_off, az_frac, rg_frac):
    _, _, rows_n, cols_n = secondary.shape
    width = primary.shape[2]
    dates_n = lax.axis_size("date")
    tiles_n = lax.axis_size("tile")
    bf16, f32 = jnp.bfloat16, jnp.float32
    shape = jax.ShapeDtypeStruct
    looks_n = cols_n // LR
    middle_n = rows_n - 2 * LAG
    edges = jnp.concatenate([primary[:, :LAG], primary[:, rows_n - LAG :]], axis=1)
    edges_two = swap(edges, "date", 2)
    edges_one = swap(edges, "date", 1)
    down, up = secondary[0, :, rows_n - HALO :], secondary[0, :, :HALO]
    low = ring(down, "tile", 1)
    high = ring(up, "tile", -1)
    az_band, rg_band = call(
        bands_kernel,
        (shape((BAND, BAND + 2 * HALO), bf16), shape((3, LANE, LANE), bf16)),
        [],
        (0, 0),
        az_off, rg_off, az_frac, rg_frac,
    )
    passed = call(
        relay_kernel, shape(edges.shape, bf16), [], (0, 0), edges_two
    )
    edges_three = swap(passed, "date", 1)
    middle = call(
        cut_middle_kernel,
        shape((2, middle_n + 16, width), bf16),
        [],
        (0, 0),
        primary, edges_two, edges_one,
    )
    weight = jnp.broadcast_to(margin_mask[rows_n - LAG :].astype(f32)[:, None], (LAG, LANE))
    res = call(
        resample_kernel,
        shape((dates_n, 2, rows_n, width), bf16),
        [pltpu.VMEM((2, rows_n, cols_n), bf16)],
        (0, 0),
        secondary, low, high, az_band, rg_band,
    )
    two, one = [swap(middle, "date", step) for step in (2, 1)]
    margin = shape((2, LAG, cols_n), bf16)
    first, last, looks = call(
        margin_kernel,
        (margin, margin, shape((2, 2 * LAG // LA, looks_n), f32)),
        [pltpu.VMEM((2, 2 * LAG, looks_n), f32)],
        (0, 0),
        primary, edges_one, edges_two, edges_three, res,
    )
    later = ring(first, "tile", -1)
    stats = call(
        stats_kernel,
        shape((8, LANE), f32),
        [],
        (0, 0),
        last, later, weight,
    )
    before = call(
        middle_kernel,
        shape((2, middle_n, looks_n), f32),
        [],
        (2 * 2 * middle_n * cols_n * looks_n, 8 * rows_n * cols_n),
        primary, one, two, res,
    )
    other = swap(stats, "tile", 1)
    block = shape((2, middle_n, width), bf16)
    relayed = call(relay_kernel, block, [], (0, 0), two, other,one)
    three = swap(relayed, "date", 1)
    stride = 2
    while stride < tiles_n:
        stats = stats + other
        other = swap(stats, "tile", stride)
        stride *= 2
    unit = call(unit_kernel, shape((8, LANE), f32), [], (0, 0), stats, other)
    return call(
        finish_kernel,
        shape((1, 2, rows_n // LA, looks_n), f32),
        [pltpu.VMEM((2, middle_n, looks_n), f32)],
        (2 * middle_n * cols_n * looks_n, 4 * rows_n * cols_n),
        three, res, before, looks, unit,
    )


def padded(block, sides, width):
    for axis, dim in sides:
        low = passed_along(
            lax.slice_in_dim(block, block.shape[dim] - width, None, axis=dim), axis, 1
        )
        high = passed_along(lax.slice_in_dim(block, 0, width, axis=dim), axis, -1)
        block = jnp.concatenate([low, block, high], axis=dim)
    return block


def band_taps(offset, frac):
    inside = (offset >= -3) & (offset <= 4)
    return jnp.where(inside, window(offset.astype(jnp.float32) - frac), 0.0).astype(jnp.bfloat16)


def multilook(values):
    depth, rows_n, cols_n = values.shape
    return values.reshape(depth, rows_n // LA, LA, cols_n // LR, LR).mean(axis=(2, 4))


def plain(secondary, primary, margin_mask, az_off, rg_off, az_frac, rg_frac):
    rim_rows = KA + 4
    block_cols = 256
    image = secondary[0]
    rows_n = image.shape[1]
    cols_n = image.shape[2]
    extended = padded(image, (("tile", 1),), rim_rows)
    row_out = lax.broadcasted_iota(jnp.int32, (rows_n, rows_n + 2 * rim_rows), 0)
    row_in = lax.broadcasted_iota(jnp.int32, (rows_n, rows_n + 2 * rim_rows), 1)
    azim_taps = band_taps(row_in - row_out - az_off[0, 0] - rim_rows, az_frac[0, 0])
    azim = jnp.einsum(
        "im,kmc->kic", azim_taps, extended, preferred_element_type=jnp.float32
    ).astype(jnp.bfloat16)
    blocks_n = cols_n // block_cols
    col_pad = jnp.pad(azim, ((0, 0), (0, 0), (block_cols // 2, block_cols // 2)))
    pieces = col_pad.reshape(2, rows_n, blocks_n + 1, block_cols)
    inputs = jnp.concatenate([pieces[:, :, :-1], pieces[:, :, 1:]], axis=3)
    col_in = lax.broadcasted_iota(jnp.int32, (2 * block_cols, block_cols), 0)
    col_out = lax.broadcasted_iota(jnp.int32, (2 * block_cols, block_cols), 1)
    range_taps = band_taps(col_in - block_cols // 2 - col_out - rg_off[0, 0], rg_frac[0, 0])
    resampled = jnp.einsum("kibm,mn->kibn", inputs, range_taps, preferred_element_type=jnp.float32)
    resampled = resampled.reshape(2, rows_n, cols_n).astype(jnp.bfloat16)
    prim = lax.all_gather(primary, "date", axis=2, tiled=True)[None]
    sec_f = resampled[None].astype(jnp.float32)
    prim_f = prim.astype(jnp.float32)
    ifg_re = prim_f[:, 0] * sec_f[:, 0] + prim_f[:, 1] * sec_f[:, 1]
    ifg_im = prim_f[:, 1] * sec_f[:, 0] - prim_f[:, 0] * sec_f[:, 1]
    interf = jnp.stack((ifg_re, ifg_im), axis=1)
    upcoming = passed_along(interf[:, :, :LAG, :], "tile", -1)
    later = jnp.concatenate([interf[:, :, LAG:, :], upcoming], axis=2)
    l_re = later[:, 0]
    l_im = later[:, 1]
    weight = margin_mask.astype(jnp.float32)[None, :, None]
    e_re = jnp.sum(weight * (ifg_re * l_re + ifg_im * l_im), axis=(1, 2))
    e_im = jnp.sum(weight * (ifg_im * l_re - ifg_re * l_im), axis=(1, 2))
    power = jnp.sum(
        weight * 0.5 * (ifg_re * ifg_re + ifg_im * ifg_im + l_re * l_re + l_im * l_im), axis=(1, 2)
    )
    count = jnp.zeros_like(e_re) + jnp.sum(margin_mask.astype(jnp.float32)) * interf.shape[3]
    stats = jnp.stack((e_re, e_im, power, count), axis=1)
    totals = lax.psum(stats, "tile")
    magnitude = jnp.sqrt(totals[:, 0] * totals[:, 0] + totals[:, 1] * totals[:, 1])
    floor_val = (totals[:, 2] + 1e-06) / jnp.sqrt(jnp.maximum(totals[:, 3], 1.0))
    denom = jnp.maximum(magnitude, floor_val)
    u_re = (totals[:, 0] / denom)[:, None, None]
    u_im = (totals[:, 1] / denom)[:, None, None]
    c_re = multilook(ifg_re * u_re + ifg_im * u_im)
    c_im = multilook(ifg_im * u_re - ifg_re * u_im)
    return jnp.stack((c_re, c_im), axis=1)


def shards(secondary, primary, *rest):
    rows_n, width = primary.shape[1:]
    fits = rows_n % BAND == 0 and rows_n > 2 * LAG + BAND and width % LANE == 0
    tiles_n = lax.axis_size("tile")
    fits = fits and lax.axis_size("date") == 4 and tiles_n & (tiles_n - 1) == 0
    return (fused if fits else plain)(secondary, primary, *rest)


def solution(mesh):
    return jax.shard_map(
        shards,
        mesh=mesh,
        in_specs=(
            P("date", None, "tile", None),
            P(None, "tile", "date"),
            P("tile"),
            P("date", "tile"),
            P("date", "tile"),
            P("date", "tile"),
            P("date", "tile"),
        ),
        out_specs=P("date", None, "tile", None),
        check_vma=False,
    )
```

```python
import functools

import jax
import jax.numpy as jnp
from jax import lax
from jax.experimental import pallas as pl
from jax.experimental.pallas import tpu as pltpu
from jax.sharding import PartitionSpec as P

KA = 16
LAG = 64
LA = 2
LR = 8
LANE = 128
BAND = 128
HALO = 32
VMEM_LIMIT = 40 * 1024 * 1024


def passed_along(value, axis, steps):
    count = lax.axis_size(axis)
    initial, last = (max(0, -steps), min(count, count - steps))
    return lax.ppermute(value, axis, [(source, source + steps) for source in range(initial, last)])


def window(dist):
    return jnp.sinc(dist) * (0.5 + 0.5 * jnp.cos(jnp.pi * dist / 4.0))


def tap_rows(frac):
    dist = lax.broadcasted_iota(jnp.int32, (8, LANE), 0).astype(jnp.float32) - 3.0 - frac
    angle = jnp.pi * dist
    sinc = jnp.where(dist == 0.0, 1.0, jnp.sin(angle) / jnp.where(dist == 0.0, 1.0, angle))
    taps = sinc * (0.5 + 0.5 * jnp.cos(jnp.pi * dist / 4.0))
    return taps.astype(jnp.bfloat16).astype(jnp.float32)


def band(shape, distance, taps):
    total = jnp.zeros(shape, jnp.float32)
    for j in range(8):
        total = jnp.where(distance == j - 3, taps[j : j + 1, :1], total)
    return total.astype(jnp.bfloat16)


def cut_middle_kernel(prim_ref, *refs):
    cut_ref = refs[-1]
    cut_ref[...] = prim_ref[:, LAG : LAG + cut_ref.shape[1]]


def relay_kernel(block_ref, *refs):
    out_ref = refs[-1]
    out_ref[...] = block_ref[:, : out_ref.shape[1]]


def bands_kernel(ao_ref, ro_ref, af_ref, rf_ref, az_ref, rg_ref):
    shape = az_ref.shape
    offset = lax.broadcasted_iota(jnp.int32, shape, 1) - lax.broadcasted_iota(jnp.int32, shape, 0)
    az_ref[...] = band(shape, offset - HALO - ao_ref[...], tap_rows(af_ref[...]))
    square = rg_ref.shape[1:]
    offset = lax.broadcasted_iota(jnp.int32, square, 0) - lax.broadcasted_iota(jnp.int32, square, 1)
    taps = tap_rows(rf_ref[...])
    for at, shift in enumerate((-LANE, 0, LANE)):
        rg_ref[at] = band(square, offset + shift - ro_ref[...], taps)


def resample_kernel(sec_ref, low_ref, high_ref, az_ref, rg_ref, out_ref, azim_ref):
    rows_n, cols_n = sec_ref.shape[2:]
    az_band = az_ref[...]
    here, tiles_n = lax.axis_index("tile"), lax.axis_size("tile")
    none = jnp.zeros(low_ref.shape[1:], jnp.bfloat16)
    for part in range(2):
        for start in range(0, rows_n, BAND):
            pieces = []
            if start == 0:
                pieces.append(jnp.where(here == 0, none, low_ref[part]))
            pieces.append(sec_ref[0, part, max(0, start - HALO) : min(rows_n, start + BAND + HALO)])
            if start + BAND == rows_n:
                pieces.append(jnp.where(here == tiles_n - 1, none, high_ref[part]))
            rows = jnp.concatenate(pieces, axis=0) if len(pieces) > 1 else pieces[0]
            azim_ref[part, start : start + BAND] = jnp.dot(
                az_band, rows, preferred_element_type=jnp.float32
            ).astype(jnp.bfloat16)

    before, same, after = [rg_ref[at] for at in range(3)]
    none = jnp.zeros((LANE, LANE), jnp.bfloat16)
    blocks_n, _, _, width = out_ref.shape
    lanes_n = width // LANE
    columns = []
    for lane in range(lanes_n):
        column = [none] * (lanes_n + 2)
        column[lane], column[lane + 1], column[lane + 2] = before, same, after
        columns.append(jnp.concatenate(column, axis=0))
    rg_band = jnp.concatenate(columns, axis=1)
    for block in range(blocks_n):
        first = block * width - LANE
        last = (block + 1) * width + LANE
        taken = slice(max(first, 0), min(last, cols_n))
        used = rg_band[taken.start - first : taken.stop - first]
        for part in range(2):
            out_ref[block, part] = jnp.dot(
                azim_ref[part, :, taken], used, preferred_element_type=jnp.float32
            ).astype(jnp.bfloat16)


def interfere(prim_re, prim_im, sec_re, sec_im):
    p_re, p_im = prim_re.astype(jnp.float32), prim_im.astype(jnp.float32)
    s_re, s_im = sec_re.astype(jnp.float32), sec_im.astype(jnp.float32)
    return p_re * s_re + p_im * s_im, p_im * s_re - p_re * s_im


def look_columns(width, block, looks_n):
    shape = (width, looks_n)
    col = lax.broadcasted_iota(jnp.int32, shape, 0) + block * width
    look = lax.broadcasted_iota(jnp.int32, shape, 1) * LR
    return jnp.where((col >= look) & (col < look + LR), 1.0, 0.0).astype(jnp.bfloat16)


def look_rows(sums_ref, part, start, rows_n):
    count = rows_n // LA
    total = sums_ref[part, pl.ds(start, count, LA)]
    for row in range(1, LA):
        total = total + sums_ref[part, pl.ds(start + row, count, LA)]
    return total


def margin_kernel(
    own_ref, one_ref, two_ref, three_ref, res_ref, first_ref, last_ref, looks_ref, sums_ref
):
    here = lax.axis_index("date")
    _, _, rows_n, width = res_ref.shape
    whole, edges = (0, rows_n - LAG), (0, LAG)
    looks_n = looks_ref.shape[2]
    totals = [None, None]
    for step, (prim_ref, starts) in enumerate(
        ((own_ref, whole), (one_ref, edges), (two_ref, edges), (three_ref, edges))
    ):
        block = jnp.bitwise_xor(here, step)
        select = look_columns(width, block, looks_n)
        columns = pl.ds(pl.multiple_of(block * width, width), width)
        halves = []
        for held, start, target in zip(starts, whole, (first_ref, last_ref)):
            pair = interfere(
                prim_ref[0, held : held + LAG],
                prim_ref[1, held : held + LAG],
                res_ref[block, 0, start : start + LAG],
                res_ref[block, 1, start : start + LAG],
            )
            pair = [value.astype(jnp.bfloat16) for value in pair]
            for part in range(2):
                target[part, :, columns] = pair[part]
            halves.append(pair)
        for part in range(2):
            both = jnp.concatenate([halves[0][part], halves[1][part]], axis=0)
            summed = jnp.dot(both, select, preferred_element_type=jnp.float32)
            totals[part] = summed if step == 0 else totals[part] + summed
    for part in range(2):
        sums_ref[part] = totals[part]
        looks_ref[part] = look_rows(sums_ref, part, 0, 2 * LAG)


def stats_kernel(last_ref, later_ref, weight_ref, stats_ref):
    cols_n = last_ref.shape[2]
    weight = weight_ref[...]
    i_re, i_im = last_ref[0].astype(jnp.float32), last_ref[1].astype(jnp.float32)
    inside = jnp.where(lax.axis_index("tile") == lax.axis_size("tile") - 1, 0.0, 1.0)
    l_re, l_im = [later_ref[part].astype(jnp.float32) * inside for part in range(2)]
    values = (
        i_re * l_re + i_im * l_im,
        i_im * l_re - i_re * l_im,
        0.5 * (i_re * i_re + i_im * i_im + l_re * l_re + l_im * l_im),
    )
    rows = []
    for value in values:
        folded = value[:, :LANE]
        for start in range(LANE, cols_n, LANE):
            folded = folded + value[:, start : start + LANE]
        rows.append(jnp.sum(folded * weight, axis=0, keepdims=True))
    rows.append(jnp.sum(weight, axis=0, keepdims=True) * (cols_n // LANE))
    rows.append(jnp.zeros((4, LANE), jnp.float32))
    stats_ref[...] = jnp.concatenate(rows, axis=0)


def look_sums(pieces, res_ref, looks_n):
    here = lax.axis_index("date")
    _, _, rows_n, width = res_ref.shape
    middle_n = rows_n - 2 * LAG
    totals = [None, None]
    for at, (step, prim_ref) in enumerate(pieces):
        block = jnp.bitwise_xor(here, step)
        first = LAG if prim_ref.shape[1] == rows_n else 0
        select = look_columns(width, block, looks_n)
        pair = interfere(
            prim_ref[0, first : first + middle_n],
            prim_ref[1, first : first + middle_n],
            res_ref[block, 0, LAG : rows_n - LAG],
            res_ref[block, 1, LAG : rows_n - LAG],
        )
        for part in range(2):
            summed = jnp.dot(
                pair[part].astype(jnp.bfloat16), select, preferred_element_type=jnp.float32
            )
            totals[part] = summed if at == 0 else totals[part] + summed
    return totals


def middle_kernel(own_ref, one_ref, two_ref, res_ref, out_ref):
    pieces = ((0, own_ref), (1, one_ref), (2, two_ref))
    for part, total in enumerate(look_sums(pieces, res_ref, out_ref.shape[2])):
        out_ref[part] = total


def last_kernel(three_ref, res_ref, before_ref, looks_ref, out_ref, sums_ref):
    middle_n = before_ref.shape[1]
    edge = LAG // LA
    totals = look_sums(((3, three_ref),), res_ref, out_ref.shape[2])
    for part, total in enumerate(totals):
        sums_ref[part] = total + before_ref[part]
        out_ref[part, :edge] = looks_ref[part, :edge]
        out_ref[part, edge : edge + middle_n // LA] = look_rows(sums_ref, part, 0, middle_n)
        out_ref[part, edge + middle_n // LA :] = looks_ref[part, edge:]


def scale_kernel(looks_ref, mine_ref, other_ref, out_ref):
    stats = jnp.sum(mine_ref[...] + other_ref[...], axis=1, keepdims=True)
    e_re, e_im, power, count = [stats[row : row + 1] for row in range(4)]
    magnitude = jnp.sqrt(e_re * e_re + e_im * e_im)
    floor_val = (power + 1e-06) / jnp.sqrt(jnp.maximum(count, 1.0))
    denom = jnp.maximum(magnitude, floor_val)
    u_re = e_re / denom * (1.0 / (LA * LR))
    u_im = e_im / denom * (1.0 / (LA * LR))
    out_ref[0, 0] = looks_ref[0] * u_re + looks_ref[1] * u_im
    out_ref[0, 1] = looks_ref[1] * u_re - looks_ref[0] * u_im


def call(kernel, outs, scratch, cost, *args):
    vmem = pl.BlockSpec(memory_space=pltpu.VMEM)
    return pl.pallas_call(
        kernel,
        out_shape=outs,
        in_specs=[vmem] * len(args),
        out_specs=jax.tree.map(lambda _: vmem, outs),
        scratch_shapes=scratch,
        compiler_params=pltpu.CompilerParams(vmem_limit_bytes=VMEM_LIMIT),
        cost_estimate=pl.CostEstimate(flops=cost[0], bytes_accessed=cost[1], transcendentals=0),
    )(*args)


def ring(value, axis, step):
    count = lax.axis_size(axis)
    return lax.ppermute(value, axis, [(at, (at + step) % count) for at in range(count)])


def swap(value, axis, step):
    return lax.ppermute(value, axis, [(at, at ^ step) for at in range(lax.axis_size(axis))])


def fused(secondary, primary, margin_mask, az_off, rg_off, az_frac, rg_frac):
    _, _, rows_n, cols_n = secondary.shape
    width = primary.shape[2]
    dates_n = lax.axis_size("date")
    tiles_n = lax.axis_size("tile")
    bf16, f32 = jnp.bfloat16, jnp.float32
    shape = jax.ShapeDtypeStruct
    looks_n = cols_n // LR
    middle_n = rows_n - 2 * LAG
    edges = jnp.concatenate([primary[:, :LAG], primary[:, rows_n - LAG :]], axis=1)
    edges_two = swap(edges, "date", 2)
    edges_one = swap(edges, "date", 1)
    down, up = secondary[0, :, rows_n - HALO :], secondary[0, :, :HALO]
    low = ring(down, "tile", 1)
    high = ring(up, "tile", -1)
    az_band, rg_band = call(
        bands_kernel,
        (shape((BAND, BAND + 2 * HALO), bf16), shape((3, LANE, LANE), bf16)),
        [],
        (0, 0),
        az_off, rg_off, az_frac, rg_frac,
    )
    passed = call(
        relay_kernel, shape(edges.shape, bf16), [], (0, 0), edges_two
    )
    edges_three = swap(passed, "date", 1)
    middle = call(
        cut_middle_kernel,
        shape((2, middle_n + 16, width), bf16),
        [],
        (0, 0),
        primary, edges_two, edges_one,
    )
    weight = jnp.broadcast_to(margin_mask[rows_n - LAG :].astype(f32)[:, None], (LAG, LANE))
    res = call(
        resample_kernel,
        shape((dates_n, 2, rows_n, width), bf16),
        [pltpu.VMEM((2, rows_n, cols_n), bf16)],
        (0, 0),
        secondary, low, high, az_band, rg_band,
    )
    two, one = [swap(middle, "date", step) for step in (2, 1)]
    margin = shape((2, LAG, cols_n), bf16)
    first, last, looks = call(
        margin_kernel,
        (margin, margin, shape((2, 2 * LAG // LA, looks_n), f32)),
        [pltpu.VMEM((2, 2 * LAG, looks_n), f32)],
        (0, 0),
        primary, edges_one, edges_two, edges_three, res,
    )
    later = ring(first, "tile", -1)
    stats = call(
        stats_kernel,
        shape((8, LANE), f32),
        [],
        (0, 0),
        last, later, weight,
    )
    before = call(
        middle_kernel,
        shape((2, middle_n, looks_n), f32),
        [],
        (2 * 2 * middle_n * cols_n * looks_n, 8 * rows_n * cols_n),
        primary, one, two, res,
    )
    other = swap(stats, "tile", 1)
    block = shape((2, middle_n, width), bf16)
    relayed = call(relay_kernel, block, [], (0, 0), two, other,one)
    three = swap(relayed, "date", 1)
    stride = 2
    while stride < tiles_n:
        stats = stats + other
        other = swap(stats, "tile", stride)
        stride *= 2
    looks = call(
        last_kernel,
        shape((2, rows_n // LA, looks_n), f32),
        [pltpu.VMEM((2, middle_n, looks_n), f32)],
        (2 * middle_n * cols_n * looks_n, 4 * rows_n * cols_n),
        three, res, before, looks,
    )
    return call(
        scale_kernel,
        shape((1, 2, rows_n // LA, looks_n), f32),
        [],
        (8 * rows_n * looks_n, 8 * rows_n * looks_n),
        looks, stats, other,
    )


def padded(block, sides, width):
    for axis, dim in sides:
        low = passed_along(
            lax.slice_in_dim(block, block.shape[dim] - width, None, axis=dim), axis, 1
        )
        high = passed_along(lax.slice_in_dim(block, 0, width, axis=dim), axis, -1)
        block = jnp.concatenate([low, block, high], axis=dim)
    return block


def band_taps(offset, frac):
    inside = (offset >= -3) & (offset <= 4)
    return jnp.where(inside, window(offset.astype(jnp.float32) - frac), 0.0).astype(jnp.bfloat16)


def multilook(values):
    depth, rows_n, cols_n = values.shape
    return values.reshape(depth, rows_n // LA, LA, cols_n // LR, LR).mean(axis=(2, 4))


def plain(secondary, primary, margin_mask, az_off, rg_off, az_frac, rg_frac):
    rim_rows = KA + 4
    block_cols = 256
    image = secondary[0]
    rows_n = image.shape[1]
    cols_n = image.shape[2]
    extended = padded(image, (("tile", 1),), rim_rows)
    row_out = lax.broadcasted_iota(jnp.int32, (rows_n, rows_n + 2 * rim_rows), 0)
    row_in = lax.broadcasted_iota(jnp.int32, (rows_n, rows_n + 2 * rim_rows), 1)
    azim_taps = band_taps(row_in - row_out - az_off[0, 0] - rim_rows, az_frac[0, 0])
    azim = jnp.einsum(
        "im,kmc->kic", azim_taps, extended, preferred_element_type=jnp.float32
    ).astype(jnp.bfloat16)
    blocks_n = cols_n // block_cols
    col_pad = jnp.pad(azim, ((0, 0), (0, 0), (block_cols // 2, block_cols // 2)))
    pieces = col_pad.reshape(2, rows_n, blocks_n + 1, block_cols)
    inputs = jnp.concatenate([pieces[:, :, :-1], pieces[:, :, 1:]], axis=3)
    col_in = lax.broadcasted_iota(jnp.int32, (2 * block_cols, block_cols), 0)
    col_out = lax.broadcasted_iota(jnp.int32, (2 * block_cols, block_cols), 1)
    range_taps = band_taps(col_in - block_cols // 2 - col_out - rg_off[0, 0], rg_frac[0, 0])
    resampled = jnp.einsum("kibm,mn->kibn", inputs, range_taps, preferred_element_type=jnp.float32)
    resampled = resampled.reshape(2, rows_n, cols_n).astype(jnp.bfloat16)
    prim = lax.all_gather(primary, "date", axis=2, tiled=True)[None]
    sec_f = resampled[None].astype(jnp.float32)
    prim_f = prim.astype(jnp.float32)
    ifg_re = prim_f[:, 0] * sec_f[:, 0] + prim_f[:, 1] * sec_f[:, 1]
    ifg_im = prim_f[:, 1] * sec_f[:, 0] - prim_f[:, 0] * sec_f[:, 1]
    interf = jnp.stack((ifg_re, ifg_im), axis=1)
    upcoming = passed_along(interf[:, :, :LAG, :], "tile", -1)
    later = jnp.concatenate([interf[:, :, LAG:, :], upcoming], axis=2)
    l_re = later[:, 0]
    l_im = later[:, 1]
    weight = margin_mask.astype(jnp.float32)[None, :, None]
    e_re = jnp.sum(weight * (ifg_re * l_re + ifg_im * l_im), axis=(1, 2))
    e_im = jnp.sum(weight * (ifg_im * l_re - ifg_re * l_im), axis=(1, 2))
    power = jnp.sum(
        weight * 0.5 * (ifg_re * ifg_re + ifg_im * ifg_im + l_re * l_re + l_im * l_im), axis=(1, 2)
    )
    count = jnp.zeros_like(e_re) + jnp.sum(margin_mask.astype(jnp.float32)) * interf.shape[3]
    stats = jnp.stack((e_re, e_im, power, count), axis=1)
    totals = lax.psum(stats, "tile")
    magnitude = jnp.sqrt(totals[:, 0] * totals[:, 0] + totals[:, 1] * totals[:, 1])
    floor_val = (totals[:, 2] + 1e-06) / jnp.sqrt(jnp.maximum(totals[:, 3], 1.0))
    denom = jnp.maximum(magnitude, floor_val)
    u_re = (totals[:, 0] / denom)[:, None, None]
    u_im = (totals[:, 1] / denom)[:, None, None]
    c_re = multilook(ifg_re * u_re + ifg_im * u_im)
    c_im = multilook(ifg_im * u_re - ifg_re * u_im)
    return jnp.stack((c_re, c_im), axis=1)


def shards(secondary, primary, *rest):
    rows_n, width = primary.shape[1:]
    fits = rows_n % BAND == 0 and rows_n > 2 * LAG + BAND and width % LANE == 0
    tiles_n = lax.axis_size("tile")
    fits = fits and lax.axis_size("date") == 4 and tiles_n & (tiles_n - 1) == 0
    return (fused if fits else plain)(secondary, primary, *rest)


def solution(mesh):
    return jax.shard_map(
        shards,
        mesh=mesh,
        in_specs=(
            P("date", None, "tile", None),
            P(None, "tile", "date"),
            P("tile"),
            P("date", "tile"),
            P("date", "tile"),
            P("date", "tile"),
            P("date", "tile"),
        ),
        out_specs=P("date", None, "tile", None),
        check_vma=False,
    )
```

```python
import functools

import jax
import jax.numpy as jnp
from jax import lax
from jax.experimental import pallas as pl
from jax.experimental.pallas import tpu as pltpu
from jax.sharding import PartitionSpec as P

KA = 16
LAG = 64
LA = 2
LR = 8
LANE = 128
BAND = 128
HALO = 32
VMEM_LIMIT = 40 * 1024 * 1024


def passed_along(value, axis, steps):
    count = lax.axis_size(axis)
    initial, last = (max(0, -steps), min(count, count - steps))
    return lax.ppermute(value, axis, [(source, source + steps) for source in range(initial, last)])


def window(dist):
    return jnp.sinc(dist) * (0.5 + 0.5 * jnp.cos(jnp.pi * dist / 4.0))


def tap_rows(frac):
    dist = lax.broadcasted_iota(jnp.int32, (8, LANE), 0).astype(jnp.float32) - 3.0 - frac
    angle = jnp.pi * dist
    sinc = jnp.where(dist == 0.0, 1.0, jnp.sin(angle) / jnp.where(dist == 0.0, 1.0, angle))
    taps = sinc * (0.5 + 0.5 * jnp.cos(jnp.pi * dist / 4.0))
    return taps.astype(jnp.bfloat16).astype(jnp.float32)


def band(shape, distance, taps):
    total = jnp.zeros(shape, jnp.float32)
    for j in range(8):
        total = jnp.where(distance == j - 3, taps[j : j + 1, :1], total)
    return total.astype(jnp.bfloat16)


def cut_middle_kernel(prim_ref, *refs):
    cut_ref = refs[-1]
    cut_ref[...] = prim_ref[:, LAG : LAG + cut_ref.shape[1]]


def relay_kernel(block_ref, *refs):
    out_ref = refs[-1]
    out_ref[...] = block_ref[:, : out_ref.shape[1]]


def bands_kernel(ao_ref, ro_ref, af_ref, rf_ref, az_ref, rg_ref):
    shape = az_ref.shape
    offset = lax.broadcasted_iota(jnp.int32, shape, 1) - lax.broadcasted_iota(jnp.int32, shape, 0)
    az_ref[...] = band(shape, offset - HALO - ao_ref[...], tap_rows(af_ref[...]))
    square = rg_ref.shape[1:]
    offset = lax.broadcasted_iota(jnp.int32, square, 0) - lax.broadcasted_iota(jnp.int32, square, 1)
    taps = tap_rows(rf_ref[...])
    for at, shift in enumerate((-LANE, 0, LANE)):
        rg_ref[at] = band(square, offset + shift - ro_ref[...], taps)


def resample_kernel(sec_ref, low_ref, high_ref, az_ref, rg_ref, out_ref, azim_ref):
    rows_n, cols_n = sec_ref.shape[2:]
    az_band = az_ref[...]
    here, tiles_n = lax.axis_index("tile"), lax.axis_size("tile")
    none = jnp.zeros(low_ref.shape[1:], jnp.bfloat16)
    for part in range(2):
        for start in range(0, rows_n, BAND):
            pieces = []
            if start == 0:
                pieces.append(jnp.where(here == 0, none, low_ref[part]))
            pieces.append(sec_ref[0, part, max(0, start - HALO) : min(rows_n, start + BAND + HALO)])
            if start + BAND == rows_n:
                pieces.append(jnp.where(here == tiles_n - 1, none, high_ref[part]))
            rows = jnp.concatenate(pieces, axis=0) if len(pieces) > 1 else pieces[0]
            azim_ref[part, start : start + BAND] = jnp.dot(
                az_band, rows, preferred_element_type=jnp.float32
            ).astype(jnp.bfloat16)

    before, same, after = [rg_ref[at] for at in range(3)]
    none = jnp.zeros((LANE, LANE), jnp.bfloat16)
    blocks_n, _, _, width = out_ref.shape
    lanes_n = width // LANE
    columns = []
    for lane in range(lanes_n):
        column = [none] * (lanes_n + 2)
        column[lane], column[lane + 1], column[lane + 2] = before, same, after
        columns.append(jnp.concatenate(column, axis=0))
    rg_band = jnp.concatenate(columns, axis=1)
    for block in range(blocks_n):
        first = block * width - LANE
        last = (block + 1) * width + LANE
        taken = slice(max(first, 0), min(last, cols_n))
        used = rg_band[taken.start - first : taken.stop - first]
        for part in range(2):
            out_ref[block, part] = jnp.dot(
                azim_ref[part, :, taken], used, preferred_element_type=jnp.float32
            ).astype(jnp.bfloat16)


def interfere(prim_re, prim_im, sec_re, sec_im):
    p_re, p_im = prim_re.astype(jnp.float32), prim_im.astype(jnp.float32)
    s_re, s_im = sec_re.astype(jnp.float32), sec_im.astype(jnp.float32)
    return p_re * s_re + p_im * s_im, p_im * s_re - p_re * s_im


def look_columns(width, block, looks_n):
    shape = (width, looks_n)
    col = lax.broadcasted_iota(jnp.int32, shape, 0) + block * width
    look = lax.broadcasted_iota(jnp.int32, shape, 1) * LR
    return jnp.where((col >= look) & (col < look + LR), 1.0, 0.0).astype(jnp.bfloat16)


def look_rows(sums_ref, part, start, rows_n):
    count = rows_n // LA
    total = sums_ref[part, pl.ds(start, count, LA)]
    for row in range(1, LA):
        total = total + sums_ref[part, pl.ds(start + row, count, LA)]
    return total


def margin_kernel(
    own_ref, one_ref, two_ref, three_ref, res_ref, first_ref, last_ref, looks_ref, sums_ref
):
    here = lax.axis_index("date")
    _, _, rows_n, width = res_ref.shape
    whole, edges = (0, rows_n - LAG), (0, LAG)
    looks_n = looks_ref.shape[2]
    totals = [None, None]
    for step, (prim_ref, starts) in enumerate(
        ((own_ref, whole), (one_ref, edges), (two_ref, edges), (three_ref, edges))
    ):
        block = jnp.bitwise_xor(here, step)
        select = look_columns(width, block, looks_n)
        columns = pl.ds(pl.multiple_of(block * width, width), width)
        halves = []
        for held, start, target in zip(starts, whole, (first_ref, last_ref)):
            pair = interfere(
                prim_ref[0, held : held + LAG],
                prim_ref[1, held : held + LAG],
                res_ref[block, 0, start : start + LAG],
                res_ref[block, 1, start : start + LAG],
            )
            pair = [value.astype(jnp.bfloat16) for value in pair]
            for part in range(2):
                target[part, :, columns] = pair[part]
            halves.append(pair)
        for part in range(2):
            both = jnp.concatenate([halves[0][part], halves[1][part]], axis=0)
            summed = jnp.dot(both, select, preferred_element_type=jnp.float32)
            totals[part] = summed if step == 0 else totals[part] + summed
    for part in range(2):
        sums_ref[part] = totals[part]
        looks_ref[part] = look_rows(sums_ref, part, 0, 2 * LAG)


def stats_kernel(last_ref, later_ref, weight_ref, stats_ref):
    cols_n = last_ref.shape[2]
    weight = weight_ref[...]
    i_re, i_im = last_ref[0].astype(jnp.float32), last_ref[1].astype(jnp.float32)
    inside = jnp.where(lax.axis_index("tile") == lax.axis_size("tile") - 1, 0.0, 1.0)
    l_re, l_im = [later_ref[part].astype(jnp.float32) * inside for part in range(2)]
    values = (
        i_re * l_re + i_im * l_im,
        i_im * l_re - i_re * l_im,
        0.5 * (i_re * i_re + i_im * i_im + l_re * l_re + l_im * l_im),
    )
    rows = []
    for value in values:
        folded = value[:, :LANE]
        for start in range(LANE, cols_n, LANE):
            folded = folded + value[:, start : start + LANE]
        rows.append(jnp.sum(folded * weight, axis=0, keepdims=True))
    rows.append(jnp.sum(weight, axis=0, keepdims=True) * (cols_n // LANE))
    rows.append(jnp.zeros((4, LANE), jnp.float32))
    stats_ref[...] = jnp.concatenate(rows, axis=0)


def look_sums(pieces, res_ref, looks_n):
    here = lax.axis_index("date")
    _, _, rows_n, width = res_ref.shape
    middle_n = rows_n - 2 * LAG
    totals = [None, None]
    for at, (step, prim_ref) in enumerate(pieces):
        block = jnp.bitwise_xor(here, step)
        first = LAG if prim_ref.shape[1] == rows_n else 0
        select = look_columns(width, block, looks_n)
        pair = interfere(
            prim_ref[0, first : first + middle_n],
            prim_ref[1, first : first + middle_n],
            res_ref[block, 0, LAG : rows_n - LAG],
            res_ref[block, 1, LAG : rows_n - LAG],
        )
        for part in range(2):
            summed = jnp.dot(
                pair[part].astype(jnp.bfloat16), select, preferred_element_type=jnp.float32
            )
            totals[part] = summed if at == 0 else totals[part] + summed
    return totals


def middle_kernel(own_ref, one_ref, two_ref, res_ref, out_ref):
    pieces = ((0, own_ref), (1, one_ref), (2, two_ref))
    for part, total in enumerate(look_sums(pieces, res_ref, out_ref.shape[2])):
        out_ref[part] = total


def last_kernel(three_ref, res_ref, before_ref, looks_ref, out_ref, sums_ref):
    middle_n = before_ref.shape[1]
    edge = LAG // LA
    totals = look_sums(((3, three_ref),), res_ref, out_ref.shape[2])
    for part, total in enumerate(totals):
        sums_ref[part] = total + before_ref[part]
        out_ref[part, :edge] = looks_ref[part, :edge]
        out_ref[part, edge : edge + middle_n // LA] = look_rows(sums_ref, part, 0, middle_n)
        out_ref[part, edge + middle_n // LA :] = looks_ref[part, edge:]


def scale_kernel(looks_ref, mine_ref, other_ref, out_ref):
    stats = jnp.sum(mine_ref[...] + other_ref[...], axis=1, keepdims=True)
    e_re, e_im, power, count = [stats[row : row + 1] for row in range(4)]
    magnitude = jnp.sqrt(e_re * e_re + e_im * e_im)
    floor_val = (power + 1e-06) / jnp.sqrt(jnp.maximum(count, 1.0))
    denom = jnp.maximum(magnitude, floor_val)
    u_re = e_re / denom * (1.0 / (LA * LR))
    u_im = e_im / denom * (1.0 / (LA * LR))
    out_ref[0, 0] = looks_ref[0] * u_re + looks_ref[1] * u_im
    out_ref[0, 1] = looks_ref[1] * u_re - looks_ref[0] * u_im


def call(kernel, outs, scratch, cost, *args):
    vmem = pl.BlockSpec(memory_space=pltpu.VMEM)
    return pl.pallas_call(
        kernel,
        out_shape=outs,
        in_specs=[vmem] * len(args),
        out_specs=jax.tree.map(lambda _: vmem, outs),
        scratch_shapes=scratch,
        compiler_params=pltpu.CompilerParams(vmem_limit_bytes=VMEM_LIMIT),
        cost_estimate=pl.CostEstimate(flops=cost[0], bytes_accessed=cost[1], transcendentals=0),
    )(*args)


def ring(value, axis, step):
    count = lax.axis_size(axis)
    return lax.ppermute(value, axis, [(at, (at + step) % count) for at in range(count)])


def swap(value, axis, step):
    return lax.ppermute(value, axis, [(at, at ^ step) for at in range(lax.axis_size(axis))])


def fused(secondary, primary, margin_mask, az_off, rg_off, az_frac, rg_frac):
    _, _, rows_n, cols_n = secondary.shape
    width = primary.shape[2]
    dates_n = lax.axis_size("date")
    tiles_n = lax.axis_size("tile")
    bf16, f32 = jnp.bfloat16, jnp.float32
    shape = jax.ShapeDtypeStruct
    looks_n = cols_n // LR
    middle_n = rows_n - 2 * LAG
    edges = jnp.concatenate([primary[:, :LAG], primary[:, rows_n - LAG :]], axis=1)
    edges_two = swap(edges, "date", 2)
    edges_one = swap(edges, "date", 1)
    down, up = secondary[0, :, rows_n - HALO :], secondary[0, :, :HALO]
    low = ring(down, "tile", 1)
    high = ring(up, "tile", -1)
    az_band, rg_band = call(
        bands_kernel,
        (shape((BAND, BAND + 2 * HALO), bf16), shape((3, LANE, LANE), bf16)),
        [],
        (0, 0),
        az_off, rg_off, az_frac, rg_frac,
    )
    passed = call(
        relay_kernel, shape(edges.shape, bf16), [], (0, 0), edges_two
    )
    edges_three = swap(passed, "date", 1)
    middle = call(
        cut_middle_kernel,
        shape((2, middle_n + 16, width), bf16),
        [],
        (0, 0),
        primary, edges_two, edges_one,
    )
    weight = jnp.broadcast_to(margin_mask[rows_n - LAG :].astype(f32)[:, None], (LAG, LANE))
    res = call(
        resample_kernel,
        shape((dates_n, 2, rows_n, width), bf16),
        [pltpu.VMEM((2, rows_n, cols_n), bf16)],
        (0, 0),
        secondary, low, high, az_band, rg_band,
    )
    two, one = [swap(middle, "date", step) for step in (2, 1)]
    margin = shape((2, LAG, cols_n), bf16)
    first, last, looks = call(
        margin_kernel,
        (margin, margin, shape((2, 2 * LAG // LA, looks_n), f32)),
        [pltpu.VMEM((2, 2 * LAG, looks_n), f32)],
        (0, 0),
        primary, edges_one, edges_two, edges_three, res,
    )
    later = ring(first, "tile", -1)
    stats = call(
        stats_kernel,
        shape((8, LANE), f32),
        [],
        (0, 0),
        last, later, weight,
    )
    before = call(
        middle_kernel,
        shape((2, middle_n, looks_n), f32),
        [],
        (2 * 2 * middle_n * cols_n * looks_n, 8 * rows_n * cols_n),
        primary, one, two, res,
    )
    other = swap(stats, "tile", tiles_n // 2)
    block = shape((2, middle_n, width), bf16)
    relayed = call(relay_kernel, block, [], (0, 0), two, other,one)
    three = swap(relayed, "date", 1)
    stride = tiles_n // 4
    while stride:
        stats = stats + other
        other = swap(stats, "tile", stride)
        stride //= 2
    looks = call(
        last_kernel,
        shape((2, rows_n // LA, looks_n), f32),
        [pltpu.VMEM((2, middle_n, looks_n), f32)],
        (2 * middle_n * cols_n * looks_n, 4 * rows_n * cols_n),
        three, res, before, looks,
    )
    return call(
        scale_kernel,
        shape((1, 2, rows_n // LA, looks_n), f32),
        [],
        (8 * rows_n * looks_n, 8 * rows_n * looks_n),
        looks, stats, other,
    )


def padded(block, sides, width):
    for axis, dim in sides:
        low = passed_along(
            lax.slice_in_dim(block, block.shape[dim] - width, None, axis=dim), axis, 1
        )
        high = passed_along(lax.slice_in_dim(block, 0, width, axis=dim), axis, -1)
        block = jnp.concatenate([low, block, high], axis=dim)
    return block


def band_taps(offset, frac):
    inside = (offset >= -3) & (offset <= 4)
    return jnp.where(inside, window(offset.astype(jnp.float32) - frac), 0.0).astype(jnp.bfloat16)


def multilook(values):
    depth, rows_n, cols_n = values.shape
    return values.reshape(depth, rows_n // LA, LA, cols_n // LR, LR).mean(axis=(2, 4))


def plain(secondary, primary, margin_mask, az_off, rg_off, az_frac, rg_frac):
    rim_rows = KA + 4
    block_cols = 256
    image = secondary[0]
    rows_n = image.shape[1]
    cols_n = image.shape[2]
    extended = padded(image, (("tile", 1),), rim_rows)
    row_out = lax.broadcasted_iota(jnp.int32, (rows_n, rows_n + 2 * rim_rows), 0)
    row_in = lax.broadcasted_iota(jnp.int32, (rows_n, rows_n + 2 * rim_rows), 1)
    azim_taps = band_taps(row_in - row_out - az_off[0, 0] - rim_rows, az_frac[0, 0])
    azim = jnp.einsum(
        "im,kmc->kic", azim_taps, extended, preferred_element_type=jnp.float32
    ).astype(jnp.bfloat16)
    blocks_n = cols_n // block_cols
    col_pad = jnp.pad(azim, ((0, 0), (0, 0), (block_cols // 2, block_cols // 2)))
    pieces = col_pad.reshape(2, rows_n, blocks_n + 1, block_cols)
    inputs = jnp.concatenate([pieces[:, :, :-1], pieces[:, :, 1:]], axis=3)
    col_in = lax.broadcasted_iota(jnp.int32, (2 * block_cols, block_cols), 0)
    col_out = lax.broadcasted_iota(jnp.int32, (2 * block_cols, block_cols), 1)
    range_taps = band_taps(col_in - block_cols // 2 - col_out - rg_off[0, 0], rg_frac[0, 0])
    resampled = jnp.einsum("kibm,mn->kibn", inputs, range_taps, preferred_element_type=jnp.float32)
    resampled = resampled.reshape(2, rows_n, cols_n).astype(jnp.bfloat16)
    prim = lax.all_gather(primary, "date", axis=2, tiled=True)[None]
    sec_f = resampled[None].astype(jnp.float32)
    prim_f = prim.astype(jnp.float32)
    ifg_re = prim_f[:, 0] * sec_f[:, 0] + prim_f[:, 1] * sec_f[:, 1]
    ifg_im = prim_f[:, 1] * sec_f[:, 0] - prim_f[:, 0] * sec_f[:, 1]
    interf = jnp.stack((ifg_re, ifg_im), axis=1)
    upcoming = passed_along(interf[:, :, :LAG, :], "tile", -1)
    later = jnp.concatenate([interf[:, :, LAG:, :], upcoming], axis=2)
    l_re = later[:, 0]
    l_im = later[:, 1]
    weight = margin_mask.astype(jnp.float32)[None, :, None]
    e_re = jnp.sum(weight * (ifg_re * l_re + ifg_im * l_im), axis=(1, 2))
    e_im = jnp.sum(weight * (ifg_im * l_re - ifg_re * l_im), axis=(1, 2))
    power = jnp.sum(
        weight * 0.5 * (ifg_re * ifg_re + ifg_im * ifg_im + l_re * l_re + l_im * l_im), axis=(1, 2)
    )
    count = jnp.zeros_like(e_re) + jnp.sum(margin_mask.astype(jnp.float32)) * interf.shape[3]
    stats = jnp.stack((e_re, e_im, power, count), axis=1)
    totals = lax.psum(stats, "tile")
    magnitude = jnp.sqrt(totals[:, 0] * totals[:, 0] + totals[:, 1] * totals[:, 1])
    floor_val = (totals[:, 2] + 1e-06) / jnp.sqrt(jnp.maximum(totals[:, 3], 1.0))
    denom = jnp.maximum(magnitude, floor_val)
    u_re = (totals[:, 0] / denom)[:, None, None]
    u_im = (totals[:, 1] / denom)[:, None, None]
    c_re = multilook(ifg_re * u_re + ifg_im * u_im)
    c_im = multilook(ifg_im * u_re - ifg_re * u_im)
    return jnp.stack((c_re, c_im), axis=1)


def shards(secondary, primary, *rest):
    rows_n, width = primary.shape[1:]
    fits = rows_n % BAND == 0 and rows_n > 2 * LAG + BAND and width % LANE == 0
    tiles_n = lax.axis_size("tile")
    fits = fits and lax.axis_size("date") == 4 and tiles_n & (tiles_n - 1) == 0
    return (fused if fits else plain)(secondary, primary, *rest)


def solution(mesh):
    return jax.shard_map(
        shards,
        mesh=mesh,
        in_specs=(
            P("date", None, "tile", None),
            P(None, "tile", "date"),
            P("tile"),
            P("date", "tile"),
            P("date", "tile"),
            P("date", "tile"),
            P("date", "tile"),
        ),
        out_specs=P("date", None, "tile", None),
        check_vma=False,
    )
```

```python
import functools

import jax
import jax.numpy as jnp
from jax import lax
from jax.experimental import pallas as pl
from jax.experimental.pallas import tpu as pltpu
from jax.sharding import PartitionSpec as P

KA = 16
LAG = 64
LA = 2
LR = 8
LANE = 128
BAND = 128
HALO = 32
VMEM_LIMIT = 40 * 1024 * 1024


def passed_along(value, axis, steps):
    count = lax.axis_size(axis)
    initial, last = (max(0, -steps), min(count, count - steps))
    return lax.ppermute(value, axis, [(source, source + steps) for source in range(initial, last)])


def window(dist):
    return jnp.sinc(dist) * (0.5 + 0.5 * jnp.cos(jnp.pi * dist / 4.0))


def tap_rows(frac):
    dist = lax.broadcasted_iota(jnp.int32, (8, LANE), 0).astype(jnp.float32) - 3.0 - frac
    angle = jnp.pi * dist
    sinc = jnp.where(dist == 0.0, 1.0, jnp.sin(angle) / jnp.where(dist == 0.0, 1.0, angle))
    taps = sinc * (0.5 + 0.5 * jnp.cos(jnp.pi * dist / 4.0))
    return taps.astype(jnp.bfloat16).astype(jnp.float32)


def band(shape, distance, taps):
    total = jnp.zeros(shape, jnp.float32)
    for j in range(8):
        total = jnp.where(distance == j - 3, taps[j : j + 1, :1], total)
    return total.astype(jnp.bfloat16)


def cut_middle_kernel(prim_ref, *refs):
    cut_ref = refs[-1]
    cut_ref[...] = prim_ref[:, LAG : LAG + cut_ref.shape[1]]


def relay_kernel(block_ref, *refs):
    out_ref = refs[-1]
    out_ref[...] = block_ref[:, : out_ref.shape[1]]


def bands_kernel(ao_ref, ro_ref, af_ref, rf_ref, az_ref, rg_ref):
    shape = az_ref.shape
    offset = lax.broadcasted_iota(jnp.int32, shape, 1) - lax.broadcasted_iota(jnp.int32, shape, 0)
    az_ref[...] = band(shape, offset - HALO - ao_ref[...], tap_rows(af_ref[...]))
    square = rg_ref.shape[1:]
    offset = lax.broadcasted_iota(jnp.int32, square, 0) - lax.broadcasted_iota(jnp.int32, square, 1)
    taps = tap_rows(rf_ref[...])
    for at, shift in enumerate((-LANE, 0, LANE)):
        rg_ref[at] = band(square, offset + shift - ro_ref[...], taps)


def resample_kernel(sec_ref, low_ref, high_ref, az_ref, rg_ref, out_ref, azim_ref):
    rows_n, cols_n = sec_ref.shape[2:]
    az_band = az_ref[...]
    here, tiles_n = lax.axis_index("tile"), lax.axis_size("tile")
    none = jnp.zeros(low_ref.shape[1:], jnp.bfloat16)
    for part in range(2):
        for start in range(0, rows_n, BAND):
            pieces = []
            if start == 0:
                pieces.append(jnp.where(here == 0, none, low_ref[part]))
            pieces.append(sec_ref[0, part, max(0, start - HALO) : min(rows_n, start + BAND + HALO)])
            if start + BAND == rows_n:
                pieces.append(jnp.where(here == tiles_n - 1, none, high_ref[part]))
            rows = jnp.concatenate(pieces, axis=0) if len(pieces) > 1 else pieces[0]
            azim_ref[part, start : start + BAND] = jnp.dot(
                az_band, rows, preferred_element_type=jnp.float32
            ).astype(jnp.bfloat16)

    before, same, after = [rg_ref[at] for at in range(3)]
    none = jnp.zeros((LANE, LANE), jnp.bfloat16)
    blocks_n, _, _, width = out_ref.shape
    lanes_n = width // LANE
    columns = []
    for lane in range(lanes_n):
        column = [none] * (lanes_n + 2)
        column[lane], column[lane + 1], column[lane + 2] = before, same, after
        columns.append(jnp.concatenate(column, axis=0))
    rg_band = jnp.concatenate(columns, axis=1)
    for block in range(blocks_n):
        first = block * width - LANE
        last = (block + 1) * width + LANE
        taken = slice(max(first, 0), min(last, cols_n))
        used = rg_band[taken.start - first : taken.stop - first]
        for part in range(2):
            out_ref[block, part] = jnp.dot(
                azim_ref[part, :, taken], used, preferred_element_type=jnp.float32
            ).astype(jnp.bfloat16)


def interfere(prim_re, prim_im, sec_re, sec_im):
    p_re, p_im = prim_re.astype(jnp.float32), prim_im.astype(jnp.float32)
    s_re, s_im = sec_re.astype(jnp.float32), sec_im.astype(jnp.float32)
    return p_re * s_re + p_im * s_im, p_im * s_re - p_re * s_im


def look_columns(width, block, looks_n):
    shape = (width, looks_n)
    col = lax.broadcasted_iota(jnp.int32, shape, 0) + block * width
    look = lax.broadcasted_iota(jnp.int32, shape, 1) * LR
    return jnp.where((col >= look) & (col < look + LR), 1.0, 0.0).astype(jnp.bfloat16)


def look_rows(sums_ref, part, start, rows_n):
    count = rows_n // LA
    total = sums_ref[part, pl.ds(start, count, LA)]
    for row in range(1, LA):
        total = total + sums_ref[part, pl.ds(start + row, count, LA)]
    return total


def margin_kernel(
    own_ref, one_ref, two_ref, three_ref, res_ref, first_ref, last_ref, looks_ref, sums_ref
):
    here = lax.axis_index("date")
    _, _, rows_n, width = res_ref.shape
    whole, edges = (0, rows_n - LAG), (0, LAG)
    looks_n = looks_ref.shape[2]
    totals = [None, None]
    for step, (prim_ref, starts) in enumerate(
        ((own_ref, whole), (one_ref, edges), (two_ref, edges), (three_ref, edges))
    ):
        block = jnp.bitwise_xor(here, step)
        select = look_columns(width, block, looks_n)
        columns = pl.ds(pl.multiple_of(block * width, width), width)
        halves = []
        for held, start, target in zip(starts, whole, (first_ref, last_ref)):
            pair = interfere(
                prim_ref[0, held : held + LAG],
                prim_ref[1, held : held + LAG],
                res_ref[block, 0, start : start + LAG],
                res_ref[block, 1, start : start + LAG],
            )
            pair = [value.astype(jnp.bfloat16) for value in pair]
            for part in range(2):
                target[part, :, columns] = pair[part]
            halves.append(pair)
        both = jnp.concatenate([halves[at][part] for part in range(2) for at in range(2)], axis=0)
        sums = jnp.dot(both, select, preferred_element_type=jnp.float32)
        for part in range(2):
            summed = sums[part * 2 * LAG : (part + 1) * 2 * LAG]
            totals[part] = summed if step == 0 else totals[part] + summed
    for part in range(2):
        sums_ref[part] = totals[part]
        looks_ref[part] = look_rows(sums_ref, part, 0, 2 * LAG)


def stats_kernel(last_ref, later_ref, weight_ref, stats_ref):
    cols_n = last_ref.shape[2]
    weight = weight_ref[...]
    i_re, i_im = last_ref[0].astype(jnp.float32), last_ref[1].astype(jnp.float32)
    inside = jnp.where(lax.axis_index("tile") == lax.axis_size("tile") - 1, 0.0, 1.0)
    l_re, l_im = [later_ref[part].astype(jnp.float32) * inside for part in range(2)]
    values = (
        i_re * l_re + i_im * l_im,
        i_im * l_re - i_re * l_im,
        0.5 * (i_re * i_re + i_im * i_im + l_re * l_re + l_im * l_im),
    )
    rows = []
    for value in values:
        folded = value[:, :LANE]
        for start in range(LANE, cols_n, LANE):
            folded = folded + value[:, start : start + LANE]
        rows.append(jnp.sum(folded * weight, axis=0, keepdims=True))
    rows.append(jnp.sum(weight, axis=0, keepdims=True) * (cols_n // LANE))
    rows.append(jnp.zeros((4, LANE), jnp.float32))
    stats_ref[...] = jnp.concatenate(rows, axis=0)


def look_sums(pieces, res_ref, looks_n):
    here = lax.axis_index("date")
    _, _, rows_n, width = res_ref.shape
    middle_n = rows_n - 2 * LAG
    totals = [None, None]
    for at, (step, prim_ref) in enumerate(pieces):
        block = jnp.bitwise_xor(here, step)
        first = LAG if prim_ref.shape[1] == rows_n else 0
        select = look_columns(width, block, looks_n)
        pair = interfere(
            prim_ref[0, first : first + middle_n],
            prim_ref[1, first : first + middle_n],
            res_ref[block, 0, LAG : rows_n - LAG],
            res_ref[block, 1, LAG : rows_n - LAG],
        )
        both = jnp.concatenate([value.astype(jnp.bfloat16) for value in pair], axis=0)
        sums = jnp.dot(both, select, preferred_element_type=jnp.float32)
        for part in range(2):
            summed = sums[part * middle_n : (part + 1) * middle_n]
            totals[part] = summed if at == 0 else totals[part] + summed
    return totals


def middle_kernel(own_ref, one_ref, two_ref, res_ref, out_ref):
    pieces = ((0, own_ref), (1, one_ref), (2, two_ref))
    for part, total in enumerate(look_sums(pieces, res_ref, out_ref.shape[2])):
        out_ref[part] = total


def last_kernel(three_ref, res_ref, before_ref, looks_ref, out_ref, sums_ref):
    middle_n = before_ref.shape[1]
    edge = LAG // LA
    totals = look_sums(((3, three_ref),), res_ref, out_ref.shape[2])
    for part, total in enumerate(totals):
        sums_ref[part] = total + before_ref[part]
        out_ref[part, :edge] = looks_ref[part, :edge]
        out_ref[part, edge : edge + middle_n // LA] = look_rows(sums_ref, part, 0, middle_n)
        out_ref[part, edge + middle_n // LA :] = looks_ref[part, edge:]


def scale_kernel(looks_ref, mine_ref, other_ref, out_ref):
    stats = jnp.sum(mine_ref[...] + other_ref[...], axis=1, keepdims=True)
    e_re, e_im, power, count = [stats[row : row + 1] for row in range(4)]
    magnitude = jnp.sqrt(e_re * e_re + e_im * e_im)
    floor_val = (power + 1e-06) / jnp.sqrt(jnp.maximum(count, 1.0))
    denom = jnp.maximum(magnitude, floor_val)
    u_re = e_re / denom * (1.0 / (LA * LR))
    u_im = e_im / denom * (1.0 / (LA * LR))
    out_ref[0, 0] = looks_ref[0] * u_re + looks_ref[1] * u_im
    out_ref[0, 1] = looks_ref[1] * u_re - looks_ref[0] * u_im


def call(kernel, outs, scratch, cost, *args):
    vmem = pl.BlockSpec(memory_space=pltpu.VMEM)
    return pl.pallas_call(
        kernel,
        out_shape=outs,
        in_specs=[vmem] * len(args),
        out_specs=jax.tree.map(lambda _: vmem, outs),
        scratch_shapes=scratch,
        compiler_params=pltpu.CompilerParams(vmem_limit_bytes=VMEM_LIMIT),
        cost_estimate=pl.CostEstimate(flops=cost[0], bytes_accessed=cost[1], transcendentals=0),
    )(*args)


def ring(value, axis, step):
    count = lax.axis_size(axis)
    return lax.ppermute(value, axis, [(at, (at + step) % count) for at in range(count)])


def swap(value, axis, step):
    return lax.ppermute(value, axis, [(at, at ^ step) for at in range(lax.axis_size(axis))])


def fused(secondary, primary, margin_mask, az_off, rg_off, az_frac, rg_frac):
    _, _, rows_n, cols_n = secondary.shape
    width = primary.shape[2]
    dates_n = lax.axis_size("date")
    tiles_n = lax.axis_size("tile")
    bf16, f32 = jnp.bfloat16, jnp.float32
    shape = jax.ShapeDtypeStruct
    looks_n = cols_n // LR
    middle_n = rows_n - 2 * LAG
    edges = jnp.concatenate([primary[:, :LAG], primary[:, rows_n - LAG :]], axis=1)
    edges_two = swap(edges, "date", 2)
    edges_one = swap(edges, "date", 1)
    down, up = secondary[0, :, rows_n - HALO :], secondary[0, :, :HALO]
    low = ring(down, "tile", 1)
    high = ring(up, "tile", -1)
    az_band, rg_band = call(
        bands_kernel,
        (shape((BAND, BAND + 2 * HALO), bf16), shape((3, LANE, LANE), bf16)),
        [],
        (0, 0),
        az_off, rg_off, az_frac, rg_frac,
    )
    passed = call(
        relay_kernel, shape(edges.shape, bf16), [], (0, 0), edges_two
    )
    edges_three = swap(passed, "date", 1)
    middle = call(
        cut_middle_kernel,
        shape((2, middle_n + 16, width), bf16),
        [],
        (0, 0),
        primary, edges_two, edges_one,
    )
    weight = jnp.broadcast_to(margin_mask[rows_n - LAG :].astype(f32)[:, None], (LAG, LANE))
    res = call(
        resample_kernel,
        shape((dates_n, 2, rows_n, width), bf16),
        [pltpu.VMEM((2, rows_n, cols_n), bf16)],
        (0, 0),
        secondary, low, high, az_band, rg_band,
    )
    two, one = [swap(middle, "date", step) for step in (2, 1)]
    margin = shape((2, LAG, cols_n), bf16)
    first, last, looks = call(
        margin_kernel,
        (margin, margin, shape((2, 2 * LAG // LA, looks_n), f32)),
        [pltpu.VMEM((2, 2 * LAG, looks_n), f32)],
        (0, 0),
        primary, edges_one, edges_two, edges_three, res,
    )
    later = ring(first, "tile", -1)
    stats = call(
        stats_kernel,
        shape((8, LANE), f32),
        [],
        (0, 0),
        last, later, weight,
    )
    before = call(
        middle_kernel,
        shape((2, middle_n, looks_n), f32),
        [],
        (2 * 2 * middle_n * cols_n * looks_n, 8 * rows_n * cols_n),
        primary, one, two, res,
    )
    other = swap(stats, "tile", 1)
    block = shape((2, middle_n, width), bf16)
    relayed = call(relay_kernel, block, [], (0, 0), two, other,one)
    three = swap(relayed, "date", 1)
    stride = 2
    while stride < tiles_n:
        stats = stats + other
        other = swap(stats, "tile", stride)
        stride *= 2
    looks = call(
        last_kernel,
        shape((2, rows_n // LA, looks_n), f32),
        [pltpu.VMEM((2, middle_n, looks_n), f32)],
        (2 * middle_n * cols_n * looks_n, 4 * rows_n * cols_n),
        three, res, before, looks,
    )
    return call(
        scale_kernel,
        shape((1, 2, rows_n // LA, looks_n), f32),
        [],
        (8 * rows_n * looks_n, 8 * rows_n * looks_n),
        looks, stats, other,
    )


def padded(block, sides, width):
    for axis, dim in sides:
        low = passed_along(
            lax.slice_in_dim(block, block.shape[dim] - width, None, axis=dim), axis, 1
        )
        high = passed_along(lax.slice_in_dim(block, 0, width, axis=dim), axis, -1)
        block = jnp.concatenate([low, block, high], axis=dim)
    return block


def band_taps(offset, frac):
    inside = (offset >= -3) & (offset <= 4)
    return jnp.where(inside, window(offset.astype(jnp.float32) - frac), 0.0).astype(jnp.bfloat16)


def multilook(values):
    depth, rows_n, cols_n = values.shape
    return values.reshape(depth, rows_n // LA, LA, cols_n // LR, LR).mean(axis=(2, 4))


def plain(secondary, primary, margin_mask, az_off, rg_off, az_frac, rg_frac):
    rim_rows = KA + 4
    block_cols = 256
    image = secondary[0]
    rows_n = image.shape[1]
    cols_n = image.shape[2]
    extended = padded(image, (("tile", 1),), rim_rows)
    row_out = lax.broadcasted_iota(jnp.int32, (rows_n, rows_n + 2 * rim_rows), 0)
    row_in = lax.broadcasted_iota(jnp.int32, (rows_n, rows_n + 2 * rim_rows), 1)
    azim_taps = band_taps(row_in - row_out - az_off[0, 0] - rim_rows, az_frac[0, 0])
    azim = jnp.einsum(
        "im,kmc->kic", azim_taps, extended, preferred_element_type=jnp.float32
    ).astype(jnp.bfloat16)
    blocks_n = cols_n // block_cols
    col_pad = jnp.pad(azim, ((0, 0), (0, 0), (block_cols // 2, block_cols // 2)))
    pieces = col_pad.reshape(2, rows_n, blocks_n + 1, block_cols)
    inputs = jnp.concatenate([pieces[:, :, :-1], pieces[:, :, 1:]], axis=3)
    col_in = lax.broadcasted_iota(jnp.int32, (2 * block_cols, block_cols), 0)
    col_out = lax.broadcasted_iota(jnp.int32, (2 * block_cols, block_cols), 1)
    range_taps = band_taps(col_in - block_cols // 2 - col_out - rg_off[0, 0], rg_frac[0, 0])
    resampled = jnp.einsum("kibm,mn->kibn", inputs, range_taps, preferred_element_type=jnp.float32)
    resampled = resampled.reshape(2, rows_n, cols_n).astype(jnp.bfloat16)
    prim = lax.all_gather(primary, "date", axis=2, tiled=True)[None]
    sec_f = resampled[None].astype(jnp.float32)
    prim_f = prim.astype(jnp.float32)
    ifg_re = prim_f[:, 0] * sec_f[:, 0] + prim_f[:, 1] * sec_f[:, 1]
    ifg_im = prim_f[:, 1] * sec_f[:, 0] - prim_f[:, 0] * sec_f[:, 1]
    interf = jnp.stack((ifg_re, ifg_im), axis=1)
    upcoming = passed_along(interf[:, :, :LAG, :], "tile", -1)
    later = jnp.concatenate([interf[:, :, LAG:, :], upcoming], axis=2)
    l_re = later[:, 0]
    l_im = later[:, 1]
    weight = margin_mask.astype(jnp.float32)[None, :, None]
    e_re = jnp.sum(weight * (ifg_re * l_re + ifg_im * l_im), axis=(1, 2))
    e_im = jnp.sum(weight * (ifg_im * l_re - ifg_re * l_im), axis=(1, 2))
    power = jnp.sum(
        weight * 0.5 * (ifg_re * ifg_re + ifg_im * ifg_im + l_re * l_re + l_im * l_im), axis=(1, 2)
    )
    count = jnp.zeros_like(e_re) + jnp.sum(margin_mask.astype(jnp.float32)) * interf.shape[3]
    stats = jnp.stack((e_re, e_im, power, count), axis=1)
    totals = lax.psum(stats, "tile")
    magnitude = jnp.sqrt(totals[:, 0] * totals[:, 0] + totals[:, 1] * totals[:, 1])
    floor_val = (totals[:, 2] + 1e-06) / jnp.sqrt(jnp.maximum(totals[:, 3], 1.0))
    denom = jnp.maximum(magnitude, floor_val)
    u_re = (totals[:, 0] / denom)[:, None, None]
    u_im = (totals[:, 1] / denom)[:, None, None]
    c_re = multilook(ifg_re * u_re + ifg_im * u_im)
    c_im = multilook(ifg_im * u_re - ifg_re * u_im)
    return jnp.stack((c_re, c_im), axis=1)


def shards(secondary, primary, *rest):
    rows_n, width = primary.shape[1:]
    fits = rows_n % BAND == 0 and rows_n > 2 * LAG + BAND and width % LANE == 0
    tiles_n = lax.axis_size("tile")
    fits = fits and lax.axis_size("date") == 4 and tiles_n & (tiles_n - 1) == 0
    return (fused if fits else plain)(secondary, primary, *rest)


def solution(mesh):
    return jax.shard_map(
        shards,
        mesh=mesh,
        in_specs=(
            P("date", None, "tile", None),
            P(None, "tile", "date"),
            P("tile"),
            P("date", "tile"),
            P("date", "tile"),
            P("date", "tile"),
            P("date", "tile"),
        ),
        out_specs=P("date", None, "tile", None),
        check_vma=False,
    )
```

```python
import functools

import jax
import jax.numpy as jnp
from jax import lax
from jax.experimental import pallas as pl
from jax.experimental.pallas import tpu as pltpu
from jax.sharding import PartitionSpec as P

KA = 16
LAG = 64
LA = 2
LR = 8
LANE = 128
BAND = 128
HALO = 32
VMEM_LIMIT = 40 * 1024 * 1024


def passed_along(value, axis, steps):
    count = lax.axis_size(axis)
    initial, last = (max(0, -steps), min(count, count - steps))
    return lax.ppermute(value, axis, [(source, source + steps) for source in range(initial, last)])


def window(dist):
    return jnp.sinc(dist) * (0.5 + 0.5 * jnp.cos(jnp.pi * dist / 4.0))


def tap_rows(frac):
    dist = lax.broadcasted_iota(jnp.int32, (8, LANE), 0).astype(jnp.float32) - 3.0 - frac
    angle = jnp.pi * dist
    sinc = jnp.where(dist == 0.0, 1.0, jnp.sin(angle) / jnp.where(dist == 0.0, 1.0, angle))
    taps = sinc * (0.5 + 0.5 * jnp.cos(jnp.pi * dist / 4.0))
    return taps.astype(jnp.bfloat16).astype(jnp.float32)


def band(shape, distance, taps):
    total = jnp.zeros(shape, jnp.float32)
    for j in range(8):
        total = jnp.where(distance == j - 3, taps[j : j + 1, :1], total)
    return total.astype(jnp.bfloat16)


def cut_middle_kernel(prim_ref, *refs):
    cut_ref = refs[-1]
    cut_ref[...] = prim_ref[:, LAG : LAG + cut_ref.shape[1]]


def relay_kernel(block_ref, *refs):
    out_ref = refs[-1]
    out_ref[...] = block_ref[:, : out_ref.shape[1]]


def bands_kernel(ao_ref, ro_ref, af_ref, rf_ref, az_ref, rg_ref):
    shape = az_ref.shape
    offset = lax.broadcasted_iota(jnp.int32, shape, 1) - lax.broadcasted_iota(jnp.int32, shape, 0)
    az_ref[...] = band(shape, offset - HALO - ao_ref[...], tap_rows(af_ref[...]))
    square = rg_ref.shape[1:]
    offset = lax.broadcasted_iota(jnp.int32, square, 0) - lax.broadcasted_iota(jnp.int32, square, 1)
    taps = tap_rows(rf_ref[...])
    for at, shift in enumerate((-LANE, 0, LANE)):
        rg_ref[at] = band(square, offset + shift - ro_ref[...], taps)


def resample_kernel(sec_ref, low_ref, high_ref, az_ref, rg_ref, out_ref, azim_ref):
    rows_n, cols_n = sec_ref.shape[2:]
    az_band = az_ref[...]
    here, tiles_n = lax.axis_index("tile"), lax.axis_size("tile")
    none = jnp.zeros(low_ref.shape[1:], jnp.bfloat16)
    for part in range(2):
        for start in range(0, rows_n, BAND):
            pieces = []
            if start == 0:
                pieces.append(jnp.where(here == 0, none, low_ref[part]))
            pieces.append(sec_ref[0, part, max(0, start - HALO) : min(rows_n, start + BAND + HALO)])
            if start + BAND == rows_n:
                pieces.append(jnp.where(here == tiles_n - 1, none, high_ref[part]))
            rows = jnp.concatenate(pieces, axis=0) if len(pieces) > 1 else pieces[0]
            azim_ref[part, start : start + BAND] = jnp.dot(
                az_band, rows, preferred_element_type=jnp.float32
            ).astype(jnp.bfloat16)

    before, same, after = [rg_ref[at] for at in range(3)]
    none = jnp.zeros((LANE, LANE), jnp.bfloat16)
    blocks_n, _, _, width = out_ref.shape
    lanes_n = width // LANE
    columns = []
    for lane in range(lanes_n):
        column = [none] * (lanes_n + 2)
        column[lane], column[lane + 1], column[lane + 2] = before, same, after
        columns.append(jnp.concatenate(column, axis=0))
    rg_band = jnp.concatenate(columns, axis=1)
    for block in range(blocks_n):
        first = block * width - LANE
        last = (block + 1) * width + LANE
        taken = slice(max(first, 0), min(last, cols_n))
        used = rg_band[taken.start - first : taken.stop - first]
        both = jnp.concatenate([azim_ref[part, :, taken] for part in range(2)], axis=0)
        sums = jnp.dot(both, used, preferred_element_type=jnp.float32).astype(jnp.bfloat16)
        for part in range(2):
            out_ref[block, part] = sums[part * rows_n : (part + 1) * rows_n]


def interfere(prim_re, prim_im, sec_re, sec_im):
    p_re, p_im = prim_re.astype(jnp.float32), prim_im.astype(jnp.float32)
    s_re, s_im = sec_re.astype(jnp.float32), sec_im.astype(jnp.float32)
    return p_re * s_re + p_im * s_im, p_im * s_re - p_re * s_im


def look_columns(width, block, looks_n):
    shape = (width, looks_n)
    col = lax.broadcasted_iota(jnp.int32, shape, 0) + block * width
    look = lax.broadcasted_iota(jnp.int32, shape, 1) * LR
    return jnp.where((col >= look) & (col < look + LR), 1.0, 0.0).astype(jnp.bfloat16)


def look_rows(sums_ref, part, start, rows_n):
    count = rows_n // LA
    total = sums_ref[part, pl.ds(start, count, LA)]
    for row in range(1, LA):
        total = total + sums_ref[part, pl.ds(start + row, count, LA)]
    return total


def margin_kernel(
    own_ref, one_ref, two_ref, three_ref, res_ref, first_ref, last_ref, looks_ref, sums_ref
):
    here = lax.axis_index("date")
    _, _, rows_n, width = res_ref.shape
    whole, edges = (0, rows_n - LAG), (0, LAG)
    looks_n = looks_ref.shape[2]
    totals = [None, None]
    for step, (prim_ref, starts) in enumerate(
        ((own_ref, whole), (one_ref, edges), (two_ref, edges), (three_ref, edges))
    ):
        block = jnp.bitwise_xor(here, step)
        select = look_columns(width, block, looks_n)
        columns = pl.ds(pl.multiple_of(block * width, width), width)
        halves = []
        for held, start, target in zip(starts, whole, (first_ref, last_ref)):
            pair = interfere(
                prim_ref[0, held : held + LAG],
                prim_ref[1, held : held + LAG],
                res_ref[block, 0, start : start + LAG],
                res_ref[block, 1, start : start + LAG],
            )
            pair = [value.astype(jnp.bfloat16) for value in pair]
            for part in range(2):
                target[part, :, columns] = pair[part]
            halves.append(pair)
        both = jnp.concatenate([halves[at][part] for part in range(2) for at in range(2)], axis=0)
        sums = jnp.dot(both, select, preferred_element_type=jnp.float32)
        for part in range(2):
            summed = sums[part * 2 * LAG : (part + 1) * 2 * LAG]
            totals[part] = summed if step == 0 else totals[part] + summed
    for part in range(2):
        sums_ref[part] = totals[part]
        looks_ref[part] = look_rows(sums_ref, part, 0, 2 * LAG)


def stats_kernel(last_ref, later_ref, weight_ref, stats_ref):
    cols_n = last_ref.shape[2]
    weight = weight_ref[...]
    i_re, i_im = last_ref[0].astype(jnp.float32), last_ref[1].astype(jnp.float32)
    inside = jnp.where(lax.axis_index("tile") == lax.axis_size("tile") - 1, 0.0, 1.0)
    l_re, l_im = [later_ref[part].astype(jnp.float32) * inside for part in range(2)]
    values = (
        i_re * l_re + i_im * l_im,
        i_im * l_re - i_re * l_im,
        0.5 * (i_re * i_re + i_im * i_im + l_re * l_re + l_im * l_im),
    )
    rows = []
    for value in values:
        folded = value[:, :LANE]
        for start in range(LANE, cols_n, LANE):
            folded = folded + value[:, start : start + LANE]
        rows.append(jnp.sum(folded * weight, axis=0, keepdims=True))
    rows.append(jnp.sum(weight, axis=0, keepdims=True) * (cols_n // LANE))
    rows.append(jnp.zeros((4, LANE), jnp.float32))
    stats_ref[...] = jnp.concatenate(rows, axis=0)


def look_sums(pieces, res_ref, looks_n):
    here = lax.axis_index("date")
    _, _, rows_n, width = res_ref.shape
    middle_n = rows_n - 2 * LAG
    totals = [None, None]
    for at, (step, prim_ref) in enumerate(pieces):
        block = jnp.bitwise_xor(here, step)
        first = LAG if prim_ref.shape[1] == rows_n else 0
        select = look_columns(width, block, looks_n)
        pair = interfere(
            prim_ref[0, first : first + middle_n],
            prim_ref[1, first : first + middle_n],
            res_ref[block, 0, LAG : rows_n - LAG],
            res_ref[block, 1, LAG : rows_n - LAG],
        )
        both = jnp.concatenate([value.astype(jnp.bfloat16) for value in pair], axis=0)
        sums = jnp.dot(both, select, preferred_element_type=jnp.float32)
        for part in range(2):
            summed = sums[part * middle_n : (part + 1) * middle_n]
            totals[part] = summed if at == 0 else totals[part] + summed
    return totals


def middle_kernel(own_ref, one_ref, two_ref, res_ref, out_ref):
    pieces = ((0, own_ref), (1, one_ref), (2, two_ref))
    for part, total in enumerate(look_sums(pieces, res_ref, out_ref.shape[2])):
        out_ref[part] = total


def last_kernel(three_ref, res_ref, before_ref, looks_ref, out_ref, sums_ref):
    middle_n = before_ref.shape[1]
    edge = LAG // LA
    totals = look_sums(((3, three_ref),), res_ref, out_ref.shape[2])
    for part, total in enumerate(totals):
        sums_ref[part] = total + before_ref[part]
        out_ref[part, :edge] = looks_ref[part, :edge]
        out_ref[part, edge : edge + middle_n // LA] = look_rows(sums_ref, part, 0, middle_n)
        out_ref[part, edge + middle_n // LA :] = looks_ref[part, edge:]


def scale_kernel(looks_ref, mine_ref, other_ref, out_ref):
    stats = jnp.sum(mine_ref[...] + other_ref[...], axis=1, keepdims=True)
    e_re, e_im, power, count = [stats[row : row + 1] for row in range(4)]
    magnitude = jnp.sqrt(e_re * e_re + e_im * e_im)
    floor_val = (power + 1e-06) / jnp.sqrt(jnp.maximum(count, 1.0))
    denom = jnp.maximum(magnitude, floor_val)
    u_re = e_re / denom * (1.0 / (LA * LR))
    u_im = e_im / denom * (1.0 / (LA * LR))
    out_ref[0, 0] = looks_ref[0] * u_re + looks_ref[1] * u_im
    out_ref[0, 1] = looks_ref[1] * u_re - looks_ref[0] * u_im


def call(kernel, outs, scratch, cost, *args):
    vmem = pl.BlockSpec(memory_space=pltpu.VMEM)
    return pl.pallas_call(
        kernel,
        out_shape=outs,
        in_specs=[vmem] * len(args),
        out_specs=jax.tree.map(lambda _: vmem, outs),
        scratch_shapes=scratch,
        compiler_params=pltpu.CompilerParams(vmem_limit_bytes=VMEM_LIMIT),
        cost_estimate=pl.CostEstimate(flops=cost[0], bytes_accessed=cost[1], transcendentals=0),
    )(*args)


def ring(value, axis, step):
    count = lax.axis_size(axis)
    return lax.ppermute(value, axis, [(at, (at + step) % count) for at in range(count)])


def swap(value, axis, step):
    return lax.ppermute(value, axis, [(at, at ^ step) for at in range(lax.axis_size(axis))])


def fused(secondary, primary, margin_mask, az_off, rg_off, az_frac, rg_frac):
    _, _, rows_n, cols_n = secondary.shape
    width = primary.shape[2]
    dates_n = lax.axis_size("date")
    tiles_n = lax.axis_size("tile")
    bf16, f32 = jnp.bfloat16, jnp.float32
    shape = jax.ShapeDtypeStruct
    looks_n = cols_n // LR
    middle_n = rows_n - 2 * LAG
    edges = jnp.concatenate([primary[:, :LAG], primary[:, rows_n - LAG :]], axis=1)
    edges_two = swap(edges, "date", 2)
    edges_one = swap(edges, "date", 1)
    down, up = secondary[0, :, rows_n - HALO :], secondary[0, :, :HALO]
    low = ring(down, "tile", 1)
    high = ring(up, "tile", -1)
    az_band, rg_band = call(
        bands_kernel,
        (shape((BAND, BAND + 2 * HALO), bf16), shape((3, LANE, LANE), bf16)),
        [],
        (0, 0),
        az_off, rg_off, az_frac, rg_frac,
    )
    passed = call(
        relay_kernel, shape(edges.shape, bf16), [], (0, 0), edges_two
    )
    edges_three = swap(passed, "date", 1)
    middle = call(
        cut_middle_kernel,
        shape((2, middle_n + 16, width), bf16),
        [],
        (0, 0),
        primary, edges_two, edges_one,
    )
    weight = jnp.broadcast_to(margin_mask[rows_n - LAG :].astype(f32)[:, None], (LAG, LANE))
    res = call(
        resample_kernel,
        shape((dates_n, 2, rows_n, width), bf16),
        [pltpu.VMEM((2, rows_n, cols_n), bf16)],
        (0, 0),
        secondary, low, high, az_band, rg_band,
    )
    two, one = [swap(middle, "date", step) for step in (2, 1)]
    margin = shape((2, LAG, cols_n), bf16)
    first, last, looks = call(
        margin_kernel,
        (margin, margin, shape((2, 2 * LAG // LA, looks_n), f32)),
        [pltpu.VMEM((2, 2 * LAG, looks_n), f32)],
        (0, 0),
        primary, edges_one, edges_two, edges_three, res,
    )
    later = ring(first, "tile", -1)
    stats = call(
        stats_kernel,
        shape((8, LANE), f32),
        [],
        (0, 0),
        last, later, weight,
    )
    before = call(
        middle_kernel,
        shape((2, middle_n, looks_n), f32),
        [],
        (2 * 2 * middle_n * cols_n * looks_n, 8 * rows_n * cols_n),
        primary, one, two, res,
    )
    other = swap(stats, "tile", 1)
    block = shape((2, middle_n, width), bf16)
    relayed = call(relay_kernel, block, [], (0, 0), two, other,one)
    three = swap(relayed, "date", 1)
    stride = 2
    while stride < tiles_n:
        stats = stats + other
        other = swap(stats, "tile", stride)
        stride *= 2
    looks = call(
        last_kernel,
        shape((2, rows_n // LA, looks_n), f32),
        [pltpu.VMEM((2, middle_n, looks_n), f32)],
        (2 * middle_n * cols_n * looks_n, 4 * rows_n * cols_n),
        three, res, before, looks,
    )
    return call(
        scale_kernel,
        shape((1, 2, rows_n // LA, looks_n), f32),
        [],
        (8 * rows_n * looks_n, 8 * rows_n * looks_n),
        looks, stats, other,
    )


def padded(block, sides, width):
    for axis, dim in sides:
        low = passed_along(
            lax.slice_in_dim(block, block.shape[dim] - width, None, axis=dim), axis, 1
        )
        high = passed_along(lax.slice_in_dim(block, 0, width, axis=dim), axis, -1)
        block = jnp.concatenate([low, block, high], axis=dim)
    return block


def band_taps(offset, frac):
    inside = (offset >= -3) & (offset <= 4)
    return jnp.where(inside, window(offset.astype(jnp.float32) - frac), 0.0).astype(jnp.bfloat16)


def multilook(values):
    depth, rows_n, cols_n = values.shape
    return values.reshape(depth, rows_n // LA, LA, cols_n // LR, LR).mean(axis=(2, 4))


def plain(secondary, primary, margin_mask, az_off, rg_off, az_frac, rg_frac):
    rim_rows = KA + 4
    block_cols = 256
    image = secondary[0]
    rows_n = image.shape[1]
    cols_n = image.shape[2]
    extended = padded(image, (("tile", 1),), rim_rows)
    row_out = lax.broadcasted_iota(jnp.int32, (rows_n, rows_n + 2 * rim_rows), 0)
    row_in = lax.broadcasted_iota(jnp.int32, (rows_n, rows_n + 2 * rim_rows), 1)
    azim_taps = band_taps(row_in - row_out - az_off[0, 0] - rim_rows, az_frac[0, 0])
    azim = jnp.einsum(
        "im,kmc->kic", azim_taps, extended, preferred_element_type=jnp.float32
    ).astype(jnp.bfloat16)
    blocks_n = cols_n // block_cols
    col_pad = jnp.pad(azim, ((0, 0), (0, 0), (block_cols // 2, block_cols // 2)))
    pieces = col_pad.reshape(2, rows_n, blocks_n + 1, block_cols)
    inputs = jnp.concatenate([pieces[:, :, :-1], pieces[:, :, 1:]], axis=3)
    col_in = lax.broadcasted_iota(jnp.int32, (2 * block_cols, block_cols), 0)
    col_out = lax.broadcasted_iota(jnp.int32, (2 * block_cols, block_cols), 1)
    range_taps = band_taps(col_in - block_cols // 2 - col_out - rg_off[0, 0], rg_frac[0, 0])
    resampled = jnp.einsum("kibm,mn->kibn", inputs, range_taps, preferred_element_type=jnp.float32)
    resampled = resampled.reshape(2, rows_n, cols_n).astype(jnp.bfloat16)
    prim = lax.all_gather(primary, "date", axis=2, tiled=True)[None]
    sec_f = resampled[None].astype(jnp.float32)
    prim_f = prim.astype(jnp.float32)
    ifg_re = prim_f[:, 0] * sec_f[:, 0] + prim_f[:, 1] * sec_f[:, 1]
    ifg_im = prim_f[:, 1] * sec_f[:, 0] - prim_f[:, 0] * sec_f[:, 1]
    interf = jnp.stack((ifg_re, ifg_im), axis=1)
    upcoming = passed_along(interf[:, :, :LAG, :], "tile", -1)
    later = jnp.concatenate([interf[:, :, LAG:, :], upcoming], axis=2)
    l_re = later[:, 0]
    l_im = later[:, 1]
    weight = margin_mask.astype(jnp.float32)[None, :, None]
    e_re = jnp.sum(weight * (ifg_re * l_re + ifg_im * l_im), axis=(1, 2))
    e_im = jnp.sum(weight * (ifg_im * l_re - ifg_re * l_im), axis=(1, 2))
    power = jnp.sum(
        weight * 0.5 * (ifg_re * ifg_re + ifg_im * ifg_im + l_re * l_re + l_im * l_im), axis=(1, 2)
    )
    count = jnp.zeros_like(e_re) + jnp.sum(margin_mask.astype(jnp.float32)) * interf.shape[3]
    stats = jnp.stack((e_re, e_im, power, count), axis=1)
    totals = lax.psum(stats, "tile")
    magnitude = jnp.sqrt(totals[:, 0] * totals[:, 0] + totals[:, 1] * totals[:, 1])
    floor_val = (totals[:, 2] + 1e-06) / jnp.sqrt(jnp.maximum(totals[:, 3], 1.0))
    denom = jnp.maximum(magnitude, floor_val)
    u_re = (totals[:, 0] / denom)[:, None, None]
    u_im = (totals[:, 1] / denom)[:, None, None]
    c_re = multilook(ifg_re * u_re + ifg_im * u_im)
    c_im = multilook(ifg_im * u_re - ifg_re * u_im)
    return jnp.stack((c_re, c_im), axis=1)


def shards(secondary, primary, *rest):
    rows_n, width = primary.shape[1:]
    fits = rows_n % BAND == 0 and rows_n > 2 * LAG + BAND and width % LANE == 0
    tiles_n = lax.axis_size("tile")
    fits = fits and lax.axis_size("date") == 4 and tiles_n & (tiles_n - 1) == 0
    return (fused if fits else plain)(secondary, primary, *rest)


def solution(mesh):
    return jax.shard_map(
        shards,
        mesh=mesh,
        in_specs=(
            P("date", None, "tile", None),
            P(None, "tile", "date"),
            P("tile"),
            P("date", "tile"),
            P("date", "tile"),
            P("date", "tile"),
            P("date", "tile"),
        ),
        out_specs=P("date", None, "tile", None),
        check_vma=False,
    )
```
